32 devices in a mesh: blk: 4 (over y, core), batch: 8 (over z, x).
Axes of the slice: x: 2, y: 2, z: 4, core: 2. Of those that a mesh axis runs over, the one named last changes fastest.
Arguments:
- features: bfloat16 [8, 32, 40, 2048], P('batch', 'blk')
- crop_rows: int32 [8], replicated, may hold values from 25 to 32, as said below
- crop_cols: int32 [8], replicated, may hold values from 20 to 40, as said below
- depth_target: float32 [8, 32, 40], P('batch', 'blk'), may hold values from -6 to 6
- labels: int32 [8, 32, 40], P('batch', 'blk'), may hold values from 0 to 39
- first_weight: bfloat16 [2048, 512], P('batch'), may hold values from -0.125 to 0.125
- spatial_weight: bfloat16 [9, 512, 512], P(None, 'batch'), may hold values from -0.09375 to 0.09375
- last_weight: bfloat16 [512, 2048], P('batch'), may hold values from -0.25 to 0.25
- shared_weight: bfloat16 [2048, 512], P('batch'), may hold values from -0.125 to 0.125
- head_weights: bfloat16 [4, 9, 512, 512], P(None, None, 'batch'), may hold values from -0.09375 to 0.09375
- message_weights: bfloat16 [4, 9, 512, 512], P(None, None, 'batch'), may hold values from -0.09375 to 0.09375
- gate_weights: bfloat16 [4, 512, 512], P(None, 'batch'), may hold values from -0.25 to 0.25
- depth_weight: bfloat16 [512], P('batch'), may hold values from -0.5 to 0.5
- class_weight: bfloat16 [512, 40], P('batch'), may hold values from -0.5 to 0.5
- mid_gain: bfloat16 [7, 512], P(None, 'batch'), may hold values from 0.099609375 to 1.8984375
- mid_bias: bfloat16 [7, 512], P(None, 'batch'), may hold values from -0.5 to 0.5
- out_gain: bfloat16 [2048], P('batch'), may hold values from 0.099609375 to 1.8984375
- out_bias: bfloat16 [2048], P('batch'), may hold values from -0.5 to 0.5
Outputs:
- depth_map: float32 [8, 32, 40], P('batch', 'blk')
- class_logits: float32 [8, 32, 40, 40], P('batch', 'blk')
- grad_features: float32 [8, 32, 40, 2048], P('batch', 'blk')
- grad_first: float32 [2048, 512], P('batch')
- grad_spatial: float32 [9, 512, 512], P(None, 'batch')
- grad_last: float32 [512, 2048], P('batch')
- grad_shared: float32 [2048, 512], P('batch')
- grad_heads: float32 [4, 9, 512, 512], P(None, None, 'batch')
- grad_messages: float32 [4, 9, 512, 512], P(None, None, 'batch')
- grad_gates: float32 [4, 512, 512], P(None, 'batch')
- grad_depth: float32 [512], P('batch')
- grad_classes: float32 [512, 40], P('batch')
- grad_mid_gain: float32 [7, 512], P(None, 'batch')
- grad_mid_bias: float32 [7, 512], P(None, 'batch')
- grad_out_gain: float32 [2048], P('batch')
- grad_out_bias: float32 [2048], P('batch')
The draws below stay inside these ranges and needn't reach their ends.
Inputs may be any that keep to these rules, and one draw needn't show every extreme that they name: `crop_rows`: some image keeps all 32 rows and some keeps the fewest. `crop_cols`: some image keeps all 40 columns and some keeps the fewest.
All inputs are finite; a program needn't handle non-finite values.
Results may differ from the reference program's by a relative error of at most 0.025.
Values may be sent and summed in bfloat16 or wider, within the bound.
A program may use at most 320 MiB of HBM per device.

```python
import jax
import jax.numpy as jnp
from jax import lax

C_IN = 2048
C_MID = 512
CLASSES = 40
TASKS = 4
ROWS_DEV = 8
COLS = 40
HEIGHT = 32
IMAGES = 8


def draw_features(key, part):
    key = jax.random.fold_in(key, 11)
    base_key, chan_key, offset_key = jax.random.split(key, 3)
    full_shape = (IMAGES, HEIGHT, COLS, C_IN)
    image_scale = 1.0 + 2.0 * jnp.arange(IMAGES, dtype=jnp.float32) / max(IMAGES - 1, 1)
    row_scale = 0.6 + 0.8 * jnp.arange(HEIGHT, dtype=jnp.float32) / max(HEIGHT - 1, 1)
    chan_scale = jnp.exp(jax.random.uniform(chan_key, (C_IN,), jnp.float32, -0.7, 0.7))
    base_draw = jax.random.normal(base_key, full_shape, jnp.float32)
    offset_draw = 0.5 * jax.random.normal(offset_key, (C_IN,), jnp.float32)
    scales = image_scale[:, None, None, None] * row_scale[None, :, None, None] * chan_scale
    return ((base_draw + offset_draw) * scales).astype(jnp.bfloat16)


def draw_crop_rows(key, part):
    key = jax.random.fold_in(key, 23)
    value_key, place_key = jax.random.split(key)
    lowest = HEIGHT - ROWS_DEV + 1
    drawn = jax.random.randint(value_key, (IMAGES,), lowest, HEIGHT + 1, jnp.int32)
    places = jax.random.permutation(place_key, IMAGES)
    return drawn.at[places[0]].set(HEIGHT).at[places[1]].set(lowest)


def draw_crop_cols(key, part):
    key = jax.random.fold_in(key, 37)
    value_key, place_key = jax.random.split(key)
    lowest = COLS // 2
    drawn = jax.random.randint(value_key, (IMAGES,), lowest, COLS + 1, jnp.int32)
    places = jax.random.permutation(place_key, IMAGES)
    return drawn.at[places[0]].set(COLS).at[places[1]].set(lowest)


def with_ends(result, own_key, smallest, largest):
    dims = result.shape
    index_at = [jax.random.randint(jax.random.fold_in(own_key, axis), (), 0, dims[axis]) for axis in range(len(dims))]
    result = result.at[tuple(index_at)].set(smallest)
    longest = dims.index(max(dims))
    index_at[longest] = (index_at[longest] + 1) % dims[longest]
    return result.at[tuple(index_at)].set(largest)


def steps_of(stream_key, dims, cuts, least, high):
    loudness, own = 1.0, jax.random.fold_in(stream_key, 6)
    for axis_at, shards_of in cuts:
        heights = jnp.exp(jax.random.uniform(jax.random.fold_in(own, axis_at), (shards_of,), jnp.float32, least / len(cuts), high / len(cuts)))
        loudness = loudness * jnp.repeat(heights, dims[axis_at] // shards_of).reshape([-1 if axis == axis_at else 1 for axis in range(len(dims))])
    return loudness


def noise(key, dims, deviation, limit, cuts=(), kind=jnp.bfloat16):
    result = deviation * jax.random.normal(key, dims, jnp.float32)
    if cuts:
        result = result * steps_of(key, dims, cuts, -0.22, 0.18)
    return jnp.clip(result, -limit, limit).astype(kind)


def setup_inputs(seed: int = 0) -> dict:
    key_of = jax.random.split(jax.random.key(seed), 19)
    features = draw_features(jax.random.fold_in(key_of[18], 71), 0)
    crop_rows = draw_crop_rows(jax.random.fold_in(key_of[18], 71), 0)
    crop_cols = draw_crop_cols(jax.random.fold_in(key_of[18], 71), 0)
    depth_target = noise(key_of[3], (IMAGES, HEIGHT, COLS), 1.0, 6.0, ((0, 8), (1, 4)), jnp.float32)
    labels = with_ends(jax.random.randint(key_of[4], (IMAGES, HEIGHT, COLS), 0, CLASSES), jax.random.fold_in(key_of[4], 1), 0, CLASSES - 1).astype(jnp.int32)
    first_weight = noise(key_of[5], (C_IN, C_MID), C_IN ** -0.5, 0.125, ((0, 8),))
    spatial_weight = noise(key_of[6], (9, C_MID, C_MID), (9 * C_MID) ** -0.5, 0.09375, ((1, 8),))
    last_weight = noise(key_of[7], (C_MID, C_IN), C_MID ** -0.5, 0.25, ((0, 8),))
    shared_weight = noise(key_of[8], (C_IN, C_MID), C_IN ** -0.5, 0.125, ((0, 8),))
    head_weights = noise(key_of[9], (TASKS, 9, C_MID, C_MID), (9 * C_MID) ** -0.5, 0.09375, ((2, 8),))
    message_weights = noise(key_of[10], (TASKS, 9, C_MID, C_MID), (9 * C_MID) ** -0.5, 0.09375, ((2, 8),))
    gate_weights = noise(key_of[11], (TASKS, C_MID, C_MID), C_MID ** -0.5, 0.25, ((1, 8),))
    depth_weight = noise(key_of[12], (C_MID,), (C_MID // 4) ** -0.5, 0.5, ((0, 8),))
    class_weight = noise(key_of[13], (C_MID, CLASSES), (C_MID // 4) ** -0.5, 0.5, ((0, 8),))
    mid_gain = jnp.clip(1.0 + 0.18 * jax.random.normal(key_of[14], (3 + TASKS, C_MID), jnp.float32), 0.099609375, 1.8984375).astype(jnp.bfloat16)
    mid_bias = jnp.clip(jax.random.uniform(key_of[15], (3 + TASKS, C_MID), jnp.float32, -0.5, 0.5) * steps_of(key_of[15], (3 + TASKS, C_MID), ((1, 8),), -0.4, 0.0), -0.5, 0.5).astype(jnp.bfloat16)
    out_gain = jnp.clip(1.0 + 0.18 * jax.random.normal(key_of[16], (C_IN,), jnp.float32), 0.099609375, 1.8984375).astype(jnp.bfloat16)
    out_bias = jnp.clip(jax.random.uniform(key_of[17], (C_IN,), jnp.float32, -0.5, 0.5) * steps_of(key_of[17], (C_IN,), ((0, 8),), -0.4, 0.0), -0.5, 0.5).astype(jnp.bfloat16)
    return dict(features=features, crop_rows=crop_rows, crop_cols=crop_cols, depth_target=depth_target, labels=labels, first_weight=first_weight, spatial_weight=spatial_weight, last_weight=last_weight, shared_weight=shared_weight, head_weights=head_weights, message_weights=message_weights, gate_weights=gate_weights, depth_weight=depth_weight, class_weight=class_weight, mid_gain=mid_gain, mid_bias=mid_bias, out_gain=out_gain, out_bias=out_bias)


EPSILON = 1e-05

@jax.custom_vjp
def low(v):
    return lax.optimization_barrier(v.astype(jnp.bfloat16)).astype(jnp.float32)

@jax.custom_vjp
def low_back(v):
    return v

def low_keep(v):
    return (low(v), None)

def low_pass(kept, grad):
    return (grad,)

def back_keep(v):
    return (v, None)

def back_low(kept, grad):
    return (low(grad),)
low.defvjp(low_keep, low_pass)
low_back.defvjp(back_keep, back_low)

def high_dot(left, right):
    return jnp.dot(left, right, precision=lax.Precision.HIGHEST)

@jax.checkpoint
def conv_apply(field, kernel):
    padded = jnp.pad(field, ((0, 0), (1, 1), (1, 1), (0, 0)))
    map_rows, map_cols = (field.shape[1], field.shape[2])
    summed = jnp.zeros(field.shape[:3] + (kernel.shape[2],), jnp.float32)
    for offset in range(9):
        row_start, col_start = (offset // 3, offset % 3)
        window = padded[:, row_start:row_start + map_rows, col_start:col_start + map_cols]
        summed = summed + high_dot(window, kernel[offset])
    return summed

def batch_norm(values, inside, valid_count, norm_gain, norm_bias):
    centre = lax.optimization_barrier(jnp.sum(values * inside, axis=(0, 1, 2))) / valid_count
    shifted = values - centre
    spread = lax.optimization_barrier(jnp.sum(shifted * shifted * inside, axis=(0, 1, 2))) / valid_count
    return shifted * lax.rsqrt(spread + EPSILON) * norm_gain + norm_bias

def forward(image_data, inside, valid_count, first_weight, spatial_weight, last_weight, shared_weight, head_weights, message_weights, gate_weights, depth_weight, class_weight, mid_gain, mid_bias, out_gain, out_bias):
    task_count = head_weights.shape[0]
    mid_width = first_weight.shape[1]
    last_task = task_count - 1
    pre_one = low_back(high_dot(image_data, first_weight))
    act_one = low(jax.nn.silu(batch_norm(pre_one, inside, valid_count, mid_gain[0], mid_bias[0])) * inside)
    pre_two = low_back(conv_apply(act_one, spatial_weight))
    act_two = low(jax.nn.silu(batch_norm(pre_two, inside, valid_count, mid_gain[1], mid_bias[1])) * inside)
    pre_three = low_back(high_dot(act_two, last_weight))
    joined = batch_norm(pre_three, inside, valid_count, out_gain, out_bias) + image_data
    act_three = low(jax.nn.silu(joined) * inside)
    pre_four = low_back(high_dot(act_three, shared_weight))
    shared_act = low(jax.nn.silu(batch_norm(pre_four, inside, valid_count, mid_gain[2], mid_bias[2])) * inside)
    pre_five = low_back(jnp.concatenate([conv_apply(shared_act, head_weights[task_id]) for task_id in range(task_count)], axis=3))
    task_gain = mid_gain[3:3 + task_count].reshape(-1)
    task_bias = mid_bias[3:3 + task_count].reshape(-1)
    task_act = low(jax.nn.silu(batch_norm(pre_five, inside, valid_count, task_gain, task_bias)) * inside)
    task_parts = [task_act[..., task_id * mid_width:(task_id + 1) * mid_width] for task_id in range(task_count)]
    messages = low_back(jnp.concatenate([conv_apply(task_parts[task_id], message_weights[task_id]) for task_id in range(task_count)], axis=3))
    gate_pre = low_back(jnp.concatenate([high_dot(task_parts[task_id], gate_weights[task_id]) for task_id in range(task_count)], axis=3))
    gated = jax.nn.sigmoid(gate_pre) * messages
    pieces = [gated[..., task_id * mid_width:(task_id + 1) * mid_width] for task_id in range(task_count)]
    summed = pieces[0]
    for task_id in range(1, task_count):
        summed = summed + pieces[task_id]
    depth_feat = low(task_parts[0] + summed - pieces[0])
    sem_feat = low(task_parts[last_task] + summed - pieces[last_task])
    depth_out = low_back(high_dot(depth_feat, depth_weight))
    logits = low_back(high_dot(sem_feat, class_weight))
    return (depth_out, logits)

def reference(features, crop_rows, crop_cols, depth_target, labels, first_weight, spatial_weight, last_weight, shared_weight, head_weights, message_weights, gate_weights, depth_weight, class_weight, mid_gain, mid_bias, out_gain, out_bias):
    row_ids = jnp.arange(HEIGHT, dtype=jnp.int32)
    col_ids = jnp.arange(COLS, dtype=jnp.int32)
    inside_map = ((row_ids[None, :, None] < crop_rows[:, None, None]) & (col_ids[None, None, :] < crop_cols[:, None, None])).astype(jnp.float32)
    inside = inside_map[..., None]
    valid_count = jnp.sum(inside_map)
    onehot = (labels[..., None] == jnp.arange(CLASSES, dtype=jnp.int32)).astype(jnp.float32)
    arguments = tuple((argument.astype(jnp.float32) for argument in (features, first_weight, spatial_weight, last_weight, shared_weight, head_weights, message_weights, gate_weights, depth_weight, class_weight, mid_gain, mid_bias, out_gain, out_bias)))

    def objective(*params):
        depth_out, logits = forward(params[0], inside, valid_count, *params[1:])
        error = depth_out - depth_target
        square_term = 0.5 * jnp.sum(error * error * inside_map)
        log_total = jax.nn.logsumexp(logits, axis=3)
        picked = lax.optimization_barrier(jnp.sum(logits * onehot, axis=3))
        return (square_term + jnp.sum((log_total - picked) * inside_map), (depth_out, logits))
    loss_value, puller, streams = jax.vjp(objective, *arguments, has_aux=True)
    grads = puller(jnp.float32(1.0))
    return (streams[0], streams[1], grads[0], grads[1], grads[2], grads[3], grads[4], grads[5], grads[6], grads[7], grads[8], grads[9], grads[10], grads[11], grads[12], grads[13])
```

```python
import functools

import jax
import jax.numpy as jnp
from jax import lax
from jax.experimental import pallas as pl
from jax.experimental.pallas import tpu as pltpu
from jax.sharding import PartitionSpec as P

EPSILON = 1e-05
MESH = pl.DeviceIdType.MESH
BF16 = jnp.bfloat16
F32 = jnp.float32
LANES = 128


def greet(peers):
    barrier = pltpu.get_barrier_semaphore()
    for peer in peers:
        pl.semaphore_signal(barrier, inc=1, device_id=peer, device_id_type=MESH)
    pl.semaphore_wait(barrier, len(peers))


def send(src, dst, send_sem, recv_sem, peer):
    copy = pltpu.make_async_remote_copy(
        src_ref=src,
        dst_ref=dst,
        send_sem=send_sem,
        recv_sem=recv_sem,
        device_id=peer,
        device_id_type=MESH,
    )
    copy.start()
    return copy


def first_kernel(images, weight, small, full, smalls, own, zs, xs, cs, ps):
    blk, batch = lax.axis_index("blk"), lax.axis_index("batch")
    half = weight.shape[0] // 2
    rows = pl.ds(pl.multiple_of(lax.rem(blk, 2) * half, half), half)
    side = (blk, batch ^ 1)
    mate = (blk ^ 1, batch)
    lines = range(1, images // 2)
    others = [(blk, batch ^ mask) for mask in range(1, images)]
    greet(others + [mate])
    copies = []
    here = pltpu.make_async_copy(weight, full.at[batch], own.at[0])
    here.start()
    here_small = pltpu.make_async_copy(small, smalls.at[batch], own.at[1])
    here_small.start()
    z_copies = {}
    for mask in lines:
        z_copies[mask] = send(
            weight.at[rows],
            full.at[batch, rows],
            zs.at[0, mask],
            zs.at[1, mask],
            (blk, batch ^ (2 * mask)),
        )
    x_copies = {
        0: send(weight.at[rows], full.at[batch, rows], xs.at[0, 0], xs.at[1, 0], side)
    }
    for place, peer in enumerate(others):
        copies.append(
            send(small, smalls.at[batch], ps.at[0, place], ps.at[1, place], peer)
        )
    core_copies = []

    def hand_over(source, mask):
        block = full.at[source, rows]
        core_copies.append(send(block, block, cs.at[0, mask], cs.at[1, mask], mate))

    for mask in lines:
        z_copies[mask].wait_recv()
        source = batch ^ (2 * mask)
        block = full.at[source, rows]
        x_copies[mask] = send(block, block, xs.at[0, mask], xs.at[1, mask], side)
        hand_over(source, 2 * mask)
    for mask in range(images // 2):
        x_copies[mask].wait_recv()
        hand_over(batch ^ (2 * mask + 1), 2 * mask + 1)
    for copy in core_copies + copies:
        copy.wait()
    for mask in lines:
        z_copies[mask].wait_send()
    for mask in range(images // 2):
        x_copies[mask].wait_send()
    here.wait()
    here_small.wait()


def gather_first(weight, small, images):
    any_place = pl.BlockSpec(memory_space=pl.ANY)
    dma = pltpu.SemaphoreType.DMA
    return pl.pallas_call(
        functools.partial(first_kernel, images),
        out_shape=(
            jax.ShapeDtypeStruct((images,) + weight.shape, weight.dtype),
            jax.ShapeDtypeStruct((images,) + small.shape, small.dtype),
        ),
        in_specs=[any_place] * 2,
        out_specs=(any_place, any_place),
        scratch_shapes=[
            dma((2,)),
            dma((2, images)),
            dma((2, images)),
            dma((2, images)),
            dma((2, images)),
        ],
        compiler_params=pltpu.CompilerParams(collective_id=0, has_side_effects=True),
    )(weight, small)


def tiles_kernel(block, every, own, sems):
    blk, batch = lax.axis_index("blk"), lax.axis_index("batch")
    mate, across = (blk ^ 1, batch), (blk ^ 2, batch)
    greet([mate, across])
    far = send(block, every.at[blk], sems.at[0, 0], sems.at[1, 0], across)
    near = send(block, every.at[blk], sems.at[0, 1], sems.at[1, 1], mate)
    here = pltpu.make_async_copy(block, every.at[blk], own.at[0])
    here.start()
    far.wait_recv()
    passed = every.at[blk ^ 2]
    last = send(passed, passed, sems.at[0, 2], sems.at[1, 2], mate)
    near.wait()
    last.wait()
    far.wait_send()
    here.wait()


def gather_tiles(block, ident):
    any_place = pl.BlockSpec(memory_space=pl.ANY)
    dma = pltpu.SemaphoreType.DMA
    return pl.pallas_call(
        tiles_kernel,
        out_shape=jax.ShapeDtypeStruct((4,) + block.shape, block.dtype),
        in_specs=[any_place],
        out_specs=any_place,
        scratch_shapes=[dma((1,)), dma((2, 3))],
        compiler_params=pltpu.CompilerParams(collective_id=ident, has_side_effects=True),
    )(block)


def sum_kernel(parts, total, near_in, pair, far_in, sems):
    blk, batch = lax.axis_index("blk"), lax.axis_index("batch")
    mate, across = (blk ^ 1, batch), (blk ^ 2, batch)
    greet([mate, across])
    far_first = send(parts.at[blk ^ 3], near_in.at[0], sems.at[0, 0], sems.at[1, 0], mate)
    near_next = send(parts.at[blk ^ 1], near_in.at[1], sems.at[0, 1], sems.at[1, 1], mate)
    far_first.wait_recv()
    pair[...] = (parts[blk ^ 2].astype(F32) + near_in[0].astype(F32)).astype(pair.dtype)
    far = send(pair, far_in, sems.at[0, 2], sems.at[1, 2], across)
    near_next.wait_recv()
    total[...] = parts[blk].astype(F32) + near_in[1].astype(F32)
    far.wait_recv()
    total[...] += far_in[...].astype(F32)
    far_first.wait_send()
    near_next.wait_send()
    far.wait_send()


def sum_tiles(parts, ident):
    dma = pltpu.SemaphoreType.DMA
    block = parts.shape[1:]
    vmem = pl.BlockSpec(memory_space=pltpu.VMEM)
    return pl.pallas_call(
        sum_kernel,
        out_shape=jax.ShapeDtypeStruct(block, F32),
        in_specs=[vmem],
        out_specs=vmem,
        scratch_shapes=[
            pltpu.VMEM((2,) + block, parts.dtype),
            pltpu.VMEM(block, parts.dtype),
            pltpu.VMEM(block, parts.dtype),
            dma((2, 3)),
        ],
        compiler_params=pltpu.CompilerParams(
            collective_id=ident, has_side_effects=True, vmem_limit_bytes=32 * 2**20
        ),
    )(parts)


def combine(slots, weights, half, centred):
    count = slots.shape[0]
    if not centred:
        total = slots[0]
        for at in range(1, count):
            total = total + slots[at]
        return total
    size = weights[0]
    mean = slots[0, :half] * weights[0]
    for at in range(1, count):
        size = size + weights[at]
        mean = mean + slots[at, :half] * weights[at]
    mean = mean / size
    spread = None
    for at in range(count):
        gap = slots[at, :half] - mean
        term = slots[at, half : 2 * half] + weights[at] * gap * gap
        spread = term if spread is None else spread + term
    rest = [jnp.zeros((slots.shape[1] - 2 * half, LANES), F32)] * (slots.shape[1] > 2 * half)
    return jnp.concatenate([mean, spread] + rest, 0)


def sums_kernel(images, half, centred, tiled, own, tile_sizes, sizes, total, *scratch):
    blk, batch = lax.axis_index("blk"), lax.axis_index("batch")
    slots, sems = scratch[0], scratch[1]
    peers = [(blk, batch ^ mask) for mask in range(1, images)]
    mates = [(blk ^ mask, batch) for mask in range(1, 4)] if tiled else []
    greet(peers + mates)
    if tiled:
        tile_slots, tile_sems = scratch[2], scratch[3]
        tile_slots[blk] = own[...]
        copies = [
            send(own, tile_slots.at[blk], tile_sems.at[0, at], tile_sems.at[1, at], peer)
            for at, peer in enumerate(mates)
        ]
        for copy in copies:
            copy.wait()
        slots[batch] = combine(tile_slots, tile_sizes, half, centred)
    else:
        slots[batch] = own[...]
    copies = [
        send(slots.at[batch], slots.at[batch], sems.at[0, at], sems.at[1, at], peer)
        for at, peer in enumerate(peers)
    ]
    for copy in copies:
        copy.wait()
    total[...] = combine(slots, sizes, half, centred)


def all_sums(first, second, tile_sizes, sizes, centred, tiled, ident):
    images = sizes.shape[0]
    channels = first.shape[0]
    half = channels // LANES
    rows = -(-2 * half // 8) * 8
    own = jnp.concatenate(
        [first, second, jnp.zeros(((rows - 2 * half) * LANES,), F32)]
    ).reshape(rows, LANES)
    dma = pltpu.SemaphoreType.DMA
    vmem = pl.BlockSpec(memory_space=pltpu.VMEM)
    scratch = [pltpu.VMEM((images, rows, LANES), F32), dma((2, images))]
    if tiled:
        scratch += [pltpu.VMEM((4, rows, LANES), F32), dma((2, 3))]
    total = pl.pallas_call(
        functools.partial(sums_kernel, images, half, centred, tiled),
        out_shape=jax.ShapeDtypeStruct((rows, LANES), F32),
        in_specs=[vmem] * 3,
        out_specs=vmem,
        scratch_shapes=scratch,
        compiler_params=pltpu.CompilerParams(collective_id=ident, has_side_effects=True),
    )(own, tile_sizes, sizes)
    flat = total.reshape(-1)
    return flat[:channels], flat[channels : 2 * channels]


def silu_slope(values):
    sigmoid_value = jax.nn.sigmoid(values)
    return sigmoid_value * (1.0 + values * (1.0 - sigmoid_value))


def windows(cells, rows, cols, back):
    channels = cells.shape[1]
    padded = jnp.pad(cells.reshape(rows, cols, channels), ((1, 1), (1, 1), (0, 0)))
    taken = []
    for offset in range(9):
        row, col = offset // 3, offset % 3
        if back:
            row, col = 2 - row, 2 - col
        taken.append(padded[row : row + rows, col : col + cols].reshape(rows * cols, channels))
    return jnp.concatenate(taken, 1)


def dot(left, right):
    return jnp.dot(left, right, preferred_element_type=F32)


def dot_t(left, right):
    return jnp.einsum("pd,cd->pc", left, right, preferred_element_type=F32)


def t_dot(left, right):
    return jnp.einsum("pc,pd->cd", left, right, preferred_element_type=F32)


def on_device(
    nt,
    nb,
    features,
    crop_rows,
    crop_cols,
    depth_target,
    labels,
    first_weight,
    spatial_weight,
    last_weight,
    shared_weight,
    head_weights,
    message_weights,
    gate_weights,
    depth_weight,
    class_weight,
    mid_gain,
    mid_bias,
    out_gain,
    out_bias,
):
    tile_rows, cols, width = features.shape[1:]
    tile = tile_rows * cols
    rows = tile_rows * nt
    pixels = rows * cols
    tasks = head_weights.shape[0]
    mid = first_weight.shape[1]
    share = mid // nb
    slim = mid // nt
    piece = width // (nb * nt)
    wide = nb * piece
    classes = class_weight.shape[1]
    blk, batch = lax.axis_index("blk"), lax.axis_index("batch")

    image_rows = lax.dynamic_index_in_dim(crop_rows, batch, 0, False)
    image_cols = lax.dynamic_index_in_dim(crop_cols, batch, 0, False)
    row_ids = jnp.arange(rows, dtype=jnp.int32)
    col_ids = jnp.arange(cols, dtype=jnp.int32)
    inside_grid = (row_ids[:, None] < image_rows) & (col_ids[None, :] < image_cols)
    inside = inside_grid.astype(F32).reshape(pixels, 1)
    inside_tile = lax.dynamic_slice_in_dim(inside, blk * tile, tile, 0)
    sizes_flat = (crop_rows * crop_cols).astype(F32)
    valid_count = jnp.sum(sizes_flat)
    sizes = jnp.broadcast_to(sizes_flat[:, None, None], (nb, 1, LANES))
    tile_counts = jnp.sum(inside.reshape(nt, tile), 1)
    tile_sizes = jnp.broadcast_to(tile_counts[:, None, None], (nt, 1, LANES))
    image_size = jnp.maximum(jnp.sum(inside), 1.0)
    tile_size = jnp.maximum(jnp.sum(inside_tile), 1.0)

    params = jnp.concatenate(
        [
            mid_gain.reshape(-1),
            mid_bias.reshape(-1),
            out_gain,
            out_bias,
            depth_weight,
            class_weight.reshape(-1),
        ]
    )
    room = -(-params.shape[0] // (16 * LANES)) * 16 * LANES
    small = jnp.pad(params, (0, room - params.shape[0])).reshape(-1, LANES)
    full_first, smalls = gather_first(first_weight, small, nb)
    full_first = full_first.reshape(width, mid)
    smalls = smalls.reshape(nb, room)
    at = 0

    def taken(count):
        nonlocal at
        found = smalls[:, at : at + count]
        at += count
        return found

    norms = mid_gain.shape[0]
    gain_mid = taken(norms * share).reshape(nb, norms, share).swapaxes(0, 1)
    gain_mid = gain_mid.reshape(norms, mid).astype(F32)
    bias_mid = taken(norms * share).reshape(nb, norms, share).swapaxes(0, 1)
    bias_mid = bias_mid.reshape(norms, mid).astype(F32)
    gain_out = lax.dynamic_index_in_dim(taken(nt * piece).reshape(nb, nt, piece), blk, 1, False)
    gain_out = gain_out.reshape(wide).astype(F32)
    bias_out = lax.dynamic_index_in_dim(taken(nt * piece).reshape(nb, nt, piece), blk, 1, False)
    bias_out = bias_out.reshape(wide).astype(F32)
    full_depth = taken(share).reshape(mid, 1)
    full_classes = taken(share * classes).reshape(mid, classes)
    stream_weight = jnp.concatenate([full_depth, full_classes], 1)

    spatial = lax.all_gather(
        lax.dynamic_slice_in_dim(spatial_weight, blk * slim, slim, 2), "batch", axis=1, tiled=True
    )
    last = lax.dynamic_index_in_dim(last_weight.reshape(share, nb, nt, piece), blk, 2, False)
    last = lax.all_gather(last.reshape(share, wide), "batch", axis=0, tiled=True)
    shared = lax.dynamic_slice_in_dim(shared_weight, blk * piece, piece, 0)
    shared = lax.all_gather(shared, "batch", axis=0, tiled=True)
    head = lax.all_gather(
        lax.dynamic_index_in_dim(head_weights, blk, 0, False), "batch", axis=1, tiled=True
    )
    message = lax.all_gather(
        lax.dynamic_index_in_dim(message_weights, blk, 0, False), "batch", axis=1, tiled=True
    )
    gate = lax.all_gather(
        lax.dynamic_index_in_dim(gate_weights, blk, 0, False), "batch", axis=0, tiled=True
    )

    flat_features = features.reshape(tile, width)
    cut = flat_features.reshape(tile, nb, nt, piece).transpose(2, 0, 1, 3).reshape(nt, tile, wide)
    wide_features = swap_tiles(cut, blk, nt)

    def slim_of(vector):
        return lax.dynamic_slice_in_dim(vector, blk * slim, slim, 0)

    def normalize(values, mask, local_size, gain, bias, tiled, ident):
        mean = jnp.sum(values * mask, 0) / local_size
        gap = values - mean
        spread = jnp.sum(gap * gap * mask, 0)
        centre, total = all_sums(mean, spread, tile_sizes, sizes, True, tiled, ident)
        inverse = lax.rsqrt(total / valid_count + EPSILON)
        normed = (values - centre) * inverse
        return normed * gain + bias, normed, inverse

    def normalize_back(grad, normed, inverse, gain, mask, tiled, ident):
        bias_sum, gain_sum = all_sums(
            jnp.sum(grad, 0), jnp.sum(grad * normed, 0), tile_sizes, sizes, False, tiled, ident
        )
        back = (
            inverse * gain * (grad - bias_sum / valid_count - normed * gain_sum / valid_count) * mask
        )
        return back.astype(BF16), gain_sum, bias_sum

    def act(values, mask):
        return (jax.nn.silu(values) * mask).astype(BF16)

    def by_rows(blocks):
        return blocks.reshape(pixels, blocks.shape[2])

    def by_channels(blocks):
        return blocks.swapaxes(0, 1).reshape(pixels, nt * blocks.shape[2])

    def cut_channels(values):
        return values.astype(BF16).reshape(pixels, nt, slim).swapaxes(0, 1)

    pre_one = dot(flat_features, full_first)
    norm_one, normed_one, inverse_one = normalize(
        pre_one, inside_tile, tile_size, gain_mid[0], bias_mid[0], True, 1
    )
    act_one = by_rows(gather_tiles(act(norm_one, inside_tile), 2))
    pre_two = dot(windows(act_one, rows, cols, False), spatial.reshape(9 * mid, slim))
    gain_two, bias_two = slim_of(gain_mid[1]), slim_of(bias_mid[1])
    norm_two, normed_two, inverse_two = normalize(
        pre_two, inside, image_size, gain_two, bias_two, False, 3
    )
    act_two = by_channels(gather_tiles(act(norm_two, inside), 4))
    pre_three = dot(act_two, last)
    norm_three, normed_three, inverse_three = normalize(
        pre_three, inside, image_size, gain_out, bias_out, False, 5
    )
    joined = norm_three + wide_features.astype(F32)
    act_three = act(joined, inside)
    pre_four = sum_tiles(cut_channels(dot(act_three, shared)), 6)
    gain_four, bias_four = slim_of(gain_mid[2]), slim_of(bias_mid[2])
    norm_four, normed_four, inverse_four = normalize(
        pre_four, inside, image_size, gain_four, bias_four, False, 3
    )
    shared_act = by_channels(gather_tiles(act(norm_four, inside), 4))

    gain_task = lax.dynamic_index_in_dim(gain_mid, 3 + blk, 0, False)
    bias_task = lax.dynamic_index_in_dim(bias_mid, 3 + blk, 0, False)
    pre_five = dot(windows(shared_act, rows, cols, False), head.reshape(9 * mid, mid))
    norm_five, normed_five, inverse_five = normalize(
        pre_five, inside, image_size, gain_task, bias_task, False, 5
    )
    task_act = act(norm_five, inside)
    messages = dot(windows(task_act, rows, cols, False), message.reshape(9 * mid, mid))
    gate_open = jax.nn.sigmoid(dot(task_act, gate))
    gated = (gate_open * messages).astype(BF16)
    is_first, is_last = blk == 0, blk == tasks - 1
    depth_part = jnp.where(is_first, task_act, gated)
    sem_part = jnp.where(is_last, task_act, gated)
    depth_share = jnp.einsum("pc,co->op", depth_part, full_depth, preferred_element_type=F32)
    class_share = jnp.einsum("pc,co->op", sem_part, full_classes, preferred_element_type=F32)
    lift = -(-(1 + classes) // 8) * 8 - 1 - classes
    shares = jnp.concatenate([depth_share, class_share, jnp.zeros((lift, pixels), F32)], 0)
    streams = jnp.sum(gather_tiles(shares, 7), 0).T
    depth_out = lax.dynamic_slice_in_dim(streams, blk * tile, tile, 0)[:, 0]
    logits = lax.dynamic_slice_in_dim(streams, blk * tile, tile, 0)[:, 1 : 1 + classes]
    targets = by_rows(gather_tiles_pair(depth_target, labels, tile))
    all_depth, all_logits = streams[:, :1], streams[:, 1 : 1 + classes]
    depth_slope = ((all_depth - targets[:, :1]) * inside).astype(BF16)
    onehot = (targets[:, 1:2] == jnp.arange(classes, dtype=jnp.int32)[None, :].astype(F32)).astype(F32)
    logit_slope = ((jax.nn.softmax(all_logits, axis=1) - onehot) * inside).astype(BF16)
    grad_depth = t_dot(depth_part, depth_slope)
    grad_classes = t_dot(sem_part, logit_slope)
    depth_back = depth_slope.astype(F32) * full_depth.astype(F32).reshape(1, mid)
    sem_back = dot_t(logit_slope, full_classes)
    zero = jnp.zeros((), F32)
    grad_gated = jnp.where(is_first, zero, depth_back) + jnp.where(is_last, zero, sem_back)
    grad_direct = jnp.where(is_first, depth_back, zero) + jnp.where(is_last, sem_back, zero)

    grad_msg = (grad_gated * gate_open).astype(BF16)
    grad_gate = (grad_gated * messages * gate_open * (1.0 - gate_open)).astype(BF16)
    msg_windows = windows(grad_msg, rows, cols, True)
    gate_grads = t_dot(task_act, grad_gate).astype(BF16)
    message_grads = t_dot(task_act, msg_windows).astype(BF16)
    share_messages = lax.psum_scatter(message_grads, "batch", scatter_dimension=0, tiled=True)
    task_grad = (
        grad_direct
        + dot_t(grad_gate, gate)
        + dot(msg_windows, message.swapaxes(1, 2).reshape(9 * mid, mid))
    )
    grad_norm_five = task_grad * inside * silu_slope(norm_five)
    grad_pre_five, gain_sum_five, bias_sum_five = normalize_back(
        grad_norm_five, normed_five, inverse_five, gain_task, inside, False, 8
    )
    five_windows = windows(grad_pre_five, rows, cols, True)
    head_grads = t_dot(shared_act, five_windows).astype(BF16)
    share_heads = lax.psum_scatter(head_grads, "batch", scatter_dimension=0, tiled=True)
    shared_back = dot(five_windows, head.swapaxes(1, 2).reshape(9 * mid, mid))
    shared_back = sum_tiles(cut_channels(shared_back), 6)

    grad_norm_four = shared_back * inside * silu_slope(norm_four)
    grad_pre_four, gain_sum_four, bias_sum_four = normalize_back(
        grad_norm_four, normed_four, inverse_four, gain_four, inside, False, 9
    )
    grad_four = by_channels(gather_tiles(grad_pre_four, 4))
    shared_grads = t_dot(act_three, grad_four).astype(BF16)
    grad_joined = dot_t(grad_four, shared) * inside * silu_slope(joined)
    grad_three, gain_sum_three, bias_sum_three = normalize_back(
        grad_joined, normed_three, inverse_three, gain_out, inside, False, 8
    )
    last_grads = t_dot(act_two, grad_three).astype(BF16)
    two_back = sum_tiles(cut_channels(dot_t(grad_three, last)), 6)
    grad_norm_two = two_back * inside * silu_slope(norm_two)
    grad_two, gain_sum_two, bias_sum_two = normalize_back(
        grad_norm_two, normed_two, inverse_two, gain_two, inside, False, 9
    )
    two_windows = windows(grad_two, rows, cols, True)
    spatial_grads = t_dot(act_one, two_windows).astype(BF16)
    one_back = dot(two_windows, spatial.swapaxes(1, 2).reshape(9 * slim, mid))
    one_back = sum_tiles(one_back.astype(BF16).reshape(nt, tile, mid), 10)
    grad_norm_one = one_back * inside_tile * silu_slope(norm_one)
    grad_one, gain_sum_one, bias_sum_one = normalize_back(
        grad_norm_one, normed_one, inverse_one, gain_mid[0], inside_tile, True, 11
    )
    all_one = by_rows(gather_tiles(grad_one, 2))
    first_grads = t_dot(wide_features, all_one).astype(BF16)
    joined_tiles = swap_tiles(grad_joined.astype(BF16).reshape(nt, tile, wide), blk, nt)
    joined_tiles = joined_tiles.reshape(nt, tile, nb, piece).transpose(1, 2, 0, 3).reshape(tile, width)
    grad_input = dot_t(grad_one, full_first) + joined_tiles.astype(F32)

    stream_grads = jnp.concatenate([grad_depth, grad_classes], 1)
    stream_grads = jnp.pad(stream_grads, ((0, 0), (0, LANES - 1 - classes))).astype(BF16)
    late = jnp.concatenate(
        [spatial_grads, shared_grads.reshape(nb, piece, mid).reshape(mid, -1),
         last_grads, first_grads.reshape(mid, -1), gate_grads, stream_grads],
        1,
    )
    late_share = lax.psum_scatter(late, "batch", scatter_dimension=0, tiled=True)
    early_share = jnp.concatenate([share_messages, share_heads], 1)
    early = lax.all_gather(early_share, "blk", axis=0, tiled=False).astype(F32)
    late_all = gather_tiles(late_share, 12).astype(F32)
    early = early.reshape(nt, share, 2, 9, mid).transpose(2, 0, 3, 1, 4)
    red_messages, red_heads = early[0], early[1]
    at = 0

    def part(count):
        nonlocal at
        found = late_all[:, :, at : at + count]
        at += count
        return found

    red_spatial = part(9 * slim).reshape(nt, share, 9, slim).transpose(2, 1, 0, 3).reshape(9, share, mid)
    red_shared = part(wide * mid // mid).reshape(nt * piece, mid)
    red_last = part(wide).reshape(nt, share, nb, piece).transpose(1, 2, 0, 3).reshape(share, width)
    red_first = part(wide * mid // mid).reshape(nt * piece, mid)
    red_gates = part(mid)
    streams_red = jnp.sum(part(LANES), 0)
    red_depth = streams_red[:, 0]
    red_classes = streams_red[:, 1 : 1 + classes]

    sums = jnp.concatenate(
        [
            gain_sum_five,
            bias_sum_five,
            gain_sum_three,
            bias_sum_three,
            gain_sum_two,
            bias_sum_two,
            gain_sum_four,
            bias_sum_four,
        ]
    ).reshape(-1, LANES)
    sums = jnp.pad(sums, ((0, -sums.shape[0] % 8), (0, 0)))
    sums = gather_tiles(sums, 13).reshape(nt, -1)
    five_gain, five_bias = sums[:, :mid], sums[:, mid : 2 * mid]
    at_out = 2 * mid
    three_gain = sums[:, at_out : at_out + wide].reshape(nt, nb, piece)
    three_bias = sums[:, at_out + wide : at_out + 2 * wide].reshape(nt, nb, piece)
    at_slim = at_out + 2 * wide
    slims = [
        sums[:, at_slim + i * slim : at_slim + (i + 1) * slim].reshape(1, mid) for i in range(4)
    ]
    mid_gains = jnp.concatenate([gain_sum_one[None], slims[0], slims[2], five_gain], 0)
    mid_biases = jnp.concatenate([bias_sum_one[None], slims[1], slims[3], five_bias], 0)
    grad_mid_gain = lax.dynamic_slice_in_dim(mid_gains, batch * share, share, 1)
    grad_mid_bias = lax.dynamic_slice_in_dim(mid_biases, batch * share, share, 1)
    grad_out_gain = lax.dynamic_index_in_dim(three_gain, batch, 1, False).reshape(nt * piece)
    grad_out_bias = lax.dynamic_index_in_dim(three_bias, batch, 1, False).reshape(nt * piece)
    return (
        depth_out.reshape(1, tile_rows, cols),
        logits.reshape(1, tile_rows, cols, classes),
        grad_input.reshape(1, tile_rows, cols, width),
        red_first,
        red_spatial,
        red_last,
        red_shared,
        red_heads,
        red_messages,
        red_gates,
        red_depth,
        red_classes,
        grad_mid_gain,
        grad_mid_bias,
        grad_out_gain,
        grad_out_bias,
    )


def swap_tiles(blocks, blk, nt):
    out = jnp.zeros_like(blocks)
    out = lax.dynamic_update_index_in_dim(
        out, lax.dynamic_index_in_dim(blocks, blk, 0, False), blk, 0
    )
    for mask in range(1, nt):
        sent = lax.dynamic_index_in_dim(blocks, blk ^ mask, 0, False)
        came = lax.ppermute(sent, "blk", [(i, i ^ mask) for i in range(nt)])
        out = lax.dynamic_update_index_in_dim(out, came, blk ^ mask, 0)
    return out.reshape(-1, blocks.shape[2])


def gather_tiles_pair(depth_target, labels, tile):
    pair = jnp.stack([depth_target.reshape(tile), labels.reshape(tile).astype(F32)], 0)
    pair = jnp.pad(pair, ((0, 6), (0, 0)))
    return gather_tiles(pair, 14).swapaxes(1, 2)


def solution(mesh):
    nt, nb = mesh.shape["blk"], mesh.shape["batch"]
    placed = (
        P("batch", "blk", None, None),
        P(),
        P(),
        P("batch", "blk", None),
        P("batch", "blk", None),
        P("batch", None),
        P(None, "batch", None),
        P("batch", None),
        P("batch", None),
        P(None, None, "batch", None),
        P(None, None, "batch", None),
        P(None, "batch", None),
        P("batch"),
        P("batch", None),
        P(None, "batch"),
        P(None, "batch"),
        P("batch"),
        P("batch"),
    )
    return jax.shard_map(
        functools.partial(on_device, nt, nb),
        mesh=mesh,
        in_specs=placed,
        out_specs=(
            P("batch", "blk", None),
            P("batch", "blk", None, None),
            P("batch", "blk", None, None),
            P("batch", None),
            P(None, "batch", None),
            P("batch", None),
            P("batch", None),
            P(None, None, "batch", None),
            P(None, None, "batch", None),
            P(None, "batch", None),
            P("batch"),
            P("batch", None),
            P(None, "batch"),
            P(None, "batch"),
            P("batch"),
            P("batch"),
        ),
        check_vma=False,
    )
```

```python
import functools

import jax
import jax.numpy as jnp
from jax import lax
from jax.experimental import pallas as pl
from jax.experimental.pallas import tpu as pltpu
from jax.sharding import PartitionSpec as P

EPSILON = 1e-05
MESH = pl.DeviceIdType.MESH
BF16 = jnp.bfloat16
F32 = jnp.float32
LANES = 128


def greet(peers):
    barrier = pltpu.get_barrier_semaphore()
    for peer in peers:
        pl.semaphore_signal(barrier, inc=1, device_id=peer, device_id_type=MESH)
    pl.semaphore_wait(barrier, len(peers))


def send(src, dst, send_sem, recv_sem, peer):
    copy = pltpu.make_async_remote_copy(
        src_ref=src,
        dst_ref=dst,
        send_sem=send_sem,
        recv_sem=recv_sem,
        device_id=peer,
        device_id_type=MESH,
    )
    copy.start()
    return copy


def first_kernel(images, weight, small, full, smalls, own, zs, xs, cs, ps):
    blk, batch = lax.axis_index("blk"), lax.axis_index("batch")
    half = weight.shape[0] // 2
    rows = pl.ds(pl.multiple_of(lax.rem(blk, 2) * half, half), half)
    side = (blk, batch ^ 1)
    mate = (blk ^ 1, batch)
    lines = range(1, images // 2)
    others = [(blk, batch ^ mask) for mask in range(1, images)]
    greet(others + [mate])
    copies = []
    here = pltpu.make_async_copy(weight, full.at[batch], own.at[0])
    here.start()
    here_small = pltpu.make_async_copy(small, smalls.at[batch], own.at[1])
    here_small.start()
    z_copies = {}
    for mask in lines:
        z_copies[mask] = send(
            weight.at[rows],
            full.at[batch, rows],
            zs.at[0, mask],
            zs.at[1, mask],
            (blk, batch ^ (2 * mask)),
        )
    x_copies = {
        0: send(weight.at[rows], full.at[batch, rows], xs.at[0, 0], xs.at[1, 0], side)
    }
    for place, peer in enumerate(others):
        copies.append(
            send(small, smalls.at[batch], ps.at[0, place], ps.at[1, place], peer)
        )
    core_copies = []

    def hand_over(source, mask):
        block = full.at[source, rows]
        core_copies.append(send(block, block, cs.at[0, mask], cs.at[1, mask], mate))

    for mask in lines:
        z_copies[mask].wait_recv()
        source = batch ^ (2 * mask)
        block = full.at[source, rows]
        x_copies[mask] = send(block, block, xs.at[0, mask], xs.at[1, mask], side)
        hand_over(source, 2 * mask)
    for mask in range(images // 2):
        x_copies[mask].wait_recv()
        hand_over(batch ^ (2 * mask + 1), 2 * mask + 1)
    for copy in core_copies + copies:
        copy.wait()
    for mask in lines:
        z_copies[mask].wait_send()
    for mask in range(images // 2):
        x_copies[mask].wait_send()
    here.wait()
    here_small.wait()


def gather_first(weight, small, images):
    any_place = pl.BlockSpec(memory_space=pl.ANY)
    dma = pltpu.SemaphoreType.DMA
    return pl.pallas_call(
        functools.partial(first_kernel, images),
        out_shape=(
            jax.ShapeDtypeStruct((images,) + weight.shape, weight.dtype),
            jax.ShapeDtypeStruct((images,) + small.shape, small.dtype),
        ),
        in_specs=[any_place] * 2,
        out_specs=(any_place, any_place),
        scratch_shapes=[
            dma((2,)),
            dma((2, images)),
            dma((2, images)),
            dma((2, images)),
            dma((2, images)),
        ],
        compiler_params=pltpu.CompilerParams(collective_id=0, has_side_effects=True),
    )(weight, small)


def tiles_kernel(block, every, own, sems):
    blk, batch = lax.axis_index("blk"), lax.axis_index("batch")
    mate, across = (blk ^ 1, batch), (blk ^ 2, batch)
    greet([mate, across])
    far = send(block, every.at[blk], sems.at[0, 0], sems.at[1, 0], across)
    near = send(block, every.at[blk], sems.at[0, 1], sems.at[1, 1], mate)
    here = pltpu.make_async_copy(block, every.at[blk], own.at[0])
    here.start()
    far.wait_recv()
    passed = every.at[blk ^ 2]
    last = send(passed, passed, sems.at[0, 2], sems.at[1, 2], mate)
    near.wait()
    last.wait()
    far.wait_send()
    here.wait()


def gather_tiles(block, ident):
    any_place = pl.BlockSpec(memory_space=pl.ANY)
    dma = pltpu.SemaphoreType.DMA
    return pl.pallas_call(
        tiles_kernel,
        out_shape=jax.ShapeDtypeStruct((4,) + block.shape, block.dtype),
        in_specs=[any_place],
        out_specs=any_place,
        scratch_shapes=[dma((1,)), dma((2, 3))],
        compiler_params=pltpu.CompilerParams(collective_id=ident, has_side_effects=True),
    )(block)


def sum_kernel(parts, total, near_in, pair, far_in, sems):
    blk, batch = lax.axis_index("blk"), lax.axis_index("batch")
    mate, across = (blk ^ 1, batch), (blk ^ 2, batch)
    greet([mate, across])
    far_first = send(parts.at[blk ^ 3], near_in.at[0], sems.at[0, 0], sems.at[1, 0], mate)
    near_next = send(parts.at[blk ^ 1], near_in.at[1], sems.at[0, 1], sems.at[1, 1], mate)
    far_first.wait_recv()
    pair[...] = (parts[blk ^ 2].astype(F32) + near_in[0].astype(F32)).astype(pair.dtype)
    far = send(pair, far_in, sems.at[0, 2], sems.at[1, 2], across)
    near_next.wait_recv()
    total[...] = parts[blk].astype(F32) + near_in[1].astype(F32)
    far.wait_recv()
    total[...] += far_in[...].astype(F32)
    far_first.wait_send()
    near_next.wait_send()
    far.wait_send()


def sum_tiles(parts, ident):
    dma = pltpu.SemaphoreType.DMA
    block = parts.shape[1:]
    vmem = pl.BlockSpec(memory_space=pltpu.VMEM)
    return pl.pallas_call(
        sum_kernel,
        out_shape=jax.ShapeDtypeStruct(block, F32),
        in_specs=[vmem],
        out_specs=vmem,
        scratch_shapes=[
            pltpu.VMEM((2,) + block, parts.dtype),
            pltpu.VMEM(block, parts.dtype),
            pltpu.VMEM(block, parts.dtype),
            dma((2, 3)),
        ],
        compiler_params=pltpu.CompilerParams(
            collective_id=ident, has_side_effects=True, vmem_limit_bytes=32 * 2**20
        ),
    )(parts)


def combine(slots, weights, half, centred):
    count = slots.shape[0]
    if not centred:
        total = slots[0]
        for at in range(1, count):
            total = total + slots[at]
        return total
    size = weights[0]
    mean = slots[0, :half] * weights[0]
    for at in range(1, count):
        size = size + weights[at]
        mean = mean + slots[at, :half] * weights[at]
    mean = mean / size
    spread = None
    for at in range(count):
        gap = slots[at, :half] - mean
        term = slots[at, half : 2 * half] + weights[at] * gap * gap
        spread = term if spread is None else spread + term
    rest = [jnp.zeros((slots.shape[1] - 2 * half, LANES), F32)] * (slots.shape[1] > 2 * half)
    return jnp.concatenate([mean, spread] + rest, 0)


def sums_kernel(images, half, centred, tiled, own, tile_sizes, sizes, total, *scratch):
    blk, batch = lax.axis_index("blk"), lax.axis_index("batch")
    slots, sems = scratch[0], scratch[1]
    peers = [(blk, batch ^ mask) for mask in range(1, images)]
    mates = [(blk ^ mask, batch) for mask in range(1, 4)] if tiled else []
    greet(peers + mates)
    if tiled:
        tile_slots, tile_sems = scratch[2], scratch[3]
        tile_slots[blk] = own[...]
        copies = [
            send(own, tile_slots.at[blk], tile_sems.at[0, at], tile_sems.at[1, at], peer)
            for at, peer in enumerate(mates)
        ]
        for copy in copies:
            copy.wait()
        slots[batch] = combine(tile_slots, tile_sizes, half, centred)
    else:
        slots[batch] = own[...]
    copies = [
        send(slots.at[batch], slots.at[batch], sems.at[0, at], sems.at[1, at], peer)
        for at, peer in enumerate(peers)
    ]
    for copy in copies:
        copy.wait()
    total[...] = combine(slots, sizes, half, centred)


def all_sums(first, second, tile_sizes, sizes, centred, tiled, ident):
    images = sizes.shape[0]
    channels = first.shape[0]
    half = channels // LANES
    rows = -(-2 * half // 8) * 8
    own = jnp.concatenate(
        [first, second, jnp.zeros(((rows - 2 * half) * LANES,), F32)]
    ).reshape(rows, LANES)
    dma = pltpu.SemaphoreType.DMA
    vmem = pl.BlockSpec(memory_space=pltpu.VMEM)
    scratch = [pltpu.VMEM((images, rows, LANES), F32), dma((2, images))]
    if tiled:
        scratch += [pltpu.VMEM((4, rows, LANES), F32), dma((2, 3))]
    total = pl.pallas_call(
        functools.partial(sums_kernel, images, half, centred, tiled),
        out_shape=jax.ShapeDtypeStruct((rows, LANES), F32),
        in_specs=[vmem] * 3,
        out_specs=vmem,
        scratch_shapes=scratch,
        compiler_params=pltpu.CompilerParams(collective_id=ident, has_side_effects=True),
    )(own, sizes if tile_sizes is None else tile_sizes, sizes)
    flat = total.reshape(-1)
    return flat[:channels], flat[channels : 2 * channels]


def silu_slope(values):
    sigmoid_value = jax.nn.sigmoid(values)
    return sigmoid_value * (1.0 + values * (1.0 - sigmoid_value))


def windows(cells, rows, cols, back):
    channels = cells.shape[1]
    padded = jnp.pad(cells.reshape(rows, cols, channels), ((1, 1), (1, 1), (0, 0)))
    taken = []
    for offset in range(9):
        row, col = offset // 3, offset % 3
        if back:
            row, col = 2 - row, 2 - col
        taken.append(padded[row : row + rows, col : col + cols].reshape(rows * cols, channels))
    return jnp.concatenate(taken, 1)


def dot(left, right):
    return jnp.dot(left, right, preferred_element_type=F32)


def dot_t(left, right):
    return jnp.einsum("pd,cd->pc", left, right, preferred_element_type=F32)


def t_dot(left, right):
    return jnp.einsum("pc,pd->cd", left, right, preferred_element_type=F32)


def on_device_any(
    nt,
    nb,
    features,
    crop_rows,
    crop_cols,
    depth_target,
    labels,
    first_weight,
    spatial_weight,
    last_weight,
    shared_weight,
    head_weights,
    message_weights,
    gate_weights,
    depth_weight,
    class_weight,
    mid_gain,
    mid_bias,
    out_gain,
    out_bias,
):
    tile_rows, cols, width = features.shape[1:]
    tile = tile_rows * cols
    rows = tile_rows * nt
    pixels = rows * cols
    tasks = head_weights.shape[0]
    mid = first_weight.shape[1]
    share = mid // nb
    slim = mid // nt
    piece = width // (nb * nt)
    wide = nb * piece
    classes = class_weight.shape[1]
    blk, batch = lax.axis_index("blk"), lax.axis_index("batch")

    image_rows = lax.dynamic_index_in_dim(crop_rows, batch, 0, False)
    image_cols = lax.dynamic_index_in_dim(crop_cols, batch, 0, False)
    row_ids = jnp.arange(rows, dtype=jnp.int32)
    col_ids = jnp.arange(cols, dtype=jnp.int32)
    inside_grid = (row_ids[:, None] < image_rows) & (col_ids[None, :] < image_cols)
    inside = inside_grid.astype(F32).reshape(pixels, 1)
    inside_tile = lax.dynamic_slice_in_dim(inside, blk * tile, tile, 0)
    sizes_flat = (crop_rows * crop_cols).astype(F32)
    valid_count = jnp.sum(sizes_flat)
    sizes = jnp.broadcast_to(sizes_flat[:, None, None], (nb, 1, LANES))
    tile_counts = jnp.sum(inside.reshape(nt, tile), 1)
    tile_sizes = jnp.broadcast_to(tile_counts[:, None, None], (nt, 1, LANES))
    image_size = jnp.maximum(jnp.sum(inside), 1.0)
    tile_size = jnp.maximum(jnp.sum(inside_tile), 1.0)

    params = jnp.concatenate(
        [
            mid_gain.reshape(-1),
            mid_bias.reshape(-1),
            out_gain,
            out_bias,
            depth_weight,
            class_weight.reshape(-1),
        ]
    )
    room = -(-params.shape[0] // (16 * LANES)) * 16 * LANES
    small = jnp.pad(params, (0, room - params.shape[0])).reshape(-1, LANES)
    full_first, smalls = gather_first(first_weight, small, nb)
    full_first = full_first.reshape(width, mid)
    smalls = smalls.reshape(nb, room)
    at = 0

    def taken(count):
        nonlocal at
        found = smalls[:, at : at + count]
        at += count
        return found

    norms = mid_gain.shape[0]
    gain_mid = taken(norms * share).reshape(nb, norms, share).swapaxes(0, 1)
    gain_mid = gain_mid.reshape(norms, mid).astype(F32)
    bias_mid = taken(norms * share).reshape(nb, norms, share).swapaxes(0, 1)
    bias_mid = bias_mid.reshape(norms, mid).astype(F32)
    gain_out = lax.dynamic_index_in_dim(taken(nt * piece).reshape(nb, nt, piece), blk, 1, False)
    gain_out = gain_out.reshape(wide).astype(F32)
    bias_out = lax.dynamic_index_in_dim(taken(nt * piece).reshape(nb, nt, piece), blk, 1, False)
    bias_out = bias_out.reshape(wide).astype(F32)
    full_depth = taken(share).reshape(mid, 1)
    full_classes = taken(share * classes).reshape(mid, classes)
    stream_weight = jnp.concatenate([full_depth, full_classes], 1)

    spatial = lax.all_gather(
        lax.dynamic_slice_in_dim(spatial_weight, blk * slim, slim, 2), "batch", axis=1, tiled=True
    )
    last = lax.dynamic_index_in_dim(last_weight.reshape(share, nb, nt, piece), blk, 2, False)
    last = lax.all_gather(last.reshape(share, wide), "batch", axis=0, tiled=True)
    shared = lax.dynamic_slice_in_dim(shared_weight, blk * piece, piece, 0)
    shared = lax.all_gather(shared, "batch", axis=0, tiled=True)
    head = lax.all_gather(
        lax.dynamic_index_in_dim(head_weights, blk, 0, False), "batch", axis=1, tiled=True
    )
    message = lax.all_gather(
        lax.dynamic_index_in_dim(message_weights, blk, 0, False), "batch", axis=1, tiled=True
    )
    gate = lax.all_gather(
        lax.dynamic_index_in_dim(gate_weights, blk, 0, False), "batch", axis=0, tiled=True
    )

    flat_features = features.reshape(tile, width)
    cut = flat_features.reshape(tile, nb, nt, piece).transpose(2, 0, 1, 3).reshape(nt, tile, wide)
    wide_features = swap_tiles(cut, blk, nt)

    def slim_of(vector):
        return lax.dynamic_slice_in_dim(vector, blk * slim, slim, 0)

    def normalize(values, mask, local_size, gain, bias, tiled, ident):
        mean = jnp.sum(values * mask, 0) / local_size
        gap = values - mean
        spread = jnp.sum(gap * gap * mask, 0)
        centre, total = all_sums(mean, spread, tile_sizes, sizes, True, tiled, ident)
        inverse = lax.rsqrt(total / valid_count + EPSILON)
        normed = (values - centre) * inverse
        return normed * gain + bias, normed, inverse

    def normalize_back(grad, normed, inverse, gain, mask, tiled, ident):
        bias_sum, gain_sum = all_sums(
            jnp.sum(grad, 0), jnp.sum(grad * normed, 0), tile_sizes, sizes, False, tiled, ident
        )
        back = (
            inverse * gain * (grad - bias_sum / valid_count - normed * gain_sum / valid_count) * mask
        )
        return back.astype(BF16), gain_sum, bias_sum

    def act(values, mask):
        return (jax.nn.silu(values) * mask).astype(BF16)

    def by_rows(blocks):
        return blocks.reshape(pixels, blocks.shape[2])

    def by_channels(blocks):
        return blocks.swapaxes(0, 1).reshape(pixels, nt * blocks.shape[2])

    def cut_channels(values):
        return values.astype(BF16).reshape(pixels, nt, slim).swapaxes(0, 1)

    pre_one = dot(flat_features, full_first)
    norm_one, normed_one, inverse_one = normalize(
        pre_one, inside_tile, tile_size, gain_mid[0], bias_mid[0], True, 1
    )
    act_one = by_rows(gather_tiles(act(norm_one, inside_tile), 2))
    pre_two = dot(windows(act_one, rows, cols, False), spatial.reshape(9 * mid, slim))
    gain_two, bias_two = slim_of(gain_mid[1]), slim_of(bias_mid[1])
    norm_two, normed_two, inverse_two = normalize(
        pre_two, inside, image_size, gain_two, bias_two, False, 3
    )
    act_two = by_channels(gather_tiles(act(norm_two, inside), 4))
    pre_three = dot(act_two, last)
    norm_three, normed_three, inverse_three = normalize(
        pre_three, inside, image_size, gain_out, bias_out, False, 5
    )
    joined = norm_three + wide_features.astype(F32)
    act_three = act(joined, inside)
    pre_four = sum_tiles(cut_channels(dot(act_three, shared)), 6)
    gain_four, bias_four = slim_of(gain_mid[2]), slim_of(bias_mid[2])
    norm_four, normed_four, inverse_four = normalize(
        pre_four, inside, image_size, gain_four, bias_four, False, 3
    )
    shared_act = by_channels(gather_tiles(act(norm_four, inside), 4))

    gain_task = lax.dynamic_index_in_dim(gain_mid, 3 + blk, 0, False)
    bias_task = lax.dynamic_index_in_dim(bias_mid, 3 + blk, 0, False)
    pre_five = dot(windows(shared_act, rows, cols, False), head.reshape(9 * mid, mid))
    norm_five, normed_five, inverse_five = normalize(
        pre_five, inside, image_size, gain_task, bias_task, False, 5
    )
    task_act = act(norm_five, inside)
    messages = dot(windows(task_act, rows, cols, False), message.reshape(9 * mid, mid))
    gate_open = jax.nn.sigmoid(dot(task_act, gate))
    gated = (gate_open * messages).astype(BF16)
    is_first, is_last = blk == 0, blk == tasks - 1
    depth_part = jnp.where(is_first, task_act, gated)
    sem_part = jnp.where(is_last, task_act, gated)
    depth_share = jnp.einsum("pc,co->op", depth_part, full_depth, preferred_element_type=F32)
    class_share = jnp.einsum("pc,co->op", sem_part, full_classes, preferred_element_type=F32)
    lift = -(-(1 + classes) // 8) * 8 - 1 - classes
    shares = jnp.concatenate([depth_share, class_share, jnp.zeros((lift, pixels), F32)], 0)
    streams = jnp.sum(gather_tiles(shares, 7), 0).T
    depth_out = lax.dynamic_slice_in_dim(streams, blk * tile, tile, 0)[:, 0]
    logits = lax.dynamic_slice_in_dim(streams, blk * tile, tile, 0)[:, 1 : 1 + classes]
    targets = by_rows(gather_tiles_pair(depth_target, labels, tile))
    all_depth, all_logits = streams[:, :1], streams[:, 1 : 1 + classes]
    depth_slope = ((all_depth - targets[:, :1]) * inside).astype(BF16)
    onehot = (targets[:, 1:2] == jnp.arange(classes, dtype=jnp.int32)[None, :].astype(F32)).astype(F32)
    logit_slope = ((jax.nn.softmax(all_logits, axis=1) - onehot) * inside).astype(BF16)
    grad_depth = t_dot(depth_part, depth_slope)
    grad_classes = t_dot(sem_part, logit_slope)
    depth_back = depth_slope.astype(F32) * full_depth.astype(F32).reshape(1, mid)
    sem_back = dot_t(logit_slope, full_classes)
    zero = jnp.zeros((), F32)
    grad_gated = jnp.where(is_first, zero, depth_back) + jnp.where(is_last, zero, sem_back)
    grad_direct = jnp.where(is_first, depth_back, zero) + jnp.where(is_last, sem_back, zero)

    grad_msg = (grad_gated * gate_open).astype(BF16)
    grad_gate = (grad_gated * messages * gate_open * (1.0 - gate_open)).astype(BF16)
    msg_windows = windows(grad_msg, rows, cols, True)
    gate_grads = t_dot(task_act, grad_gate).astype(BF16)
    message_grads = t_dot(task_act, msg_windows).astype(BF16)
    share_messages = lax.psum_scatter(message_grads, "batch", scatter_dimension=0, tiled=True)
    task_grad = (
        grad_direct
        + dot_t(grad_gate, gate)
        + dot(msg_windows, message.swapaxes(1, 2).reshape(9 * mid, mid))
    )
    grad_norm_five = task_grad * inside * silu_slope(norm_five)
    grad_pre_five, gain_sum_five, bias_sum_five = normalize_back(
        grad_norm_five, normed_five, inverse_five, gain_task, inside, False, 8
    )
    five_windows = windows(grad_pre_five, rows, cols, True)
    head_grads = t_dot(shared_act, five_windows).astype(BF16)
    share_heads = lax.psum_scatter(head_grads, "batch", scatter_dimension=0, tiled=True)
    shared_back = dot(five_windows, head.swapaxes(1, 2).reshape(9 * mid, mid))
    shared_back = sum_tiles(cut_channels(shared_back), 6)

    grad_norm_four = shared_back * inside * silu_slope(norm_four)
    grad_pre_four, gain_sum_four, bias_sum_four = normalize_back(
        grad_norm_four, normed_four, inverse_four, gain_four, inside, False, 9
    )
    grad_four = by_channels(gather_tiles(grad_pre_four, 4))
    shared_grads = t_dot(act_three, grad_four).astype(BF16)
    grad_joined = dot_t(grad_four, shared) * inside * silu_slope(joined)
    grad_three, gain_sum_three, bias_sum_three = normalize_back(
        grad_joined, normed_three, inverse_three, gain_out, inside, False, 8
    )
    last_grads = t_dot(act_two, grad_three).astype(BF16)
    two_back = sum_tiles(cut_channels(dot_t(grad_three, last)), 6)
    grad_norm_two = two_back * inside * silu_slope(norm_two)
    grad_two, gain_sum_two, bias_sum_two = normalize_back(
        grad_norm_two, normed_two, inverse_two, gain_two, inside, False, 9
    )
    two_windows = windows(grad_two, rows, cols, True)
    spatial_grads = t_dot(act_one, two_windows).astype(BF16)
    one_back = dot(two_windows, spatial.swapaxes(1, 2).reshape(9 * slim, mid))
    one_back = sum_tiles(one_back.astype(BF16).reshape(nt, tile, mid), 10)
    grad_norm_one = one_back * inside_tile * silu_slope(norm_one)
    grad_one, gain_sum_one, bias_sum_one = normalize_back(
        grad_norm_one, normed_one, inverse_one, gain_mid[0], inside_tile, True, 11
    )
    all_one = by_rows(gather_tiles(grad_one, 2))
    first_grads = t_dot(wide_features, all_one).astype(BF16)
    joined_tiles = swap_tiles(grad_joined.astype(BF16).reshape(nt, tile, wide), blk, nt)
    joined_tiles = joined_tiles.reshape(nt, tile, nb, piece).transpose(1, 2, 0, 3).reshape(tile, width)
    grad_input = dot_t(grad_one, full_first) + joined_tiles.astype(F32)

    stream_grads = jnp.concatenate([grad_depth, grad_classes], 1)
    stream_grads = jnp.pad(stream_grads, ((0, 0), (0, LANES - 1 - classes))).astype(BF16)
    late = jnp.concatenate(
        [spatial_grads, shared_grads.reshape(nb, piece, mid).reshape(mid, -1),
         last_grads, first_grads.reshape(mid, -1), gate_grads, stream_grads],
        1,
    )
    late_share = lax.psum_scatter(late, "batch", scatter_dimension=0, tiled=True)
    early_share = jnp.concatenate([share_messages, share_heads], 1)
    early = lax.all_gather(early_share, "blk", axis=0, tiled=False).astype(F32)
    late_all = gather_tiles(late_share, 12).astype(F32)
    early = early.reshape(nt, share, 2, 9, mid).transpose(2, 0, 3, 1, 4)
    red_messages, red_heads = early[0], early[1]
    at = 0

    def part(count):
        nonlocal at
        found = late_all[:, :, at : at + count]
        at += count
        return found

    red_spatial = part(9 * slim).reshape(nt, share, 9, slim).transpose(2, 1, 0, 3).reshape(9, share, mid)
    red_shared = part(wide * mid // mid).reshape(nt * piece, mid)
    red_last = part(wide).reshape(nt, share, nb, piece).transpose(1, 2, 0, 3).reshape(share, width)
    red_first = part(wide * mid // mid).reshape(nt * piece, mid)
    red_gates = part(mid)
    streams_red = jnp.sum(part(LANES), 0)
    red_depth = streams_red[:, 0]
    red_classes = streams_red[:, 1 : 1 + classes]

    sums = jnp.concatenate(
        [
            gain_sum_five,
            bias_sum_five,
            gain_sum_three,
            bias_sum_three,
            gain_sum_two,
            bias_sum_two,
            gain_sum_four,
            bias_sum_four,
        ]
    ).reshape(-1, LANES)
    sums = jnp.pad(sums, ((0, -sums.shape[0] % 8), (0, 0)))
    sums = gather_tiles(sums, 13).reshape(nt, -1)
    five_gain, five_bias = sums[:, :mid], sums[:, mid : 2 * mid]
    at_out = 2 * mid
    three_gain = sums[:, at_out : at_out + wide].reshape(nt, nb, piece)
    three_bias = sums[:, at_out + wide : at_out + 2 * wide].reshape(nt, nb, piece)
    at_slim = at_out + 2 * wide
    slims = [
        sums[:, at_slim + i * slim : at_slim + (i + 1) * slim].reshape(1, mid) for i in range(4)
    ]
    mid_gains = jnp.concatenate([gain_sum_one[None], slims[0], slims[2], five_gain], 0)
    mid_biases = jnp.concatenate([bias_sum_one[None], slims[1], slims[3], five_bias], 0)
    grad_mid_gain = lax.dynamic_slice_in_dim(mid_gains, batch * share, share, 1)
    grad_mid_bias = lax.dynamic_slice_in_dim(mid_biases, batch * share, share, 1)
    grad_out_gain = lax.dynamic_index_in_dim(three_gain, batch, 1, False).reshape(nt * piece)
    grad_out_bias = lax.dynamic_index_in_dim(three_bias, batch, 1, False).reshape(nt * piece)
    return (
        depth_out.reshape(1, tile_rows, cols),
        logits.reshape(1, tile_rows, cols, classes),
        grad_input.reshape(1, tile_rows, cols, width),
        red_first,
        red_spatial,
        red_last,
        red_shared,
        red_heads,
        red_messages,
        red_gates,
        red_depth,
        red_classes,
        grad_mid_gain,
        grad_mid_bias,
        grad_out_gain,
        grad_out_bias,
    )


def swap_tiles(blocks, blk, nt):
    out = jnp.zeros_like(blocks)
    out = lax.dynamic_update_index_in_dim(
        out, lax.dynamic_index_in_dim(blocks, blk, 0, False), blk, 0
    )
    for mask in range(1, nt):
        sent = lax.dynamic_index_in_dim(blocks, blk ^ mask, 0, False)
        came = lax.ppermute(sent, "blk", [(i, i ^ mask) for i in range(nt)])
        out = lax.dynamic_update_index_in_dim(out, came, blk ^ mask, 0)
    return out.reshape(-1, blocks.shape[2])


def gather_tiles_pair(depth_target, labels, tile):
    pair = jnp.stack([depth_target.reshape(tile), labels.reshape(tile).astype(F32)], 0)
    pair = jnp.pad(pair, ((0, 6), (0, 0)))
    return gather_tiles(pair, 14).swapaxes(1, 2)


PITCH = 48
CHUNK = 64
BLOCK = 256
ANY = pl.BlockSpec(memory_space=pl.ANY)
VMEM = pl.BlockSpec(memory_space=pltpu.VMEM)
DMA = pltpu.SemaphoreType.DMA
LONG = pl.CostEstimate(flops=80_000_000_000, bytes_accessed=30_000_000, transcendentals=2_000_000)


class Mail:
    def __init__(self, sems):
        self.sems, self.used, self.open = sems, 0, []

    def send(self, src, dst, peer):
        copy = send(src, dst, self.sems.at[0, self.used], self.sems.at[1, self.used], peer)
        self.used += 1
        self.open.append(copy.wait_send)
        return copy

    def local(self, src, dst):
        copy = pltpu.make_async_copy(src, dst, self.sems.at[0, self.used])
        copy.start()
        self.used += 1
        return copy

    def close(self):
        for wait in self.open:
            wait()
        self.open = []


class Place:
    def __init__(self, images):
        self.blk, self.batch = lax.axis_index("blk"), lax.axis_index("batch")
        self.images = images
        self.mate = (self.blk ^ 1, self.batch)
        self.across = (self.blk ^ 2, self.batch)
        self.tiles = [(self.blk ^ mask, self.batch) for mask in range(1, 4)]
        self.others = [(self.blk, self.batch ^ mask) for mask in range(1, images)]
        self.side = (self.blk, self.batch ^ 1)


class Spread:
    def __init__(self, mail, place, own, slot):
        self.mail, self.place, self.own, self.slot = mail, place, own, slot
        self.z_copies, self.x_copies = [], []

    def start(self):
        place, here = self.place, self.slot(self.place.batch)
        self.here = self.mail.local(self.own, here)
        for mask in range(1, place.images // 2):
            peer = (place.blk, place.batch ^ (2 * mask))
            self.z_copies.append(self.mail.send(self.own, here, peer))
        self.x_copies.append(self.mail.send(self.own, here, place.side))
        return self

    def forward(self):
        for mask, copy in enumerate(self.z_copies, 1):
            copy.wait_recv()
            block = self.slot(self.place.batch ^ (2 * mask))
            self.x_copies.append(self.mail.send(block, block, self.place.side))

    def finish(self):
        self.here.wait()
        for copy in self.x_copies:
            copy.wait_recv()


def share_tiles(mail, place, slot):
    own = slot(place.blk)
    far = mail.send(own, own, place.across)
    near = mail.send(own, own, place.mate)
    far.wait_recv()
    passed = slot(place.blk ^ 2)
    last = mail.send(passed, passed, place.mate)
    near.wait_recv()
    last.wait_recv()


def loop(total, step, body):
    def run(at, carry):
        body(pl.ds(pl.multiple_of(at * step, step), step))
        return carry

    lax.fori_loop(0, total // step, run, 0)


def folded(values):
    return jnp.sum(values.reshape(values.shape[0] // 8, 8, values.shape[1]), 0)


def loop_sums(total, channels, count, body):
    def run(at, carry):
        found = body(pl.ds(pl.multiple_of(at * CHUNK, CHUNK), CHUNK))
        return tuple(kept + folded(one) for kept, one in zip(carry, found))

    start = tuple(jnp.zeros((8, channels), F32) for _ in range(count))
    return [jnp.sum(one, 0, keepdims=True) for one in lax.fori_loop(0, total // CHUNK, run, start)]


def merge(slots, sizes, channels):
    count = slots.shape[0]
    size, mean = None, None
    for at in range(count):
        weight = sizes[at, :, :channels]
        term = slots[at, 0:1, :] * weight
        size = weight if size is None else size + weight
        mean = term if mean is None else mean + term
    mean = mean / size
    spread = None
    for at in range(count):
        gap = slots[at, 0:1, :] - mean
        term = slots[at, 1:2, :] + sizes[at, :, :channels] * gap * gap
        spread = term if spread is None else spread + term
    return mean, spread, size


def add_up(slots):
    total = slots[0]
    for at in range(1, slots.shape[0]):
        total = total + slots[at]
    return total[0:1, :], total[1:2, :]


def swap_sums(mail, place, slots):
    own = slots.at[place.batch]
    copies = [mail.send(own, own, peer) for peer in place.others]
    for copy in copies:
        copy.wait_recv()


def swap_tile_sums(mail, place, slots):
    own = slots.at[place.blk]
    copies = [mail.send(own, own, peer) for peer in place.tiles]
    for copy in copies:
        copy.wait_recv()


def local_stats(pre, mask, base, total, channels, size):
    def first(rows):
        return (pre[rows, :] * mask[at_base(base, rows), :],)

    (summed,) = loop_sums(total, channels, 1, first)
    mean = summed / jnp.maximum(size, 1.0)

    def second(rows):
        gap = pre[rows, :] - mean
        return (gap * gap * mask[at_base(base, rows), :],)

    (spread,) = loop_sums(total, channels, 1, second)
    return mean, spread


def at_base(base, rows):
    if base is None:
        return rows
    return pl.ds(pl.multiple_of(base + rows.start, CHUNK), rows.size)


def batch_norm_stats(mail, place, pre, mask, slots, sizes, stats, row, channels):
    total = pre.shape[0]
    mean, spread = local_stats(pre, mask, None, total, channels, sizes[place.batch, :, :channels])
    slots[place.batch] = jnp.concatenate([mean, spread], 0)
    swap_sums(mail, place, slots)
    keep_stats(slots, sizes, stats, row, channels)


def keep_stats(slots, sizes, stats, row, channels):
    mean, spread, size = merge(slots, sizes, channels)
    stats[row : row + 1, :channels] = mean
    stats[row + 1 : row + 2, :channels] = lax.rsqrt(spread / size + EPSILON)


def silu(values):
    return values * jax.nn.sigmoid(values)


def widen(cells, left, right, total):
    def body(rows):
        seen = cells[pl.ds(pl.multiple_of(rows.start + PITCH - 16, 16), CHUNK + 32), :].astype(F32)
        here = pl.ds(pl.multiple_of(rows.start + PITCH, 16), CHUNK)
        left[here, :] = seen[15 : 15 + CHUNK].astype(BF16)
        right[here, :] = seen[17 : 17 + CHUNK].astype(BF16)

    loop(total, CHUNK, body)


def clear_ends(cells, total):
    zeros = jnp.zeros((PITCH, cells.shape[1]), cells.dtype)
    cells[0:PITCH, :] = zeros
    cells[PITCH + total : 2 * PITCH + total, :] = zeros


def conv_rows(shifted, rows, weight, back):
    total = None
    for offset in range(9):
        row, col = offset // 3, offset % 3
        if back:
            row, col = 2 - row, 2 - col
        window = shifted[col][pl.ds(pl.multiple_of(rows.start + PITCH * row, 16), rows.size), :]
        product = weight(offset, window)
        total = product if total is None else total + product
    return total


def sum_over_tiles(mail, place, part, near_in, pair, far_in, total, out):
    far_first = mail.send(part(place.blk ^ 3), near_in.at[0], place.mate)
    near_next = mail.send(part(place.blk ^ 1), near_in.at[1], place.mate)
    far_first.wait_recv()
    mine_far, mine = part(place.blk ^ 2), part(place.blk)

    def pairs(rows):
        pair[rows, :] = (mine_far[rows, :].astype(F32) + near_in[0, rows, :].astype(F32)).astype(BF16)

    loop(total, CHUNK, pairs)
    far = mail.send(pair, far_in, place.across)
    near_next.wait_recv()
    far.wait_recv()

    def finish(rows):
        out[rows, :] = (
            mine[rows, :].astype(F32) + near_in[1, rows, :].astype(F32) + far_in[rows, :].astype(F32)
        )

    loop(total, CHUNK, finish)


def start_kernel(
    images,
    weight,
    small,
    spatial_own,
    feat,
    mask,
    sizes,
    tile_sizes,
    full,
    smalls,
    wide,
    spatial,
    pre_one,
    stats,
    slots_tile,
    slots_one,
    sems,
):
    place = Place(images)
    mail = Mail(sems)
    blk, batch = place.blk, place.batch
    depth = weight.shape[0]
    half = depth // 2
    mid = weight.shape[1]
    tile = feat.shape[0]
    slim = mid // 4
    share = spatial_own.shape[1]
    mine = pl.ds(pl.multiple_of(lax.rem(blk, 2) * half, half), half)
    greet(place.others + place.tiles)
    here = mail.local(weight, full.at[batch])
    here_small = mail.local(small, smalls.at[batch])
    z_copies, x_copies, arrived, late = {}, [], [], []
    for peer in place.others:
        late.append(mail.send(small, smalls.at[batch], peer))
    for mask_z in range(1, images // 2):
        z_copies[mask_z] = mail.send(
            weight.at[mine], full.at[batch, mine], (blk, batch ^ (2 * mask_z))
        )
    x_copies.append(mail.send(weight.at[mine], full.at[batch, mine], place.side))
    lanes = pl.ds(pl.multiple_of(blk * slim, slim), slim)
    got_spatial = Spread(
        mail,
        place,
        spatial_own.at[:, :, lanes],
        lambda index: spatial.at[:, pl.ds(pl.multiple_of(index * share, share), share), :],
    ).start()

    def columns(index):
        return feat.at[:, pl.ds(pl.multiple_of(index * mid, mid), mid)]

    landing = wide.at[pl.ds(pl.multiple_of(blk * tile, tile), tile), :]
    here_wide = mail.local(columns(blk), landing)
    for mask_t in range(1, 4):
        late.append(mail.send(columns(blk ^ mask_t), landing, (blk ^ mask_t, batch)))

    def hand_over(source):
        block = full.at[source, mine]
        arrived.append(mail.send(block, block, place.mate))

    for mask_z in range(1, images // 2):
        z_copies[mask_z].wait_recv()
        source = batch ^ (2 * mask_z)
        block = full.at[source, mine]
        x_copies.append(mail.send(block, block, place.side))
        hand_over(source)
    for mask_z in range(images // 2):
        x_copies[mask_z].wait_recv()
        hand_over(batch ^ (2 * mask_z + 1))
    stats[...] = jnp.zeros_like(stats)
    here.wait()
    for copy in arrived:
        copy.wait_recv()

    def reduce(rows):
        total = None
        for index in range(images):
            product = dot(feat[rows, index * depth : (index + 1) * depth], full[index])
            total = product if total is None else total + product
        pre_one[rows, :] = total

    loop(tile, tile // 2, reduce)
    base = blk * tile
    mean, spread = local_stats(pre_one, mask, base, tile, mid, tile_sizes[blk, :, :])
    slots_tile[blk] = jnp.concatenate([mean, spread], 0)
    swap_tile_sums(mail, place, slots_tile)
    mean, spread, _ = merge(slots_tile, tile_sizes, mid)
    slots_one[batch] = jnp.concatenate([mean, spread], 0)
    swap_sums(mail, place, slots_one)
    keep_stats(slots_one, sizes, stats, 0, mid)
    got_spatial.forward()
    got_spatial.finish()
    for copy in late:
        copy.wait_recv()
    here_small.wait()
    here_wide.wait()
    mail.close()


def begin(nb, weight, small, spatial, feat, mask, sizes, tile_sizes):
    depth, mid = weight.shape
    tile = feat.shape[0]

    def array(*shape, kind=BF16):
        return jax.ShapeDtypeStruct(shape, kind)

    return pl.pallas_call(
        functools.partial(start_kernel, nb),
        out_shape=(
            array(nb, depth, mid),
            array(nb, *small.shape),
            array(4 * tile, mid),
            array(9, mid, mid // 4),
            array(tile, mid, kind=F32),
            array(8, mid, kind=F32),
        ),
        in_specs=[ANY] * 3 + [VMEM] * 4,
        out_specs=(VMEM, ANY, VMEM, VMEM, VMEM, VMEM),
        scratch_shapes=[
            pltpu.VMEM((4, 2, mid), F32),
            pltpu.VMEM((nb, 2, mid), F32),
            DMA((2, 64)),
        ],
        cost_estimate=LONG,
        compiler_params=pltpu.CompilerParams(
            collective_id=21, has_side_effects=True, vmem_limit_bytes=40 * 2**20
        ),
    )(weight, small, spatial, feat, mask, sizes, tile_sizes)


def forward_kernel(
    images,
    early,
    pre_one,
    first_stats,
    spatial,
    wide,
    mask,
    norms,
    sizes,
    last_own,
    shared_own,
    gate_own,
    message_own,
    last,
    shared,
    gate,
    message,
    act_one,
    act_two,
    act_three,
    shared_act,
    pre_two,
    pre_three,
    pre_four,
    stats,
    one_left,
    one_right,
    parts,
    near_in,
    pair,
    far_in,
    slots_two,
    slots_three,
    slots_four,
    sems,
):
    place = Place(images)
    mail = Mail(sems)
    blk, batch = place.blk, place.batch
    tile, total = pre_one.shape[0], mask.shape[0]
    mid = pre_one.shape[1]
    slim = pre_two.shape[1]
    share = last_own.shape[0]
    base = blk * tile
    greet(place.others + place.tiles)

    def rows_of(index):
        return pl.ds(pl.multiple_of(index * share, share), share)

    def slim_lanes(index):
        return pl.ds(pl.multiple_of(index * slim, slim), slim)

    lanes = slim_lanes(blk)
    wide_lanes = pl.ds(pl.multiple_of(blk * mid, mid), mid)
    got_last = Spread(mail, place, last_own.at[:, wide_lanes], lambda index: last.at[rows_of(index), :])
    got_shared = Spread(mail, place, shared_own, lambda index: shared.at[rows_of(index), :])
    got_gate = Spread(mail, place, gate_own.at[blk], lambda index: gate.at[rows_of(index), :])
    got_message = [
        Spread(
            mail,
            place,
            message_own.at[blk, offset],
            lambda index, offset=offset: message.at[offset, rows_of(index), :],
        )
        for offset in range(early)
    ]
    got_last.start()
    got_shared.start()
    stats[...] = first_stats[...]
    clear_ends(act_one, total)
    clear_ends(one_left, total)
    clear_ends(one_right, total)

    def act_first(rows):
        value = (pre_one[rows, :] - stats[0:1, :]) * stats[1:2, :] * norms[0:1, :] + norms[1:2, :]
        value = silu(value) * mask[at_base(base, rows), :]
        act_one[pl.ds(pl.multiple_of(PITCH + base + rows.start, 16), CHUNK), :] = value.astype(BF16)

    loop(tile, CHUNK, act_first)
    share_tiles(
        mail, place, lambda index: act_one.at[pl.ds(pl.multiple_of(PITCH + index * tile, 16), tile), :]
    )
    widen(act_one, one_left, one_right, total)
    got_last.forward()
    got_shared.forward()

    shifted = (one_left, act_one, one_right)

    def conv_two(rows):
        pre_two[rows, :] = conv_rows(
            shifted, rows, lambda offset, window: dot(window, spatial[offset]), False
        )

    loop(total, BLOCK, conv_two)
    batch_norm_stats(mail, place, pre_two, mask, slots_two, sizes, stats, 2, slim)
    got_gate.start()
    got_message[0].start()

    def act_second(rows):
        value = (pre_two[rows, :] - stats[2:3, :slim]) * stats[3:4, :slim]
        value = silu(value * norms[2:3, :slim] + norms[3:4, :slim]) * mask[rows, :]
        act_two[rows, lanes] = value.astype(BF16)

    loop(total, CHUNK, act_second)
    share_tiles(mail, place, lambda index: act_two.at[:, slim_lanes(index)])

    got_last.finish()
    got_gate.forward()

    def expand(rows):
        pre_three[rows, :] = dot(act_two[rows, :], last[...])

    loop(total, BLOCK, expand)
    batch_norm_stats(mail, place, pre_three, mask, slots_three, sizes, stats, 4, mid)
    got_message[0].forward()
    got_message[1].start()
    got_message[2].start()
    got_shared.finish()

    def act_third(rows):
        normed = (pre_three[rows, :] - stats[4:5, :]) * stats[5:6, :]
        value = normed * norms[4:5, :] + norms[5:6, :] + wide[rows, :].astype(F32)
        act_three[rows, :] = (silu(value) * mask[rows, :]).astype(BF16)

    loop(total, CHUNK, act_third)

    def reduce(rows):
        parts[rows, :] = dot(act_three[rows, :], shared[...]).astype(BF16)

    loop(total, BLOCK, reduce)
    sum_over_tiles(
        mail,
        place,
        lambda index: parts.at[:, slim_lanes(index)],
        near_in,
        pair,
        far_in,
        total,
        pre_four,
    )
    got_message[1].forward()
    batch_norm_stats(mail, place, pre_four, mask, slots_four, sizes, stats, 6, slim)
    got_message[2].forward()
    for later in got_message[3:]:
        later.start()

    def act_fourth(rows):
        value = (pre_four[rows, :] - stats[6:7, :slim]) * stats[7:8, :slim]
        value = silu(value * norms[6:7, :slim] + norms[7:8, :slim]) * mask[rows, :]
        shared_act[rows, lanes] = value.astype(BF16)

    loop(total, CHUNK, act_fourth)
    share_tiles(mail, place, lambda index: shared_act.at[:, slim_lanes(index)])
    for later in got_message[3:]:
        later.forward()
    got_gate.finish()
    for one in got_message:
        one.finish()
    mail.close()


def bottleneck(nb, early, pre_one, stats, spatial, wide, mask, norms, sizes, last, shared, gate, message):
    tile, total = pre_one.shape[0], mask.shape[0]
    mid = pre_one.shape[1]
    slim = mid // 4
    padded = total + 2 * PITCH

    def array(*shape, kind=BF16):
        return jax.ShapeDtypeStruct(shape, kind)

    outs = (
        array(mid, mid),
        array(mid, mid),
        array(mid, mid),
        array(early, mid, mid),
        array(padded, mid),
        array(total, mid),
        array(total, mid),
        array(total, mid),
        array(total, slim, kind=F32),
        array(total, mid, kind=F32),
        array(total, slim, kind=F32),
        array(8, mid, kind=F32),
    )
    return pl.pallas_call(
        functools.partial(forward_kernel, nb, early),
        out_shape=outs,
        in_specs=[VMEM] * 7 + [ANY] * 4,
        out_specs=(VMEM, VMEM, ANY, ANY) + (VMEM,) * 8,
        scratch_shapes=[
            pltpu.VMEM((padded, mid), BF16),
            pltpu.VMEM((padded, mid), BF16),
            pltpu.VMEM((total, mid), BF16),
            pltpu.VMEM((2, total, slim), BF16),
            pltpu.VMEM((total, slim), BF16),
            pltpu.VMEM((total, slim), BF16),
            pltpu.VMEM((nb, 2, slim), F32),
            pltpu.VMEM((nb, 2, mid), F32),
            pltpu.VMEM((nb, 2, slim), F32),
            DMA((2, 128)),
        ],
        cost_estimate=LONG,
        compiler_params=pltpu.CompilerParams(
            collective_id=20, has_side_effects=True, vmem_limit_bytes=60 * 2**20
        ),
    )(pre_one, stats, spatial, wide, mask, norms, sizes, last, shared, gate, message)


class Reduce:
    def __init__(self, mail, place, grad, from_side, summed, from_line, out):
        self.mail, self.place = mail, place
        self.grad, self.from_side, self.summed = grad, from_side, summed
        self.from_line, self.out = from_line, out
        self.side = lax.rem(place.batch, 2)
        self.line = lax.div(place.batch, 2)

    def start(self):
        self.from_x = self.mail.send(self.grad.at[:, 1 - self.side], self.from_side, self.place.side)

    def middle(self):
        place = self.place
        self.from_x.wait_recv()
        lines = self.from_side.shape[0]
        for at in range(lines):
            self.summed[at] = (
                self.grad[at, self.side].astype(F32) + self.from_side[at].astype(F32)
            ).astype(BF16)
        self.copies = [
            self.mail.send(
                self.summed.at[self.line ^ mask],
                self.from_line.at[mask - 1],
                (place.blk, place.batch ^ (2 * mask)),
            )
            for mask in range(1, lines)
        ]

    def finish(self):
        total = self.summed[self.line].astype(F32)
        for at, copy in enumerate(self.copies):
            copy.wait_recv()
            total = total + self.from_line[at].astype(F32)
        self.out[...] = total.astype(BF16)


def reduce_scratch(lines, share, columns, own):
    found = [pltpu.VMEM((lines, 2, share, columns), BF16)] if own else []
    return found + [
        pltpu.VMEM((lines, share, columns), BF16),
        pltpu.VMEM((lines, share, columns), BF16),
        pltpu.VMEM((lines - 1, share, columns), BF16),
    ]


def send_sums(mail, place, slots, sums):
    slots[place.batch] = jnp.concatenate(sums, 0)
    own = slots.at[place.batch]
    return [mail.send(own, own, peer) for peer in place.others]


def silu_back(value):
    sigmoid_value = jax.nn.sigmoid(value)
    return sigmoid_value * (1.0 + value * (1.0 - sigmoid_value))


def backward_kernel(
    images,
    back,
    pre_one,
    pre_two,
    pre_three,
    pre_four,
    stats,
    norms,
    mask,
    sizes,
    wide,
    act_one,
    act_two,
    act_three,
    spatial,
    last,
    shared,
    first,
    gate_grads,
    stream_grads,
    grad_input,
    share_shared,
    share_last,
    share_spatial,
    share_first,
    share_gates,
    share_stream,
    sums_out,
    near_four,
    pair_four,
    far_four,
    grad_four,
    all_four,
    grad_three,
    low_three,
    low_joined,
    joined_rows,
    near_two,
    pair_two,
    far_two,
    grad_two,
    two_left,
    two_here,
    two_right,
    turned,
    strip,
    near_one,
    pair_one,
    far_one,
    grad_one,
    all_one,
    slots_four,
    slots_three,
    slots_two,
    slots_tile,
    slots_one,
    *rest,
):
    place = Place(images)
    sems = rest[-1]
    mail = Mail(sems)
    blk, batch = place.blk, place.batch
    tile, total = pre_one.shape[0], mask.shape[0]
    mid = pre_one.shape[1]
    slim = pre_two.shape[1]
    base = blk * tile
    red_shared = Reduce(mail, place, *rest[0:4], share_shared)
    red_last = Reduce(mail, place, *rest[4:8], share_last)
    red_first = Reduce(mail, place, *rest[8:12], share_first)
    red_spatial = Reduce(mail, place, *rest[12:16], share_spatial)
    red_gates = Reduce(mail, place, gate_grads, *rest[16:19], share_gates)
    red_stream = Reduce(mail, place, stream_grads, *rest[19:22], share_stream)
    count = sizes[0]
    for at in range(1, images):
        count = count + sizes[at]
    part = 1.0 / count
    greet(place.others + place.tiles)

    def slim_lanes(index):
        return pl.ds(pl.multiple_of(index * slim, slim), slim)

    def tile_rows(index):
        return pl.ds(pl.multiple_of(index * tile, tile), tile)

    def norm_back(grad, pre, row, channels, lead, offset=None, skip=None):
        height = pre.shape[0]

        def body(rows):
            normed = (pre[rows, :] - stats[row : row + 1, :channels]) * stats[row + 1 : row + 2, :channels]
            value = normed * norms[row : row + 1, :channels] + norms[row + 1 : row + 2, :channels]
            if skip is not None:
                value = value + skip[rows, :].astype(F32)
            found = lead(rows) * mask[at_base(offset, rows), :] * silu_back(value)
            grad[rows, :] = found
            return found, found * normed

        return loop_sums(height, channels, 2, body)

    def through(grad, pre, row, channels, bias_sum, gain_sum, put, offset=None):
        scale = stats[row + 1 : row + 2, :channels] * norms[row : row + 1, :channels]
        bias_part = bias_sum * part[:, :channels]
        gain_part = gain_sum * part[:, :channels]

        def body(rows):
            normed = (pre[rows, :] - stats[row : row + 1, :channels]) * stats[row + 1 : row + 2, :channels]
            found = scale * (grad[rows, :] - bias_part - normed * gain_part)
            put(rows, (found * mask[at_base(offset, rows), :]).astype(BF16))

        loop(pre.shape[0], CHUNK, body)

    def keep(row, bias_sum, gain_sum, channels):
        sums_out[row : row + 1, :channels] = gain_sum
        sums_out[row + 1 : row + 2, :channels] = bias_sum

    sums_out[...] = jnp.zeros_like(sums_out)
    for cells in (two_left, two_here, two_right):
        clear_ends(cells, total)
    red_gates.start()
    red_stream.start()

    sum_over_tiles(
        mail, place, lambda index: back.at[:, slim_lanes(index)], near_four, pair_four, far_four, total, grad_four
    )
    sums = norm_back(grad_four, pre_four, 6, slim, lambda rows: grad_four[rows, :])
    copies = send_sums(mail, place, slots_four, sums)
    for offset in range(9):
        turned[offset * slim : (offset + 1) * slim, :] = spatial[offset].T
    for copy in copies:
        copy.wait_recv()
    bias_sum, gain_sum = add_up(slots_four)
    keep(6, bias_sum, gain_sum, slim)
    lanes = slim_lanes(blk)

    def put_four(rows, value):
        all_four[rows, lanes] = value

    through(grad_four, pre_four, 6, slim, bias_sum, gain_sum, put_four)
    red_gates.middle()
    red_stream.middle()
    share_tiles(mail, place, lambda index: all_four.at[:, slim_lanes(index)])

    def joined_back(rows):
        return dot_t(all_four[rows, :], shared[...])

    sums = norm_back(grad_three, pre_three, 4, mid, joined_back, None, wide)
    copies = send_sums(mail, place, slots_three, sums)
    grads, lines = red_shared.grad, red_shared.grad.shape[0]
    grads[...] = t_dot(act_three[...], all_four[...]).astype(BF16).reshape(grads.shape)

    def lower(rows):
        low_joined[rows, :] = grad_three[rows, :].astype(BF16)

    loop(total, CHUNK, lower)
    for copy in copies:
        copy.wait_recv()
    bias_sum, gain_sum = add_up(slots_three)
    keep(4, bias_sum, gain_sum, mid)

    def put_three(rows, value):
        low_three[rows, :] = value

    through(grad_three, pre_three, 4, mid, bias_sum, gain_sum, put_three)
    red_gates.finish()
    red_stream.finish()
    mail.close()
    red_shared.start()

    def two_part(rows):
        all_four[rows, :] = dot_t(low_three[rows, :], last[...]).astype(BF16)

    loop(total, BLOCK, two_part)
    sum_over_tiles(
        mail, place, lambda index: all_four.at[:, slim_lanes(index)], near_two, pair_two, far_two, total, grad_two
    )
    landing = joined_rows.at[:, pl.ds(pl.multiple_of(blk * mid, mid), mid)]
    joined_here = mail.local(low_joined.at[tile_rows(blk)], landing)
    joined_copies = [
        mail.send(low_joined.at[tile_rows(blk ^ mask_t)], landing, (blk ^ mask_t, batch))
        for mask_t in range(1, 4)
    ]
    sums = norm_back(grad_two, pre_two, 2, slim, lambda rows: grad_two[rows, :])
    copies = send_sums(mail, place, slots_two, sums)
    grads = red_last.grad
    grads[...] = t_dot(act_two[...], low_three[...]).astype(BF16).reshape(grads.shape)
    for copy in copies:
        copy.wait_recv()
    bias_sum, gain_sum = add_up(slots_two)
    keep(2, bias_sum, gain_sum, slim)

    def put_two(rows, value):
        two_here[pl.ds(pl.multiple_of(rows.start + PITCH, 16), CHUNK), :] = value

    through(grad_two, pre_two, 2, slim, bias_sum, gain_sum, put_two)
    widen(two_here, two_left, two_right, total)
    red_shared.middle()
    red_last.start()
    shifted = (two_left, two_here, two_right)

    def one_part(rows):
        for offset in range(9):
            row, col = 2 - offset // 3, 2 - offset % 3
            window = shifted[col][pl.ds(pl.multiple_of(rows.start + PITCH * row, 16), BLOCK), :]
            strip[:, offset * slim : (offset + 1) * slim] = window
        low_three[rows, :] = dot(strip[...], turned[...]).astype(BF16)

    loop(total, BLOCK, one_part)
    sum_over_tiles(
        mail, place, lambda index: low_three.at[tile_rows(index)], near_one, pair_one, far_one, tile, grad_one
    )
    sums = norm_back(grad_one, pre_one, 0, mid, lambda rows: grad_one[rows, :], base)
    slots_tile[blk] = jnp.concatenate(sums, 0)
    swap_tile_sums(mail, place, slots_tile)
    copies = send_sums(mail, place, slots_one, list(add_up(slots_tile)))
    grads = red_spatial.grad
    for offset in range(9):
        row, col = 2 - offset // 3, 2 - offset % 3
        window = shifted[col][PITCH * row : PITCH * row + total, :]
        found = t_dot(act_one[PITCH : PITCH + total, :], window).astype(BF16)
        grads[:, :, :, offset * slim : (offset + 1) * slim] = found.reshape(grads.shape[:3] + (slim,))
    for copy in copies:
        copy.wait_recv()
    bias_sum, gain_sum = add_up(slots_one)
    keep(0, bias_sum, gain_sum, mid)

    def put_one(rows, value):
        all_one[at_base(base, rows), :] = value

    through(grad_one, pre_one, 0, mid, bias_sum, gain_sum, put_one, base)
    red_shared.finish()
    red_last.middle()
    red_spatial.start()
    share_tiles(mail, place, lambda index: all_one.at[tile_rows(index)])
    grads = red_first.grad
    grads[...] = t_dot(wide[...], all_one[...]).astype(BF16).reshape(grads.shape)
    red_first.start()
    red_spatial.middle()
    joined_here.wait()
    for copy in joined_copies:
        copy.wait_recv()

    def input_grads(rows):
        own = all_one[pl.ds(pl.multiple_of(base + rows.start, CHUNK), rows.size), :]
        grad_input[rows, :] = dot_t(own, first[...]) + joined_rows[rows, :].astype(F32)

    loop(tile, tile // 3, input_grads)
    red_last.finish()
    red_first.middle()
    red_spatial.finish()
    red_first.finish()
    mail.close()


def bottleneck_back(nb, back, pres, stats, norms, mask, sizes, wide, acts, weights, gate_grads, stream_grads):
    tile, total = pres[0].shape[0], mask.shape[0]
    mid = pres[0].shape[1]
    slim = mid // 4
    lines, share = nb // 2, mid // nb
    padded = total + 2 * PITCH
    width = weights[3].shape[0]

    def array(*shape, kind=BF16):
        return jax.ShapeDtypeStruct(shape, kind)

    def vmem(*shape, kind=BF16):
        return pltpu.VMEM(shape, kind)

    scratch = [
        vmem(2, total, slim),
        vmem(total, slim),
        vmem(total, slim),
        vmem(total, slim, kind=F32),
        vmem(total, mid),
        vmem(total, mid, kind=F32),
        vmem(total, mid),
        vmem(total, mid),
        vmem(tile, width),
        vmem(2, total, slim),
        vmem(total, slim),
        vmem(total, slim),
        vmem(total, slim, kind=F32),
        vmem(padded, slim),
        vmem(padded, slim),
        vmem(padded, slim),
        vmem(9 * slim, mid),
        vmem(BLOCK, 9 * slim),
        vmem(2, tile, mid),
        vmem(tile, mid),
        vmem(tile, mid),
        vmem(tile, mid, kind=F32),
        vmem(total, mid),
        vmem(nb, 2, slim, kind=F32),
        vmem(nb, 2, mid, kind=F32),
        vmem(nb, 2, slim, kind=F32),
        vmem(4, 2, mid, kind=F32),
        vmem(nb, 2, mid, kind=F32),
    ]
    for columns in (mid, mid, mid, 9 * slim):
        scratch += reduce_scratch(lines, share, columns, True)
    for columns in (mid, LANES):
        scratch += reduce_scratch(lines, share, columns, False)
    scratch.append(DMA((2, 128)))
    return pl.pallas_call(
        functools.partial(backward_kernel, nb),
        out_shape=(
            array(tile, width, kind=F32),
            array(share, mid),
            array(share, mid),
            array(share, 9 * slim),
            array(share, mid),
            array(share, mid),
            array(share, LANES),
            array(8, mid, kind=F32),
        ),
        in_specs=[VMEM] * 19,
        out_specs=(VMEM,) * 8,
        scratch_shapes=scratch,
        cost_estimate=LONG,
        compiler_params=pltpu.CompilerParams(
            collective_id=22, has_side_effects=True, vmem_limit_bytes=62 * 2**20
        ),
    )(
        back,
        *pres,
        stats,
        norms,
        mask,
        sizes,
        wide,
        *acts,
        *weights,
        gate_grads.reshape(lines, 2, share, mid),
        stream_grads.reshape(lines, 2, share, LANES),
    )


def on_device(
    nt,
    nb,
    features,
    crop_rows,
    crop_cols,
    depth_target,
    labels,
    first_weight,
    spatial_weight,
    last_weight,
    shared_weight,
    head_weights,
    message_weights,
    gate_weights,
    depth_weight,
    class_weight,
    mid_gain,
    mid_bias,
    out_gain,
    out_bias,
):
    tile_rows, cols, width = features.shape[1:]
    tile = tile_rows * cols
    rows = tile_rows * nt
    pixels = rows * cols
    tasks = head_weights.shape[0]
    mid = first_weight.shape[1]
    share = mid // nb
    slim = mid // nt
    classes = class_weight.shape[1]
    blk, batch = lax.axis_index("blk"), lax.axis_index("batch")

    image_rows = lax.dynamic_index_in_dim(crop_rows, batch, 0, False)
    image_cols = lax.dynamic_index_in_dim(crop_cols, batch, 0, False)
    row_ids = jnp.arange(rows, dtype=jnp.int32)
    col_ids = jnp.arange(PITCH, dtype=jnp.int32)
    inside_grid = (row_ids[:, None] < image_rows) & (col_ids[None, :] < image_cols)
    inside_grid = inside_grid.astype(F32)
    inside_wide = inside_grid.reshape(rows * PITCH, 1)
    inside = inside_grid[:, :cols].reshape(pixels, 1)
    inside_tile = lax.dynamic_slice_in_dim(inside, blk * tile, tile, 0)
    sizes_flat = (crop_rows * crop_cols).astype(F32)
    valid_count = jnp.sum(sizes_flat)
    sizes = jnp.broadcast_to(sizes_flat[:, None, None], (nb, 1, mid))
    tile_counts = jnp.sum(inside.reshape(nt, tile), 1)
    tile_sizes = jnp.broadcast_to(tile_counts[:, None, None], (nt, 1, mid))
    image_size = jnp.maximum(jnp.sum(inside), 1.0)

    params = jnp.concatenate(
        [
            mid_gain.reshape(-1),
            mid_bias.reshape(-1),
            out_gain,
            out_bias,
            depth_weight,
            class_weight.reshape(-1),
        ]
    )
    room = -(-params.shape[0] // (16 * LANES)) * 16 * LANES
    small = jnp.pad(params, (0, room - params.shape[0])).reshape(-1, LANES)
    feat = jnp.pad(features[0], ((0, 0), (0, PITCH - cols), (0, 0))).reshape(tile_rows * PITCH, width)
    piece = shared_weight.shape[0] // nt
    order = [
        (t * nb + b, (b * nt // nb) * nb + (b % (nb // nt)) * nt + t)
        for t in range(nt)
        for b in range(nb)
    ]
    shared_own = lax.ppermute(
        lax.dynamic_slice_in_dim(shared_weight, blk * piece, piece, 0), ("blk", "batch"), order
    )
    full_first, smalls, wide_features, spatial, pre_one, stats = begin(
        nb, first_weight, small, spatial_weight, feat, inside_wide, sizes, tile_sizes
    )
    full_first = full_first.reshape(width, mid)
    smalls = smalls.reshape(nb, room)
    at = 0

    def taken(count):
        nonlocal at
        found = smalls[:, at : at + count]
        at += count
        return found

    norms_count = mid_gain.shape[0]
    out_share = out_gain.shape[0]
    gain_mid = taken(norms_count * share).reshape(nb, norms_count, share).swapaxes(0, 1)
    gain_mid = gain_mid.reshape(norms_count, mid).astype(F32)
    bias_mid = taken(norms_count * share).reshape(nb, norms_count, share).swapaxes(0, 1)
    bias_mid = bias_mid.reshape(norms_count, mid).astype(F32)
    gain_out = lax.dynamic_slice_in_dim(taken(out_share).reshape(width), blk * mid, mid, 0).astype(F32)
    bias_out = lax.dynamic_slice_in_dim(taken(out_share).reshape(width), blk * mid, mid, 0).astype(F32)
    full_depth = taken(share).reshape(mid, 1)
    full_classes = taken(share * classes).reshape(mid, classes)

    def slim_of(vector):
        return lax.dynamic_slice_in_dim(vector, blk * slim, slim, 0)

    def filled(vector):
        return jnp.pad(vector, (0, mid - vector.shape[0]))

    gain_two, bias_two = slim_of(gain_mid[1]), slim_of(bias_mid[1])
    gain_four, bias_four = slim_of(gain_mid[2]), slim_of(bias_mid[2])
    norms = jnp.stack(
        [
            gain_mid[0],
            bias_mid[0],
            filled(gain_two),
            filled(bias_two),
            gain_out,
            bias_out,
            filled(gain_four),
            filled(bias_four),
        ]
    )
    head_own, stats = lax.optimization_barrier(
        (lax.dynamic_index_in_dim(head_weights, blk, 0, False), stats)
    )
    head = lax.all_gather(head_own, "batch", axis=1, tiled=True)
    early = 5
    message_rest = lax.dynamic_index_in_dim(message_weights, blk, 0, False)[early:]
    head, message_rest = lax.optimization_barrier((head, message_rest))
    message_rest = lax.all_gather(message_rest, "batch", axis=1, tiled=True)
    (
        last,
        shared,
        gate,
        message_start,
        act_one,
        act_two,
        act_three,
        shared_act,
        pre_two,
        pre_three,
        pre_four,
        stats,
    ) = bottleneck(
        nb,
        early,
        pre_one,
        stats,
        spatial,
        wide_features,
        inside_wide,
        norms,
        sizes,
        last_weight,
        shared_own,
        gate_weights,
        message_weights,
    )
    message = jnp.concatenate([message_start, message_rest], 0)

    def narrow(cells):
        channels = cells.shape[1]
        return cells.reshape(-1, PITCH, channels)[:, :cols].reshape(-1, channels)

    def act(values, mask):
        return (jax.nn.silu(values) * mask).astype(BF16)

    shared_map = narrow(shared_act)
    gain_task = lax.dynamic_index_in_dim(gain_mid, 3 + blk, 0, False)
    bias_task = lax.dynamic_index_in_dim(bias_mid, 3 + blk, 0, False)
    pre_five = dot(windows(shared_map, rows, cols, False), head.reshape(9 * mid, mid))
    mean = jnp.sum(pre_five * inside, 0) / image_size
    gap = pre_five - mean
    spread = jnp.sum(gap * gap * inside, 0)
    few = sizes[:, :, :LANES]
    centre, spread = all_sums(mean, spread, None, few, True, False, 5)
    inverse_five = lax.rsqrt(spread / valid_count + EPSILON)
    normed_five = (pre_five - centre) * inverse_five
    norm_five = normed_five * gain_task + bias_task
    task_act = act(norm_five, inside)
    messages = dot(windows(task_act, rows, cols, False), message.reshape(9 * mid, mid))
    gate_open = jax.nn.sigmoid(dot(task_act, gate))
    gated = (gate_open * messages).astype(BF16)
    is_first, is_last = blk == 0, blk == tasks - 1
    depth_part = jnp.where(is_first, task_act, gated)
    sem_part = jnp.where(is_last, task_act, gated)
    depth_share = jnp.einsum("pc,co->op", depth_part, full_depth, preferred_element_type=F32)
    class_share = jnp.einsum("pc,co->op", sem_part, full_classes, preferred_element_type=F32)
    lift = -(-(1 + classes) // 8) * 8 - 1 - classes
    shares = jnp.concatenate([depth_share, class_share, jnp.zeros((lift, pixels), F32)], 0)
    streams = jnp.sum(gather_tiles(shares, 7), 0).T
    depth_out = lax.dynamic_slice_in_dim(streams, blk * tile, tile, 0)[:, 0]
    logits = lax.dynamic_slice_in_dim(streams, blk * tile, tile, 0)[:, 1 : 1 + classes]
    targets = gather_tiles_pair(depth_target, labels, tile).reshape(pixels, 8)
    all_depth, all_logits = streams[:, :1], streams[:, 1 : 1 + classes]
    depth_slope = ((all_depth - targets[:, :1]) * inside).astype(BF16)
    onehot = (targets[:, 1:2] == jnp.arange(classes, dtype=jnp.int32)[None, :].astype(F32)).astype(F32)
    logit_slope = ((jax.nn.softmax(all_logits, axis=1) - onehot) * inside).astype(BF16)
    grad_depth = t_dot(depth_part, depth_slope)
    grad_classes = t_dot(sem_part, logit_slope)
    depth_back = depth_slope.astype(F32) * full_depth.astype(F32).reshape(1, mid)
    sem_back = dot_t(logit_slope, full_classes)
    zero = jnp.zeros((), F32)
    grad_gated = jnp.where(is_first, zero, depth_back) + jnp.where(is_last, zero, sem_back)
    grad_direct = jnp.where(is_first, depth_back, zero) + jnp.where(is_last, sem_back, zero)

    grad_msg = (grad_gated * gate_open).astype(BF16)
    grad_gate = (grad_gated * messages * gate_open * (1.0 - gate_open)).astype(BF16)
    msg_windows = windows(grad_msg, rows, cols, True)
    gate_grads = t_dot(task_act, grad_gate).astype(BF16)
    message_grads = t_dot(task_act, msg_windows).astype(BF16)
    share_messages = lax.psum_scatter(message_grads, "batch", scatter_dimension=0, tiled=True)
    task_grad = (
        grad_direct
        + dot_t(grad_gate, gate)
        + dot(msg_windows, message.swapaxes(1, 2).reshape(9 * mid, mid))
    )
    grad_norm_five = task_grad * inside * silu_slope(norm_five)
    bias_sum_five, gain_sum_five = all_sums(
        jnp.sum(grad_norm_five, 0), jnp.sum(grad_norm_five * normed_five, 0), None, few, False, False, 8
    )
    grad_pre_five = (
        inverse_five
        * gain_task
        * (grad_norm_five - bias_sum_five / valid_count - normed_five * gain_sum_five / valid_count)
        * inside
    ).astype(BF16)
    five_windows = windows(grad_pre_five, rows, cols, True)
    head_grads = t_dot(shared_map, five_windows).astype(BF16)
    share_heads = lax.psum_scatter(head_grads, "batch", scatter_dimension=0, tiled=True)
    shared_back = dot(five_windows, head.swapaxes(1, 2).reshape(9 * mid, mid))

    stream_grads = jnp.concatenate([grad_depth, grad_classes], 1)
    stream_grads = jnp.pad(stream_grads, ((0, 0), (0, LANES - 1 - classes))).astype(BF16)
    back = jnp.pad(
        shared_back.astype(BF16).reshape(rows, cols, mid), ((0, 0), (0, PITCH - cols), (0, 0))
    ).reshape(rows * PITCH, mid)
    (
        grad_input,
        share_shared,
        share_last,
        share_spatial,
        share_first,
        share_gates,
        share_stream,
        sums_wide,
    ) = bottleneck_back(
        nb,
        back,
        (pre_one, pre_two, pre_three, pre_four),
        stats,
        norms,
        inside_wide,
        sizes,
        wide_features,
        (act_one, act_two, act_three),
        (spatial, last, shared, full_first),
        gate_grads,
        stream_grads,
    )
    grad_input = grad_input.reshape(tile_rows, PITCH, width)[:, :cols]

    moved = lax.ppermute(
        jnp.concatenate([share_first, share_shared], 1), ("blk", "batch"), [(b, a) for a, b in order]
    )
    share_messages, share_heads, moved = lax.optimization_barrier((share_messages, share_heads, moved))
    early_share = jnp.concatenate([share_messages, share_heads], 1)
    early_all = lax.all_gather(early_share, "blk", axis=0, tiled=False).astype(F32)
    early_all = early_all.reshape(nt, share, 2, 9, mid).transpose(2, 0, 3, 1, 4)
    red_messages, red_heads = early_all[0], early_all[1]
    late_share = jnp.concatenate([moved, share_last, share_spatial, share_gates, share_stream], 1)
    late_all = gather_tiles(late_share, 12).astype(F32)
    at = 0

    def part(count):
        nonlocal at
        found = late_all[:, :, at : at + count]
        at += count
        return found

    red_first = part(mid).reshape(nt * share, mid)
    red_shared = part(mid).reshape(nt * share, mid)
    red_last = part(mid).transpose(1, 0, 2).reshape(share, width)
    red_spatial = part(9 * slim).reshape(nt, share, 9, slim).transpose(2, 1, 0, 3).reshape(9, share, mid)
    red_gates = part(mid)
    streams_red = jnp.sum(part(LANES), 0)
    red_depth = streams_red[:, 0]
    red_classes = streams_red[:, 1 : 1 + classes]

    sums = jnp.concatenate([sums_wide, gain_sum_five[None], bias_sum_five[None]], 0)
    sums = jnp.pad(sums, ((0, 6), (0, 0)))
    sums = gather_tiles(sums, 13)
    two_gain, two_bias = sums[:, 2, :slim].reshape(1, mid), sums[:, 3, :slim].reshape(1, mid)
    four_gain, four_bias = sums[:, 6, :slim].reshape(1, mid), sums[:, 7, :slim].reshape(1, mid)
    mid_gains = jnp.concatenate([sums[0, 0:1], two_gain, four_gain, sums[:, 8]], 0)
    mid_biases = jnp.concatenate([sums[0, 1:2], two_bias, four_bias, sums[:, 9]], 0)
    grad_mid_gain = lax.dynamic_slice_in_dim(mid_gains, batch * share, share, 1)
    grad_mid_bias = lax.dynamic_slice_in_dim(mid_biases, batch * share, share, 1)
    grad_out_gain = lax.dynamic_slice_in_dim(sums[:, 4].reshape(width), batch * out_share, out_share, 0)
    grad_out_bias = lax.dynamic_slice_in_dim(sums[:, 5].reshape(width), batch * out_share, out_share, 0)
    return (
        depth_out.reshape(1, tile_rows, cols),
        logits.reshape(1, tile_rows, cols, classes),
        grad_input.reshape(1, tile_rows, cols, width),
        red_first,
        red_spatial,
        red_last,
        red_shared,
        red_heads,
        red_messages,
        red_gates,
        red_depth,
        red_classes,
        grad_mid_gain,
        grad_mid_bias,
        grad_out_gain,
        grad_out_bias,
    )


def solution(mesh):
    nt, nb = mesh.shape["blk"], mesh.shape["batch"]
    placed = (
        P("batch", "blk", None, None),
        P(),
        P(),
        P("batch", "blk", None),
        P("batch", "blk", None),
        P("batch", None),
        P(None, "batch", None),
        P("batch", None),
        P("batch", None),
        P(None, None, "batch", None),
        P(None, None, "batch", None),
        P(None, "batch", None),
        P("batch"),
        P("batch", None),
        P(None, "batch"),
        P(None, "batch"),
        P("batch"),
        P("batch"),
    )
    return jax.shard_map(
        functools.partial(on_device if nb == 8 else on_device_any, nt, nb),
        mesh=mesh,
        in_specs=placed,
        out_specs=(
            P("batch", "blk", None),
            P("batch", "blk", None, None),
            P("batch", "blk", None, None),
            P("batch", None),
            P(None, "batch", None),
            P("batch", None),
            P("batch", None),
            P(None, None, "batch", None),
            P(None, None, "batch", None),
            P(None, "batch", None),
            P("batch"),
            P("batch", None),
            P(None, "batch"),
            P(None, "batch"),
            P("batch"),
            P("batch"),
        ),
        check_vma=False,
    )
```

```python
import functools

import jax
import jax.numpy as jnp
from jax import lax
from jax.experimental import pallas as pl
from jax.experimental.pallas import tpu as pltpu
from jax.sharding import PartitionSpec as P

EPSILON = 1e-05
MESH = pl.DeviceIdType.MESH
BF16 = jnp.bfloat16
F32 = jnp.float32
LANES = 128


def greet(peers):
    barrier = pltpu.get_barrier_semaphore()
    for peer in peers:
        pl.semaphore_signal(barrier, inc=1, device_id=peer, device_id_type=MESH)
    pl.semaphore_wait(barrier, len(peers))


def send(src, dst, send_sem, recv_sem, peer):
    copy = pltpu.make_async_remote_copy(
        src_ref=src,
        dst_ref=dst,
        send_sem=send_sem,
        recv_sem=recv_sem,
        device_id=peer,
        device_id_type=MESH,
    )
    copy.start()
    return copy


def first_kernel(images, weight, small, full, smalls, own, zs, xs, cs, ps):
    blk, batch = lax.axis_index("blk"), lax.axis_index("batch")
    half = weight.shape[0] // 2
    rows = pl.ds(pl.multiple_of(lax.rem(blk, 2) * half, half), half)
    side = (blk, batch ^ 1)
    mate = (blk ^ 1, batch)
    lines = range(1, images // 2)
    others = [(blk, batch ^ mask) for mask in range(1, images)]
    greet(others + [mate])
    copies = []
    here = pltpu.make_async_copy(weight, full.at[batch], own.at[0])
    here.start()
    here_small = pltpu.make_async_copy(small, smalls.at[batch], own.at[1])
    here_small.start()
    z_copies = {}
    for mask in lines:
        z_copies[mask] = send(
            weight.at[rows],
            full.at[batch, rows],
            zs.at[0, mask],
            zs.at[1, mask],
            (blk, batch ^ (2 * mask)),
        )
    x_copies = {
        0: send(weight.at[rows], full.at[batch, rows], xs.at[0, 0], xs.at[1, 0], side)
    }
    for place, peer in enumerate(others):
        copies.append(
            send(small, smalls.at[batch], ps.at[0, place], ps.at[1, place], peer)
        )
    core_copies = []

    def hand_over(source, mask):
        block = full.at[source, rows]
        core_copies.append(send(block, block, cs.at[0, mask], cs.at[1, mask], mate))

    for mask in lines:
        z_copies[mask].wait_recv()
        source = batch ^ (2 * mask)
        block = full.at[source, rows]
        x_copies[mask] = send(block, block, xs.at[0, mask], xs.at[1, mask], side)
        hand_over(source, 2 * mask)
    for mask in range(images // 2):
        x_copies[mask].wait_recv()
        hand_over(batch ^ (2 * mask + 1), 2 * mask + 1)
    for copy in core_copies + copies:
        copy.wait()
    for mask in lines:
        z_copies[mask].wait_send()
    for mask in range(images // 2):
        x_copies[mask].wait_send()
    here.wait()
    here_small.wait()


def gather_first(weight, small, images):
    any_place = pl.BlockSpec(memory_space=pl.ANY)
    dma = pltpu.SemaphoreType.DMA
    return pl.pallas_call(
        functools.partial(first_kernel, images),
        out_shape=(
            jax.ShapeDtypeStruct((images,) + weight.shape, weight.dtype),
            jax.ShapeDtypeStruct((images,) + small.shape, small.dtype),
        ),
        in_specs=[any_place] * 2,
        out_specs=(any_place, any_place),
        scratch_shapes=[
            dma((2,)),
            dma((2, images)),
            dma((2, images)),
            dma((2, images)),
            dma((2, images)),
        ],
        compiler_params=pltpu.CompilerParams(collective_id=0, has_side_effects=True),
    )(weight, small)


def tiles_kernel(block, every, own, sems):
    blk, batch = lax.axis_index("blk"), lax.axis_index("batch")
    mate, across = (blk ^ 1, batch), (blk ^ 2, batch)
    greet([mate, across])
    far = send(block, every.at[blk], sems.at[0, 0], sems.at[1, 0], across)
    near = send(block, every.at[blk], sems.at[0, 1], sems.at[1, 1], mate)
    here = pltpu.make_async_copy(block, every.at[blk], own.at[0])
    here.start()
    far.wait_recv()
    passed = every.at[blk ^ 2]
    last = send(passed, passed, sems.at[0, 2], sems.at[1, 2], mate)
    near.wait()
    last.wait()
    far.wait_send()
    here.wait()


def gather_tiles(block, ident):
    any_place = pl.BlockSpec(memory_space=pl.ANY)
    dma = pltpu.SemaphoreType.DMA
    return pl.pallas_call(
        tiles_kernel,
        out_shape=jax.ShapeDtypeStruct((4,) + block.shape, block.dtype),
        in_specs=[any_place],
        out_specs=any_place,
        scratch_shapes=[dma((1,)), dma((2, 3))],
        compiler_params=pltpu.CompilerParams(collective_id=ident, has_side_effects=True),
    )(block)


def sum_kernel(parts, total, near_in, pair, far_in, sems):
    blk, batch = lax.axis_index("blk"), lax.axis_index("batch")
    mate, across = (blk ^ 1, batch), (blk ^ 2, batch)
    greet([mate, across])
    far_first = send(parts.at[blk ^ 3], near_in.at[0], sems.at[0, 0], sems.at[1, 0], mate)
    near_next = send(parts.at[blk ^ 1], near_in.at[1], sems.at[0, 1], sems.at[1, 1], mate)
    far_first.wait_recv()
    pair[...] = (parts[blk ^ 2].astype(F32) + near_in[0].astype(F32)).astype(pair.dtype)
    far = send(pair, far_in, sems.at[0, 2], sems.at[1, 2], across)
    near_next.wait_recv()
    total[...] = parts[blk].astype(F32) + near_in[1].astype(F32)
    far.wait_recv()
    total[...] += far_in[...].astype(F32)
    far_first.wait_send()
    near_next.wait_send()
    far.wait_send()


def sum_tiles(parts, ident):
    dma = pltpu.SemaphoreType.DMA
    block = parts.shape[1:]
    vmem = pl.BlockSpec(memory_space=pltpu.VMEM)
    return pl.pallas_call(
        sum_kernel,
        out_shape=jax.ShapeDtypeStruct(block, F32),
        in_specs=[vmem],
        out_specs=vmem,
        scratch_shapes=[
            pltpu.VMEM((2,) + block, parts.dtype),
            pltpu.VMEM(block, parts.dtype),
            pltpu.VMEM(block, parts.dtype),
            dma((2, 3)),
        ],
        compiler_params=pltpu.CompilerParams(
            collective_id=ident, has_side_effects=True, vmem_limit_bytes=32 * 2**20
        ),
    )(parts)


def combine(slots, weights, half, centred):
    count = slots.shape[0]
    if not centred:
        total = slots[0]
        for at in range(1, count):
            total = total + slots[at]
        return total
    size = weights[0]
    mean = slots[0, :half] * weights[0]
    for at in range(1, count):
        size = size + weights[at]
        mean = mean + slots[at, :half] * weights[at]
    mean = mean / size
    spread = None
    for at in range(count):
        gap = slots[at, :half] - mean
        term = slots[at, half : 2 * half] + weights[at] * gap * gap
        spread = term if spread is None else spread + term
    rest = [jnp.zeros((slots.shape[1] - 2 * half, LANES), F32)] * (slots.shape[1] > 2 * half)
    return jnp.concatenate([mean, spread] + rest, 0)


def sums_kernel(images, half, centred, tiled, own, tile_sizes, sizes, total, *scratch):
    blk, batch = lax.axis_index("blk"), lax.axis_index("batch")
    slots, sems = scratch[0], scratch[1]
    peers = [(blk, batch ^ mask) for mask in range(1, images)]
    mates = [(blk ^ mask, batch) for mask in range(1, 4)] if tiled else []
    greet(peers + mates)
    if tiled:
        tile_slots, tile_sems = scratch[2], scratch[3]
        tile_slots[blk] = own[...]
        copies = [
            send(own, tile_slots.at[blk], tile_sems.at[0, at], tile_sems.at[1, at], peer)
            for at, peer in enumerate(mates)
        ]
        for copy in copies:
            copy.wait()
        slots[batch] = combine(tile_slots, tile_sizes, half, centred)
    else:
        slots[batch] = own[...]
    copies = [
        send(slots.at[batch], slots.at[batch], sems.at[0, at], sems.at[1, at], peer)
        for at, peer in enumerate(peers)
    ]
    for copy in copies:
        copy.wait()
    total[...] = combine(slots, sizes, half, centred)


def all_sums(first, second, tile_sizes, sizes, centred, tiled, ident):
    images = sizes.shape[0]
    channels = first.shape[0]
    half = channels // LANES
    rows = -(-2 * half // 8) * 8
    own = jnp.concatenate(
        [first, second, jnp.zeros(((rows - 2 * half) * LANES,), F32)]
    ).reshape(rows, LANES)
    dma = pltpu.SemaphoreType.DMA
    vmem = pl.BlockSpec(memory_space=pltpu.VMEM)
    scratch = [pltpu.VMEM((images, rows, LANES), F32), dma((2, images))]
    if tiled:
        scratch += [pltpu.VMEM((4, rows, LANES), F32), dma((2, 3))]
    total = pl.pallas_call(
        functools.partial(sums_kernel, images, half, centred, tiled),
        out_shape=jax.ShapeDtypeStruct((rows, LANES), F32),
        in_specs=[vmem] * 3,
        out_specs=vmem,
        scratch_shapes=scratch,
        compiler_params=pltpu.CompilerParams(collective_id=ident, has_side_effects=True),
    )(own, sizes if tile_sizes is None else tile_sizes, sizes)
    flat = total.reshape(-1)
    return flat[:channels], flat[channels : 2 * channels]


def silu_slope(values):
    sigmoid_value = jax.nn.sigmoid(values)
    return sigmoid_value * (1.0 + values * (1.0 - sigmoid_value))


def windows(cells, rows, cols, back):
    channels = cells.shape[1]
    padded = jnp.pad(cells.reshape(rows, cols, channels), ((1, 1), (1, 1), (0, 0)))
    taken = []
    for offset in range(9):
        row, col = offset // 3, offset % 3
        if back:
            row, col = 2 - row, 2 - col
        taken.append(padded[row : row + rows, col : col + cols].reshape(rows * cols, channels))
    return jnp.concatenate(taken, 1)


def dot(left, right):
    return jnp.dot(left, right, preferred_element_type=F32)


def dot_t(left, right):
    return jnp.einsum("pd,cd->pc", left, right, preferred_element_type=F32)


def t_dot(left, right):
    return jnp.einsum("pc,pd->cd", left, right, preferred_element_type=F32)


def on_device_any(
    nt,
    nb,
    features,
    crop_rows,
    crop_cols,
    depth_target,
    labels,
    first_weight,
    spatial_weight,
    last_weight,
    shared_weight,
    head_weights,
    message_weights,
    gate_weights,
    depth_weight,
    class_weight,
    mid_gain,
    mid_bias,
    out_gain,
    out_bias,
):
    tile_rows, cols, width = features.shape[1:]
    tile = tile_rows * cols
    rows = tile_rows * nt
    pixels = rows * cols
    tasks = head_weights.shape[0]
    mid = first_weight.shape[1]
    share = mid // nb
    slim = mid // nt
    piece = width // (nb * nt)
    wide = nb * piece
    classes = class_weight.shape[1]
    blk, batch = lax.axis_index("blk"), lax.axis_index("batch")

    image_rows = lax.dynamic_index_in_dim(crop_rows, batch, 0, False)
    image_cols = lax.dynamic_index_in_dim(crop_cols, batch, 0, False)
    row_ids = jnp.arange(rows, dtype=jnp.int32)
    col_ids = jnp.arange(cols, dtype=jnp.int32)
    inside_grid = (row_ids[:, None] < image_rows) & (col_ids[None, :] < image_cols)
    inside = inside_grid.astype(F32).reshape(pixels, 1)
    inside_tile = lax.dynamic_slice_in_dim(inside, blk * tile, tile, 0)
    sizes_flat = (crop_rows * crop_cols).astype(F32)
    valid_count = jnp.sum(sizes_flat)
    sizes = jnp.broadcast_to(sizes_flat[:, None, None], (nb, 1, LANES))
    tile_counts = jnp.sum(inside.reshape(nt, tile), 1)
    tile_sizes = jnp.broadcast_to(tile_counts[:, None, None], (nt, 1, LANES))
    image_size = jnp.maximum(jnp.sum(inside), 1.0)
    tile_size = jnp.maximum(jnp.sum(inside_tile), 1.0)

    params = jnp.concatenate(
        [
            mid_gain.reshape(-1),
            mid_bias.reshape(-1),
            out_gain,
            out_bias,
            depth_weight,
            class_weight.reshape(-1),
        ]
    )
    room = -(-params.shape[0] // (16 * LANES)) * 16 * LANES
    small = jnp.pad(params, (0, room - params.shape[0])).reshape(-1, LANES)
    full_first, smalls = gather_first(first_weight, small, nb)
    full_first = full_first.reshape(width, mid)
    smalls = smalls.reshape(nb, room)
    at = 0

    def taken(count):
        nonlocal at
        found = smalls[:, at : at + count]
        at += count
        return found

    norms = mid_gain.shape[0]
    gain_mid = taken(norms * share).reshape(nb, norms, share).swapaxes(0, 1)
    gain_mid = gain_mid.reshape(norms, mid).astype(F32)
    bias_mid = taken(norms * share).reshape(nb, norms, share).swapaxes(0, 1)
    bias_mid = bias_mid.reshape(norms, mid).astype(F32)
    gain_out = lax.dynamic_index_in_dim(taken(nt * piece).reshape(nb, nt, piece), blk, 1, False)
    gain_out = gain_out.reshape(wide).astype(F32)
    bias_out = lax.dynamic_index_in_dim(taken(nt * piece).reshape(nb, nt, piece), blk, 1, False)
    bias_out = bias_out.reshape(wide).astype(F32)
    full_depth = taken(share).reshape(mid, 1)
    full_classes = taken(share * classes).reshape(mid, classes)
    stream_weight = jnp.concatenate([full_depth, full_classes], 1)

    spatial = lax.all_gather(
        lax.dynamic_slice_in_dim(spatial_weight, blk * slim, slim, 2), "batch", axis=1, tiled=True
    )
    last = lax.dynamic_index_in_dim(last_weight.reshape(share, nb, nt, piece), blk, 2, False)
    last = lax.all_gather(last.reshape(share, wide), "batch", axis=0, tiled=True)
    shared = lax.dynamic_slice_in_dim(shared_weight, blk * piece, piece, 0)
    shared = lax.all_gather(shared, "batch", axis=0, tiled=True)
    head = lax.all_gather(
        lax.dynamic_index_in_dim(head_weights, blk, 0, False), "batch", axis=1, tiled=True
    )
    message = lax.all_gather(
        lax.dynamic_index_in_dim(message_weights, blk, 0, False), "batch", axis=1, tiled=True
    )
    gate = lax.all_gather(
        lax.dynamic_index_in_dim(gate_weights, blk, 0, False), "batch", axis=0, tiled=True
    )

    flat_features = features.reshape(tile, width)
    cut = flat_features.reshape(tile, nb, nt, piece).transpose(2, 0, 1, 3).reshape(nt, tile, wide)
    wide_features = swap_tiles(cut, blk, nt)

    def slim_of(vector):
        return lax.dynamic_slice_in_dim(vector, blk * slim, slim, 0)

    def normalize(values, mask, local_size, gain, bias, tiled, ident):
        mean = jnp.sum(values * mask, 0) / local_size
        gap = values - mean
        spread = jnp.sum(gap * gap * mask, 0)
        centre, total = all_sums(mean, spread, tile_sizes, sizes, True, tiled, ident)
        inverse = lax.rsqrt(total / valid_count + EPSILON)
        normed = (values - centre) * inverse
        return normed * gain + bias, normed, inverse

    def normalize_back(grad, normed, inverse, gain, mask, tiled, ident):
        bias_sum, gain_sum = all_sums(
            jnp.sum(grad, 0), jnp.sum(grad * normed, 0), tile_sizes, sizes, False, tiled, ident
        )
        back = (
            inverse * gain * (grad - bias_sum / valid_count - normed * gain_sum / valid_count) * mask
        )
        return back.astype(BF16), gain_sum, bias_sum

    def act(values, mask):
        return (jax.nn.silu(values) * mask).astype(BF16)

    def by_rows(blocks):
        return blocks.reshape(pixels, blocks.shape[2])

    def by_channels(blocks):
        return blocks.swapaxes(0, 1).reshape(pixels, nt * blocks.shape[2])

    def cut_channels(values):
        return values.astype(BF16).reshape(pixels, nt, slim).swapaxes(0, 1)

    pre_one = dot(flat_features, full_first)
    norm_one, normed_one, inverse_one = normalize(
        pre_one, inside_tile, tile_size, gain_mid[0], bias_mid[0], True, 1
    )
    act_one = by_rows(gather_tiles(act(norm_one, inside_tile), 2))
    pre_two = dot(windows(act_one, rows, cols, False), spatial.reshape(9 * mid, slim))
    gain_two, bias_two = slim_of(gain_mid[1]), slim_of(bias_mid[1])
    norm_two, normed_two, inverse_two = normalize(
        pre_two, inside, image_size, gain_two, bias_two, False, 3
    )
    act_two = by_channels(gather_tiles(act(norm_two, inside), 4))
    pre_three = dot(act_two, last)
    norm_three, normed_three, inverse_three = normalize(
        pre_three, inside, image_size, gain_out, bias_out, False, 5
    )
    joined = norm_three + wide_features.astype(F32)
    act_three = act(joined, inside)
    pre_four = sum_tiles(cut_channels(dot(act_three, shared)), 6)
    gain_four, bias_four = slim_of(gain_mid[2]), slim_of(bias_mid[2])
    norm_four, normed_four, inverse_four = normalize(
        pre_four, inside, image_size, gain_four, bias_four, False, 3
    )
    shared_act = by_channels(gather_tiles(act(norm_four, inside), 4))

    gain_task = lax.dynamic_index_in_dim(gain_mid, 3 + blk, 0, False)
    bias_task = lax.dynamic_index_in_dim(bias_mid, 3 + blk, 0, False)
    pre_five = dot(windows(shared_act, rows, cols, False), head.reshape(9 * mid, mid))
    norm_five, normed_five, inverse_five = normalize(
        pre_five, inside, image_size, gain_task, bias_task, False, 5
    )
    task_act = act(norm_five, inside)
    messages = dot(windows(task_act, rows, cols, False), message.reshape(9 * mid, mid))
    gate_open = jax.nn.sigmoid(dot(task_act, gate))
    gated = (gate_open * messages).astype(BF16)
    is_first, is_last = blk == 0, blk == tasks - 1
    depth_part = jnp.where(is_first, task_act, gated)
    sem_part = jnp.where(is_last, task_act, gated)
    depth_share = jnp.einsum("pc,co->op", depth_part, full_depth, preferred_element_type=F32)
    class_share = jnp.einsum("pc,co->op", sem_part, full_classes, preferred_element_type=F32)
    lift = -(-(1 + classes) // 8) * 8 - 1 - classes
    shares = jnp.concatenate([depth_share, class_share, jnp.zeros((lift, pixels), F32)], 0)
    streams = jnp.sum(gather_tiles(shares, 7), 0).T
    depth_out = lax.dynamic_slice_in_dim(streams, blk * tile, tile, 0)[:, 0]
    logits = lax.dynamic_slice_in_dim(streams, blk * tile, tile, 0)[:, 1 : 1 + classes]
    targets = by_rows(gather_tiles_pair(depth_target, labels, tile))
    all_depth, all_logits = streams[:, :1], streams[:, 1 : 1 + classes]
    depth_slope = ((all_depth - targets[:, :1]) * inside).astype(BF16)
    onehot = (targets[:, 1:2] == jnp.arange(classes, dtype=jnp.int32)[None, :].astype(F32)).astype(F32)
    logit_slope = ((jax.nn.softmax(all_logits, axis=1) - onehot) * inside).astype(BF16)
    grad_depth = t_dot(depth_part, depth_slope)
    grad_classes = t_dot(sem_part, logit_slope)
    depth_back = depth_slope.astype(F32) * full_depth.astype(F32).reshape(1, mid)
    sem_back = dot_t(logit_slope, full_classes)
    zero = jnp.zeros((), F32)
    grad_gated = jnp.where(is_first, zero, depth_back) + jnp.where(is_last, zero, sem_back)
    grad_direct = jnp.where(is_first, depth_back, zero) + jnp.where(is_last, sem_back, zero)

    grad_msg = (grad_gated * gate_open).astype(BF16)
    grad_gate = (grad_gated * messages * gate_open * (1.0 - gate_open)).astype(BF16)
    msg_windows = windows(grad_msg, rows, cols, True)
    gate_grads = t_dot(task_act, grad_gate).astype(BF16)
    message_grads = t_dot(task_act, msg_windows).astype(BF16)
    share_messages = lax.psum_scatter(message_grads, "batch", scatter_dimension=0, tiled=True)
    task_grad = (
        grad_direct
        + dot_t(grad_gate, gate)
        + dot(msg_windows, message.swapaxes(1, 2).reshape(9 * mid, mid))
    )
    grad_norm_five = task_grad * inside * silu_slope(norm_five)
    grad_pre_five, gain_sum_five, bias_sum_five = normalize_back(
        grad_norm_five, normed_five, inverse_five, gain_task, inside, False, 8
    )
    five_windows = windows(grad_pre_five, rows, cols, True)
    head_grads = t_dot(shared_act, five_windows).astype(BF16)
    share_heads = lax.psum_scatter(head_grads, "batch", scatter_dimension=0, tiled=True)
    shared_back = dot(five_windows, head.swapaxes(1, 2).reshape(9 * mid, mid))
    shared_back = sum_tiles(cut_channels(shared_back), 6)

    grad_norm_four = shared_back * inside * silu_slope(norm_four)
    grad_pre_four, gain_sum_four, bias_sum_four = normalize_back(
        grad_norm_four, normed_four, inverse_four, gain_four, inside, False, 9
    )
    grad_four = by_channels(gather_tiles(grad_pre_four, 4))
    shared_grads = t_dot(act_three, grad_four).astype(BF16)
    grad_joined = dot_t(grad_four, shared) * inside * silu_slope(joined)
    grad_three, gain_sum_three, bias_sum_three = normalize_back(
        grad_joined, normed_three, inverse_three, gain_out, inside, False, 8
    )
    last_grads = t_dot(act_two, grad_three).astype(BF16)
    two_back = sum_tiles(cut_channels(dot_t(grad_three, last)), 6)
    grad_norm_two = two_back * inside * silu_slope(norm_two)
    grad_two, gain_sum_two, bias_sum_two = normalize_back(
        grad_norm_two, normed_two, inverse_two, gain_two, inside, False, 9
    )
    two_windows = windows(grad_two, rows, cols, True)
    spatial_grads = t_dot(act_one, two_windows).astype(BF16)
    one_back = dot(two_windows, spatial.swapaxes(1, 2).reshape(9 * slim, mid))
    one_back = sum_tiles(one_back.astype(BF16).reshape(nt, tile, mid), 10)
    grad_norm_one = one_back * inside_tile * silu_slope(norm_one)
    grad_one, gain_sum_one, bias_sum_one = normalize_back(
        grad_norm_one, normed_one, inverse_one, gain_mid[0], inside_tile, True, 11
    )
    all_one = by_rows(gather_tiles(grad_one, 2))
    first_grads = t_dot(wide_features, all_one).astype(BF16)
    joined_tiles = swap_tiles(grad_joined.astype(BF16).reshape(nt, tile, wide), blk, nt)
    joined_tiles = joined_tiles.reshape(nt, tile, nb, piece).transpose(1, 2, 0, 3).reshape(tile, width)
    grad_input = dot_t(grad_one, full_first) + joined_tiles.astype(F32)

    stream_grads = jnp.concatenate([grad_depth, grad_classes], 1)
    stream_grads = jnp.pad(stream_grads, ((0, 0), (0, LANES - 1 - classes))).astype(BF16)
    late = jnp.concatenate(
        [spatial_grads, shared_grads.reshape(nb, piece, mid).reshape(mid, -1),
         last_grads, first_grads.reshape(mid, -1), gate_grads, stream_grads],
        1,
    )
    late_share = lax.psum_scatter(late, "batch", scatter_dimension=0, tiled=True)
    early_share = jnp.concatenate([share_messages, share_heads], 1)
    early = lax.all_gather(early_share, "blk", axis=0, tiled=False).astype(F32)
    late_all = gather_tiles(late_share, 12).astype(F32)
    early = early.reshape(nt, share, 2, 9, mid).transpose(2, 0, 3, 1, 4)
    red_messages, red_heads = early[0], early[1]
    at = 0

    def part(count):
        nonlocal at
        found = late_all[:, :, at : at + count]
        at += count
        return found

    red_spatial = part(9 * slim).reshape(nt, share, 9, slim).transpose(2, 1, 0, 3).reshape(9, share, mid)
    red_shared = part(wide * mid // mid).reshape(nt * piece, mid)
    red_last = part(wide).reshape(nt, share, nb, piece).transpose(1, 2, 0, 3).reshape(share, width)
    red_first = part(wide * mid // mid).reshape(nt * piece, mid)
    red_gates = part(mid)
    streams_red = jnp.sum(part(LANES), 0)
    red_depth = streams_red[:, 0]
    red_classes = streams_red[:, 1 : 1 + classes]

    sums = jnp.concatenate(
        [
            gain_sum_five,
            bias_sum_five,
            gain_sum_three,
            bias_sum_three,
            gain_sum_two,
            bias_sum_two,
            gain_sum_four,
            bias_sum_four,
        ]
    ).reshape(-1, LANES)
    sums = jnp.pad(sums, ((0, -sums.shape[0] % 8), (0, 0)))
    sums = gather_tiles(sums, 13).reshape(nt, -1)
    five_gain, five_bias = sums[:, :mid], sums[:, mid : 2 * mid]
    at_out = 2 * mid
    three_gain = sums[:, at_out : at_out + wide].reshape(nt, nb, piece)
    three_bias = sums[:, at_out + wide : at_out + 2 * wide].reshape(nt, nb, piece)
    at_slim = at_out + 2 * wide
    slims = [
        sums[:, at_slim + i * slim : at_slim + (i + 1) * slim].reshape(1, mid) for i in range(4)
    ]
    mid_gains = jnp.concatenate([gain_sum_one[None], slims[0], slims[2], five_gain], 0)
    mid_biases = jnp.concatenate([bias_sum_one[None], slims[1], slims[3], five_bias], 0)
    grad_mid_gain = lax.dynamic_slice_in_dim(mid_gains, batch * share, share, 1)
    grad_mid_bias = lax.dynamic_slice_in_dim(mid_biases, batch * share, share, 1)
    grad_out_gain = lax.dynamic_index_in_dim(three_gain, batch, 1, False).reshape(nt * piece)
    grad_out_bias = lax.dynamic_index_in_dim(three_bias, batch, 1, False).reshape(nt * piece)
    return (
        depth_out.reshape(1, tile_rows, cols),
        logits.reshape(1, tile_rows, cols, classes),
        grad_input.reshape(1, tile_rows, cols, width),
        red_first,
        red_spatial,
        red_last,
        red_shared,
        red_heads,
        red_messages,
        red_gates,
        red_depth,
        red_classes,
        grad_mid_gain,
        grad_mid_bias,
        grad_out_gain,
        grad_out_bias,
    )


def swap_tiles(blocks, blk, nt):
    out = jnp.zeros_like(blocks)
    out = lax.dynamic_update_index_in_dim(
        out, lax.dynamic_index_in_dim(blocks, blk, 0, False), blk, 0
    )
    for mask in range(1, nt):
        sent = lax.dynamic_index_in_dim(blocks, blk ^ mask, 0, False)
        came = lax.ppermute(sent, "blk", [(i, i ^ mask) for i in range(nt)])
        out = lax.dynamic_update_index_in_dim(out, came, blk ^ mask, 0)
    return out.reshape(-1, blocks.shape[2])


def gather_tiles_pair(depth_target, labels, tile):
    pair = jnp.stack([depth_target.reshape(tile), labels.reshape(tile).astype(F32)], 0)
    pair = jnp.pad(pair, ((0, 6), (0, 0)))
    return gather_tiles(pair, 14).swapaxes(1, 2)


PITCH = 48
CHUNK = 64
BLOCK = 256
ANY = pl.BlockSpec(memory_space=pl.ANY)
VMEM = pl.BlockSpec(memory_space=pltpu.VMEM)
DMA = pltpu.SemaphoreType.DMA
LONG = pl.CostEstimate(flops=80_000_000_000, bytes_accessed=30_000_000, transcendentals=2_000_000)


class Mail:
    def __init__(self, sems):
        self.sems, self.used, self.open = sems, 0, []

    def send(self, src, dst, peer):
        copy = send(src, dst, self.sems.at[0, self.used], self.sems.at[1, self.used], peer)
        self.used += 1
        self.open.append(copy.wait_send)
        return copy

    def local(self, src, dst):
        copy = pltpu.make_async_copy(src, dst, self.sems.at[0, self.used])
        copy.start()
        self.used += 1
        return copy

    def close(self):
        for wait in self.open:
            wait()
        self.open = []


class Place:
    def __init__(self, images):
        self.blk, self.batch = lax.axis_index("blk"), lax.axis_index("batch")
        self.images = images
        self.mate = (self.blk ^ 1, self.batch)
        self.across = (self.blk ^ 2, self.batch)
        self.tiles = [(self.blk ^ mask, self.batch) for mask in range(1, 4)]
        self.others = [(self.blk, self.batch ^ mask) for mask in range(1, images)]
        self.side = (self.blk, self.batch ^ 1)


class Spread:
    def __init__(self, mail, place, own, slot):
        self.mail, self.place, self.own, self.slot = mail, place, own, slot
        self.z_copies, self.x_copies = [], []

    def start(self):
        place, here = self.place, self.slot(self.place.batch)
        self.here = self.mail.local(self.own, here)
        for mask in range(1, place.images // 2):
            peer = (place.blk, place.batch ^ (2 * mask))
            self.z_copies.append(self.mail.send(self.own, here, peer))
        self.x_copies.append(self.mail.send(self.own, here, place.side))
        return self

    def forward(self):
        for mask, copy in enumerate(self.z_copies, 1):
            copy.wait_recv()
            block = self.slot(self.place.batch ^ (2 * mask))
            self.x_copies.append(self.mail.send(block, block, self.place.side))

    def finish(self):
        self.here.wait()
        for copy in self.x_copies:
            copy.wait_recv()


def share_tiles(mail, place, slot):
    own = slot(place.blk)
    far = mail.send(own, own, place.across)
    near = mail.send(own, own, place.mate)
    far.wait_recv()
    passed = slot(place.blk ^ 2)
    last = mail.send(passed, passed, place.mate)
    near.wait_recv()
    last.wait_recv()


def loop(total, step, body):
    def run(at, carry):
        body(pl.ds(pl.multiple_of(at * step, step), step))
        return carry

    lax.fori_loop(0, total // step, run, 0)


def folded(values):
    return jnp.sum(values.reshape(values.shape[0] // 8, 8, values.shape[1]), 0)


def loop_sums(total, channels, count, body):
    def run(at, carry):
        found = body(pl.ds(pl.multiple_of(at * CHUNK, CHUNK), CHUNK))
        return tuple(kept + folded(one) for kept, one in zip(carry, found))

    start = tuple(jnp.zeros((8, channels), F32) for _ in range(count))
    return [jnp.sum(one, 0, keepdims=True) for one in lax.fori_loop(0, total // CHUNK, run, start)]


def merge(slots, sizes, channels):
    count = slots.shape[0]
    size, mean = None, None
    for at in range(count):
        weight = sizes[at, :, :channels]
        term = slots[at, 0:1, :] * weight
        size = weight if size is None else size + weight
        mean = term if mean is None else mean + term
    mean = mean / size
    spread = None
    for at in range(count):
        gap = slots[at, 0:1, :] - mean
        term = slots[at, 1:2, :] + sizes[at, :, :channels] * gap * gap
        spread = term if spread is None else spread + term
    return mean, spread, size


def add_up(slots):
    total = slots[0]
    for at in range(1, slots.shape[0]):
        total = total + slots[at]
    return total[0:1, :], total[1:2, :]


def swap_sums(mail, place, slots):
    own = slots.at[place.batch]
    copies = [mail.send(own, own, peer) for peer in place.others]
    for copy in copies:
        copy.wait_recv()


def swap_tile_sums(mail, place, slots):
    own = slots.at[place.blk]
    copies = [mail.send(own, own, peer) for peer in place.tiles]
    for copy in copies:
        copy.wait_recv()


def local_stats(pre, mask, base, total, channels, size):
    def first(rows):
        return (pre[rows, :] * mask[at_base(base, rows), :],)

    (summed,) = loop_sums(total, channels, 1, first)
    mean = summed / jnp.maximum(size, 1.0)

    def second(rows):
        gap = pre[rows, :] - mean
        return (gap * gap * mask[at_base(base, rows), :],)

    (spread,) = loop_sums(total, channels, 1, second)
    return mean, spread


def at_base(base, rows):
    if base is None:
        return rows
    return pl.ds(pl.multiple_of(base + rows.start, CHUNK), rows.size)


def batch_norm_stats(mail, place, pre, mask, slots, sizes, stats, row, channels):
    total = pre.shape[0]
    mean, spread = local_stats(pre, mask, None, total, channels, sizes[place.batch, :, :channels])
    slots[place.batch] = jnp.concatenate([mean, spread], 0)
    swap_sums(mail, place, slots)
    keep_stats(slots, sizes, stats, row, channels)


def keep_stats(slots, sizes, stats, row, channels):
    mean, spread, size = merge(slots, sizes, channels)
    stats[row : row + 1, :channels] = mean
    stats[row + 1 : row + 2, :channels] = lax.rsqrt(spread / size + EPSILON)


def silu(values):
    return values * jax.nn.sigmoid(values)


def widen(cells, left, right, total):
    def body(rows):
        seen = cells[pl.ds(pl.multiple_of(rows.start + PITCH - 16, 16), CHUNK + 32), :].astype(F32)
        here = pl.ds(pl.multiple_of(rows.start + PITCH, 16), CHUNK)
        left[here, :] = seen[15 : 15 + CHUNK].astype(BF16)
        right[here, :] = seen[17 : 17 + CHUNK].astype(BF16)

    loop(total, CHUNK, body)


def clear_ends(cells, total):
    zeros = jnp.zeros((PITCH, cells.shape[1]), cells.dtype)
    cells[0:PITCH, :] = zeros
    cells[PITCH + total : 2 * PITCH + total, :] = zeros


def conv_rows(shifted, rows, weight, back):
    total = None
    for offset in range(9):
        row, col = offset // 3, offset % 3
        if back:
            row, col = 2 - row, 2 - col
        window = shifted[col][pl.ds(pl.multiple_of(rows.start + PITCH * row, 16), rows.size), :]
        product = weight(offset, window)
        total = product if total is None else total + product
    return total


def sum_over_tiles(mail, place, part, near_in, pair, far_in, total, out):
    far_first = mail.send(part(place.blk ^ 3), near_in.at[0], place.mate)
    near_next = mail.send(part(place.blk ^ 1), near_in.at[1], place.mate)
    far_first.wait_recv()
    mine_far, mine = part(place.blk ^ 2), part(place.blk)

    def pairs(rows):
        pair[rows, :] = (mine_far[rows, :].astype(F32) + near_in[0, rows, :].astype(F32)).astype(BF16)

    loop(total, CHUNK, pairs)
    far = mail.send(pair, far_in, place.across)
    near_next.wait_recv()
    far.wait_recv()

    def finish(rows):
        out[rows, :] = (
            mine[rows, :].astype(F32) + near_in[1, rows, :].astype(F32) + far_in[rows, :].astype(F32)
        )

    loop(total, CHUNK, finish)


def start_kernel(
    images,
    weight,
    small,
    spatial_own,
    pair,
    feat,
    mask,
    sizes,
    tile_sizes,
    full,
    smalls,
    targets,
    wide,
    spatial,
    pre_one,
    stats,
    slots_tile,
    slots_one,
    sems,
):
    place = Place(images)
    mail = Mail(sems)
    blk, batch = place.blk, place.batch
    depth = weight.shape[0]
    half = depth // 2
    mid = weight.shape[1]
    tile = feat.shape[0]
    slim = mid // 4
    share = spatial_own.shape[1]
    mine = pl.ds(pl.multiple_of(lax.rem(blk, 2) * half, half), half)
    greet(place.others + place.tiles)
    here = mail.local(weight, full.at[batch])
    here_small = mail.local(small, smalls.at[batch])
    z_copies, x_copies, arrived, late = {}, [], [], []
    for peer in place.others:
        late.append(mail.send(small, smalls.at[batch], peer))
    for mask_z in range(1, images // 2):
        z_copies[mask_z] = mail.send(
            weight.at[mine], full.at[batch, mine], (blk, batch ^ (2 * mask_z))
        )
    x_copies.append(mail.send(weight.at[mine], full.at[batch, mine], place.side))
    lanes = pl.ds(pl.multiple_of(blk * slim, slim), slim)
    got_spatial = Spread(
        mail,
        place,
        spatial_own.at[:, :, lanes],
        lambda index: spatial.at[:, pl.ds(pl.multiple_of(index * share, share), share), :],
    ).start()

    def columns(index):
        return feat.at[:, pl.ds(pl.multiple_of(index * mid, mid), mid)]

    landing = wide.at[pl.ds(pl.multiple_of(blk * tile, tile), tile), :]
    here_wide = mail.local(columns(blk), landing)
    line = targets.at[:, pl.ds(pl.multiple_of(blk * tile, tile), tile)]
    here_line = mail.local(pair, line)
    for mask_t in range(1, 4):
        late.append(mail.send(pair, line, (blk ^ mask_t, batch)))
        late.append(mail.send(columns(blk ^ mask_t), landing, (blk ^ mask_t, batch)))

    def hand_over(source):
        block = full.at[source, mine]
        arrived.append(mail.send(block, block, place.mate))

    for mask_z in range(1, images // 2):
        z_copies[mask_z].wait_recv()
        source = batch ^ (2 * mask_z)
        block = full.at[source, mine]
        x_copies.append(mail.send(block, block, place.side))
        hand_over(source)
    for mask_z in range(images // 2):
        x_copies[mask_z].wait_recv()
        hand_over(batch ^ (2 * mask_z + 1))
    stats[...] = jnp.zeros_like(stats)
    here.wait()
    for copy in arrived:
        copy.wait_recv()

    def reduce(rows):
        total = None
        for index in range(images):
            product = dot(feat[rows, index * depth : (index + 1) * depth], full[index])
            total = product if total is None else total + product
        pre_one[rows, :] = total

    loop(tile, tile // 2, reduce)
    base = blk * tile
    mean, spread = local_stats(pre_one, mask, base, tile, mid, tile_sizes[blk, :, :])
    slots_tile[blk] = jnp.concatenate([mean, spread], 0)
    swap_tile_sums(mail, place, slots_tile)
    mean, spread, _ = merge(slots_tile, tile_sizes, mid)
    slots_one[batch] = jnp.concatenate([mean, spread], 0)
    swap_sums(mail, place, slots_one)
    keep_stats(slots_one, sizes, stats, 0, mid)
    got_spatial.forward()
    got_spatial.finish()
    for copy in late:
        copy.wait_recv()
    here_small.wait()
    here_wide.wait()
    here_line.wait()
    mail.close()


def begin(nb, weight, small, spatial, pair, feat, mask, sizes, tile_sizes):
    depth, mid = weight.shape
    tile = feat.shape[0]

    def array(*shape, kind=BF16):
        return jax.ShapeDtypeStruct(shape, kind)

    return pl.pallas_call(
        functools.partial(start_kernel, nb),
        out_shape=(
            array(nb, depth, mid),
            array(nb, *small.shape),
            array(8, 4 * tile, kind=F32),
            array(4 * tile, mid),
            array(9, mid, mid // 4),
            array(tile, mid, kind=F32),
            array(8, mid, kind=F32),
        ),
        in_specs=[ANY] * 4 + [VMEM] * 4,
        out_specs=(VMEM, ANY, ANY, VMEM, VMEM, VMEM, VMEM),
        scratch_shapes=[
            pltpu.VMEM((4, 2, mid), F32),
            pltpu.VMEM((nb, 2, mid), F32),
            DMA((2, 64)),
        ],
        cost_estimate=LONG,
        compiler_params=pltpu.CompilerParams(
            collective_id=21, has_side_effects=True, vmem_limit_bytes=40 * 2**20
        ),
    )(weight, small, spatial, pair, feat, mask, sizes, tile_sizes)


def forward_kernel(
    images,
    early,
    pre_one,
    first_stats,
    spatial,
    wide,
    mask,
    norms,
    sizes,
    last_own,
    shared_own,
    gate_own,
    message_own,
    last,
    shared,
    gate,
    message,
    act_one,
    act_two,
    act_three,
    shared_act,
    pre_two,
    pre_three,
    pre_four,
    stats,
    one_left,
    one_right,
    parts,
    near_in,
    pair,
    far_in,
    slots_two,
    slots_three,
    slots_four,
    sems,
):
    place = Place(images)
    mail = Mail(sems)
    blk, batch = place.blk, place.batch
    tile, total = pre_one.shape[0], mask.shape[0]
    mid = pre_one.shape[1]
    slim = pre_two.shape[1]
    share = last_own.shape[0]
    base = blk * tile
    greet(place.others + place.tiles)

    def rows_of(index):
        return pl.ds(pl.multiple_of(index * share, share), share)

    def slim_lanes(index):
        return pl.ds(pl.multiple_of(index * slim, slim), slim)

    lanes = slim_lanes(blk)
    wide_lanes = pl.ds(pl.multiple_of(blk * mid, mid), mid)
    got_last = Spread(mail, place, last_own.at[:, wide_lanes], lambda index: last.at[rows_of(index), :])
    got_shared = Spread(mail, place, shared_own, lambda index: shared.at[rows_of(index), :])
    got_gate = Spread(mail, place, gate_own.at[blk], lambda index: gate.at[rows_of(index), :])
    got_message = [
        Spread(
            mail,
            place,
            message_own.at[blk, offset],
            lambda index, offset=offset: message.at[offset, rows_of(index), :],
        )
        for offset in range(early)
    ]
    got_last.start()
    got_shared.start()
    stats[...] = first_stats[...]
    clear_ends(act_one, total)
    clear_ends(shared_act, total)
    clear_ends(one_left, total)
    clear_ends(one_right, total)

    def act_first(rows):
        value = (pre_one[rows, :] - stats[0:1, :]) * stats[1:2, :] * norms[0:1, :] + norms[1:2, :]
        value = silu(value) * mask[at_base(base, rows), :]
        act_one[pl.ds(pl.multiple_of(PITCH + base + rows.start, 16), CHUNK), :] = value.astype(BF16)

    loop(tile, CHUNK, act_first)
    share_tiles(
        mail, place, lambda index: act_one.at[pl.ds(pl.multiple_of(PITCH + index * tile, 16), tile), :]
    )
    widen(act_one, one_left, one_right, total)
    got_last.forward()
    got_shared.forward()

    shifted = (one_left, act_one, one_right)

    def conv_two(rows):
        pre_two[rows, :] = conv_rows(
            shifted, rows, lambda offset, window: dot(window, spatial[offset]), False
        )

    loop(total, BLOCK, conv_two)
    batch_norm_stats(mail, place, pre_two, mask, slots_two, sizes, stats, 2, slim)
    got_gate.start()
    got_message[0].start()

    def act_second(rows):
        value = (pre_two[rows, :] - stats[2:3, :slim]) * stats[3:4, :slim]
        value = silu(value * norms[2:3, :slim] + norms[3:4, :slim]) * mask[rows, :]
        act_two[rows, lanes] = value.astype(BF16)

    loop(total, CHUNK, act_second)
    share_tiles(mail, place, lambda index: act_two.at[:, slim_lanes(index)])

    got_last.finish()
    got_gate.forward()

    def expand(rows):
        pre_three[rows, :] = dot(act_two[rows, :], last[...])

    loop(total, BLOCK, expand)
    batch_norm_stats(mail, place, pre_three, mask, slots_three, sizes, stats, 4, mid)
    got_message[0].forward()
    got_message[1].start()
    got_message[2].start()
    got_shared.finish()

    def act_third(rows):
        normed = (pre_three[rows, :] - stats[4:5, :]) * stats[5:6, :]
        value = normed * norms[4:5, :] + norms[5:6, :] + wide[rows, :].astype(F32)
        act_three[rows, :] = (silu(value) * mask[rows, :]).astype(BF16)

    loop(total, CHUNK, act_third)

    def reduce(rows):
        parts[rows, :] = dot(act_three[rows, :], shared[...]).astype(BF16)

    loop(total, BLOCK, reduce)
    sum_over_tiles(
        mail,
        place,
        lambda index: parts.at[:, slim_lanes(index)],
        near_in,
        pair,
        far_in,
        total,
        pre_four,
    )
    got_message[1].forward()
    batch_norm_stats(mail, place, pre_four, mask, slots_four, sizes, stats, 6, slim)
    got_message[2].forward()
    for later in got_message[3:]:
        later.start()

    def act_fourth(rows):
        value = (pre_four[rows, :] - stats[6:7, :slim]) * stats[7:8, :slim]
        value = silu(value * norms[6:7, :slim] + norms[7:8, :slim]) * mask[rows, :]
        shared_act[pl.ds(pl.multiple_of(PITCH + rows.start, 16), CHUNK), lanes] = value.astype(BF16)

    loop(total, CHUNK, act_fourth)
    share_tiles(
        mail, place, lambda index: shared_act.at[pl.ds(PITCH, total), slim_lanes(index)]
    )
    for later in got_message[3:]:
        later.forward()
    got_gate.finish()
    for one in got_message:
        one.finish()
    mail.close()


def bottleneck(nb, early, pre_one, stats, spatial, wide, mask, norms, sizes, last, shared, gate, message):
    tile, total = pre_one.shape[0], mask.shape[0]
    mid = pre_one.shape[1]
    slim = mid // 4
    padded = total + 2 * PITCH

    def array(*shape, kind=BF16):
        return jax.ShapeDtypeStruct(shape, kind)

    outs = (
        array(mid, mid),
        array(mid, mid),
        array(mid, mid),
        array(early, mid, mid),
        array(padded, mid),
        array(total, mid),
        array(total, mid),
        array(padded, mid),
        array(total, slim, kind=F32),
        array(total, mid, kind=F32),
        array(total, slim, kind=F32),
        array(8, mid, kind=F32),
    )
    return pl.pallas_call(
        functools.partial(forward_kernel, nb, early),
        out_shape=outs,
        in_specs=[VMEM] * 7 + [ANY] * 4,
        out_specs=(VMEM, VMEM, ANY, ANY) + (VMEM,) * 8,
        scratch_shapes=[
            pltpu.VMEM((padded, mid), BF16),
            pltpu.VMEM((padded, mid), BF16),
            pltpu.VMEM((total, mid), BF16),
            pltpu.VMEM((2, total, slim), BF16),
            pltpu.VMEM((total, slim), BF16),
            pltpu.VMEM((total, slim), BF16),
            pltpu.VMEM((nb, 2, slim), F32),
            pltpu.VMEM((nb, 2, mid), F32),
            pltpu.VMEM((nb, 2, slim), F32),
            DMA((2, 128)),
        ],
        cost_estimate=LONG,
        compiler_params=pltpu.CompilerParams(
            collective_id=20, has_side_effects=True, vmem_limit_bytes=60 * 2**20
        ),
    )(pre_one, stats, spatial, wide, mask, norms, sizes, last, shared, gate, message)


class Reduce:
    def __init__(self, mail, place, grad, from_side, summed, from_line, out):
        self.mail, self.place = mail, place
        self.grad, self.from_side, self.summed = grad, from_side, summed
        self.from_line, self.out = from_line, out
        self.side = lax.rem(place.batch, 2)
        self.line = lax.div(place.batch, 2)

    def start(self):
        self.from_x = self.mail.send(self.grad.at[:, 1 - self.side], self.from_side, self.place.side)

    def middle(self):
        place = self.place
        self.from_x.wait_recv()
        lines = self.from_side.shape[0]
        for at in range(lines):
            self.summed[at] = (
                self.grad[at, self.side].astype(F32) + self.from_side[at].astype(F32)
            ).astype(BF16)
        self.copies = [
            self.mail.send(
                self.summed.at[self.line ^ mask],
                self.from_line.at[mask - 1],
                (place.blk, place.batch ^ (2 * mask)),
            )
            for mask in range(1, lines)
        ]

    def finish(self):
        total = self.summed[self.line].astype(F32)
        for at, copy in enumerate(self.copies):
            copy.wait_recv()
            total = total + self.from_line[at].astype(F32)
        self.out[...] = total.astype(BF16)


def reduce_scratch(lines, share, columns, own):
    found = [pltpu.VMEM((lines, 2, share, columns), BF16)] if own else []
    return found + [
        pltpu.VMEM((lines, share, columns), BF16),
        pltpu.VMEM((lines, share, columns), BF16),
        pltpu.VMEM((lines - 1, share, columns), BF16),
    ]


def send_sums(mail, place, slots, sums):
    slots[place.batch] = jnp.concatenate(sums, 0)
    own = slots.at[place.batch]
    return [mail.send(own, own, peer) for peer in place.others]


def silu_back(value):
    sigmoid_value = jax.nn.sigmoid(value)
    return sigmoid_value * (1.0 + value * (1.0 - sigmoid_value))


def norm_back(stats, norms, mask, grad, pre, row, channels, lead, offset=None, skip=None):
    def body(rows):
        normed = (pre[rows, :] - stats[row : row + 1, :channels]) * stats[row + 1 : row + 2, :channels]
        value = normed * norms[row : row + 1, :channels] + norms[row + 1 : row + 2, :channels]
        if skip is not None:
            value = value + skip[rows, :].astype(F32)
        found = lead(rows) * mask[at_base(offset, rows), :] * silu_back(value)
        grad[rows, :] = found
        return found, found * normed

    return loop_sums(pre.shape[0], channels, 2, body)


def through(stats, norms, mask, sizes, grad, pre, row, channels, bias_sum, gain_sum, put, offset=None):
    count = sizes[0, :, :channels]
    for at in range(1, sizes.shape[0]):
        count = count + sizes[at, :, :channels]
    scale = stats[row + 1 : row + 2, :channels] * norms[row : row + 1, :channels]
    bias_part, gain_part = bias_sum / count, gain_sum / count

    def body(rows):
        normed = (pre[rows, :] - stats[row : row + 1, :channels]) * stats[row + 1 : row + 2, :channels]
        found = scale * (grad[rows, :] - bias_part - normed * gain_part)
        put(rows, (found * mask[at_base(offset, rows), :]).astype(BF16))

    loop(pre.shape[0], CHUNK, body)


def backward_kernel(
    images,
    back,
    pre_one,
    pre_two,
    pre_three,
    pre_four,
    stats,
    norms,
    mask,
    sizes,
    wide,
    act_one,
    act_two,
    act_three,
    spatial,
    last,
    shared,
    first,
    gate_grads,
    stream_grads,
    grad_input,
    share_shared,
    share_last,
    share_spatial,
    share_first,
    share_gates,
    share_stream,
    sums_out,
    near_four,
    pair_four,
    far_four,
    grad_four,
    all_four,
    grad_three,
    low_three,
    low_joined,
    joined_rows,
    near_two,
    pair_two,
    far_two,
    grad_two,
    two_left,
    two_here,
    two_right,
    turned,
    strip,
    near_one,
    pair_one,
    far_one,
    grad_one,
    all_one,
    slots_four,
    slots_three,
    slots_two,
    slots_tile,
    slots_one,
    *rest,
):
    place = Place(images)
    sems = rest[-1]
    mail = Mail(sems)
    blk, batch = place.blk, place.batch
    tile, total = pre_one.shape[0], mask.shape[0]
    mid = pre_one.shape[1]
    slim = pre_two.shape[1]
    base = blk * tile
    red_shared = Reduce(mail, place, *rest[0:4], share_shared)
    red_last = Reduce(mail, place, *rest[4:8], share_last)
    red_first = Reduce(mail, place, *rest[8:12], share_first)
    red_spatial = Reduce(mail, place, *rest[12:16], share_spatial)
    red_gates = Reduce(mail, place, gate_grads, *rest[16:19], share_gates)
    red_stream = Reduce(mail, place, stream_grads, *rest[19:22], share_stream)
    greet(place.others + place.tiles)

    def slim_lanes(index):
        return pl.ds(pl.multiple_of(index * slim, slim), slim)

    def tile_rows(index):
        return pl.ds(pl.multiple_of(index * tile, tile), tile)

    def keep(row, bias_sum, gain_sum, channels):
        sums_out[row : row + 1, :channels] = gain_sum
        sums_out[row + 1 : row + 2, :channels] = bias_sum

    sums_out[...] = jnp.zeros_like(sums_out)
    for cells in (two_left, two_here, two_right):
        clear_ends(cells, total)
    red_gates.start()
    red_stream.start()

    sum_over_tiles(
        mail, place, lambda index: back.at[:, slim_lanes(index)], near_four, pair_four, far_four, total, grad_four
    )
    sums = norm_back(stats, norms, mask, grad_four, pre_four, 6, slim, lambda rows: grad_four[rows, :])
    copies = send_sums(mail, place, slots_four, sums)
    for offset in range(9):
        turned[offset * slim : (offset + 1) * slim, :] = spatial[offset].T
    for copy in copies:
        copy.wait_recv()
    bias_sum, gain_sum = add_up(slots_four)
    keep(6, bias_sum, gain_sum, slim)
    lanes = slim_lanes(blk)

    def put_four(rows, value):
        all_four[rows, lanes] = value

    through(stats, norms, mask, sizes, grad_four, pre_four, 6, slim, bias_sum, gain_sum, put_four)
    red_gates.middle()
    red_stream.middle()
    share_tiles(mail, place, lambda index: all_four.at[:, slim_lanes(index)])

    def joined_back(rows):
        return dot_t(all_four[rows, :], shared[...])

    sums = norm_back(stats, norms, mask, grad_three, pre_three, 4, mid, joined_back, None, wide)
    copies = send_sums(mail, place, slots_three, sums)
    grads, lines = red_shared.grad, red_shared.grad.shape[0]
    grads[...] = t_dot(act_three[...], all_four[...]).astype(BF16).reshape(grads.shape)

    def lower(rows):
        low_joined[rows, :] = grad_three[rows, :].astype(BF16)

    loop(total, CHUNK, lower)
    for copy in copies:
        copy.wait_recv()
    bias_sum, gain_sum = add_up(slots_three)
    keep(4, bias_sum, gain_sum, mid)

    def put_three(rows, value):
        low_three[rows, :] = value

    through(stats, norms, mask, sizes, grad_three, pre_three, 4, mid, bias_sum, gain_sum, put_three)
    red_gates.finish()
    red_stream.finish()
    mail.close()
    red_shared.start()

    def two_part(rows):
        all_four[rows, :] = dot_t(low_three[rows, :], last[...]).astype(BF16)

    loop(total, BLOCK, two_part)
    sum_over_tiles(
        mail, place, lambda index: all_four.at[:, slim_lanes(index)], near_two, pair_two, far_two, total, grad_two
    )
    landing = joined_rows.at[:, pl.ds(pl.multiple_of(blk * mid, mid), mid)]
    joined_here = mail.local(low_joined.at[tile_rows(blk)], landing)
    joined_copies = [
        mail.send(low_joined.at[tile_rows(blk ^ mask_t)], landing, (blk ^ mask_t, batch))
        for mask_t in range(1, 4)
    ]
    sums = norm_back(stats, norms, mask, grad_two, pre_two, 2, slim, lambda rows: grad_two[rows, :])
    copies = send_sums(mail, place, slots_two, sums)
    grads = red_last.grad
    grads[...] = t_dot(act_two[...], low_three[...]).astype(BF16).reshape(grads.shape)
    for copy in copies:
        copy.wait_recv()
    bias_sum, gain_sum = add_up(slots_two)
    keep(2, bias_sum, gain_sum, slim)

    def put_two(rows, value):
        two_here[pl.ds(pl.multiple_of(rows.start + PITCH, 16), CHUNK), :] = value

    through(stats, norms, mask, sizes, grad_two, pre_two, 2, slim, bias_sum, gain_sum, put_two)
    widen(two_here, two_left, two_right, total)
    red_shared.middle()
    red_last.start()
    shifted = (two_left, two_here, two_right)

    def one_part(rows):
        for offset in range(9):
            row, col = 2 - offset // 3, 2 - offset % 3
            window = shifted[col][pl.ds(pl.multiple_of(rows.start + PITCH * row, 16), BLOCK), :]
            strip[:, offset * slim : (offset + 1) * slim] = window
        low_three[rows, :] = dot(strip[...], turned[...]).astype(BF16)

    loop(total, BLOCK, one_part)
    sum_over_tiles(
        mail, place, lambda index: low_three.at[tile_rows(index)], near_one, pair_one, far_one, tile, grad_one
    )
    sums = norm_back(stats, norms, mask, grad_one, pre_one, 0, mid, lambda rows: grad_one[rows, :], base)
    slots_tile[blk] = jnp.concatenate(sums, 0)
    swap_tile_sums(mail, place, slots_tile)
    copies = send_sums(mail, place, slots_one, list(add_up(slots_tile)))
    grads = red_spatial.grad
    for offset in range(9):
        row, col = 2 - offset // 3, 2 - offset % 3
        window = shifted[col][PITCH * row : PITCH * row + total, :]
        found = t_dot(act_one[PITCH : PITCH + total, :], window).astype(BF16)
        grads[:, :, :, offset * slim : (offset + 1) * slim] = found.reshape(grads.shape[:3] + (slim,))
    for copy in copies:
        copy.wait_recv()
    bias_sum, gain_sum = add_up(slots_one)
    keep(0, bias_sum, gain_sum, mid)

    def put_one(rows, value):
        all_one[at_base(base, rows), :] = value

    through(stats, norms, mask, sizes, grad_one, pre_one, 0, mid, bias_sum, gain_sum, put_one, base)
    red_shared.finish()
    red_last.middle()
    red_spatial.start()
    share_tiles(mail, place, lambda index: all_one.at[tile_rows(index)])
    grads = red_first.grad
    grads[...] = t_dot(wide[...], all_one[...]).astype(BF16).reshape(grads.shape)
    red_first.start()
    red_spatial.middle()
    joined_here.wait()
    for copy in joined_copies:
        copy.wait_recv()

    def input_grads(rows):
        own = all_one[pl.ds(pl.multiple_of(base + rows.start, CHUNK), rows.size), :]
        grad_input[rows, :] = dot_t(own, first[...]) + joined_rows[rows, :].astype(F32)

    loop(tile, tile // 3, input_grads)
    red_last.finish()
    red_first.middle()
    red_spatial.finish()
    red_first.finish()
    mail.close()


def bottleneck_back(nb, back, pres, stats, norms, mask, sizes, wide, acts, weights, gate_grads, stream_grads):
    tile, total = pres[0].shape[0], mask.shape[0]
    mid = pres[0].shape[1]
    slim = mid // 4
    lines, share = nb // 2, mid // nb
    padded = total + 2 * PITCH
    width = weights[3].shape[0]

    def array(*shape, kind=BF16):
        return jax.ShapeDtypeStruct(shape, kind)

    def vmem(*shape, kind=BF16):
        return pltpu.VMEM(shape, kind)

    scratch = [
        vmem(2, total, slim),
        vmem(total, slim),
        vmem(total, slim),
        vmem(total, slim, kind=F32),
        vmem(total, mid),
        vmem(total, mid, kind=F32),
        vmem(total, mid),
        vmem(total, mid),
        vmem(tile, width),
        vmem(2, total, slim),
        vmem(total, slim),
        vmem(total, slim),
        vmem(total, slim, kind=F32),
        vmem(padded, slim),
        vmem(padded, slim),
        vmem(padded, slim),
        vmem(9 * slim, mid),
        vmem(BLOCK, 9 * slim),
        vmem(2, tile, mid),
        vmem(tile, mid),
        vmem(tile, mid),
        vmem(tile, mid, kind=F32),
        vmem(total, mid),
        vmem(nb, 2, slim, kind=F32),
        vmem(nb, 2, mid, kind=F32),
        vmem(nb, 2, slim, kind=F32),
        vmem(4, 2, mid, kind=F32),
        vmem(nb, 2, mid, kind=F32),
    ]
    for columns in (mid, mid, mid, 9 * slim):
        scratch += reduce_scratch(lines, share, columns, True)
    for columns in (mid, LANES):
        scratch += reduce_scratch(lines, share, columns, False)
    scratch.append(DMA((2, 128)))
    return pl.pallas_call(
        functools.partial(backward_kernel, nb),
        out_shape=(
            array(tile, width, kind=F32),
            array(share, mid),
            array(share, mid),
            array(share, 9 * slim),
            array(share, mid),
            array(share, mid),
            array(share, LANES),
            array(8, mid, kind=F32),
        ),
        in_specs=[VMEM] * 19,
        out_specs=(VMEM,) * 8,
        scratch_shapes=scratch,
        cost_estimate=LONG,
        compiler_params=pltpu.CompilerParams(
            collective_id=22, has_side_effects=True, vmem_limit_bytes=62 * 2**20
        ),
    )(
        back,
        *pres,
        stats,
        norms,
        mask,
        sizes,
        wide,
        *acts,
        *weights,
        gate_grads.reshape(lines, 2, share, mid),
        stream_grads.reshape(lines, 2, share, LANES),
    )


class Tiles:
    def __init__(self, mail, place, slot):
        self.mail, self.place, self.slot = mail, place, slot

    def start(self):
        own = self.slot(self.place.blk)
        self.far = self.mail.send(own, own, self.place.across)
        self.near = self.mail.send(own, own, self.place.mate)

    def forward(self):
        self.far.wait_recv()
        passed = self.slot(self.place.blk ^ 2)
        self.last = self.mail.send(passed, passed, self.place.mate)

    def finish(self):
        self.near.wait_recv()
        self.last.wait_recv()


def task_kernel(
    images,
    early,
    shared_act,
    mask,
    mask_line,
    targets,
    sizes,
    norms,
    head,
    message_start,
    gate,
    to_depth,
    to_classes,
    from_gated,
    streams,
    slopes,
    pre_five,
    stats,
    grad_msg,
    grad_gate,
    gate_grads,
    stream_grads,
    message_grads,
    left,
    right,
    task,
    messages,
    opened,
    gated,
    slots,
    slots_five,
    sems,
):
    place = Place(images)
    mail = Mail(sems)
    total = mask.shape[0]
    mid = pre_five.shape[1]
    is_first, is_last = place.blk == 0, place.blk == 3
    greet(place.others + [place.mate, place.across])
    stats[...] = jnp.zeros_like(stats)
    for cells in (left, right, task, grad_msg):
        clear_ends(cells, total)
    widen(shared_act, left, right, total)

    def heads(rows):
        pre_five[rows, :] = conv_rows(
            (left, shared_act, right), rows, lambda offset, window: dot(window, head[offset]), False
        )

    loop(total, BLOCK, heads)
    batch_norm_stats(mail, place, pre_five, mask, slots_five, sizes, stats, 0, mid)

    def act_task(rows):
        value = (pre_five[rows, :] - stats[0:1, :]) * stats[1:2, :] * norms[0:1, :] + norms[1:2, :]
        task[pl.ds(pl.multiple_of(PITCH + rows.start, 16), CHUNK), :] = (
            silu(value) * mask[rows, :]
        ).astype(BF16)

    loop(total, CHUNK, act_task)
    widen(task, left, right, total)

    def message_weight(offset):
        return message_start[offset] if offset < early else head[9 + offset - early]

    def here(rows):
        return pl.ds(pl.multiple_of(PITCH + rows.start, 16), rows.size)

    def send_messages(rows):
        messages[rows, :] = conv_rows(
            (left, task, right), rows, lambda offset, window: dot(window, message_weight(offset)), False
        )
        own = task[here(rows), :]
        opened[rows, :] = jax.nn.sigmoid(dot(own, gate[...]))
        part = (opened[rows, :] * messages[rows, :]).astype(BF16)
        gated[rows, :] = part
        depth_part = jnp.where(is_first, own, part)
        sem_part = jnp.where(is_last, own, part)
        slots[place.blk, :, rows] = dot_t(to_depth[...], depth_part) + dot_t(to_classes[...], sem_part)

    loop(total, BLOCK, send_messages)
    share_tiles(mail, place, lambda index: slots.at[index])
    classes = to_depth.shape[0]
    kind = lax.broadcasted_iota(jnp.int32, (classes, 2 * BLOCK), 0)

    def compare(rows):
        value = slots[0, :, rows] + slots[1, :, rows] + slots[2, :, rows] + slots[3, :, rows]
        streams[:, rows] = value
        is_class = (kind >= 1) & (kind <= CLASSES)
        top = jnp.max(jnp.where(is_class, value, -jnp.inf), 0, keepdims=True)
        power = jnp.where(is_class, jnp.exp(value - top), 0.0)
        chance = power / jnp.sum(power, 0, keepdims=True)
        label = targets[1:2, rows]
        chance = chance - jnp.where((kind - 1).astype(F32) == label, 1.0, 0.0)
        slope = jnp.where(kind == 0, value - targets[0:1, rows], jnp.where(is_class, chance, 0.0))
        slopes[:, rows] = (slope * mask_line[0:1, rows]).astype(BF16)

    loop(total, 2 * BLOCK, compare)
    by_part = dot(slopes[...], gated[...])
    by_task = dot(slopes[...], task[PITCH : PITCH + total, :])
    row = lax.broadcasted_iota(jnp.int32, by_part.shape, 0)
    use_task = ((row == 0) & is_first) | ((row > 0) & is_last)
    found = jnp.where(use_task, by_task, by_part)
    found = jnp.concatenate([found, jnp.zeros((LANES - classes, mid), F32)], 0)
    stream_grads[...] = found.T.astype(BF16)

    def grads(rows):
        grad = t_dot(slopes[:, rows], from_gated[...])
        open_part = opened[rows, :]
        grad_msg[here(rows), :] = (grad * open_part).astype(BF16)
        grad_gate[rows, :] = (grad * messages[rows, :] * open_part * (1.0 - open_part)).astype(BF16)

    loop(total, BLOCK, grads)
    gate_grads[...] = t_dot(task[PITCH : PITCH + total, :], grad_gate[...]).astype(BF16)
    widen(grad_msg, left, right, total)
    shifted = (left, grad_msg, right)
    for offset in range(9):
        row, col = 2 - offset // 3, 2 - offset % 3
        window = shifted[col][PITCH * row : PITCH * row + total, :]
        message_grads[:, offset * mid : (offset + 1) * mid] = t_dot(
            task[PITCH : PITCH + total, :], window
        ).astype(BF16)
    mail.close()


CLASSES = 40


def one_task(nb, early, shared_act, mask, mask_line, targets, sizes, norms, weights, streams_weights):
    total = mask.shape[0]
    padded, mid = shared_act.shape
    lines = streams_weights[0].shape[0]

    def array(*shape, kind=BF16):
        return jax.ShapeDtypeStruct(shape, kind)

    def vmem(*shape, kind=BF16):
        return pltpu.VMEM(shape, kind)

    return pl.pallas_call(
        functools.partial(task_kernel, nb, early),
        out_shape=(
            array(lines, total, kind=F32),
            array(lines, total),
            array(total, mid, kind=F32),
            array(8, mid, kind=F32),
            array(padded, mid),
            array(total, mid),
            array(mid, mid),
            array(mid, LANES),
            array(mid, 9 * mid),
        ),
        in_specs=[VMEM] * 12,
        out_specs=(VMEM,) * 9,
        scratch_shapes=[
            vmem(padded, mid),
            vmem(padded, mid),
            vmem(padded, mid),
            vmem(total, mid, kind=F32),
            vmem(total, mid, kind=F32),
            vmem(total, mid),
            vmem(4, lines, total, kind=F32),
            vmem(nb, 2, mid, kind=F32),
            DMA((2, 32)),
        ],
        cost_estimate=LONG,
        compiler_params=pltpu.CompilerParams(
            collective_id=23, has_side_effects=True, vmem_limit_bytes=60 * 2**20
        ),
    )(shared_act, mask, mask_line, targets, sizes, norms, *weights, *streams_weights)


def task_back_kernel(
    images,
    early,
    shared_act,
    mask,
    sizes,
    norms,
    head,
    message_start,
    gate,
    from_direct,
    slopes,
    pre_five,
    stats,
    grad_msg,
    grad_gate,
    back,
    head_grads,
    sums_out,
    left,
    right,
    grad_five,
    grad,
    slots_five,
    sems,
):
    place = Place(images)
    mail = Mail(sems)
    total = mask.shape[0]
    mid = pre_five.shape[1]
    greet(place.others)
    sums_out[...] = jnp.zeros_like(sums_out)
    for cells in (left, right, grad_five):
        clear_ends(cells, total)
    widen(grad_msg, left, right, total)

    def message_weight(offset):
        return message_start[offset] if offset < early else head[9 + offset - early]

    def task_grads(rows):
        found = conv_rows(
            (left, grad_msg, right), rows, lambda offset, window: dot_t(window, message_weight(offset)), True
        )
        found = found + dot_t(grad_gate[rows, :], gate[...])
        grad[rows, :] = found + t_dot(slopes[:, rows], from_direct[...])

    loop(total, BLOCK, task_grads)
    sums = norm_back(stats, norms, mask, grad, pre_five, 0, mid, lambda rows: grad[rows, :])
    for copy in send_sums(mail, place, slots_five, sums):
        copy.wait_recv()
    bias_sum, gain_sum = add_up(slots_five)
    sums_out[0:1, :] = gain_sum
    sums_out[1:2, :] = bias_sum

    def put(rows, value):
        grad_five[pl.ds(pl.multiple_of(PITCH + rows.start, 16), CHUNK), :] = value

    through(stats, norms, mask, sizes, grad, pre_five, 0, mid, bias_sum, gain_sum, put)
    widen(grad_five, left, right, total)
    shifted = (left, grad_five, right)

    def head_back(rows):
        back[rows, :] = conv_rows(
            shifted, rows, lambda offset, window: dot_t(window, head[offset]), True
        ).astype(BF16)

    loop(total, BLOCK, head_back)
    for offset in range(9):
        row, col = 2 - offset // 3, 2 - offset % 3
        window = shifted[col][PITCH * row : PITCH * row + total, :]
        head_grads[:, offset * mid : (offset + 1) * mid] = t_dot(
            shared_act[PITCH : PITCH + total, :], window
        ).astype(BF16)
    mail.close()


def one_task_back(nb, early, shared_act, mask, sizes, norms, weights, from_direct, slopes, rest):
    total = mask.shape[0]
    padded, mid = shared_act.shape

    def array(*shape, kind=BF16):
        return jax.ShapeDtypeStruct(shape, kind)

    def vmem(*shape, kind=BF16):
        return pltpu.VMEM(shape, kind)

    return pl.pallas_call(
        functools.partial(task_back_kernel, nb, early),
        out_shape=(array(total, mid), array(mid, 9 * mid), array(8, mid, kind=F32)),
        in_specs=[VMEM] * 13,
        out_specs=(VMEM,) * 3,
        scratch_shapes=[
            vmem(padded, mid),
            vmem(padded, mid),
            vmem(padded, mid),
            vmem(total, mid, kind=F32),
            vmem(nb, 2, mid, kind=F32),
            DMA((2, 16)),
        ],
        cost_estimate=LONG,
        compiler_params=pltpu.CompilerParams(
            collective_id=24, has_side_effects=True, vmem_limit_bytes=60 * 2**20
        ),
    )(shared_act, mask, sizes, norms, *weights, from_direct, slopes, *rest)


def last_kernel(shares, sums, all_shares, all_sums, sems):
    place = Place(2)
    mail = Mail(sems)
    blk = place.blk
    greet([place.mate, place.across])
    here = [mail.local(shares, all_shares.at[blk]), mail.local(sums, all_sums.at[blk])]
    both = []
    for source, slots in ((sums, all_sums), (shares, all_shares)):
        far = mail.send(source, slots.at[blk], place.across)
        near = mail.send(source, slots.at[blk], place.mate)
        both.append((far, near, slots))
    for far, near, slots in both:
        far.wait_recv()
        passed = slots.at[blk ^ 2]
        last = mail.send(passed, passed, place.mate)
        near.wait_recv()
        last.wait_recv()
    for copy in here:
        copy.wait()
    mail.close()


def gather_last(shares, sums):
    return pl.pallas_call(
        last_kernel,
        out_shape=(
            jax.ShapeDtypeStruct((4,) + shares.shape, shares.dtype),
            jax.ShapeDtypeStruct((4,) + sums.shape, sums.dtype),
        ),
        in_specs=[ANY] * 2,
        out_specs=(ANY, ANY),
        scratch_shapes=[DMA((2, 16))],
        compiler_params=pltpu.CompilerParams(collective_id=25, has_side_effects=True),
    )(shares, sums)


def on_device(
    nt,
    nb,
    features,
    crop_rows,
    crop_cols,
    depth_target,
    labels,
    first_weight,
    spatial_weight,
    last_weight,
    shared_weight,
    head_weights,
    message_weights,
    gate_weights,
    depth_weight,
    class_weight,
    mid_gain,
    mid_bias,
    out_gain,
    out_bias,
):
    tile_rows, cols, width = features.shape[1:]
    tile = tile_rows * cols
    rows = tile_rows * nt
    pixels = rows * cols
    tasks = head_weights.shape[0]
    mid = first_weight.shape[1]
    share = mid // nb
    slim = mid // nt
    classes = class_weight.shape[1]
    blk, batch = lax.axis_index("blk"), lax.axis_index("batch")

    image_rows = lax.dynamic_index_in_dim(crop_rows, batch, 0, False)
    image_cols = lax.dynamic_index_in_dim(crop_cols, batch, 0, False)
    row_ids = jnp.arange(rows, dtype=jnp.int32)
    col_ids = jnp.arange(PITCH, dtype=jnp.int32)
    inside_grid = (row_ids[:, None] < image_rows) & (col_ids[None, :] < image_cols)
    inside_grid = inside_grid.astype(F32)
    inside_wide = inside_grid.reshape(rows * PITCH, 1)
    inside = inside_grid[:, :cols].reshape(pixels, 1)
    inside_tile = lax.dynamic_slice_in_dim(inside, blk * tile, tile, 0)
    sizes_flat = (crop_rows * crop_cols).astype(F32)
    valid_count = jnp.sum(sizes_flat)
    sizes = jnp.broadcast_to(sizes_flat[:, None, None], (nb, 1, mid))
    tile_counts = jnp.sum(inside.reshape(nt, tile), 1)
    tile_sizes = jnp.broadcast_to(tile_counts[:, None, None], (nt, 1, mid))
    image_size = jnp.maximum(jnp.sum(inside), 1.0)

    params = jnp.concatenate(
        [
            mid_gain.reshape(-1),
            mid_bias.reshape(-1),
            out_gain,
            out_bias,
            depth_weight,
            class_weight.reshape(-1),
        ]
    )
    room = -(-params.shape[0] // (16 * LANES)) * 16 * LANES
    small = jnp.pad(params, (0, room - params.shape[0])).reshape(-1, LANES)
    feat = jnp.pad(features[0], ((0, 0), (0, PITCH - cols), (0, 0))).reshape(tile_rows * PITCH, width)
    piece = shared_weight.shape[0] // nt
    order = [
        (t * nb + b, (b * nt // nb) * nb + (b % (nb // nt)) * nt + t)
        for t in range(nt)
        for b in range(nb)
    ]
    shared_own = lax.ppermute(
        lax.dynamic_slice_in_dim(shared_weight, blk * piece, piece, 0), ("blk", "batch"), order
    )
    pair = jnp.stack([depth_target[0], labels[0].astype(F32)])
    pair = jnp.pad(pair, ((0, 6), (0, 0), (0, PITCH - cols))).reshape(8, tile_rows * PITCH)
    full_first, smalls, targets, wide_features, spatial, pre_one, stats = begin(
        nb, first_weight, small, spatial_weight, pair, feat, inside_wide, sizes, tile_sizes
    )
    full_first = full_first.reshape(width, mid)
    smalls = smalls.reshape(nb, room)
    at = 0

    def taken(count):
        nonlocal at
        found = smalls[:, at : at + count]
        at += count
        return found

    norms_count = mid_gain.shape[0]
    out_share = out_gain.shape[0]
    gain_mid = taken(norms_count * share).reshape(nb, norms_count, share).swapaxes(0, 1)
    gain_mid = gain_mid.reshape(norms_count, mid).astype(F32)
    bias_mid = taken(norms_count * share).reshape(nb, norms_count, share).swapaxes(0, 1)
    bias_mid = bias_mid.reshape(norms_count, mid).astype(F32)
    gain_out = lax.dynamic_slice_in_dim(taken(out_share).reshape(width), blk * mid, mid, 0).astype(F32)
    bias_out = lax.dynamic_slice_in_dim(taken(out_share).reshape(width), blk * mid, mid, 0).astype(F32)
    full_depth = taken(share).reshape(mid, 1)
    full_classes = taken(share * classes).reshape(mid, classes)

    def slim_of(vector):
        return lax.dynamic_slice_in_dim(vector, blk * slim, slim, 0)

    def filled(vector):
        return jnp.pad(vector, (0, mid - vector.shape[0]))

    gain_two, bias_two = slim_of(gain_mid[1]), slim_of(bias_mid[1])
    gain_four, bias_four = slim_of(gain_mid[2]), slim_of(bias_mid[2])
    norms = jnp.stack(
        [
            gain_mid[0],
            bias_mid[0],
            filled(gain_two),
            filled(bias_two),
            gain_out,
            bias_out,
            filled(gain_four),
            filled(bias_four),
        ]
    )
    early = 5
    large = jnp.concatenate(
        [
            lax.dynamic_index_in_dim(head_weights, blk, 0, False),
            lax.dynamic_index_in_dim(message_weights, blk, 0, False)[early:],
        ],
        0,
    )
    large, stats = lax.optimization_barrier((large, stats))
    large = lax.all_gather(large, "batch", axis=1, tiled=True)
    (
        last,
        shared,
        gate,
        message_start,
        act_one,
        act_two,
        act_three,
        shared_act,
        pre_two,
        pre_three,
        pre_four,
        stats,
    ) = bottleneck(
        nb,
        early,
        pre_one,
        stats,
        spatial,
        wide_features,
        inside_wide,
        norms,
        sizes,
        last_weight,
        shared_own,
        gate_weights,
        message_weights,
    )

    task_norms = jnp.stack(
        [
            lax.dynamic_index_in_dim(gain_mid, 3 + blk, 0, False),
            lax.dynamic_index_in_dim(bias_mid, 3 + blk, 0, False),
        ]
    )
    task_norms = jnp.pad(task_norms, ((0, 6), (0, 0)))
    lines = -(-(1 + classes) // 16) * 16
    stream_weight = jnp.concatenate([full_depth, full_classes], 1).T
    stream_weight = jnp.pad(stream_weight, ((0, lines - 1 - classes), (0, 0)))
    is_depth = jnp.arange(lines)[:, None] == 0
    none = jnp.zeros((), BF16)
    is_first, is_last = blk == 0, blk == tasks - 1
    own_stream = jnp.where(is_depth, is_first, is_last)
    to_depth = jnp.where(is_depth, stream_weight, none)
    to_classes = jnp.where(is_depth, none, stream_weight)
    from_gated = jnp.where(own_stream, none, stream_weight)
    from_direct = jnp.where(own_stream, stream_weight, none)
    mask_line = jnp.broadcast_to(inside_wide.reshape(1, -1), (8, rows * PITCH))
    weights = (large, message_start, gate)
    (
        streams,
        slopes,
        pre_five,
        task_stats,
        grad_msg,
        grad_gate,
        gate_grads,
        stream_grads,
        message_grads,
    ) = one_task(
        nb,
        early,
        shared_act,
        inside_wide,
        mask_line,
        targets,
        sizes,
        task_norms,
        weights,
        (to_depth, to_classes, from_gated),
    )
    own_streams = lax.dynamic_slice_in_dim(streams, blk * tile_rows * PITCH, tile_rows * PITCH, 1)
    own_streams = own_streams.reshape(lines, tile_rows, PITCH)[:, :, :cols]
    depth_out = own_streams[0]
    logits = own_streams[1 : 1 + classes].transpose(1, 2, 0)
    share_messages = lax.psum_scatter(message_grads, "batch", scatter_dimension=0, tiled=True)
    back, head_grads, task_sums = one_task_back(
        nb,
        early,
        shared_act,
        inside_wide,
        sizes,
        task_norms,
        weights,
        from_direct,
        slopes,
        (pre_five, task_stats, grad_msg, grad_gate),
    )

    share_heads = lax.psum_scatter(head_grads, "batch", scatter_dimension=0, tiled=True)
    (
        grad_input,
        share_shared,
        share_last,
        share_spatial,
        share_first,
        share_gates,
        share_stream,
        sums_wide,
    ) = bottleneck_back(
        nb,
        back,
        (pre_one, pre_two, pre_three, pre_four),
        stats,
        norms,
        inside_wide,
        sizes,
        wide_features,
        (act_one, act_two, act_three),
        (spatial, last, shared, full_first),
        gate_grads,
        stream_grads,
    )
    grad_input = grad_input.reshape(tile_rows, PITCH, width)[:, :cols]

    moved = lax.ppermute(
        jnp.concatenate([share_first, share_shared], 0), ("blk", "batch"), [(b, a) for a, b in order]
    )
    share_messages, share_heads, moved = lax.optimization_barrier((share_messages, share_heads, moved))
    shares = jnp.concatenate(
        [
            moved,
            share_last,
            share_gates,
            share_spatial.reshape(share, 9, slim).swapaxes(0, 1).reshape(-1, mid),
            share_stream.reshape(-1, mid),
            share_messages.reshape(share, 9, mid).swapaxes(0, 1).reshape(9 * share, mid),
            share_heads.reshape(share, 9, mid).swapaxes(0, 1).reshape(9 * share, mid),
        ],
        0,
    )
    sums = jnp.pad(jnp.concatenate([sums_wide, task_sums[:2]], 0), ((0, 6), (0, 0)))
    all_shares, sums = gather_last(shares, sums)
    at = 0

    def part(count):
        nonlocal at
        found = all_shares[:, at : at + count].astype(F32)
        at += count
        return found

    red_first = part(share).reshape(nt * share, mid)
    red_shared = part(share).reshape(nt * share, mid)
    red_last = part(share).transpose(1, 0, 2).reshape(share, width)
    red_gates = part(share)
    red_spatial = part(9 * share * slim // mid).reshape(nt, 9, share, slim)
    red_spatial = red_spatial.transpose(1, 2, 0, 3).reshape(9, share, mid)
    streams_red = jnp.sum(part(share * LANES // mid).reshape(nt, share, LANES), 0)
    red_depth = streams_red[:, 0]
    red_classes = streams_red[:, 1 : 1 + classes]
    red_messages = part(9 * share).reshape(nt, 9, share, mid)
    red_heads = part(9 * share).reshape(nt, 9, share, mid)
    two_gain, two_bias = sums[:, 2, :slim].reshape(1, mid), sums[:, 3, :slim].reshape(1, mid)
    four_gain, four_bias = sums[:, 6, :slim].reshape(1, mid), sums[:, 7, :slim].reshape(1, mid)
    mid_gains = jnp.concatenate([sums[0, 0:1], two_gain, four_gain, sums[:, 8]], 0)
    mid_biases = jnp.concatenate([sums[0, 1:2], two_bias, four_bias, sums[:, 9]], 0)
    grad_mid_gain = lax.dynamic_slice_in_dim(mid_gains, batch * share, share, 1)
    grad_mid_bias = lax.dynamic_slice_in_dim(mid_biases, batch * share, share, 1)
    grad_out_gain = lax.dynamic_slice_in_dim(sums[:, 4].reshape(width), batch * out_share, out_share, 0)
    grad_out_bias = lax.dynamic_slice_in_dim(sums[:, 5].reshape(width), batch * out_share, out_share, 0)
    return (
        depth_out.reshape(1, tile_rows, cols),
        logits.reshape(1, tile_rows, cols, classes),
        grad_input.reshape(1, tile_rows, cols, width),
        red_first,
        red_spatial,
        red_last,
        red_shared,
        red_heads,
        red_messages,
        red_gates,
        red_depth,
        red_classes,
        grad_mid_gain,
        grad_mid_bias,
        grad_out_gain,
        grad_out_bias,
    )


def solution(mesh):
    nt, nb = mesh.shape["blk"], mesh.shape["batch"]
    placed = (
        P("batch", "blk", None, None),
        P(),
        P(),
        P("batch", "blk", None),
        P("batch", "blk", None),
        P("batch", None),
        P(None, "batch", None),
        P("batch", None),
        P("batch", None),
        P(None, None, "batch", None),
        P(None, None, "batch", None),
        P(None, "batch", None),
        P("batch"),
        P("batch", None),
        P(None, "batch"),
        P(None, "batch"),
        P("batch"),
        P("batch"),
    )
    return jax.shard_map(
        functools.partial(on_device if nb == 8 else on_device_any, nt, nb),
        mesh=mesh,
        in_specs=placed,
        out_specs=(
            P("batch", "blk", None),
            P("batch", "blk", None, None),
            P("batch", "blk", None, None),
            P("batch", None),
            P(None, "batch", None),
            P("batch", None),
            P("batch", None),
            P(None, None, "batch", None),
            P(None, None, "batch", None),
            P(None, "batch", None),
            P("batch"),
            P("batch", None),
            P(None, "batch"),
            P(None, "batch"),
            P("batch"),
            P("batch"),
        ),
        check_vma=False,
    )
```

```python
import functools

import jax
import jax.numpy as jnp
from jax import lax
from jax.experimental import pallas as pl
from jax.experimental.pallas import tpu as pltpu
from jax.sharding import PartitionSpec as P

EPSILON = 1e-05
MESH = pl.DeviceIdType.MESH
BF16 = jnp.bfloat16
F32 = jnp.float32
LANES = 128


def greet(peers):
    barrier = pltpu.get_barrier_semaphore()
    for peer in peers:
        pl.semaphore_signal(barrier, inc=1, device_id=peer, device_id_type=MESH)
    pl.semaphore_wait(barrier, len(peers))


def send(src, dst, send_sem, recv_sem, peer):
    copy = pltpu.make_async_remote_copy(
        src_ref=src,
        dst_ref=dst,
        send_sem=send_sem,
        recv_sem=recv_sem,
        device_id=peer,
        device_id_type=MESH,
    )
    copy.start()
    return copy


def first_kernel(images, weight, small, full, smalls, own, zs, xs, cs, ps):
    blk, batch = lax.axis_index("blk"), lax.axis_index("batch")
    half = weight.shape[0] // 2
    rows = pl.ds(pl.multiple_of(lax.rem(blk, 2) * half, half), half)
    side = (blk, batch ^ 1)
    mate = (blk ^ 1, batch)
    lines = range(1, images // 2)
    others = [(blk, batch ^ mask) for mask in range(1, images)]
    greet(others + [mate])
    copies = []
    here = pltpu.make_async_copy(weight, full.at[batch], own.at[0])
    here.start()
    here_small = pltpu.make_async_copy(small, smalls.at[batch], own.at[1])
    here_small.start()
    z_copies = {}
    for mask in lines:
        z_copies[mask] = send(
            weight.at[rows],
            full.at[batch, rows],
            zs.at[0, mask],
            zs.at[1, mask],
            (blk, batch ^ (2 * mask)),
        )
    x_copies = {
        0: send(weight.at[rows], full.at[batch, rows], xs.at[0, 0], xs.at[1, 0], side)
    }
    for place, peer in enumerate(others):
        copies.append(
            send(small, smalls.at[batch], ps.at[0, place], ps.at[1, place], peer)
        )
    core_copies = []

    def hand_over(source, mask):
        block = full.at[source, rows]
        core_copies.append(send(block, block, cs.at[0, mask], cs.at[1, mask], mate))

    for mask in lines:
        z_copies[mask].wait_recv()
        source = batch ^ (2 * mask)
        block = full.at[source, rows]
        x_copies[mask] = send(block, block, xs.at[0, mask], xs.at[1, mask], side)
        hand_over(source, 2 * mask)
    for mask in range(images // 2):
        x_copies[mask].wait_recv()
        hand_over(batch ^ (2 * mask + 1), 2 * mask + 1)
    for copy in core_copies + copies:
        copy.wait()
    for mask in lines:
        z_copies[mask].wait_send()
    for mask in range(images // 2):
        x_copies[mask].wait_send()
    here.wait()
    here_small.wait()


def gather_first(weight, small, images):
    any_place = pl.BlockSpec(memory_space=pl.ANY)
    dma = pltpu.SemaphoreType.DMA
    return pl.pallas_call(
        functools.partial(first_kernel, images),
        out_shape=(
            jax.ShapeDtypeStruct((images,) + weight.shape, weight.dtype),
            jax.ShapeDtypeStruct((images,) + small.shape, small.dtype),
        ),
        in_specs=[any_place] * 2,
        out_specs=(any_place, any_place),
        scratch_shapes=[
            dma((2,)),
            dma((2, images)),
            dma((2, images)),
            dma((2, images)),
            dma((2, images)),
        ],
        compiler_params=pltpu.CompilerParams(collective_id=0, has_side_effects=True),
    )(weight, small)


def tiles_kernel(block, every, own, sems):
    blk, batch = lax.axis_index("blk"), lax.axis_index("batch")
    mate, across = (blk ^ 1, batch), (blk ^ 2, batch)
    greet([mate, across])
    far = send(block, every.at[blk], sems.at[0, 0], sems.at[1, 0], across)
    near = send(block, every.at[blk], sems.at[0, 1], sems.at[1, 1], mate)
    here = pltpu.make_async_copy(block, every.at[blk], own.at[0])
    here.start()
    far.wait_recv()
    passed = every.at[blk ^ 2]
    last = send(passed, passed, sems.at[0, 2], sems.at[1, 2], mate)
    near.wait()
    last.wait()
    far.wait_send()
    here.wait()


def gather_tiles(block, ident):
    any_place = pl.BlockSpec(memory_space=pl.ANY)
    dma = pltpu.SemaphoreType.DMA
    return pl.pallas_call(
        tiles_kernel,
        out_shape=jax.ShapeDtypeStruct((4,) + block.shape, block.dtype),
        in_specs=[any_place],
        out_specs=any_place,
        scratch_shapes=[dma((1,)), dma((2, 3))],
        compiler_params=pltpu.CompilerParams(collective_id=ident, has_side_effects=True),
    )(block)


def sum_kernel(parts, total, near_in, pair, far_in, sems):
    blk, batch = lax.axis_index("blk"), lax.axis_index("batch")
    mate, across = (blk ^ 1, batch), (blk ^ 2, batch)
    greet([mate, across])
    far_first = send(parts.at[blk ^ 3], near_in.at[0], sems.at[0, 0], sems.at[1, 0], mate)
    near_next = send(parts.at[blk ^ 1], near_in.at[1], sems.at[0, 1], sems.at[1, 1], mate)
    far_first.wait_recv()
    pair[...] = (parts[blk ^ 2].astype(F32) + near_in[0].astype(F32)).astype(pair.dtype)
    far = send(pair, far_in, sems.at[0, 2], sems.at[1, 2], across)
    near_next.wait_recv()
    total[...] = parts[blk].astype(F32) + near_in[1].astype(F32)
    far.wait_recv()
    total[...] += far_in[...].astype(F32)
    far_first.wait_send()
    near_next.wait_send()
    far.wait_send()


def sum_tiles(parts, ident):
    dma = pltpu.SemaphoreType.DMA
    block = parts.shape[1:]
    vmem = pl.BlockSpec(memory_space=pltpu.VMEM)
    return pl.pallas_call(
        sum_kernel,
        out_shape=jax.ShapeDtypeStruct(block, F32),
        in_specs=[vmem],
        out_specs=vmem,
        scratch_shapes=[
            pltpu.VMEM((2,) + block, parts.dtype),
            pltpu.VMEM(block, parts.dtype),
            pltpu.VMEM(block, parts.dtype),
            dma((2, 3)),
        ],
        compiler_params=pltpu.CompilerParams(
            collective_id=ident, has_side_effects=True, vmem_limit_bytes=32 * 2**20
        ),
    )(parts)


def combine(slots, weights, half, centred):
    count = slots.shape[0]
    if not centred:
        total = slots[0]
        for at in range(1, count):
            total = total + slots[at]
        return total
    size = weights[0]
    mean = slots[0, :half] * weights[0]
    for at in range(1, count):
        size = size + weights[at]
        mean = mean + slots[at, :half] * weights[at]
    mean = mean / size
    spread = None
    for at in range(count):
        gap = slots[at, :half] - mean
        term = slots[at, half : 2 * half] + weights[at] * gap * gap
        spread = term if spread is None else spread + term
    rest = [jnp.zeros((slots.shape[1] - 2 * half, LANES), F32)] * (slots.shape[1] > 2 * half)
    return jnp.concatenate([mean, spread] + rest, 0)


def sums_kernel(images, half, centred, tiled, own, tile_sizes, sizes, total, *scratch):
    blk, batch = lax.axis_index("blk"), lax.axis_index("batch")
    slots, sems = scratch[0], scratch[1]
    peers = [(blk, batch ^ mask) for mask in range(1, images)]
    mates = [(blk ^ mask, batch) for mask in range(1, 4)] if tiled else []
    greet(peers + mates)
    if tiled:
        tile_slots, tile_sems = scratch[2], scratch[3]
        tile_slots[blk] = own[...]
        copies = [
            send(own, tile_slots.at[blk], tile_sems.at[0, at], tile_sems.at[1, at], peer)
            for at, peer in enumerate(mates)
        ]
        for copy in copies:
            copy.wait()
        slots[batch] = combine(tile_slots, tile_sizes, half, centred)
    else:
        slots[batch] = own[...]
    copies = [
        send(slots.at[batch], slots.at[batch], sems.at[0, at], sems.at[1, at], peer)
        for at, peer in enumerate(peers)
    ]
    for copy in copies:
        copy.wait()
    total[...] = combine(slots, sizes, half, centred)


def all_sums(first, second, tile_sizes, sizes, centred, tiled, ident):
    images = sizes.shape[0]
    channels = first.shape[0]
    half = channels // LANES
    rows = -(-2 * half // 8) * 8
    own = jnp.concatenate(
        [first, second, jnp.zeros(((rows - 2 * half) * LANES,), F32)]
    ).reshape(rows, LANES)
    dma = pltpu.SemaphoreType.DMA
    vmem = pl.BlockSpec(memory_space=pltpu.VMEM)
    scratch = [pltpu.VMEM((images, rows, LANES), F32), dma((2, images))]
    if tiled:
        scratch += [pltpu.VMEM((4, rows, LANES), F32), dma((2, 3))]
    total = pl.pallas_call(
        functools.partial(sums_kernel, images, half, centred, tiled),
        out_shape=jax.ShapeDtypeStruct((rows, LANES), F32),
        in_specs=[vmem] * 3,
        out_specs=vmem,
        scratch_shapes=scratch,
        compiler_params=pltpu.CompilerParams(collective_id=ident, has_side_effects=True),
    )(own, sizes if tile_sizes is None else tile_sizes, sizes)
    flat = total.reshape(-1)
    return flat[:channels], flat[channels : 2 * channels]


def silu_slope(values):
    sigmoid_value = jax.nn.sigmoid(values)
    return sigmoid_value * (1.0 + values * (1.0 - sigmoid_value))


def windows(cells, rows, cols, back):
    channels = cells.shape[1]
    padded = jnp.pad(cells.reshape(rows, cols, channels), ((1, 1), (1, 1), (0, 0)))
    taken = []
    for offset in range(9):
        row, col = offset // 3, offset % 3
        if back:
            row, col = 2 - row, 2 - col
        taken.append(padded[row : row + rows, col : col + cols].reshape(rows * cols, channels))
    return jnp.concatenate(taken, 1)


def dot(left, right):
    return jnp.dot(left, right, preferred_element_type=F32)


def dot_t(left, right):
    return jnp.einsum("pd,cd->pc", left, right, preferred_element_type=F32)


def t_dot(left, right):
    return jnp.einsum("pc,pd->cd", left, right, preferred_element_type=F32)


def on_device_any(
    nt,
    nb,
    features,
    crop_rows,
    crop_cols,
    depth_target,
    labels,
    first_weight,
    spatial_weight,
    last_weight,
    shared_weight,
    head_weights,
    message_weights,
    gate_weights,
    depth_weight,
    class_weight,
    mid_gain,
    mid_bias,
    out_gain,
    out_bias,
):
    tile_rows, cols, width = features.shape[1:]
    tile = tile_rows * cols
    rows = tile_rows * nt
    pixels = rows * cols
    tasks = head_weights.shape[0]
    mid = first_weight.shape[1]
    share = mid // nb
    slim = mid // nt
    piece = width // (nb * nt)
    wide = nb * piece
    classes = class_weight.shape[1]
    blk, batch = lax.axis_index("blk"), lax.axis_index("batch")

    image_rows = lax.dynamic_index_in_dim(crop_rows, batch, 0, False)
    image_cols = lax.dynamic_index_in_dim(crop_cols, batch, 0, False)
    row_ids = jnp.arange(rows, dtype=jnp.int32)
    col_ids = jnp.arange(cols, dtype=jnp.int32)
    inside_grid = (row_ids[:, None] < image_rows) & (col_ids[None, :] < image_cols)
    inside = inside_grid.astype(F32).reshape(pixels, 1)
    inside_tile = lax.dynamic_slice_in_dim(inside, blk * tile, tile, 0)
    sizes_flat = (crop_rows * crop_cols).astype(F32)
    valid_count = jnp.sum(sizes_flat)
    sizes = jnp.broadcast_to(sizes_flat[:, None, None], (nb, 1, LANES))
    tile_counts = jnp.sum(inside.reshape(nt, tile), 1)
    tile_sizes = jnp.broadcast_to(tile_counts[:, None, None], (nt, 1, LANES))
    image_size = jnp.maximum(jnp.sum(inside), 1.0)
    tile_size = jnp.maximum(jnp.sum(inside_tile), 1.0)

    params = jnp.concatenate(
        [
            mid_gain.reshape(-1),
            mid_bias.reshape(-1),
            out_gain,
            out_bias,
            depth_weight,
            class_weight.reshape(-1),
        ]
    )
    room = -(-params.shape[0] // (16 * LANES)) * 16 * LANES
    small = jnp.pad(params, (0, room - params.shape[0])).reshape(-1, LANES)
    full_first, smalls = gather_first(first_weight, small, nb)
    full_first = full_first.reshape(width, mid)
    smalls = smalls.reshape(nb, room)
    at = 0

    def taken(count):
        nonlocal at
        found = smalls[:, at : at + count]
        at += count
        return found

    norms = mid_gain.shape[0]
    gain_mid = taken(norms * share).reshape(nb, norms, share).swapaxes(0, 1)
    gain_mid = gain_mid.reshape(norms, mid).astype(F32)
    bias_mid = taken(norms * share).reshape(nb, norms, share).swapaxes(0, 1)
    bias_mid = bias_mid.reshape(norms, mid).astype(F32)
    gain_out = lax.dynamic_index_in_dim(taken(nt * piece).reshape(nb, nt, piece), blk, 1, False)
    gain_out = gain_out.reshape(wide).astype(F32)
    bias_out = lax.dynamic_index_in_dim(taken(nt * piece).reshape(nb, nt, piece), blk, 1, False)
    bias_out = bias_out.reshape(wide).astype(F32)
    full_depth = taken(share).reshape(mid, 1)
    full_classes = taken(share * classes).reshape(mid, classes)
    stream_weight = jnp.concatenate([full_depth, full_classes], 1)

    spatial = lax.all_gather(
        lax.dynamic_slice_in_dim(spatial_weight, blk * slim, slim, 2), "batch", axis=1, tiled=True
    )
    last = lax.dynamic_index_in_dim(last_weight.reshape(share, nb, nt, piece), blk, 2, False)
    last = lax.all_gather(last.reshape(share, wide), "batch", axis=0, tiled=True)
    shared = lax.dynamic_slice_in_dim(shared_weight, blk * piece, piece, 0)
    shared = lax.all_gather(shared, "batch", axis=0, tiled=True)
    head = lax.all_gather(
        lax.dynamic_index_in_dim(head_weights, blk, 0, False), "batch", axis=1, tiled=True
    )
    message = lax.all_gather(
        lax.dynamic_index_in_dim(message_weights, blk, 0, False), "batch", axis=1, tiled=True
    )
    gate = lax.all_gather(
        lax.dynamic_index_in_dim(gate_weights, blk, 0, False), "batch", axis=0, tiled=True
    )

    flat_features = features.reshape(tile, width)
    cut = flat_features.reshape(tile, nb, nt, piece).transpose(2, 0, 1, 3).reshape(nt, tile, wide)
    wide_features = swap_tiles(cut, blk, nt)

    def slim_of(vector):
        return lax.dynamic_slice_in_dim(vector, blk * slim, slim, 0)

    def normalize(values, mask, local_size, gain, bias, tiled, ident):
        mean = jnp.sum(values * mask, 0) / local_size
        gap = values - mean
        spread = jnp.sum(gap * gap * mask, 0)
        centre, total = all_sums(mean, spread, tile_sizes, sizes, True, tiled, ident)
        inverse = lax.rsqrt(total / valid_count + EPSILON)
        normed = (values - centre) * inverse
        return normed * gain + bias, normed, inverse

    def normalize_back(grad, normed, inverse, gain, mask, tiled, ident):
        bias_sum, gain_sum = all_sums(
            jnp.sum(grad, 0), jnp.sum(grad * normed, 0), tile_sizes, sizes, False, tiled, ident
        )
        back = (
            inverse * gain * (grad - bias_sum / valid_count - normed * gain_sum / valid_count) * mask
        )
        return back.astype(BF16), gain_sum, bias_sum

    def act(values, mask):
        return (jax.nn.silu(values) * mask).astype(BF16)

    def by_rows(blocks):
        return blocks.reshape(pixels, blocks.shape[2])

    def by_channels(blocks):
        return blocks.swapaxes(0, 1).reshape(pixels, nt * blocks.shape[2])

    def cut_channels(values):
        return values.astype(BF16).reshape(pixels, nt, slim).swapaxes(0, 1)

    pre_one = dot(flat_features, full_first)
    norm_one, normed_one, inverse_one = normalize(
        pre_one, inside_tile, tile_size, gain_mid[0], bias_mid[0], True, 1
    )
    act_one = by_rows(gather_tiles(act(norm_one, inside_tile), 2))
    pre_two = dot(windows(act_one, rows, cols, False), spatial.reshape(9 * mid, slim))
    gain_two, bias_two = slim_of(gain_mid[1]), slim_of(bias_mid[1])
    norm_two, normed_two, inverse_two = normalize(
        pre_two, inside, image_size, gain_two, bias_two, False, 3
    )
    act_two = by_channels(gather_tiles(act(norm_two, inside), 4))
    pre_three = dot(act_two, last)
    norm_three, normed_three, inverse_three = normalize(
        pre_three, inside, image_size, gain_out, bias_out, False, 5
    )
    joined = norm_three + wide_features.astype(F32)
    act_three = act(joined, inside)
    pre_four = sum_tiles(cut_channels(dot(act_three, shared)), 6)
    gain_four, bias_four = slim_of(gain_mid[2]), slim_of(bias_mid[2])
    norm_four, normed_four, inverse_four = normalize(
        pre_four, inside, image_size, gain_four, bias_four, False, 3
    )
    shared_act = by_channels(gather_tiles(act(norm_four, inside), 4))

    gain_task = lax.dynamic_index_in_dim(gain_mid, 3 + blk, 0, False)
    bias_task = lax.dynamic_index_in_dim(bias_mid, 3 + blk, 0, False)
    pre_five = dot(windows(shared_act, rows, cols, False), head.reshape(9 * mid, mid))
    norm_five, normed_five, inverse_five = normalize(
        pre_five, inside, image_size, gain_task, bias_task, False, 5
    )
    task_act = act(norm_five, inside)
    messages = dot(windows(task_act, rows, cols, False), message.reshape(9 * mid, mid))
    gate_open = jax.nn.sigmoid(dot(task_act, gate))
    gated = (gate_open * messages).astype(BF16)
    is_first, is_last = blk == 0, blk == tasks - 1
    depth_part = jnp.where(is_first, task_act, gated)
    sem_part = jnp.where(is_last, task_act, gated)
    depth_share = jnp.einsum("pc,co->op", depth_part, full_depth, preferred_element_type=F32)
    class_share = jnp.einsum("pc,co->op", sem_part, full_classes, preferred_element_type=F32)
    lift = -(-(1 + classes) // 8) * 8 - 1 - classes
    shares = jnp.concatenate([depth_share, class_share, jnp.zeros((lift, pixels), F32)], 0)
    streams = jnp.sum(gather_tiles(shares, 7), 0).T
    depth_out = lax.dynamic_slice_in_dim(streams, blk * tile, tile, 0)[:, 0]
    logits = lax.dynamic_slice_in_dim(streams, blk * tile, tile, 0)[:, 1 : 1 + classes]
    targets = by_rows(gather_tiles_pair(depth_target, labels, tile))
    all_depth, all_logits = streams[:, :1], streams[:, 1 : 1 + classes]
    depth_slope = ((all_depth - targets[:, :1]) * inside).astype(BF16)
    onehot = (targets[:, 1:2] == jnp.arange(classes, dtype=jnp.int32)[None, :].astype(F32)).astype(F32)
    logit_slope = ((jax.nn.softmax(all_logits, axis=1) - onehot) * inside).astype(BF16)
    grad_depth = t_dot(depth_part, depth_slope)
    grad_classes = t_dot(sem_part, logit_slope)
    depth_back = depth_slope.astype(F32) * full_depth.astype(F32).reshape(1, mid)
    sem_back = dot_t(logit_slope, full_classes)
    zero = jnp.zeros((), F32)
    grad_gated = jnp.where(is_first, zero, depth_back) + jnp.where(is_last, zero, sem_back)
    grad_direct = jnp.where(is_first, depth_back, zero) + jnp.where(is_last, sem_back, zero)

    grad_msg = (grad_gated * gate_open).astype(BF16)
    grad_gate = (grad_gated * messages * gate_open * (1.0 - gate_open)).astype(BF16)
    msg_windows = windows(grad_msg, rows, cols, True)
    gate_grads = t_dot(task_act, grad_gate).astype(BF16)
    message_grads = t_dot(task_act, msg_windows).astype(BF16)
    share_messages = lax.psum_scatter(message_grads, "batch", scatter_dimension=0, tiled=True)
    task_grad = (
        grad_direct
        + dot_t(grad_gate, gate)
        + dot(msg_windows, message.swapaxes(1, 2).reshape(9 * mid, mid))
    )
    grad_norm_five = task_grad * inside * silu_slope(norm_five)
    grad_pre_five, gain_sum_five, bias_sum_five = normalize_back(
        grad_norm_five, normed_five, inverse_five, gain_task, inside, False, 8
    )
    five_windows = windows(grad_pre_five, rows, cols, True)
    head_grads = t_dot(shared_act, five_windows).astype(BF16)
    share_heads = lax.psum_scatter(head_grads, "batch", scatter_dimension=0, tiled=True)
    shared_back = dot(five_windows, head.swapaxes(1, 2).reshape(9 * mid, mid))
    shared_back = sum_tiles(cut_channels(shared_back), 6)

    grad_norm_four = shared_back * inside * silu_slope(norm_four)
    grad_pre_four, gain_sum_four, bias_sum_four = normalize_back(
        grad_norm_four, normed_four, inverse_four, gain_four, inside, False, 9
    )
    grad_four = by_channels(gather_tiles(grad_pre_four, 4))
    shared_grads = t_dot(act_three, grad_four).astype(BF16)
    grad_joined = dot_t(grad_four, shared) * inside * silu_slope(joined)
    grad_three, gain_sum_three, bias_sum_three = normalize_back(
        grad_joined, normed_three, inverse_three, gain_out, inside, False, 8
    )
    last_grads = t_dot(act_two, grad_three).astype(BF16)
    two_back = sum_tiles(cut_channels(dot_t(grad_three, last)), 6)
    grad_norm_two = two_back * inside * silu_slope(norm_two)
    grad_two, gain_sum_two, bias_sum_two = normalize_back(
        grad_norm_two, normed_two, inverse_two, gain_two, inside, False, 9
    )
    two_windows = windows(grad_two, rows, cols, True)
    spatial_grads = t_dot(act_one, two_windows).astype(BF16)
    one_back = dot(two_windows, spatial.swapaxes(1, 2).reshape(9 * slim, mid))
    one_back = sum_tiles(one_back.astype(BF16).reshape(nt, tile, mid), 10)
    grad_norm_one = one_back * inside_tile * silu_slope(norm_one)
    grad_one, gain_sum_one, bias_sum_one = normalize_back(
        grad_norm_one, normed_one, inverse_one, gain_mid[0], inside_tile, True, 11
    )
    all_one = by_rows(gather_tiles(grad_one, 2))
    first_grads = t_dot(wide_features, all_one).astype(BF16)
    joined_tiles = swap_tiles(grad_joined.astype(BF16).reshape(nt, tile, wide), blk, nt)
    joined_tiles = joined_tiles.reshape(nt, tile, nb, piece).transpose(1, 2, 0, 3).reshape(tile, width)
    grad_input = dot_t(grad_one, full_first) + joined_tiles.astype(F32)

    stream_grads = jnp.concatenate([grad_depth, grad_classes], 1)
    stream_grads = jnp.pad(stream_grads, ((0, 0), (0, LANES - 1 - classes))).astype(BF16)
    late = jnp.concatenate(
        [spatial_grads, shared_grads.reshape(nb, piece, mid).reshape(mid, -1),
         last_grads, first_grads.reshape(mid, -1), gate_grads, stream_grads],
        1,
    )
    late_share = lax.psum_scatter(late, "batch", scatter_dimension=0, tiled=True)
    early_share = jnp.concatenate([share_messages, share_heads], 1)
    early = lax.all_gather(early_share, "blk", axis=0, tiled=False).astype(F32)
    late_all = gather_tiles(late_share, 12).astype(F32)
    early = early.reshape(nt, share, 2, 9, mid).transpose(2, 0, 3, 1, 4)
    red_messages, red_heads = early[0], early[1]
    at = 0

    def part(count):
        nonlocal at
        found = late_all[:, :, at : at + count]
        at += count
        return found

    red_spatial = part(9 * slim).reshape(nt, share, 9, slim).transpose(2, 1, 0, 3).reshape(9, share, mid)
    red_shared = part(wide * mid // mid).reshape(nt * piece, mid)
    red_last = part(wide).reshape(nt, share, nb, piece).transpose(1, 2, 0, 3).reshape(share, width)
    red_first = part(wide * mid // mid).reshape(nt * piece, mid)
    red_gates = part(mid)
    streams_red = jnp.sum(part(LANES), 0)
    red_depth = streams_red[:, 0]
    red_classes = streams_red[:, 1 : 1 + classes]

    sums = jnp.concatenate(
        [
            gain_sum_five,
            bias_sum_five,
            gain_sum_three,
            bias_sum_three,
            gain_sum_two,
            bias_sum_two,
            gain_sum_four,
            bias_sum_four,
        ]
    ).reshape(-1, LANES)
    sums = jnp.pad(sums, ((0, -sums.shape[0] % 8), (0, 0)))
    sums = gather_tiles(sums, 13).reshape(nt, -1)
    five_gain, five_bias = sums[:, :mid], sums[:, mid : 2 * mid]
    at_out = 2 * mid
    three_gain = sums[:, at_out : at_out + wide].reshape(nt, nb, piece)
    three_bias = sums[:, at_out + wide : at_out + 2 * wide].reshape(nt, nb, piece)
    at_slim = at_out + 2 * wide
    slims = [
        sums[:, at_slim + i * slim : at_slim + (i + 1) * slim].reshape(1, mid) for i in range(4)
    ]
    mid_gains = jnp.concatenate([gain_sum_one[None], slims[0], slims[2], five_gain], 0)
    mid_biases = jnp.concatenate([bias_sum_one[None], slims[1], slims[3], five_bias], 0)
    grad_mid_gain = lax.dynamic_slice_in_dim(mid_gains, batch * share, share, 1)
    grad_mid_bias = lax.dynamic_slice_in_dim(mid_biases, batch * share, share, 1)
    grad_out_gain = lax.dynamic_index_in_dim(three_gain, batch, 1, False).reshape(nt * piece)
    grad_out_bias = lax.dynamic_index_in_dim(three_bias, batch, 1, False).reshape(nt * piece)
    return (
        depth_out.reshape(1, tile_rows, cols),
        logits.reshape(1, tile_rows, cols, classes),
        grad_input.reshape(1, tile_rows, cols, width),
        red_first,
        red_spatial,
        red_last,
        red_shared,
        red_heads,
        red_messages,
        red_gates,
        red_depth,
        red_classes,
        grad_mid_gain,
        grad_mid_bias,
        grad_out_gain,
        grad_out_bias,
    )


def swap_tiles(blocks, blk, nt):
    out = jnp.zeros_like(blocks)
    out = lax.dynamic_update_index_in_dim(
        out, lax.dynamic_index_in_dim(blocks, blk, 0, False), blk, 0
    )
    for mask in range(1, nt):
        sent = lax.dynamic_index_in_dim(blocks, blk ^ mask, 0, False)
        came = lax.ppermute(sent, "blk", [(i, i ^ mask) for i in range(nt)])
        out = lax.dynamic_update_index_in_dim(out, came, blk ^ mask, 0)
    return out.reshape(-1, blocks.shape[2])


def gather_tiles_pair(depth_target, labels, tile):
    pair = jnp.stack([depth_target.reshape(tile), labels.reshape(tile).astype(F32)], 0)
    pair = jnp.pad(pair, ((0, 6), (0, 0)))
    return gather_tiles(pair, 14).swapaxes(1, 2)


PITCH = 48
CHUNK = 64
BLOCK = 256
ANY = pl.BlockSpec(memory_space=pl.ANY)
VMEM = pl.BlockSpec(memory_space=pltpu.VMEM)
DMA = pltpu.SemaphoreType.DMA
LONG = pl.CostEstimate(flops=80_000_000_000, bytes_accessed=30_000_000, transcendentals=2_000_000)


class Mail:
    def __init__(self, sems):
        self.sems, self.used, self.open = sems, 0, []

    def send(self, src, dst, peer, keep=True):
        copy = send(src, dst, self.sems.at[0, self.used], self.sems.at[1, self.used], peer)
        self.used += 1
        if keep:
            self.open.append(copy.wait_send)
        return copy

    def local(self, src, dst):
        copy = pltpu.make_async_copy(src, dst, self.sems.at[0, self.used])
        copy.start()
        self.used += 1
        return copy

    def close(self):
        for wait in self.open:
            wait()
        self.open = []


class Place:
    def __init__(self, images):
        self.blk, self.batch = lax.axis_index("blk"), lax.axis_index("batch")
        self.images = images
        self.mate = (self.blk ^ 1, self.batch)
        self.across = (self.blk ^ 2, self.batch)
        self.tiles = [(self.blk ^ mask, self.batch) for mask in range(1, 4)]
        self.others = [(self.blk, self.batch ^ mask) for mask in range(1, images)]
        self.side = (self.blk, self.batch ^ 1)


class Spread:
    def __init__(self, mail, place, own, slot):
        self.mail, self.place, self.own, self.slot = mail, place, own, slot
        self.z_copies, self.x_copies = [], []

    def start(self):
        place, here = self.place, self.slot(self.place.batch)
        self.here = self.mail.local(self.own, here)
        for mask in range(1, place.images // 2):
            peer = (place.blk, place.batch ^ (2 * mask))
            self.z_copies.append(self.mail.send(self.own, here, peer))
        self.x_copies.append(self.mail.send(self.own, here, place.side))
        return self

    def forward(self):
        for mask, copy in enumerate(self.z_copies, 1):
            copy.wait_recv()
            block = self.slot(self.place.batch ^ (2 * mask))
            self.x_copies.append(self.mail.send(block, block, self.place.side))

    def finish(self):
        self.here.wait()
        for copy in self.x_copies:
            copy.wait_recv()


def share_tiles(mail, place, slot):
    own = slot(place.blk)
    far = mail.send(own, own, place.across, False)
    near = mail.send(own, own, place.mate, False)
    far.wait_recv()
    passed = slot(place.blk ^ 2)
    last = mail.send(passed, passed, place.mate, False)
    near.wait()
    last.wait()
    far.wait_send()


def loop(total, step, body):
    def run(at, carry):
        body(pl.ds(pl.multiple_of(at * step, step), step))
        return carry

    lax.fori_loop(0, total // step, run, 0)


def folded(values):
    return jnp.sum(values.reshape(values.shape[0] // 8, 8, values.shape[1]), 0)


def loop_sums(total, channels, count, body):
    def run(at, carry):
        found = body(pl.ds(pl.multiple_of(at * CHUNK, CHUNK), CHUNK))
        return tuple(kept + folded(one) for kept, one in zip(carry, found))

    start = tuple(jnp.zeros((8, channels), F32) for _ in range(count))
    return [jnp.sum(one, 0, keepdims=True) for one in lax.fori_loop(0, total // CHUNK, run, start)]


def merge(slots, sizes, channels):
    count = slots.shape[0]
    size, mean = None, None
    for at in range(count):
        weight = sizes[at, :, :channels]
        term = slots[at, 0:1, :] * weight
        size = weight if size is None else size + weight
        mean = term if mean is None else mean + term
    mean = mean / size
    spread = None
    for at in range(count):
        gap = slots[at, 0:1, :] - mean
        term = slots[at, 1:2, :] + sizes[at, :, :channels] * gap * gap
        spread = term if spread is None else spread + term
    return mean, spread, size


def add_up(slots):
    total = slots[0]
    for at in range(1, slots.shape[0]):
        total = total + slots[at]
    return total[0:1, :], total[1:2, :]


def swap_sums(mail, place, slots, meanwhile=None):
    own = slots.at[place.batch]
    copies = [mail.send(own, own, peer) for peer in place.others]
    if meanwhile is not None:
        meanwhile()
    for copy in copies:
        copy.wait_recv()


def swap_tile_sums(mail, place, slots):
    own = slots.at[place.blk]
    copies = [mail.send(own, own, peer) for peer in place.tiles]
    for copy in copies:
        copy.wait_recv()


def local_stats(pre, mask, base, total, channels, size):
    def first(rows):
        return (pre[rows, :] * mask[at_base(base, rows), :],)

    (summed,) = loop_sums(total, channels, 1, first)
    mean = summed / jnp.maximum(size, 1.0)

    def second(rows):
        gap = pre[rows, :] - mean
        return (gap * gap * mask[at_base(base, rows), :],)

    (spread,) = loop_sums(total, channels, 1, second)
    return mean, spread


def at_base(base, rows):
    if base is None:
        return rows
    return pl.ds(pl.multiple_of(base + rows.start, CHUNK), rows.size)


def batch_norm_stats(mail, place, pre, mask, slots, sizes, stats, row, channels, meanwhile=None):
    total = pre.shape[0]
    mean, spread = local_stats(pre, mask, None, total, channels, sizes[place.batch, :, :channels])
    slots[place.batch] = jnp.concatenate([mean, spread], 0)
    swap_sums(mail, place, slots, meanwhile)
    keep_stats(slots, sizes, stats, row, channels)


def keep_stats(slots, sizes, stats, row, channels):
    mean, spread, size = merge(slots, sizes, channels)
    stats[row : row + 1, :channels] = mean
    stats[row + 1 : row + 2, :channels] = lax.rsqrt(spread / size + EPSILON)


def silu(values):
    return values * jax.nn.sigmoid(values)


def widen(cells, left, right, total):
    def body(rows):
        seen = cells[pl.ds(pl.multiple_of(rows.start + PITCH - 16, 16), CHUNK + 32), :].astype(F32)
        here = pl.ds(pl.multiple_of(rows.start + PITCH, 16), CHUNK)
        left[here, :] = seen[15 : 15 + CHUNK].astype(BF16)
        right[here, :] = seen[17 : 17 + CHUNK].astype(BF16)

    loop(total, CHUNK, body)


def clear_ends(cells, total):
    zeros = jnp.zeros((PITCH, cells.shape[1]), cells.dtype)
    cells[0:PITCH, :] = zeros
    cells[PITCH + total : 2 * PITCH + total, :] = zeros


def conv_rows(shifted, rows, weight, back):
    total = None
    for offset in range(9):
        row, col = offset // 3, offset % 3
        if back:
            row, col = 2 - row, 2 - col
        window = shifted[col][pl.ds(pl.multiple_of(rows.start + PITCH * row, 16), rows.size), :]
        product = weight(offset, window)
        total = product if total is None else total + product
    return total


def sum_over_tiles(mail, place, part, near_in, pair, far_in, total, out, meanwhile=None):
    far_first = mail.send(part(place.blk ^ 3), near_in.at[0], place.mate)
    near_next = mail.send(part(place.blk ^ 1), near_in.at[1], place.mate)
    far_first.wait_recv()
    mine_far, mine = part(place.blk ^ 2), part(place.blk)

    def pairs(rows):
        pair[rows, :] = (mine_far[rows, :].astype(F32) + near_in[0, rows, :].astype(F32)).astype(BF16)

    loop(total, CHUNK, pairs)
    far = mail.send(pair, far_in, place.across)
    if meanwhile is not None:
        meanwhile()
    near_next.wait_recv()
    far.wait_recv()

    def finish(rows):
        out[rows, :] = (
            mine[rows, :].astype(F32) + near_in[1, rows, :].astype(F32) + far_in[rows, :].astype(F32)
        )

    loop(total, CHUNK, finish)


def start_kernel(
    images,
    weight,
    small,
    spatial_own,
    pair,
    feat,
    mask,
    sizes,
    tile_sizes,
    full,
    smalls,
    targets,
    wide,
    spatial,
    pre_one,
    stats,
    slots_tile,
    slots_one,
    sems,
):
    place = Place(images)
    mail = Mail(sems)
    blk, batch = place.blk, place.batch
    depth = weight.shape[0]
    half = depth // 2
    mid = weight.shape[1]
    tile = feat.shape[0]
    slim = mid // 4
    share = spatial_own.shape[1]
    mine = pl.ds(pl.multiple_of(lax.rem(blk, 2) * half, half), half)
    greet(place.others + place.tiles)
    here = mail.local(weight, full.at[batch])
    here_small = mail.local(small, smalls.at[batch])
    z_copies, x_copies, arrived, late = {}, [], [], []
    for peer in place.others:
        late.append(mail.send(small, smalls.at[batch], peer))
    for mask_z in range(1, images // 2):
        z_copies[mask_z] = mail.send(
            weight.at[mine], full.at[batch, mine], (blk, batch ^ (2 * mask_z))
        )
    x_copies.append(mail.send(weight.at[mine], full.at[batch, mine], place.side))
    lanes = pl.ds(pl.multiple_of(blk * slim, slim), slim)
    got_spatial = Spread(
        mail,
        place,
        spatial_own.at[:, :, lanes],
        lambda index: spatial.at[:, pl.ds(pl.multiple_of(index * share, share), share), :],
    ).start()

    def columns(index):
        return feat.at[:, pl.ds(pl.multiple_of(index * mid, mid), mid)]

    landing = wide.at[pl.ds(pl.multiple_of(blk * tile, tile), tile), :]
    here_wide = mail.local(columns(blk), landing)
    line = targets.at[:, pl.ds(pl.multiple_of(blk * tile, tile), tile)]
    here_line = mail.local(pair, line)
    for mask_t in range(1, 4):
        late.append(mail.send(pair, line, (blk ^ mask_t, batch)))
        late.append(mail.send(columns(blk ^ mask_t), landing, (blk ^ mask_t, batch)))

    def hand_over(source):
        block = full.at[source, mine]
        arrived.append(mail.send(block, block, place.mate))

    for mask_z in range(1, images // 2):
        z_copies[mask_z].wait_recv()
        source = batch ^ (2 * mask_z)
        block = full.at[source, mine]
        x_copies.append(mail.send(block, block, place.side))
        hand_over(source)
    for mask_z in range(images // 2):
        x_copies[mask_z].wait_recv()
        hand_over(batch ^ (2 * mask_z + 1))
    stats[...] = jnp.zeros_like(stats)
    here.wait()
    for copy in arrived:
        copy.wait_recv()

    def reduce(rows):
        total = None
        for index in range(images):
            product = dot(feat[rows, index * depth : (index + 1) * depth], full[index])
            total = product if total is None else total + product
        pre_one[rows, :] = total

    loop(tile, tile // 2, reduce)
    base = blk * tile
    mean, spread = local_stats(pre_one, mask, base, tile, mid, tile_sizes[blk, :, :])
    slots_tile[blk] = jnp.concatenate([mean, spread], 0)
    swap_tile_sums(mail, place, slots_tile)
    mean, spread, _ = merge(slots_tile, tile_sizes, mid)
    slots_one[batch] = jnp.concatenate([mean, spread], 0)
    swap_sums(mail, place, slots_one, got_spatial.forward)
    keep_stats(slots_one, sizes, stats, 0, mid)
    got_spatial.finish()
    for copy in late:
        copy.wait_recv()
    here_small.wait()
    here_wide.wait()
    here_line.wait()
    mail.close()


def begin(nb, weight, small, spatial, pair, feat, mask, sizes, tile_sizes):
    depth, mid = weight.shape
    tile = feat.shape[0]

    def array(*shape, kind=BF16):
        return jax.ShapeDtypeStruct(shape, kind)

    return pl.pallas_call(
        functools.partial(start_kernel, nb),
        out_shape=(
            array(nb, depth, mid),
            array(nb, *small.shape),
            array(8, 4 * tile, kind=F32),
            array(4 * tile, mid),
            array(9, mid, mid // 4),
            array(tile, mid, kind=F32),
            array(8, mid, kind=F32),
        ),
        in_specs=[ANY] * 4 + [VMEM] * 4,
        out_specs=(VMEM, ANY, ANY, VMEM, VMEM, VMEM, VMEM),
        scratch_shapes=[
            pltpu.VMEM((4, 2, mid), F32),
            pltpu.VMEM((nb, 2, mid), F32),
            DMA((2, 64)),
        ],
        cost_estimate=LONG,
        compiler_params=pltpu.CompilerParams(
            collective_id=21, has_side_effects=True, vmem_limit_bytes=40 * 2**20
        ),
    )(weight, small, spatial, pair, feat, mask, sizes, tile_sizes)


def forward_kernel(
    images,
    early,
    pre_one,
    first_stats,
    spatial,
    wide,
    mask,
    norms,
    sizes,
    last_own,
    shared_own,
    gate_own,
    message_own,
    last,
    shared,
    gate,
    message,
    act_one,
    act_two,
    act_three,
    shared_act,
    pre_two,
    pre_three,
    pre_four,
    stats,
    one_left,
    one_right,
    parts,
    near_in,
    pair,
    far_in,
    slots_two,
    slots_three,
    slots_four,
    sems,
):
    place = Place(images)
    mail = Mail(sems)
    blk, batch = place.blk, place.batch
    tile, total = pre_one.shape[0], mask.shape[0]
    mid = pre_one.shape[1]
    slim = pre_two.shape[1]
    share = last_own.shape[0]
    base = blk * tile
    greet(place.others + place.tiles)

    def rows_of(index):
        return pl.ds(pl.multiple_of(index * share, share), share)

    def slim_lanes(index):
        return pl.ds(pl.multiple_of(index * slim, slim), slim)

    lanes = slim_lanes(blk)
    wide_lanes = pl.ds(pl.multiple_of(blk * mid, mid), mid)
    got_last = Spread(mail, place, last_own.at[:, wide_lanes], lambda index: last.at[rows_of(index), :])
    got_shared = Spread(mail, place, shared_own, lambda index: shared.at[rows_of(index), :])
    got_gate = Spread(mail, place, gate_own.at[blk], lambda index: gate.at[rows_of(index), :])
    got_message = [
        Spread(
            mail,
            place,
            message_own.at[blk, offset],
            lambda index, offset=offset: message.at[offset, rows_of(index), :],
        )
        for offset in range(early)
    ]
    got_last.start()
    got_shared.start()
    stats[...] = first_stats[...]
    clear_ends(act_one, total)
    clear_ends(shared_act, total)
    clear_ends(one_left, total)
    clear_ends(one_right, total)

    def act_first(rows):
        value = (pre_one[rows, :] - stats[0:1, :]) * stats[1:2, :] * norms[0:1, :] + norms[1:2, :]
        value = silu(value) * mask[at_base(base, rows), :]
        act_one[pl.ds(pl.multiple_of(PITCH + base + rows.start, 16), CHUNK), :] = value.astype(BF16)

    loop(tile, CHUNK, act_first)
    share_tiles(
        mail, place, lambda index: act_one.at[pl.ds(pl.multiple_of(PITCH + index * tile, 16), tile), :]
    )
    widen(act_one, one_left, one_right, total)
    got_last.forward()
    got_shared.forward()

    shifted = (one_left, act_one, one_right)

    def conv_two(rows):
        pre_two[rows, :] = conv_rows(
            shifted, rows, lambda offset, window: dot(window, spatial[offset]), False
        )

    loop(total, BLOCK, conv_two)

    def after_two():
        got_gate.start()
        got_message[0].start()
        got_message[1].start()

    batch_norm_stats(mail, place, pre_two, mask, slots_two, sizes, stats, 2, slim, after_two)

    def act_second(rows):
        value = (pre_two[rows, :] - stats[2:3, :slim]) * stats[3:4, :slim]
        value = silu(value * norms[2:3, :slim] + norms[3:4, :slim]) * mask[rows, :]
        act_two[rows, lanes] = value.astype(BF16)

    loop(total, CHUNK, act_second)
    share_tiles(mail, place, lambda index: act_two.at[:, slim_lanes(index)])

    got_last.finish()
    got_gate.forward()

    def expand(rows):
        pre_three[rows, :] = dot(act_two[rows, :], last[...])

    loop(total, BLOCK, expand)

    def after_three():
        got_message[0].forward()
        got_message[1].forward()
        got_message[2].start()
        got_message[3].start()

    batch_norm_stats(mail, place, pre_three, mask, slots_three, sizes, stats, 4, mid, after_three)
    got_shared.finish()

    def act_third(rows):
        normed = (pre_three[rows, :] - stats[4:5, :]) * stats[5:6, :]
        value = normed * norms[4:5, :] + norms[5:6, :] + wide[rows, :].astype(F32)
        act_three[rows, :] = (silu(value) * mask[rows, :]).astype(BF16)

    loop(total, CHUNK, act_third)

    def reduce(rows):
        parts[rows, :] = dot(act_three[rows, :], shared[...]).astype(BF16)

    loop(total, BLOCK, reduce)
    sum_over_tiles(
        mail,
        place,
        lambda index: parts.at[:, slim_lanes(index)],
        near_in,
        pair,
        far_in,
        total,
        pre_four,
    )

    def after_four():
        got_message[2].forward()
        got_message[3].forward()
        for later in got_message[4:]:
            later.start()

    batch_norm_stats(mail, place, pre_four, mask, slots_four, sizes, stats, 6, slim, after_four)

    def act_fourth(rows):
        value = (pre_four[rows, :] - stats[6:7, :slim]) * stats[7:8, :slim]
        value = silu(value * norms[6:7, :slim] + norms[7:8, :slim]) * mask[rows, :]
        shared_act[pl.ds(pl.multiple_of(PITCH + rows.start, 16), CHUNK), lanes] = value.astype(BF16)

    loop(total, CHUNK, act_fourth)
    share_tiles(
        mail, place, lambda index: shared_act.at[pl.ds(PITCH, total), slim_lanes(index)]
    )
    for later in got_message[4:]:
        later.forward()
    got_gate.finish()
    for one in got_message:
        one.finish()
    mail.close()


def bottleneck(nb, early, pre_one, stats, spatial, wide, mask, norms, sizes, last, shared, gate, message):
    tile, total = pre_one.shape[0], mask.shape[0]
    mid = pre_one.shape[1]
    slim = mid // 4
    padded = total + 2 * PITCH

    def array(*shape, kind=BF16):
        return jax.ShapeDtypeStruct(shape, kind)

    outs = (
        array(mid, mid),
        array(mid, mid),
        array(mid, mid),
        array(early, mid, mid),
        array(padded, mid),
        array(total, mid),
        array(total, mid),
        array(padded, mid),
        array(total, slim, kind=F32),
        array(total, mid, kind=F32),
        array(total, slim, kind=F32),
        array(8, mid, kind=F32),
    )
    return pl.pallas_call(
        functools.partial(forward_kernel, nb, early),
        out_shape=outs,
        in_specs=[VMEM] * 7 + [ANY] * 4,
        out_specs=(VMEM, VMEM, ANY, ANY) + (VMEM,) * 8,
        scratch_shapes=[
            pltpu.VMEM((padded, mid), BF16),
            pltpu.VMEM((padded, mid), BF16),
            pltpu.VMEM((total, mid), BF16),
            pltpu.VMEM((2, total, slim), BF16),
            pltpu.VMEM((total, slim), BF16),
            pltpu.VMEM((total, slim), BF16),
            pltpu.VMEM((nb, 2, slim), F32),
            pltpu.VMEM((nb, 2, mid), F32),
            pltpu.VMEM((nb, 2, slim), F32),
            DMA((2, 128)),
        ],
        cost_estimate=LONG,
        compiler_params=pltpu.CompilerParams(
            collective_id=20, has_side_effects=True, vmem_limit_bytes=60 * 2**20
        ),
    )(pre_one, stats, spatial, wide, mask, norms, sizes, last, shared, gate, message)


class Tiles:
    def __init__(self, mail, place, slot, own=None):
        self.mail, self.place, self.slot, self.own = mail, place, slot, own

    def start(self):
        own, here = self.own, self.slot(self.place.blk)
        if own is None:
            own = here
        else:
            self.mail.open.append(self.mail.local(own, here).wait)
        self.far = self.mail.send(own, here, self.place.across)
        self.near = self.mail.send(own, here, self.place.mate)

    def forward(self):
        self.far.wait_recv()
        passed = self.slot(self.place.blk ^ 2)
        self.last = self.mail.send(passed, passed, self.place.mate)

    def end(self):
        self.near.wait_recv()
        self.last.wait_recv()


class Reduce:
    def __init__(self, mail, place, grad, from_side, summed, from_line, out):
        self.mail, self.place = mail, place
        self.grad, self.from_side, self.summed = grad, from_side, summed
        self.from_line, self.out = from_line, out
        self.side = lax.rem(place.batch, 2)
        self.line = lax.div(place.batch, 2)

    def start(self):
        self.from_x = self.mail.send(self.grad.at[:, 1 - self.side], self.from_side, self.place.side)

    def own_half(self, at):
        return self.grad[at, self.side]

    def add_side(self):
        self.from_x.wait_recv()
        lines = self.from_side.shape[0]
        for at in range(lines):
            self.summed[at] = (self.own_half(at).astype(F32) + self.from_side[at].astype(F32)).astype(BF16)

    def middle(self):
        self.add_side()
        self.send_lines()

    def send_lines(self):
        place = self.place
        lines = self.summed.shape[0]
        self.copies = [
            self.mail.send(
                self.summed.at[self.line ^ mask],
                self.from_line.at[mask - 1],
                (place.blk, place.batch ^ (2 * mask)),
            )
            for mask in range(1, lines)
        ]

    def finish(self):
        total = self.summed[self.line].astype(F32)
        for at, copy in enumerate(self.copies):
            copy.wait_recv()
            total = total + self.from_line[at].astype(F32)
        self.out[...] = total.astype(BF16)


class ReduceFar(Reduce):
    def start(self):
        super().start()
        self.fetch = self.mail.local(self.grad.at[:, self.side], self.summed)

    def own_half(self, at):
        if at == 0:
            self.fetch.wait()
        return self.summed[at]


class Owners:
    def __init__(self, mail, place, result, slots):
        self.mail, self.place, self.result, self.slots = mail, place, result, slots
        self.base = mail.used
        mail.used += 5
        self.owner = 2 * place.blk + lax.div(place.batch, 4)
        self.quarter = lax.rem(place.batch, 4)
        self.at_home = self.owner == place.batch

    def copy(self, mask):
        place, mail = self.place, self.mail
        return pltpu.make_async_remote_copy(
            src_ref=self.result,
            dst_ref=self.slots.at[self.quarter],
            send_sem=mail.sems.at[0, self.base + mask],
            recv_sem=mail.sems.at[1, self.base + self.quarter],
            device_id=(place.blk ^ mask, self.owner),
            device_id_type=MESH,
        )

    def local(self):
        return pltpu.make_async_copy(
            self.result, self.slots.at[self.quarter], self.mail.sems.at[0, self.base + 4]
        )

    def start(self):
        for mask in range(1, 4):
            self.copy(mask).start()

        @pl.when(self.at_home)
        def _():
            self.local().start()

        @pl.when(jnp.logical_not(self.at_home))
        def _():
            self.copy(0).start()

    def forward(self):
        for mask in range(1, 4):
            self.copy(mask).wait_send()

        @pl.when(self.at_home)
        def _():
            self.local().wait()

        @pl.when(jnp.logical_not(self.at_home))
        def _():
            self.copy(0).wait_send()

    def end(self):
        place, mail = self.place, self.mail
        for quarter in range(4):
            source = 4 * lax.rem(place.batch, 2) + quarter
            at_home = (lax.div(place.batch, 2) == place.blk) & (source == place.batch)

            @pl.when(jnp.logical_not(at_home))
            def _():
                pltpu.make_async_remote_copy(
                    src_ref=self.result,
                    dst_ref=self.slots.at[quarter],
                    send_sem=mail.sems.at[0, self.base],
                    recv_sem=mail.sems.at[1, self.base + quarter],
                    device_id=place.mate,
                    device_id_type=MESH,
                ).wait_recv()


def greet_owners(place):
    barrier = pltpu.get_barrier_semaphore()
    regular = [place.mate, place.across]
    for peer in regular:
        pl.semaphore_signal(barrier, inc=1, device_id=peer, device_id_type=MESH)
    for quarter in range(4):
        source = (lax.div(place.batch, 2), 4 * lax.rem(place.batch, 2) + quarter)
        at_home = (source[0] == place.blk) & (source[1] == place.batch)

        @pl.when(jnp.logical_not(at_home))
        def _():
            pl.semaphore_signal(barrier, inc=1, device_id=source, device_id_type=MESH)

    owner = 2 * place.blk + lax.div(place.batch, 4)

    @pl.when(owner == place.batch)
    def _():
        pl.semaphore_wait(barrier, len(regular) + 3)

    @pl.when(owner != place.batch)
    def _():
        pl.semaphore_wait(barrier, len(regular) + 4)


class Job:
    def __init__(self, reduce, tiles):
        self.steps = []
        if reduce is not None:
            self.steps += [reduce.start, reduce.middle, reduce.finish]
        if tiles is not None:
            self.steps += [tiles.start, tiles.forward, tiles.end]


def step(*jobs):
    for job in jobs:
        job.steps.pop(0)()


def reduce_scratch(lines, share, columns, own):
    found = [pltpu.VMEM((lines, 2, share, columns), BF16)] if own else []
    return found + [
        pltpu.VMEM((lines, share, columns), BF16),
        pltpu.VMEM((lines, share, columns), BF16),
        pltpu.VMEM((lines - 1, share, columns), BF16),
    ]


def send_sums(mail, place, slots, sums):
    slots[place.batch] = jnp.concatenate(sums, 0)
    own = slots.at[place.batch]
    return [mail.send(own, own, peer) for peer in place.others]


def silu_back(value):
    sigmoid_value = jax.nn.sigmoid(value)
    return sigmoid_value * (1.0 + value * (1.0 - sigmoid_value))


def norm_back(stats, norms, mask, grad, pre, row, channels, lead, offset=None, skip=None):
    def body(rows):
        normed = (pre[rows, :] - stats[row : row + 1, :channels]) * stats[row + 1 : row + 2, :channels]
        value = normed * norms[row : row + 1, :channels] + norms[row + 1 : row + 2, :channels]
        if skip is not None:
            value = value + skip[rows, :].astype(F32)
        found = lead(rows) * mask[at_base(offset, rows), :] * silu_back(value)
        grad[rows, :] = found
        return found, found * normed

    return loop_sums(pre.shape[0], channels, 2, body)


def through(stats, norms, mask, sizes, grad, pre, row, channels, bias_sum, gain_sum, put, offset=None):
    count = sizes[0, :, :channels]
    for at in range(1, sizes.shape[0]):
        count = count + sizes[at, :, :channels]
    scale = stats[row + 1 : row + 2, :channels] * norms[row : row + 1, :channels]
    bias_part, gain_part = bias_sum / count, gain_sum / count

    def body(rows):
        normed = (pre[rows, :] - stats[row : row + 1, :channels]) * stats[row + 1 : row + 2, :channels]
        found = scale * (grad[rows, :] - bias_part - normed * gain_part)
        put(rows, (found * mask[at_base(offset, rows), :]).astype(BF16))

    loop(pre.shape[0], CHUNK, body)


def backward_kernel(
    images,
    back,
    pre_one,
    pre_two,
    pre_three,
    pre_four,
    stats,
    norms,
    mask,
    sizes,
    wide,
    act_one,
    act_two,
    act_three,
    spatial,
    last,
    shared,
    first,
    gate_grads,
    stream_grads,
    message_share,
    head_grads,
    task_sums,
    grad_input,
    share_shared,
    share_first,
    all_last,
    all_spatial,
    all_gates,
    all_stream,
    all_heads,
    all_messages,
    all_sums,
    near_four,
    pair_four,
    far_four,
    grad_four,
    all_four,
    grad_three,
    low_three,
    low_joined,
    joined_rows,
    near_two,
    pair_two,
    far_two,
    grad_two,
    two_left,
    two_here,
    two_right,
    turned,
    strip,
    near_one,
    pair_one,
    far_one,
    grad_one,
    all_one,
    slots_four,
    slots_three,
    slots_two,
    slots_tile,
    slots_one,
    *rest,
):
    place = Place(images)
    sems = rest[-1]
    mail = Mail(sems)
    blk, batch = place.blk, place.batch
    tile, total = pre_one.shape[0], mask.shape[0]
    mid = pre_one.shape[1]
    slim = pre_two.shape[1]
    base = blk * tile
    red_shared = Reduce(mail, place, *rest[0:4], share_shared)
    red_last = Reduce(mail, place, *rest[4:8], all_last.at[blk])
    red_first = Reduce(mail, place, *rest[8:12], share_first)
    red_spatial = Reduce(mail, place, *rest[12:16], all_spatial.at[blk])
    red_gates = Reduce(mail, place, gate_grads, *rest[16:19], all_gates.at[blk])
    red_stream = Reduce(mail, place, stream_grads, *rest[19:22], all_stream.at[blk])
    share = share_shared.shape[0]
    results, sums_out, at = rest[22], rest[23], 24
    heads, messages = [], []

    def tiles_of(slots, first_row, count, own):
        rows_at = pl.ds(first_row, count)
        return Tiles(mail, place, lambda index: slots.at[index, rows_at], own)

    def slots_of(slots):
        return Tiles(mail, place, lambda index: slots.at[index])

    for offset in range(9):
        result = results.at[offset]
        reduce = ReduceFar(mail, place, head_grads.at[offset], *rest[at : at + 3], result)
        at += 3
        heads.append(Job(reduce, tiles_of(all_heads, offset * share, share, result)))
    early = message_share.shape[0] // share
    ends = [0, early // 3, 2 * early // 3, early]
    for begin_at, end_at in zip(ends[:-1], ends[1:]):
        count = (end_at - begin_at) * share
        own = message_share.at[pl.ds(begin_at * share, count)]
        messages.append(Job(None, tiles_of(all_messages, begin_at * share, count, own)))
    job_shared, job_first = Job(red_shared, None), Job(red_first, None)
    job_sums = Job(None, Tiles(mail, place, lambda index: all_sums.at[index], sums_out))
    job_last, job_spatial = Job(red_last, slots_of(all_last)), Job(red_spatial, slots_of(all_spatial))
    job_gates, job_stream = Job(red_gates, slots_of(all_gates)), Job(red_stream, slots_of(all_stream))
    greet(place.others + place.tiles)

    def slim_lanes(index):
        return pl.ds(pl.multiple_of(index * slim, slim), slim)

    def tile_rows(index):
        return pl.ds(pl.multiple_of(index * tile, tile), tile)

    def keep(row, bias_sum, gain_sum, channels):
        sums_out[row : row + 1, :channels] = gain_sum
        sums_out[row + 1 : row + 2, :channels] = bias_sum

    sums_out[...] = jnp.zeros_like(sums_out)
    sums_out[8:10, :] = task_sums[0:2, :]
    for cells in (two_left, two_here, two_right):
        clear_ends(cells, total)
    step(heads[0], heads[1], job_gates, job_stream)

    sum_over_tiles(
        mail, place, lambda index: back.at[:, slim_lanes(index)], near_four, pair_four, far_four, total, grad_four
    )
    sums = norm_back(stats, norms, mask, grad_four, pre_four, 6, slim, lambda rows: grad_four[rows, :])
    copies = send_sums(mail, place, slots_four, sums)
    step(heads[0], heads[1], job_gates, job_stream)
    step(heads[2], heads[3], heads[4])
    for offset in range(9):
        turned[offset * slim : (offset + 1) * slim, :] = spatial[offset].T
    for copy in copies:
        copy.wait_recv()
    bias_sum, gain_sum = add_up(slots_four)
    keep(6, bias_sum, gain_sum, slim)
    lanes = slim_lanes(blk)

    def put_four(rows, value):
        all_four[rows, lanes] = value

    through(stats, norms, mask, sizes, grad_four, pre_four, 6, slim, bias_sum, gain_sum, put_four)
    share_tiles(mail, place, lambda index: all_four.at[:, slim_lanes(index)])
    step(messages[0])

    def joined_back(rows):
        return dot_t(all_four[rows, :], shared[...])

    sums = norm_back(stats, norms, mask, grad_three, pre_three, 4, mid, joined_back, None, wide)
    copies = send_sums(mail, place, slots_three, sums)
    step(heads[2], heads[3], heads[4])
    step(heads[5], heads[6])
    step(heads[0], heads[1], job_gates, job_stream)
    step(messages[0])
    grads, lines = red_shared.grad, red_shared.grad.shape[0]
    grads[...] = t_dot(act_three[...], all_four[...]).astype(BF16).reshape(grads.shape)
    step(job_shared)

    def lower(rows):
        low_joined[rows, :] = grad_three[rows, :].astype(BF16)

    loop(total, CHUNK, lower)
    for copy in copies:
        copy.wait_recv()
    bias_sum, gain_sum = add_up(slots_three)
    keep(4, bias_sum, gain_sum, mid)

    def put_three(rows, value):
        low_three[rows, :] = value

    through(stats, norms, mask, sizes, grad_three, pre_three, 4, mid, bias_sum, gain_sum, put_three)

    def two_part(rows):
        all_four[rows, :] = dot_t(low_three[rows, :], last[...]).astype(BF16)

    loop(total, BLOCK, two_part)
    sum_over_tiles(
        mail, place, lambda index: all_four.at[:, slim_lanes(index)], near_two, pair_two, far_two, total, grad_two
    )
    step(messages[1])
    landing = joined_rows.at[:, pl.ds(pl.multiple_of(blk * mid, mid), mid)]
    joined_here = mail.local(low_joined.at[tile_rows(blk)], landing)
    joined_copies = [
        mail.send(low_joined.at[tile_rows(blk ^ mask_t)], landing, (blk ^ mask_t, batch))
        for mask_t in range(1, 4)
    ]
    sums = norm_back(stats, norms, mask, grad_two, pre_two, 2, slim, lambda rows: grad_two[rows, :])
    copies = send_sums(mail, place, slots_two, sums)
    step(heads[5], heads[6], job_shared)
    step(heads[7], heads[8])
    step(heads[2], heads[3], heads[4])
    grads = red_last.grad
    grads[...] = t_dot(act_two[...], low_three[...]).astype(BF16).reshape(grads.shape)
    step(job_last)
    for copy in copies:
        copy.wait_recv()
    bias_sum, gain_sum = add_up(slots_two)
    keep(2, bias_sum, gain_sum, slim)

    def put_two(rows, value):
        two_here[pl.ds(pl.multiple_of(rows.start + PITCH, 16), CHUNK), :] = value

    through(stats, norms, mask, sizes, grad_two, pre_two, 2, slim, bias_sum, gain_sum, put_two)
    widen(two_here, two_left, two_right, total)
    shifted = (two_left, two_here, two_right)

    def one_part(rows):
        for offset in range(9):
            row, col = 2 - offset // 3, 2 - offset % 3
            window = shifted[col][pl.ds(pl.multiple_of(rows.start + PITCH * row, 16), BLOCK), :]
            strip[:, offset * slim : (offset + 1) * slim] = window
        low_three[rows, :] = dot(strip[...], turned[...]).astype(BF16)

    loop(total, BLOCK, one_part)

    def spatial_grads():
        grads = red_spatial.grad
        for offset in range(9):
            row, col = 2 - offset // 3, 2 - offset % 3
            window = shifted[col][PITCH * row : PITCH * row + total, :]
            found = t_dot(act_one[PITCH : PITCH + total, :], window).astype(BF16)
            grads[:, :, :, offset * slim : (offset + 1) * slim] = found.reshape(grads.shape[:3] + (slim,))
        step(job_spatial)

    sum_over_tiles(
        mail,
        place,
        lambda index: low_three.at[tile_rows(index)],
        near_one,
        pair_one,
        far_one,
        tile,
        grad_one,
        spatial_grads,
    )
    step(messages[1])
    step(messages[2])
    step(heads[0], heads[1], job_gates, job_stream)
    sums = norm_back(stats, norms, mask, grad_one, pre_one, 0, mid, lambda rows: grad_one[rows, :], base)
    slots_tile[blk] = jnp.concatenate(sums, 0)
    swap_tile_sums(mail, place, slots_tile)
    copies = send_sums(mail, place, slots_one, list(add_up(slots_tile)))
    step(heads[7], heads[8], job_last, job_spatial)
    step(heads[5], heads[6], job_shared)
    for copy in copies:
        copy.wait_recv()
    bias_sum, gain_sum = add_up(slots_one)
    keep(0, bias_sum, gain_sum, mid)

    def put_one(rows, value):
        all_one[at_base(base, rows), :] = value

    through(stats, norms, mask, sizes, grad_one, pre_one, 0, mid, bias_sum, gain_sum, put_one, base)
    share_tiles(mail, place, lambda index: all_one.at[tile_rows(index)])
    grads = red_first.grad
    grads[...] = t_dot(wide[...], all_one[...]).astype(BF16).reshape(grads.shape)
    step(job_first)
    step(messages[2], job_sums)
    step(heads[0], heads[1], job_gates, job_stream)
    step(heads[2], heads[3], heads[4], heads[5], heads[6])
    joined_here.wait()
    for copy in joined_copies:
        copy.wait_recv()

    def input_grads(rows):
        own = all_one[pl.ds(pl.multiple_of(base + rows.start, CHUNK), rows.size), :]
        grad_input[rows, :] = dot_t(own, first[...]) + joined_rows[rows, :].astype(F32)

    loop(tile, tile // 3, input_grads)
    step(job_first)
    step(heads[2], heads[3], heads[4], heads[5], heads[6], job_sums)
    step(heads[7], heads[8], job_last, job_spatial)
    step(heads[7], heads[8], job_last, job_spatial)
    step(job_first)
    step(heads[7], heads[8], job_last, job_spatial)
    for job in messages + heads + [job_gates, job_stream, job_last, job_spatial, job_sums]:
        step(job)
    mail.close()


def bottleneck_back(nb, back, pres, stats, norms, mask, sizes, wide, acts, weights, gate_grads, stream_grads, task_grads):
    tile, total = pres[0].shape[0], mask.shape[0]
    mid = pres[0].shape[1]
    slim = mid // 4
    lines, share = nb // 2, mid // nb
    padded = total + 2 * PITCH
    width = weights[3].shape[0]

    def array(*shape, kind=BF16):
        return jax.ShapeDtypeStruct(shape, kind)

    def vmem(*shape, kind=BF16):
        return pltpu.VMEM(shape, kind)

    scratch = [
        vmem(2, total, slim),
        vmem(total, slim),
        vmem(total, slim),
        vmem(total, slim, kind=F32),
        vmem(total, mid),
        vmem(total, mid, kind=F32),
        vmem(total, mid),
        vmem(total, mid),
        vmem(tile, width),
        vmem(2, total, slim),
        vmem(total, slim),
        vmem(total, slim),
        vmem(total, slim, kind=F32),
        vmem(padded, slim),
        vmem(padded, slim),
        vmem(padded, slim),
        vmem(9 * slim, mid),
        vmem(BLOCK, 9 * slim),
        vmem(2, tile, mid),
        vmem(tile, mid),
        vmem(tile, mid),
        vmem(tile, mid, kind=F32),
        vmem(total, mid),
        vmem(nb, 2, slim, kind=F32),
        vmem(nb, 2, mid, kind=F32),
        vmem(nb, 2, slim, kind=F32),
        vmem(4, 2, mid, kind=F32),
        vmem(nb, 2, mid, kind=F32),
    ]
    for columns in (mid, mid, mid, 9 * slim):
        scratch += reduce_scratch(lines, share, columns, True)
    for columns in (mid, LANES):
        scratch += reduce_scratch(lines, share, columns, False)
    message_share, head_grads, task_sums = task_grads
    scratch += [vmem(9, share, mid), vmem(16, mid, kind=F32)]
    for _ in range(9):
        scratch += reduce_scratch(lines, share, mid, False)
    scratch.append(DMA((2, 256)))
    return pl.pallas_call(
        functools.partial(backward_kernel, nb),
        out_shape=(
            array(tile, width, kind=F32),
            array(share, mid),
            array(share, mid),
            array(4, share, mid),
            array(4, share, 9 * slim),
            array(4, share, mid),
            array(4, share, LANES),
            array(4, 9 * share, mid),
            array(4, message_share.shape[0], mid),
            array(4, 16, mid, kind=F32),
        ),
        in_specs=[VMEM] * 19 + [ANY] * 2 + [VMEM],
        out_specs=(VMEM,) * 7 + (ANY, ANY, VMEM),
        scratch_shapes=scratch,
        cost_estimate=LONG,
        compiler_params=pltpu.CompilerParams(
            collective_id=22, has_side_effects=True, vmem_limit_bytes=62 * 2**20
        ),
    )(
        back,
        *pres,
        stats,
        norms,
        mask,
        sizes,
        wide,
        *acts,
        *weights,
        gate_grads.reshape(lines, 2, share, mid),
        stream_grads.reshape(lines, 2, share, LANES),
        message_share,
        head_grads.reshape(9, lines, 2, share, mid),
        task_sums,
    )


def finish_kernel(images, first, shared, rest, first_rows, shared_rows, all_rest, sems):
    place = Place(images)
    mail = Mail(sems)
    greet_owners(place)
    jobs = [
        Tiles(mail, place, lambda index: all_rest.at[index], rest),
        Owners(mail, place, first, first_rows),
        Owners(mail, place, shared, shared_rows),
    ]
    for job in jobs:
        job.start()
    for job in jobs:
        job.forward()
    for job in jobs:
        job.end()
    mail.close()


def finish(nb, first, shared, rest):
    share, mid = first.shape
    return pl.pallas_call(
        functools.partial(finish_kernel, nb),
        out_shape=(
            jax.ShapeDtypeStruct((4, share, mid), BF16),
            jax.ShapeDtypeStruct((4, share, mid), BF16),
            jax.ShapeDtypeStruct((4,) + rest.shape, BF16),
        ),
        in_specs=[ANY] * 3,
        out_specs=(ANY,) * 3,
        scratch_shapes=[DMA((2, 32))],
        compiler_params=pltpu.CompilerParams(collective_id=26, has_side_effects=True),
    )(first, shared, rest)


def task_kernel(
    images,
    early,
    shared_act,
    mask,
    mask_line,
    targets,
    sizes,
    norms,
    head,
    message_start,
    gate,
    to_depth,
    to_classes,
    from_gated,
    message_own,
    streams,
    slopes,
    pre_five,
    stats,
    grad_msg,
    grad_gate,
    gate_grads,
    stream_grads,
    message_grads,
    message_rest,
    message_end,
    left,
    right,
    task,
    messages,
    opened,
    gated,
    slots,
    slots_five,
    sems,
):
    place = Place(images)
    mail = Mail(sems)
    total = mask.shape[0]
    mid = pre_five.shape[1]
    is_first, is_last = place.blk == 0, place.blk == 3
    greet(place.others + [place.mate, place.across])
    late = message_end.shape[0]
    share = message_own.shape[2]
    got = [
        Spread(
            mail,
            place,
            message_own.at[place.blk, 9 - late + at],
            lambda index, at=at: message_end.at[at, pl.ds(pl.multiple_of(index * share, share), share), :],
        )
        for at in range(late)
    ]
    for one in got[: late // 2]:
        one.start()
    stats[...] = jnp.zeros_like(stats)
    for cells in (left, right, task, grad_msg):
        clear_ends(cells, total)
    widen(shared_act, left, right, total)

    def heads(rows):
        pre_five[rows, :] = conv_rows(
            (left, shared_act, right), rows, lambda offset, window: dot(window, head[offset]), False
        )

    loop(total, BLOCK, heads)

    def behind():
        for one in got[: late // 2]:
            one.forward()
        for one in got[late // 2 :]:
            one.start()

    batch_norm_stats(mail, place, pre_five, mask, slots_five, sizes, stats, 0, mid, behind)
    for one in got[late // 2 :]:
        one.forward()

    def act_task(rows):
        value = (pre_five[rows, :] - stats[0:1, :]) * stats[1:2, :] * norms[0:1, :] + norms[1:2, :]
        task[pl.ds(pl.multiple_of(PITCH + rows.start, 16), CHUNK), :] = (
            silu(value) * mask[rows, :]
        ).astype(BF16)

    loop(total, CHUNK, act_task)
    widen(task, left, right, total)
    for one in got:
        one.finish()

    def message_weight(offset):
        if offset < early:
            return message_start[offset]
        return head[9 + offset - early] if offset < 9 - late else message_end[offset - 9 + late]

    def here(rows):
        return pl.ds(pl.multiple_of(PITCH + rows.start, 16), rows.size)

    def send_messages(rows):
        messages[rows, :] = conv_rows(
            (left, task, right), rows, lambda offset, window: dot(window, message_weight(offset)), False
        )
        own = task[here(rows), :]
        opened[rows, :] = jax.nn.sigmoid(dot(own, gate[...]))
        part = (opened[rows, :] * messages[rows, :]).astype(BF16)
        gated[rows, :] = part
        depth_part = jnp.where(is_first, own, part)
        sem_part = jnp.where(is_last, own, part)
        slots[place.blk, :, rows] = dot_t(to_depth[...], depth_part) + dot_t(to_classes[...], sem_part)

    loop(total, BLOCK, send_messages)
    share_tiles(mail, place, lambda index: slots.at[index])
    classes = to_depth.shape[0]
    kind = lax.broadcasted_iota(jnp.int32, (classes, 2 * BLOCK), 0)

    def compare(rows):
        value = slots[0, :, rows] + slots[1, :, rows] + slots[2, :, rows] + slots[3, :, rows]
        streams[:, rows] = value
        is_class = (kind >= 1) & (kind <= CLASSES)
        top = jnp.max(jnp.where(is_class, value, -jnp.inf), 0, keepdims=True)
        power = jnp.where(is_class, jnp.exp(value - top), 0.0)
        chance = power / jnp.sum(power, 0, keepdims=True)
        label = targets[1:2, rows]
        chance = chance - jnp.where((kind - 1).astype(F32) == label, 1.0, 0.0)
        slope = jnp.where(kind == 0, value - targets[0:1, rows], jnp.where(is_class, chance, 0.0))
        slopes[:, rows] = (slope * mask_line[0:1, rows]).astype(BF16)

    loop(total, 2 * BLOCK, compare)
    by_part = dot(slopes[...], gated[...])
    by_task = dot(slopes[...], task[PITCH : PITCH + total, :])
    row = lax.broadcasted_iota(jnp.int32, by_part.shape, 0)
    use_task = ((row == 0) & is_first) | ((row > 0) & is_last)
    found = jnp.where(use_task, by_task, by_part)
    found = jnp.concatenate([found, jnp.zeros((LANES - classes, mid), F32)], 0)
    stream_grads[...] = found.T.astype(BF16)

    def grads(rows):
        grad = t_dot(slopes[:, rows], from_gated[...])
        open_part = opened[rows, :]
        grad_msg[here(rows), :] = (grad * open_part).astype(BF16)
        grad_gate[rows, :] = (grad * messages[rows, :] * open_part * (1.0 - open_part)).astype(BF16)

    loop(total, BLOCK, grads)
    gate_grads[...] = t_dot(task[PITCH : PITCH + total, :], grad_gate[...]).astype(BF16)
    widen(grad_msg, left, right, total)
    shifted = (left, grad_msg, right)
    for offset in range(9):
        row, col = 2 - offset // 3, 2 - offset % 3
        window = shifted[col][PITCH * row : PITCH * row + total, :]
        found = t_dot(task[PITCH : PITCH + total, :], window).astype(BF16)
        if offset < early:
            message_grads[offset] = found
        else:
            message_rest[:, (offset - early) * mid : (offset - early + 1) * mid] = found
    mail.close()


CLASSES = 40


def one_task(nb, early, late, shared_act, mask, mask_line, targets, sizes, norms, weights, streams_weights, own):
    total = mask.shape[0]
    padded, mid = shared_act.shape
    lines = streams_weights[0].shape[0]

    def array(*shape, kind=BF16):
        return jax.ShapeDtypeStruct(shape, kind)

    def vmem(*shape, kind=BF16):
        return pltpu.VMEM(shape, kind)

    return pl.pallas_call(
        functools.partial(task_kernel, nb, early),
        out_shape=(
            array(lines, total, kind=F32),
            array(lines, total),
            array(total, mid, kind=F32),
            array(8, mid, kind=F32),
            array(padded, mid),
            array(total, mid),
            array(mid, mid),
            array(mid, LANES),
            array(early, mid, mid),
            array(mid, (9 - early) * mid),
            array(late, mid, mid),
        ),
        in_specs=[VMEM] * 12 + [ANY],
        out_specs=(VMEM,) * 11,
        scratch_shapes=[
            vmem(padded, mid),
            vmem(padded, mid),
            vmem(padded, mid),
            vmem(total, mid, kind=F32),
            vmem(total, mid, kind=F32),
            vmem(total, mid),
            vmem(4, lines, total, kind=F32),
            vmem(nb, 2, mid, kind=F32),
            DMA((2, 64)),
        ],
        cost_estimate=LONG,
        compiler_params=pltpu.CompilerParams(
            collective_id=23, has_side_effects=True, vmem_limit_bytes=60 * 2**20
        ),
    )(shared_act, mask, mask_line, targets, sizes, norms, *weights, *streams_weights, own)


def task_back_kernel(
    images,
    early,
    shared_act,
    mask,
    sizes,
    norms,
    head,
    message_start,
    gate,
    message_end,
    from_direct,
    slopes,
    pre_five,
    stats,
    grad_msg,
    grad_gate,
    message_grads,
    back,
    head_grads,
    message_done,
    sums_out,
    left,
    right,
    grad_five,
    grad,
    slots_five,
    *rest,
):
    place = Place(images)
    mail = Mail(rest[-1])
    sums_of = [
        Reduce(
            mail,
            place,
            message_grads.at[offset],
            *rest[3 * offset : 3 * offset + 3],
            message_done.at[offset],
        )
        for offset in range(early)
    ]
    total = mask.shape[0]
    late = message_end.shape[0]
    mid = pre_five.shape[1]
    greet(place.others)
    sums_out[...] = jnp.zeros_like(sums_out)
    sums_of[0].start()
    sums_of[1].start()
    for cells in (left, right, grad_five):
        clear_ends(cells, total)
    widen(grad_msg, left, right, total)

    def message_weight(offset):
        if offset < early:
            return message_start[offset]
        return head[9 + offset - early] if offset < 9 - late else message_end[offset - 9 + late]

    def task_grads(rows):
        found = conv_rows(
            (left, grad_msg, right), rows, lambda offset, window: dot_t(window, message_weight(offset)), True
        )
        found = found + dot_t(grad_gate[rows, :], gate[...])
        grad[rows, :] = found + t_dot(slopes[:, rows], from_direct[...])

    loop(total, BLOCK, task_grads)
    sums = norm_back(stats, norms, mask, grad, pre_five, 0, mid, lambda rows: grad[rows, :])
    copies = send_sums(mail, place, slots_five, sums)
    sums_of[0].middle()
    sums_of[1].middle()
    for one in sums_of[2:]:
        one.start()
    for copy in copies:
        copy.wait_recv()
    bias_sum, gain_sum = add_up(slots_five)
    sums_out[0:1, :] = gain_sum
    sums_out[1:2, :] = bias_sum

    def put(rows, value):
        grad_five[pl.ds(pl.multiple_of(PITCH + rows.start, 16), CHUNK), :] = value

    through(stats, norms, mask, sizes, grad, pre_five, 0, mid, bias_sum, gain_sum, put)
    widen(grad_five, left, right, total)
    shifted = (left, grad_five, right)

    def head_back(rows):
        back[rows, :] = conv_rows(
            shifted, rows, lambda offset, window: dot_t(window, head[offset]), True
        ).astype(BF16)

    loop(total, BLOCK, head_back)
    for one in sums_of[2:]:
        one.middle()
    sums_of[0].finish()
    sums_of[1].finish()
    for offset in range(9):
        row, col = 2 - offset // 3, 2 - offset % 3
        window = shifted[col][PITCH * row : PITCH * row + total, :]
        head_grads[offset] = t_dot(shared_act[PITCH : PITCH + total, :], window).astype(BF16)
    for one in sums_of[2:]:
        one.finish()
    mail.close()


def one_task_back(nb, early, shared_act, mask, sizes, norms, weights, from_direct, slopes, rest):
    total = mask.shape[0]
    padded, mid = shared_act.shape
    lines, share = nb // 2, mid // nb

    def array(*shape, kind=BF16):
        return jax.ShapeDtypeStruct(shape, kind)

    def vmem(*shape, kind=BF16):
        return pltpu.VMEM(shape, kind)

    return pl.pallas_call(
        functools.partial(task_back_kernel, nb, early),
        out_shape=(
            array(total, mid),
            array(9, mid, mid),
            array(early, share, mid),
            array(8, mid, kind=F32),
        ),
        in_specs=[VMEM] * 15,
        out_specs=(VMEM,) * 4,
        scratch_shapes=[
            vmem(padded, mid),
            vmem(padded, mid),
            vmem(padded, mid),
            vmem(total, mid, kind=F32),
            vmem(nb, 2, mid, kind=F32),
        ]
        + early * reduce_scratch(lines, share, mid, False)
        + [DMA((2, 48))],
        cost_estimate=LONG,
        compiler_params=pltpu.CompilerParams(
            collective_id=24, has_side_effects=True, vmem_limit_bytes=60 * 2**20
        ),
    )(shared_act, mask, sizes, norms, *weights, from_direct, slopes, *rest)


def last_kernel(shares, sums, all_shares, all_sums, sems):
    place = Place(2)
    mail = Mail(sems)
    blk = place.blk
    greet([place.mate, place.across])
    here = [mail.local(shares, all_shares.at[blk]), mail.local(sums, all_sums.at[blk])]
    both = []
    for source, slots in ((sums, all_sums), (shares, all_shares)):
        far = mail.send(source, slots.at[blk], place.across)
        near = mail.send(source, slots.at[blk], place.mate)
        both.append((far, near, slots))
    for far, near, slots in both:
        far.wait_recv()
        passed = slots.at[blk ^ 2]
        last = mail.send(passed, passed, place.mate)
        near.wait_recv()
        last.wait_recv()
    for copy in here:
        copy.wait()
    mail.close()


def gather_last(shares, sums):
    return pl.pallas_call(
        last_kernel,
        out_shape=(
            jax.ShapeDtypeStruct((4,) + shares.shape, shares.dtype),
            jax.ShapeDtypeStruct((4,) + sums.shape, sums.dtype),
        ),
        in_specs=[ANY] * 2,
        out_specs=(ANY, ANY),
        scratch_shapes=[DMA((2, 16))],
        compiler_params=pltpu.CompilerParams(collective_id=25, has_side_effects=True),
    )(shares, sums)


def on_device(
    nt,
    nb,
    features,
    crop_rows,
    crop_cols,
    depth_target,
    labels,
    first_weight,
    spatial_weight,
    last_weight,
    shared_weight,
    head_weights,
    message_weights,
    gate_weights,
    depth_weight,
    class_weight,
    mid_gain,
    mid_bias,
    out_gain,
    out_bias,
):
    tile_rows, cols, width = features.shape[1:]
    tile = tile_rows * cols
    rows = tile_rows * nt
    pixels = rows * cols
    tasks = head_weights.shape[0]
    mid = first_weight.shape[1]
    share = mid // nb
    slim = mid // nt
    classes = class_weight.shape[1]
    blk, batch = lax.axis_index("blk"), lax.axis_index("batch")

    image_rows = lax.dynamic_index_in_dim(crop_rows, batch, 0, False)
    image_cols = lax.dynamic_index_in_dim(crop_cols, batch, 0, False)
    row_ids = jnp.arange(rows, dtype=jnp.int32)
    col_ids = jnp.arange(PITCH, dtype=jnp.int32)
    inside_grid = (row_ids[:, None] < image_rows) & (col_ids[None, :] < image_cols)
    inside_grid = inside_grid.astype(F32)
    inside_wide = inside_grid.reshape(rows * PITCH, 1)
    inside = inside_grid[:, :cols].reshape(pixels, 1)
    inside_tile = lax.dynamic_slice_in_dim(inside, blk * tile, tile, 0)
    sizes_flat = (crop_rows * crop_cols).astype(F32)
    valid_count = jnp.sum(sizes_flat)
    sizes = jnp.broadcast_to(sizes_flat[:, None, None], (nb, 1, mid))
    tile_counts = jnp.sum(inside.reshape(nt, tile), 1)
    tile_sizes = jnp.broadcast_to(tile_counts[:, None, None], (nt, 1, mid))
    image_size = jnp.maximum(jnp.sum(inside), 1.0)

    params = jnp.concatenate(
        [
            mid_gain.reshape(-1),
            mid_bias.reshape(-1),
            out_gain,
            out_bias,
            depth_weight,
            class_weight.reshape(-1),
        ]
    )
    room = -(-params.shape[0] // (16 * LANES)) * 16 * LANES
    small = jnp.pad(params, (0, room - params.shape[0])).reshape(-1, LANES)
    feat = jnp.pad(features[0], ((0, 0), (0, PITCH - cols), (0, 0))).reshape(tile_rows * PITCH, width)
    piece = shared_weight.shape[0] // nt
    order = [
        (t * nb + b, (b * nt // nb) * nb + (b % (nb // nt)) * nt + t)
        for t in range(nt)
        for b in range(nb)
    ]
    shared_own = lax.ppermute(
        lax.dynamic_slice_in_dim(shared_weight, blk * piece, piece, 0), ("blk", "batch"), order
    )
    pair = jnp.stack([depth_target[0], labels[0].astype(F32)])
    pair = jnp.pad(pair, ((0, 6), (0, 0), (0, PITCH - cols))).reshape(8, tile_rows * PITCH)
    full_first, smalls, targets, wide_features, spatial, pre_one, stats = begin(
        nb, first_weight, small, spatial_weight, pair, feat, inside_wide, sizes, tile_sizes
    )
    full_first = full_first.reshape(width, mid)
    smalls = smalls.reshape(nb, room)
    at = 0

    def taken(count):
        nonlocal at
        found = smalls[:, at : at + count]
        at += count
        return found

    norms_count = mid_gain.shape[0]
    out_share = out_gain.shape[0]
    gain_mid = taken(norms_count * share).reshape(nb, norms_count, share).swapaxes(0, 1)
    gain_mid = gain_mid.reshape(norms_count, mid).astype(F32)
    bias_mid = taken(norms_count * share).reshape(nb, norms_count, share).swapaxes(0, 1)
    bias_mid = bias_mid.reshape(norms_count, mid).astype(F32)
    gain_out = lax.dynamic_slice_in_dim(taken(out_share).reshape(width), blk * mid, mid, 0).astype(F32)
    bias_out = lax.dynamic_slice_in_dim(taken(out_share).reshape(width), blk * mid, mid, 0).astype(F32)
    full_depth = taken(share).reshape(mid, 1)
    full_classes = taken(share * classes).reshape(mid, classes)

    def slim_of(vector):
        return lax.dynamic_slice_in_dim(vector, blk * slim, slim, 0)

    def filled(vector):
        return jnp.pad(vector, (0, mid - vector.shape[0]))

    gain_two, bias_two = slim_of(gain_mid[1]), slim_of(bias_mid[1])
    gain_four, bias_four = slim_of(gain_mid[2]), slim_of(bias_mid[2])
    norms = jnp.stack(
        [
            gain_mid[0],
            bias_mid[0],
            filled(gain_two),
            filled(bias_two),
            gain_out,
            bias_out,
            filled(gain_four),
            filled(bias_four),
        ]
    )
    early, late = 5, 4
    large = jnp.concatenate(
        [
            lax.dynamic_index_in_dim(head_weights, blk, 0, False),
            lax.dynamic_index_in_dim(message_weights, blk, 0, False)[early : 9 - late],
        ],
        0,
    )
    large, stats = lax.optimization_barrier((large, stats))
    large = lax.all_gather(large, "batch", axis=1, tiled=True)
    (
        last,
        shared,
        gate,
        message_start,
        act_one,
        act_two,
        act_three,
        shared_act,
        pre_two,
        pre_three,
        pre_four,
        stats,
    ) = bottleneck(
        nb,
        early,
        pre_one,
        stats,
        spatial,
        wide_features,
        inside_wide,
        norms,
        sizes,
        last_weight,
        shared_own,
        gate_weights,
        message_weights,
    )

    task_norms = jnp.stack(
        [
            lax.dynamic_index_in_dim(gain_mid, 3 + blk, 0, False),
            lax.dynamic_index_in_dim(bias_mid, 3 + blk, 0, False),
        ]
    )
    task_norms = jnp.pad(task_norms, ((0, 6), (0, 0)))
    lines = -(-(1 + classes) // 16) * 16
    stream_weight = jnp.concatenate([full_depth, full_classes], 1).T
    stream_weight = jnp.pad(stream_weight, ((0, lines - 1 - classes), (0, 0)))
    is_depth = jnp.arange(lines)[:, None] == 0
    none = jnp.zeros((), BF16)
    is_first, is_last = blk == 0, blk == tasks - 1
    own_stream = jnp.where(is_depth, is_first, is_last)
    to_depth = jnp.where(is_depth, stream_weight, none)
    to_classes = jnp.where(is_depth, none, stream_weight)
    from_gated = jnp.where(own_stream, none, stream_weight)
    from_direct = jnp.where(own_stream, stream_weight, none)
    mask_line = jnp.broadcast_to(inside_wide.reshape(1, -1), (8, rows * PITCH))
    weights = (large, message_start, gate)
    (
        streams,
        slopes,
        pre_five,
        task_stats,
        grad_msg,
        grad_gate,
        gate_grads,
        stream_grads,
        message_grads,
        message_rest,
        message_end,
    ) = one_task(
        nb,
        early,
        late,
        shared_act,
        inside_wide,
        mask_line,
        targets,
        sizes,
        task_norms,
        weights,
        (to_depth, to_classes, from_gated),
        message_weights,
    )
    own_streams = lax.dynamic_slice_in_dim(streams, blk * tile_rows * PITCH, tile_rows * PITCH, 1)
    own_streams = own_streams.reshape(lines, tile_rows, PITCH)[:, :, :cols]
    depth_out = own_streams[0]
    logits = own_streams[1 : 1 + classes].transpose(1, 2, 0)
    rest_share = lax.psum_scatter(message_rest, "batch", scatter_dimension=0, tiled=True)
    message_grads = message_grads.reshape(early, nb // 2, 2, share, mid)
    back, head_grads, message_done, task_sums = one_task_back(
        nb,
        early,
        shared_act,
        inside_wide,
        sizes,
        task_norms,
        weights + (message_end,),
        from_direct,
        slopes,
        (pre_five, task_stats, grad_msg, grad_gate, message_grads),
    )
    message_share = message_done.reshape(early * share, mid)

    (
        grad_input,
        share_shared,
        share_first,
        all_last,
        all_spatial,
        all_gates,
        all_stream,
        all_heads,
        all_messages,
        sums,
    ) = bottleneck_back(
        nb,
        back,
        (pre_one, pre_two, pre_three, pre_four),
        stats,
        norms,
        inside_wide,
        sizes,
        wide_features,
        (act_one, act_two, act_three),
        (spatial, last, shared, full_first),
        gate_grads,
        stream_grads,
        (message_share, head_grads, task_sums),
    )
    grad_input = grad_input.reshape(tile_rows, PITCH, width)[:, :cols]

    rest_share, share_first = lax.optimization_barrier((rest_share, share_first))
    rest_share = rest_share.reshape(share, 9 - early, mid).swapaxes(0, 1).reshape((9 - early) * share, mid)
    red_first, red_shared, all_rest = finish(nb, share_first, share_shared, rest_share)
    red_first = red_first.astype(F32).reshape(nt * share, mid)
    red_shared = red_shared.astype(F32).reshape(nt * share, mid)
    red_messages = jnp.concatenate(
        [all_messages.reshape(nt, early, share, mid), all_rest.reshape(nt, 9 - early, share, mid)], 1
    ).astype(F32)
    red_last = all_last.astype(F32).transpose(1, 0, 2).reshape(share, width)
    red_gates = all_gates.astype(F32)
    red_spatial = all_spatial.astype(F32).reshape(nt, share, 9, slim)
    red_spatial = red_spatial.transpose(2, 1, 0, 3).reshape(9, share, mid)
    streams_red = jnp.sum(all_stream.astype(F32), 0)
    red_depth = streams_red[:, 0]
    red_classes = streams_red[:, 1 : 1 + classes]
    red_heads = all_heads.astype(F32).reshape(nt, 9, share, mid)
    two_gain, two_bias = sums[:, 2, :slim].reshape(1, mid), sums[:, 3, :slim].reshape(1, mid)
    four_gain, four_bias = sums[:, 6, :slim].reshape(1, mid), sums[:, 7, :slim].reshape(1, mid)
    mid_gains = jnp.concatenate([sums[0, 0:1], two_gain, four_gain, sums[:, 8]], 0)
    mid_biases = jnp.concatenate([sums[0, 1:2], two_bias, four_bias, sums[:, 9]], 0)
    grad_mid_gain = lax.dynamic_slice_in_dim(mid_gains, batch * share, share, 1)
    grad_mid_bias = lax.dynamic_slice_in_dim(mid_biases, batch * share, share, 1)
    grad_out_gain = lax.dynamic_slice_in_dim(sums[:, 4].reshape(width), batch * out_share, out_share, 0)
    grad_out_bias = lax.dynamic_slice_in_dim(sums[:, 5].reshape(width), batch * out_share, out_share, 0)
    return (
        depth_out.reshape(1, tile_rows, cols),
        logits.reshape(1, tile_rows, cols, classes),
        grad_input.reshape(1, tile_rows, cols, width),
        red_first,
        red_spatial,
        red_last,
        red_shared,
        red_heads,
        red_messages,
        red_gates,
        red_depth,
        red_classes,
        grad_mid_gain,
        grad_mid_bias,
        grad_out_gain,
        grad_out_bias,
    )


def solution(mesh):
    nt, nb = mesh.shape["blk"], mesh.shape["batch"]
    placed = (
        P("batch", "blk", None, None),
        P(),
        P(),
        P("batch", "blk", None),
        P("batch", "blk", None),
        P("batch", None),
        P(None, "batch", None),
        P("batch", None),
        P("batch", None),
        P(None, None, "batch", None),
        P(None, None, "batch", None),
        P(None, "batch", None),
        P("batch"),
        P("batch", None),
        P(None, "batch"),
        P(None, "batch"),
        P("batch"),
        P("batch"),
    )
    return jax.shard_map(
        functools.partial(on_device if nb == 8 else on_device_any, nt, nb),
        mesh=mesh,
        in_specs=placed,
        out_specs=(
            P("batch", "blk", None),
            P("batch", "blk", None, None),
            P("batch", "blk", None, None),
            P("batch", None),
            P(None, "batch", None),
            P("batch", None),
            P("batch", None),
            P(None, None, "batch", None),
            P(None, None, "batch", None),
            P(None, "batch", None),
            P("batch"),
            P("batch", None),
            P(None, "batch"),
            P(None, "batch"),
            P("batch"),
            P("batch"),
        ),
        check_vma=False,
    )
```

```python
import functools

import jax
import jax.numpy as jnp
from jax import lax
from jax.experimental import pallas as pl
from jax.experimental.pallas import tpu as pltpu
from jax.sharding import PartitionSpec as P

EPSILON = 1e-05
MESH = pl.DeviceIdType.MESH
BF16 = jnp.bfloat16
F32 = jnp.float32
LANES = 128


def greet(peers):
    barrier = pltpu.get_barrier_semaphore()
    for peer in peers:
        pl.semaphore_signal(barrier, inc=1, device_id=peer, device_id_type=MESH)
    pl.semaphore_wait(barrier, len(peers))


def send(src, dst, send_sem, recv_sem, peer):
    copy = pltpu.make_async_remote_copy(
        src_ref=src,
        dst_ref=dst,
        send_sem=send_sem,
        recv_sem=recv_sem,
        device_id=peer,
        device_id_type=MESH,
    )
    copy.start()
    return copy


def first_kernel(images, weight, small, full, smalls, own, zs, xs, cs, ps):
    blk, batch = lax.axis_index("blk"), lax.axis_index("batch")
    half = weight.shape[0] // 2
    rows = pl.ds(pl.multiple_of(lax.rem(blk, 2) * half, half), half)
    side = (blk, batch ^ 1)
    mate = (blk ^ 1, batch)
    lines = range(1, images // 2)
    others = [(blk, batch ^ mask) for mask in range(1, images)]
    greet(others + [mate])
    copies = []
    here = pltpu.make_async_copy(weight, full.at[batch], own.at[0])
    here.start()
    here_small = pltpu.make_async_copy(small, smalls.at[batch], own.at[1])
    here_small.start()
    z_copies = {}
    for mask in lines:
        z_copies[mask] = send(
            weight.at[rows],
            full.at[batch, rows],
            zs.at[0, mask],
            zs.at[1, mask],
            (blk, batch ^ (2 * mask)),
        )
    x_copies = {
        0: send(weight.at[rows], full.at[batch, rows], xs.at[0, 0], xs.at[1, 0], side)
    }
    for place, peer in enumerate(others):
        copies.append(
            send(small, smalls.at[batch], ps.at[0, place], ps.at[1, place], peer)
        )
    core_copies = []

    def hand_over(source, mask):
        block = full.at[source, rows]
        core_copies.append(send(block, block, cs.at[0, mask], cs.at[1, mask], mate))

    for mask in lines:
        z_copies[mask].wait_recv()
        source = batch ^ (2 * mask)
        block = full.at[source, rows]
        x_copies[mask] = send(block, block, xs.at[0, mask], xs.at[1, mask], side)
        hand_over(source, 2 * mask)
    for mask in range(images // 2):
        x_copies[mask].wait_recv()
        hand_over(batch ^ (2 * mask + 1), 2 * mask + 1)
    for copy in core_copies + copies:
        copy.wait()
    for mask in lines:
        z_copies[mask].wait_send()
    for mask in range(images // 2):
        x_copies[mask].wait_send()
    here.wait()
    here_small.wait()


def gather_first(weight, small, images):
    any_place = pl.BlockSpec(memory_space=pl.ANY)
    dma = pltpu.SemaphoreType.DMA
    return pl.pallas_call(
        functools.partial(first_kernel, images),
        out_shape=(
            jax.ShapeDtypeStruct((images,) + weight.shape, weight.dtype),
            jax.ShapeDtypeStruct((images,) + small.shape, small.dtype),
        ),
        in_specs=[any_place] * 2,
        out_specs=(any_place, any_place),
        scratch_shapes=[
            dma((2,)),
            dma((2, images)),
            dma((2, images)),
            dma((2, images)),
            dma((2, images)),
        ],
        compiler_params=pltpu.CompilerParams(collective_id=0, has_side_effects=True),
    )(weight, small)


def tiles_kernel(block, every, own, sems):
    blk, batch = lax.axis_index("blk"), lax.axis_index("batch")
    mate, across = (blk ^ 1, batch), (blk ^ 2, batch)
    greet([mate, across])
    far = send(block, every.at[blk], sems.at[0, 0], sems.at[1, 0], across)
    near = send(block, every.at[blk], sems.at[0, 1], sems.at[1, 1], mate)
    here = pltpu.make_async_copy(block, every.at[blk], own.at[0])
    here.start()
    far.wait_recv()
    passed = every.at[blk ^ 2]
    last = send(passed, passed, sems.at[0, 2], sems.at[1, 2], mate)
    near.wait()
    last.wait()
    far.wait_send()
    here.wait()


def gather_tiles(block, ident):
    any_place = pl.BlockSpec(memory_space=pl.ANY)
    dma = pltpu.SemaphoreType.DMA
    return pl.pallas_call(
        tiles_kernel,
        out_shape=jax.ShapeDtypeStruct((4,) + block.shape, block.dtype),
        in_specs=[any_place],
        out_specs=any_place,
        scratch_shapes=[dma((1,)), dma((2, 3))],
        compiler_params=pltpu.CompilerParams(collective_id=ident, has_side_effects=True),
    )(block)


def sum_kernel(parts, total, near_in, pair, far_in, sems):
    blk, batch = lax.axis_index("blk"), lax.axis_index("batch")
    mate, across = (blk ^ 1, batch), (blk ^ 2, batch)
    greet([mate, across])
    far_first = send(parts.at[blk ^ 3], near_in.at[0], sems.at[0, 0], sems.at[1, 0], mate)
    near_next = send(parts.at[blk ^ 1], near_in.at[1], sems.at[0, 1], sems.at[1, 1], mate)
    far_first.wait_recv()
    pair[...] = (parts[blk ^ 2].astype(F32) + near_in[0].astype(F32)).astype(pair.dtype)
    far = send(pair, far_in, sems.at[0, 2], sems.at[1, 2], across)
    near_next.wait_recv()
    total[...] = parts[blk].astype(F32) + near_in[1].astype(F32)
    far.wait_recv()
    total[...] += far_in[...].astype(F32)
    far_first.wait_send()
    near_next.wait_send()
    far.wait_send()


def sum_tiles(parts, ident):
    dma = pltpu.SemaphoreType.DMA
    block = parts.shape[1:]
    vmem = pl.BlockSpec(memory_space=pltpu.VMEM)
    return pl.pallas_call(
        sum_kernel,
        out_shape=jax.ShapeDtypeStruct(block, F32),
        in_specs=[vmem],
        out_specs=vmem,
        scratch_shapes=[
            pltpu.VMEM((2,) + block, parts.dtype),
            pltpu.VMEM(block, parts.dtype),
            pltpu.VMEM(block, parts.dtype),
            dma((2, 3)),
        ],
        compiler_params=pltpu.CompilerParams(
            collective_id=ident, has_side_effects=True, vmem_limit_bytes=32 * 2**20
        ),
    )(parts)


def combine(slots, weights, half, centred):
    count = slots.shape[0]
    if not centred:
        total = slots[0]
        for at in range(1, count):
            total = total + slots[at]
        return total
    size = weights[0]
    mean = slots[0, :half] * weights[0]
    for at in range(1, count):
        size = size + weights[at]
        mean = mean + slots[at, :half] * weights[at]
    mean = mean / size
    spread = None
    for at in range(count):
        gap = slots[at, :half] - mean
        term = slots[at, half : 2 * half] + weights[at] * gap * gap
        spread = term if spread is None else spread + term
    rest = [jnp.zeros((slots.shape[1] - 2 * half, LANES), F32)] * (slots.shape[1] > 2 * half)
    return jnp.concatenate([mean, spread] + rest, 0)


def sums_kernel(images, half, centred, tiled, own, tile_sizes, sizes, total, *scratch):
    blk, batch = lax.axis_index("blk"), lax.axis_index("batch")
    slots, sems = scratch[0], scratch[1]
    peers = [(blk, batch ^ mask) for mask in range(1, images)]
    mates = [(blk ^ mask, batch) for mask in range(1, 4)] if tiled else []
    greet(peers + mates)
    if tiled:
        tile_slots, tile_sems = scratch[2], scratch[3]
        tile_slots[blk] = own[...]
        copies = [
            send(own, tile_slots.at[blk], tile_sems.at[0, at], tile_sems.at[1, at], peer)
            for at, peer in enumerate(mates)
        ]
        for copy in copies:
            copy.wait()
        slots[batch] = combine(tile_slots, tile_sizes, half, centred)
    else:
        slots[batch] = own[...]
    copies = [
        send(slots.at[batch], slots.at[batch], sems.at[0, at], sems.at[1, at], peer)
        for at, peer in enumerate(peers)
    ]
    for copy in copies:
        copy.wait()
    total[...] = combine(slots, sizes, half, centred)


def all_sums(first, second, tile_sizes, sizes, centred, tiled, ident):
    images = sizes.shape[0]
    channels = first.shape[0]
    half = channels // LANES
    rows = -(-2 * half // 8) * 8
    own = jnp.concatenate(
        [first, second, jnp.zeros(((rows - 2 * half) * LANES,), F32)]
    ).reshape(rows, LANES)
    dma = pltpu.SemaphoreType.DMA
    vmem = pl.BlockSpec(memory_space=pltpu.VMEM)
    scratch = [pltpu.VMEM((images, rows, LANES), F32), dma((2, images))]
    if tiled:
        scratch += [pltpu.VMEM((4, rows, LANES), F32), dma((2, 3))]
    total = pl.pallas_call(
        functools.partial(sums_kernel, images, half, centred, tiled),
        out_shape=jax.ShapeDtypeStruct((rows, LANES), F32),
        in_specs=[vmem] * 3,
        out_specs=vmem,
        scratch_shapes=scratch,
        compiler_params=pltpu.CompilerParams(collective_id=ident, has_side_effects=True),
    )(own, sizes if tile_sizes is None else tile_sizes, sizes)
    flat = total.reshape(-1)
    return flat[:channels], flat[channels : 2 * channels]


def silu_slope(values):
    sigmoid_value = jax.nn.sigmoid(values)
    return sigmoid_value * (1.0 + values * (1.0 - sigmoid_value))


def windows(cells, rows, cols, back):
    channels = cells.shape[1]
    padded = jnp.pad(cells.reshape(rows, cols, channels), ((1, 1), (1, 1), (0, 0)))
    taken = []
    for offset in range(9):
        row, col = offset // 3, offset % 3
        if back:
            row, col = 2 - row, 2 - col
        taken.append(padded[row : row + rows, col : col + cols].reshape(rows * cols, channels))
    return jnp.concatenate(taken, 1)


def dot(left, right):
    return jnp.dot(left, right, preferred_element_type=F32)


def dot_t(left, right):
    return jnp.einsum("pd,cd->pc", left, right, preferred_element_type=F32)


def t_dot(left, right):
    return jnp.einsum("pc,pd->cd", left, right, preferred_element_type=F32)


def on_device_any(
    nt,
    nb,
    features,
    crop_rows,
    crop_cols,
    depth_target,
    labels,
    first_weight,
    spatial_weight,
    last_weight,
    shared_weight,
    head_weights,
    message_weights,
    gate_weights,
    depth_weight,
    class_weight,
    mid_gain,
    mid_bias,
    out_gain,
    out_bias,
):
    tile_rows, cols, width = features.shape[1:]
    tile = tile_rows * cols
    rows = tile_rows * nt
    pixels = rows * cols
    tasks = head_weights.shape[0]
    mid = first_weight.shape[1]
    share = mid // nb
    slim = mid // nt
    piece = width // (nb * nt)
    wide = nb * piece
    classes = class_weight.shape[1]
    blk, batch = lax.axis_index("blk"), lax.axis_index("batch")

    image_rows = lax.dynamic_index_in_dim(crop_rows, batch, 0, False)
    image_cols = lax.dynamic_index_in_dim(crop_cols, batch, 0, False)
    row_ids = jnp.arange(rows, dtype=jnp.int32)
    col_ids = jnp.arange(cols, dtype=jnp.int32)
    inside_grid = (row_ids[:, None] < image_rows) & (col_ids[None, :] < image_cols)
    inside = inside_grid.astype(F32).reshape(pixels, 1)
    inside_tile = lax.dynamic_slice_in_dim(inside, blk * tile, tile, 0)
    sizes_flat = (crop_rows * crop_cols).astype(F32)
    valid_count = jnp.sum(sizes_flat)
    sizes = jnp.broadcast_to(sizes_flat[:, None, None], (nb, 1, LANES))
    tile_counts = jnp.sum(inside.reshape(nt, tile), 1)
    tile_sizes = jnp.broadcast_to(tile_counts[:, None, None], (nt, 1, LANES))
    image_size = jnp.maximum(jnp.sum(inside), 1.0)
    tile_size = jnp.maximum(jnp.sum(inside_tile), 1.0)

    params = jnp.concatenate(
        [
            mid_gain.reshape(-1),
            mid_bias.reshape(-1),
            out_gain,
            out_bias,
            depth_weight,
            class_weight.reshape(-1),
        ]
    )
    room = -(-params.shape[0] // (16 * LANES)) * 16 * LANES
    small = jnp.pad(params, (0, room - params.shape[0])).reshape(-1, LANES)
    full_first, smalls = gather_first(first_weight, small, nb)
    full_first = full_first.reshape(width, mid)
    smalls = smalls.reshape(nb, room)
    at = 0

    def taken(count):
        nonlocal at
        found = smalls[:, at : at + count]
        at += count
        return found

    norms = mid_gain.shape[0]
    gain_mid = taken(norms * share).reshape(nb, norms, share).swapaxes(0, 1)
    gain_mid = gain_mid.reshape(norms, mid).astype(F32)
    bias_mid = taken(norms * share).reshape(nb, norms, share).swapaxes(0, 1)
    bias_mid = bias_mid.reshape(norms, mid).astype(F32)
    gain_out = lax.dynamic_index_in_dim(taken(nt * piece).reshape(nb, nt, piece), blk, 1, False)
    gain_out = gain_out.reshape(wide).astype(F32)
    bias_out = lax.dynamic_index_in_dim(taken(nt * piece).reshape(nb, nt, piece), blk, 1, False)
    bias_out = bias_out.reshape(wide).astype(F32)
    full_depth = taken(share).reshape(mid, 1)
    full_classes = taken(share * classes).reshape(mid, classes)
    stream_weight = jnp.concatenate([full_depth, full_classes], 1)

    spatial = lax.all_gather(
        lax.dynamic_slice_in_dim(spatial_weight, blk * slim, slim, 2), "batch", axis=1, tiled=True
    )
    last = lax.dynamic_index_in_dim(last_weight.reshape(share, nb, nt, piece), blk, 2, False)
    last = lax.all_gather(last.reshape(share, wide), "batch", axis=0, tiled=True)
    shared = lax.dynamic_slice_in_dim(shared_weight, blk * piece, piece, 0)
    shared = lax.all_gather(shared, "batch", axis=0, tiled=True)
    head = lax.all_gather(
        lax.dynamic_index_in_dim(head_weights, blk, 0, False), "batch", axis=1, tiled=True
    )
    message = lax.all_gather(
        lax.dynamic_index_in_dim(message_weights, blk, 0, False), "batch", axis=1, tiled=True
    )
    gate = lax.all_gather(
        lax.dynamic_index_in_dim(gate_weights, blk, 0, False), "batch", axis=0, tiled=True
    )

    flat_features = features.reshape(tile, width)
    cut = flat_features.reshape(tile, nb, nt, piece).transpose(2, 0, 1, 3).reshape(nt, tile, wide)
    wide_features = swap_tiles(cut, blk, nt)

    def slim_of(vector):
        return lax.dynamic_slice_in_dim(vector, blk * slim, slim, 0)

    def normalize(values, mask, local_size, gain, bias, tiled, ident):
        mean = jnp.sum(values * mask, 0) / local_size
        gap = values - mean
        spread = jnp.sum(gap * gap * mask, 0)
        centre, total = all_sums(mean, spread, tile_sizes, sizes, True, tiled, ident)
        inverse = lax.rsqrt(total / valid_count + EPSILON)
        normed = (values - centre) * inverse
        return normed * gain + bias, normed, inverse

    def normalize_back(grad, normed, inverse, gain, mask, tiled, ident):
        bias_sum, gain_sum = all_sums(
            jnp.sum(grad, 0), jnp.sum(grad * normed, 0), tile_sizes, sizes, False, tiled, ident
        )
        back = (
            inverse * gain * (grad - bias_sum / valid_count - normed * gain_sum / valid_count) * mask
        )
        return back.astype(BF16), gain_sum, bias_sum

    def act(values, mask):
        return (jax.nn.silu(values) * mask).astype(BF16)

    def by_rows(blocks):
        return blocks.reshape(pixels, blocks.shape[2])

    def by_channels(blocks):
        return blocks.swapaxes(0, 1).reshape(pixels, nt * blocks.shape[2])

    def cut_channels(values):
        return values.astype(BF16).reshape(pixels, nt, slim).swapaxes(0, 1)

    pre_one = dot(flat_features, full_first)
    norm_one, normed_one, inverse_one = normalize(
        pre_one, inside_tile, tile_size, gain_mid[0], bias_mid[0], True, 1
    )
    act_one = by_rows(gather_tiles(act(norm_one, inside_tile), 2))
    pre_two = dot(windows(act_one, rows, cols, False), spatial.reshape(9 * mid, slim))
    gain_two, bias_two = slim_of(gain_mid[1]), slim_of(bias_mid[1])
    norm_two, normed_two, inverse_two = normalize(
        pre_two, inside, image_size, gain_two, bias_two, False, 3
    )
    act_two = by_channels(gather_tiles(act(norm_two, inside), 4))
    pre_three = dot(act_two, last)
    norm_three, normed_three, inverse_three = normalize(
        pre_three, inside, image_size, gain_out, bias_out, False, 5
    )
    joined = norm_three + wide_features.astype(F32)
    act_three = act(joined, inside)
    pre_four = sum_tiles(cut_channels(dot(act_three, shared)), 6)
    gain_four, bias_four = slim_of(gain_mid[2]), slim_of(bias_mid[2])
    norm_four, normed_four, inverse_four = normalize(
        pre_four, inside, image_size, gain_four, bias_four, False, 3
    )
    shared_act = by_channels(gather_tiles(act(norm_four, inside), 4))

    gain_task = lax.dynamic_index_in_dim(gain_mid, 3 + blk, 0, False)
    bias_task = lax.dynamic_index_in_dim(bias_mid, 3 + blk, 0, False)
    pre_five = dot(windows(shared_act, rows, cols, False), head.reshape(9 * mid, mid))
    norm_five, normed_five, inverse_five = normalize(
        pre_five, inside, image_size, gain_task, bias_task, False, 5
    )
    task_act = act(norm_five, inside)
    messages = dot(windows(task_act, rows, cols, False), message.reshape(9 * mid, mid))
    gate_open = jax.nn.sigmoid(dot(task_act, gate))
    gated = (gate_open * messages).astype(BF16)
    is_first, is_last = blk == 0, blk == tasks - 1
    depth_part = jnp.where(is_first, task_act, gated)
    sem_part = jnp.where(is_last, task_act, gated)
    depth_share = jnp.einsum("pc,co->op", depth_part, full_depth, preferred_element_type=F32)
    class_share = jnp.einsum("pc,co->op", sem_part, full_classes, preferred_element_type=F32)
    lift = -(-(1 + classes) // 8) * 8 - 1 - classes
    shares = jnp.concatenate([depth_share, class_share, jnp.zeros((lift, pixels), F32)], 0)
    streams = jnp.sum(gather_tiles(shares, 7), 0).T
    depth_out = lax.dynamic_slice_in_dim(streams, blk * tile, tile, 0)[:, 0]
    logits = lax.dynamic_slice_in_dim(streams, blk * tile, tile, 0)[:, 1 : 1 + classes]
    targets = by_rows(gather_tiles_pair(depth_target, labels, tile))
    all_depth, all_logits = streams[:, :1], streams[:, 1 : 1 + classes]
    depth_slope = ((all_depth - targets[:, :1]) * inside).astype(BF16)
    onehot = (targets[:, 1:2] == jnp.arange(classes, dtype=jnp.int32)[None, :].astype(F32)).astype(F32)
    logit_slope = ((jax.nn.softmax(all_logits, axis=1) - onehot) * inside).astype(BF16)
    grad_depth = t_dot(depth_part, depth_slope)
    grad_classes = t_dot(sem_part, logit_slope)
    depth_back = depth_slope.astype(F32) * full_depth.astype(F32).reshape(1, mid)
    sem_back = dot_t(logit_slope, full_classes)
    zero = jnp.zeros((), F32)
    grad_gated = jnp.where(is_first, zero, depth_back) + jnp.where(is_last, zero, sem_back)
    grad_direct = jnp.where(is_first, depth_back, zero) + jnp.where(is_last, sem_back, zero)

    grad_msg = (grad_gated * gate_open).astype(BF16)
    grad_gate = (grad_gated * messages * gate_open * (1.0 - gate_open)).astype(BF16)
    msg_windows = windows(grad_msg, rows, cols, True)
    gate_grads = t_dot(task_act, grad_gate).astype(BF16)
    message_grads = t_dot(task_act, msg_windows).astype(BF16)
    share_messages = lax.psum_scatter(message_grads, "batch", scatter_dimension=0, tiled=True)
    task_grad = (
        grad_direct
        + dot_t(grad_gate, gate)
        + dot(msg_windows, message.swapaxes(1, 2).reshape(9 * mid, mid))
    )
    grad_norm_five = task_grad * inside * silu_slope(norm_five)
    grad_pre_five, gain_sum_five, bias_sum_five = normalize_back(
        grad_norm_five, normed_five, inverse_five, gain_task, inside, False, 8
    )
    five_windows = windows(grad_pre_five, rows, cols, True)
    head_grads = t_dot(shared_act, five_windows).astype(BF16)
    share_heads = lax.psum_scatter(head_grads, "batch", scatter_dimension=0, tiled=True)
    shared_back = dot(five_windows, head.swapaxes(1, 2).reshape(9 * mid, mid))
    shared_back = sum_tiles(cut_channels(shared_back), 6)

    grad_norm_four = shared_back * inside * silu_slope(norm_four)
    grad_pre_four, gain_sum_four, bias_sum_four = normalize_back(
        grad_norm_four, normed_four, inverse_four, gain_four, inside, False, 9
    )
    grad_four = by_channels(gather_tiles(grad_pre_four, 4))
    shared_grads = t_dot(act_three, grad_four).astype(BF16)
    grad_joined = dot_t(grad_four, shared) * inside * silu_slope(joined)
    grad_three, gain_sum_three, bias_sum_three = normalize_back(
        grad_joined, normed_three, inverse_three, gain_out, inside, False, 8
    )
    last_grads = t_dot(act_two, grad_three).astype(BF16)
    two_back = sum_tiles(cut_channels(dot_t(grad_three, last)), 6)
    grad_norm_two = two_back * inside * silu_slope(norm_two)
    grad_two, gain_sum_two, bias_sum_two = normalize_back(
        grad_norm_two, normed_two, inverse_two, gain_two, inside, False, 9
    )
    two_windows = windows(grad_two, rows, cols, True)
    spatial_grads = t_dot(act_one, two_windows).astype(BF16)
    one_back = dot(two_windows, spatial.swapaxes(1, 2).reshape(9 * slim, mid))
    one_back = sum_tiles(one_back.astype(BF16).reshape(nt, tile, mid), 10)
    grad_norm_one = one_back * inside_tile * silu_slope(norm_one)
    grad_one, gain_sum_one, bias_sum_one = normalize_back(
        grad_norm_one, normed_one, inverse_one, gain_mid[0], inside_tile, True, 11
    )
    all_one = by_rows(gather_tiles(grad_one, 2))
    first_grads = t_dot(wide_features, all_one).astype(BF16)
    joined_tiles = swap_tiles(grad_joined.astype(BF16).reshape(nt, tile, wide), blk, nt)
    joined_tiles = joined_tiles.reshape(nt, tile, nb, piece).transpose(1, 2, 0, 3).reshape(tile, width)
    grad_input = dot_t(grad_one, full_first) + joined_tiles.astype(F32)

    stream_grads = jnp.concatenate([grad_depth, grad_classes], 1)
    stream_grads = jnp.pad(stream_grads, ((0, 0), (0, LANES - 1 - classes))).astype(BF16)
    late = jnp.concatenate(
        [spatial_grads, shared_grads.reshape(nb, piece, mid).reshape(mid, -1),
         last_grads, first_grads.reshape(mid, -1), gate_grads, stream_grads],
        1,
    )
    late_share = lax.psum_scatter(late, "batch", scatter_dimension=0, tiled=True)
    early_share = jnp.concatenate([share_messages, share_heads], 1)
    early = lax.all_gather(early_share, "blk", axis=0, tiled=False).astype(F32)
    late_all = gather_tiles(late_share, 12).astype(F32)
    early = early.reshape(nt, share, 2, 9, mid).transpose(2, 0, 3, 1, 4)
    red_messages, red_heads = early[0], early[1]
    at = 0

    def part(count):
        nonlocal at
        found = late_all[:, :, at : at + count]
        at += count
        return found

    red_spatial = part(9 * slim).reshape(nt, share, 9, slim).transpose(2, 1, 0, 3).reshape(9, share, mid)
    red_shared = part(wide * mid // mid).reshape(nt * piece, mid)
    red_last = part(wide).reshape(nt, share, nb, piece).transpose(1, 2, 0, 3).reshape(share, width)
    red_first = part(wide * mid // mid).reshape(nt * piece, mid)
    red_gates = part(mid)
    streams_red = jnp.sum(part(LANES), 0)
    red_depth = streams_red[:, 0]
    red_classes = streams_red[:, 1 : 1 + classes]

    sums = jnp.concatenate(
        [
            gain_sum_five,
            bias_sum_five,
            gain_sum_three,
            bias_sum_three,
            gain_sum_two,
            bias_sum_two,
            gain_sum_four,
            bias_sum_four,
        ]
    ).reshape(-1, LANES)
    sums = jnp.pad(sums, ((0, -sums.shape[0] % 8), (0, 0)))
    sums = gather_tiles(sums, 13).reshape(nt, -1)
    five_gain, five_bias = sums[:, :mid], sums[:, mid : 2 * mid]
    at_out = 2 * mid
    three_gain = sums[:, at_out : at_out + wide].reshape(nt, nb, piece)
    three_bias = sums[:, at_out + wide : at_out + 2 * wide].reshape(nt, nb, piece)
    at_slim = at_out + 2 * wide
    slims = [
        sums[:, at_slim + i * slim : at_slim + (i + 1) * slim].reshape(1, mid) for i in range(4)
    ]
    mid_gains = jnp.concatenate([gain_sum_one[None], slims[0], slims[2], five_gain], 0)
    mid_biases = jnp.concatenate([bias_sum_one[None], slims[1], slims[3], five_bias], 0)
    grad_mid_gain = lax.dynamic_slice_in_dim(mid_gains, batch * share, share, 1)
    grad_mid_bias = lax.dynamic_slice_in_dim(mid_biases, batch * share, share, 1)
    grad_out_gain = lax.dynamic_index_in_dim(three_gain, batch, 1, False).reshape(nt * piece)
    grad_out_bias = lax.dynamic_index_in_dim(three_bias, batch, 1, False).reshape(nt * piece)
    return (
        depth_out.reshape(1, tile_rows, cols),
        logits.reshape(1, tile_rows, cols, classes),
        grad_input.reshape(1, tile_rows, cols, width),
        red_first,
        red_spatial,
        red_last,
        red_shared,
        red_heads,
        red_messages,
        red_gates,
        red_depth,
        red_classes,
        grad_mid_gain,
        grad_mid_bias,
        grad_out_gain,
        grad_out_bias,
    )


def swap_tiles(blocks, blk, nt):
    out = jnp.zeros_like(blocks)
    out = lax.dynamic_update_index_in_dim(
        out, lax.dynamic_index_in_dim(blocks, blk, 0, False), blk, 0
    )
    for mask in range(1, nt):
        sent = lax.dynamic_index_in_dim(blocks, blk ^ mask, 0, False)
        came = lax.ppermute(sent, "blk", [(i, i ^ mask) for i in range(nt)])
        out = lax.dynamic_update_index_in_dim(out, came, blk ^ mask, 0)
    return out.reshape(-1, blocks.shape[2])


def gather_tiles_pair(depth_target, labels, tile):
    pair = jnp.stack([depth_target.reshape(tile), labels.reshape(tile).astype(F32)], 0)
    pair = jnp.pad(pair, ((0, 6), (0, 0)))
    return gather_tiles(pair, 14).swapaxes(1, 2)


PITCH = 48
CHUNK = 64
BLOCK = 256
ANY = pl.BlockSpec(memory_space=pl.ANY)
VMEM = pl.BlockSpec(memory_space=pltpu.VMEM)
DMA = pltpu.SemaphoreType.DMA
LONG = pl.CostEstimate(flops=80_000_000_000, bytes_accessed=30_000_000, transcendentals=2_000_000)


class Mail:
    def __init__(self, sems):
        self.sems, self.used, self.open = sems, 0, []

    def send(self, src, dst, peer, keep=True):
        copy = send(src, dst, self.sems.at[0, self.used], self.sems.at[1, self.used], peer)
        self.used += 1
        if keep:
            self.open.append(copy.wait_send)
        return copy

    def local(self, src, dst):
        copy = pltpu.make_async_copy(src, dst, self.sems.at[0, self.used])
        copy.start()
        self.used += 1
        return copy

    def close(self):
        for wait in self.open:
            wait()
        self.open = []


class Place:
    def __init__(self, images):
        self.blk, self.batch = lax.axis_index("blk"), lax.axis_index("batch")
        self.images = images
        self.mate = (self.blk ^ 1, self.batch)
        self.across = (self.blk ^ 2, self.batch)
        self.tiles = [(self.blk ^ mask, self.batch) for mask in range(1, 4)]
        self.others = [(self.blk, self.batch ^ mask) for mask in range(1, images)]
        self.side = (self.blk, self.batch ^ 1)


class Spread:
    def __init__(self, mail, place, own, slot):
        self.mail, self.place, self.own, self.slot = mail, place, own, slot
        self.z_copies, self.x_copies = [], []

    def start(self):
        place, here = self.place, self.slot(self.place.batch)
        self.here = self.mail.local(self.own, here)
        for mask in range(1, place.images // 2):
            peer = (place.blk, place.batch ^ (2 * mask))
            self.z_copies.append(self.mail.send(self.own, here, peer))
        self.x_copies.append(self.mail.send(self.own, here, place.side))
        return self

    def forward(self):
        for mask, copy in enumerate(self.z_copies, 1):
            copy.wait_recv()
            block = self.slot(self.place.batch ^ (2 * mask))
            self.x_copies.append(self.mail.send(block, block, self.place.side))

    def finish(self):
        self.here.wait()
        for copy in self.x_copies:
            copy.wait_recv()


def share_tiles(mail, place, slot):
    own = slot(place.blk)
    far = mail.send(own, own, place.across, False)
    near = mail.send(own, own, place.mate, False)
    far.wait_recv()
    passed = slot(place.blk ^ 2)
    last = mail.send(passed, passed, place.mate, False)
    near.wait()
    last.wait()
    far.wait_send()


def loop(total, step, body, base=0):
    def run(at, carry):
        body(pl.ds(pl.multiple_of(base + at * step, step), step))
        return carry

    lax.fori_loop(0, total // step, run, 0)


PIECES = 3


def pieces_of(total):
    size = total // PIECES
    return [(at * size, size) for at in range(PIECES)]


def share_pieces(mail, place, slot, total, produce=None, consume=None, meanwhile=None):
    pieces = pieces_of(total)
    far, near, last = [], [], []
    for first, size in pieces:
        if produce is not None:
            produce(first, size)
        own = slot(place.blk, first, size)
        far.append(mail.send(own, own, place.across, False))
        near.append(mail.send(own, own, place.mate, False))
    if meanwhile is not None:
        meanwhile()

    def use(at):
        near[at].wait_recv()
        last[at].wait_recv()
        if consume is not None:
            consume(*pieces[at])

    for at, (first, size) in enumerate(pieces):
        far[at].wait_recv()
        passed = slot(place.blk ^ 2, first, size)
        last.append(mail.send(passed, passed, place.mate, False))
        if at > 0:
            use(at - 1)
    use(len(pieces) - 1)
    for copy in far + near + last:
        copy.wait_send()


def folded(values):
    return jnp.sum(values.reshape(values.shape[0] // 8, 8, values.shape[1]), 0)


def loop_sums(total, channels, count, body, base=0):
    def run(at, carry):
        found = body(pl.ds(pl.multiple_of(base + at * CHUNK, CHUNK), CHUNK))
        return tuple(kept + folded(one) for kept, one in zip(carry, found))

    start = tuple(jnp.zeros((8, channels), F32) for _ in range(count))
    return [jnp.sum(one, 0, keepdims=True) for one in lax.fori_loop(0, total // CHUNK, run, start)]


def merge(slots, sizes, channels):
    count = slots.shape[0]
    size, mean = None, None
    for at in range(count):
        weight = sizes[at, :, :channels]
        term = slots[at, 0:1, :] * weight
        size = weight if size is None else size + weight
        mean = term if mean is None else mean + term
    mean = mean / size
    spread = None
    for at in range(count):
        gap = slots[at, 0:1, :] - mean
        term = slots[at, 1:2, :] + sizes[at, :, :channels] * gap * gap
        spread = term if spread is None else spread + term
    return mean, spread, size


def add_up(slots):
    total = slots[0]
    for at in range(1, slots.shape[0]):
        total = total + slots[at]
    return total[0:1, :], total[1:2, :]


def swap_sums(mail, place, slots, meanwhile=None):
    own = slots.at[place.batch]
    copies = [mail.send(own, own, peer) for peer in place.others]
    if meanwhile is not None:
        meanwhile()
    for copy in copies:
        copy.wait_recv()


def swap_tile_sums(mail, place, slots):
    own = slots.at[place.blk]
    copies = [mail.send(own, own, peer) for peer in place.tiles]
    for copy in copies:
        copy.wait_recv()


def local_stats(pre, mask, base, total, channels, size):
    def first(rows):
        return (pre[rows, :] * mask[at_base(base, rows), :],)

    (summed,) = loop_sums(total, channels, 1, first)
    mean = summed / jnp.maximum(size, 1.0)

    def second(rows):
        gap = pre[rows, :] - mean
        return (gap * gap * mask[at_base(base, rows), :],)

    (spread,) = loop_sums(total, channels, 1, second)
    return mean, spread


def at_base(base, rows):
    if base is None:
        return rows
    return pl.ds(pl.multiple_of(base + rows.start, CHUNK), rows.size)


def batch_norm_stats(mail, place, pre, mask, slots, sizes, stats, row, channels, meanwhile=None):
    total = pre.shape[0]
    mean, spread = local_stats(pre, mask, None, total, channels, sizes[place.batch, :, :channels])
    slots[place.batch] = jnp.concatenate([mean, spread], 0)
    swap_sums(mail, place, slots, meanwhile)
    keep_stats(slots, sizes, stats, row, channels)


def keep_stats(slots, sizes, stats, row, channels):
    mean, spread, size = merge(slots, sizes, channels)
    stats[row : row + 1, :channels] = mean
    stats[row + 1 : row + 2, :channels] = lax.rsqrt(spread / size + EPSILON)


def silu(values):
    return values * jax.nn.sigmoid(values)


def widen(cells, left, right, total):
    def body(rows):
        seen = cells[pl.ds(pl.multiple_of(rows.start + PITCH - 16, 16), CHUNK + 32), :].astype(F32)
        here = pl.ds(pl.multiple_of(rows.start + PITCH, 16), CHUNK)
        left[here, :] = seen[15 : 15 + CHUNK].astype(BF16)
        right[here, :] = seen[17 : 17 + CHUNK].astype(BF16)

    loop(total, CHUNK, body)


def clear_ends(cells, total):
    zeros = jnp.zeros((PITCH, cells.shape[1]), cells.dtype)
    cells[0:PITCH, :] = zeros
    cells[PITCH + total : 2 * PITCH + total, :] = zeros


def conv_rows(shifted, rows, weight, back):
    total = None
    for offset in range(9):
        row, col = offset // 3, offset % 3
        if back:
            row, col = 2 - row, 2 - col
        window = shifted[col][pl.ds(pl.multiple_of(rows.start + PITCH * row, 16), rows.size), :]
        product = weight(offset, window)
        total = product if total is None else total + product
    return total


def sum_over_tiles(mail, place, part, near_in, pair, far_in, total, out, meanwhile=None, produce=None):
    mine_far, mine = part(place.blk ^ 2), part(place.blk)
    pieces = pieces_of(total)
    near_far, near_own, far = [], [], []

    def pairs(rows):
        pair[rows, :] = (mine_far[rows, :].astype(F32) + near_in[0, rows, :].astype(F32)).astype(BF16)

    def pass_on(at):
        first, size = pieces[at]
        near_far[at].wait_recv()
        loop(size, CHUNK, pairs, first)
        here = pl.ds(first, size)
        far.append(mail.send(pair.at[here], far_in.at[here], place.across))

    for at, (first, size) in enumerate(pieces):
        if produce is not None:
            produce(first, size)
        here = pl.ds(first, size)
        near_far.append(mail.send(part(place.blk ^ 3).at[here], near_in.at[0, here], place.mate))
        near_own.append(mail.send(part(place.blk ^ 1).at[here], near_in.at[1, here], place.mate))
        if at > 0:
            pass_on(at - 1)
    pass_on(len(pieces) - 1)
    if meanwhile is not None:
        meanwhile()

    def finish(rows):
        out[rows, :] = (
            mine[rows, :].astype(F32) + near_in[1, rows, :].astype(F32) + far_in[rows, :].astype(F32)
        )

    for at, (first, size) in enumerate(pieces):
        near_own[at].wait_recv()
        far[at].wait_recv()
        loop(size, CHUNK, finish, first)


def start_kernel(
    images,
    weight,
    small,
    spatial_own,
    pair,
    feat,
    mask,
    sizes,
    tile_sizes,
    full,
    smalls,
    targets,
    wide,
    spatial,
    pre_one,
    stats,
    slots_tile,
    slots_one,
    sems,
):
    place = Place(images)
    mail = Mail(sems)
    blk, batch = place.blk, place.batch
    depth = weight.shape[0]
    half = depth // 2
    mid = weight.shape[1]
    tile = feat.shape[0]
    slim = mid // 4
    share = spatial_own.shape[1]
    mine = pl.ds(pl.multiple_of(lax.rem(blk, 2) * half, half), half)
    greet(place.others + place.tiles)
    here = mail.local(weight, full.at[batch])
    here_small = mail.local(small, smalls.at[batch])
    z_copies, x_copies, arrived, late = {}, [], [], []
    for peer in place.others:
        late.append(mail.send(small, smalls.at[batch], peer))
    for mask_z in range(1, images // 2):
        z_copies[mask_z] = mail.send(
            weight.at[mine], full.at[batch, mine], (blk, batch ^ (2 * mask_z))
        )
    x_copies.append(mail.send(weight.at[mine], full.at[batch, mine], place.side))
    lanes = pl.ds(pl.multiple_of(blk * slim, slim), slim)
    got_spatial = Spread(
        mail,
        place,
        spatial_own.at[:, :, lanes],
        lambda index: spatial.at[:, pl.ds(pl.multiple_of(index * share, share), share), :],
    ).start()

    def columns(index):
        return feat.at[:, pl.ds(pl.multiple_of(index * mid, mid), mid)]

    landing = wide.at[pl.ds(pl.multiple_of(blk * tile, tile), tile), :]
    here_wide = mail.local(columns(blk), landing)
    line = targets.at[:, pl.ds(pl.multiple_of(blk * tile, tile), tile)]
    here_line = mail.local(pair, line)
    for mask_t in range(1, 4):
        late.append(mail.send(pair, line, (blk ^ mask_t, batch)))
        late.append(mail.send(columns(blk ^ mask_t), landing, (blk ^ mask_t, batch)))

    def hand_over(source):
        block = full.at[source, mine]
        arrived.append(mail.send(block, block, place.mate))

    for mask_z in range(1, images // 2):
        z_copies[mask_z].wait_recv()
        source = batch ^ (2 * mask_z)
        block = full.at[source, mine]
        x_copies.append(mail.send(block, block, place.side))
        hand_over(source)
    for mask_z in range(images // 2):
        x_copies[mask_z].wait_recv()
        hand_over(batch ^ (2 * mask_z + 1))
    stats[...] = jnp.zeros_like(stats)
    here.wait()
    for copy in arrived:
        copy.wait_recv()

    def reduce(rows):
        total = None
        for index in range(images):
            product = dot(feat[rows, index * depth : (index + 1) * depth], full[index])
            total = product if total is None else total + product
        pre_one[rows, :] = total

    loop(tile, tile // 2, reduce)
    base = blk * tile
    mean, spread = local_stats(pre_one, mask, base, tile, mid, tile_sizes[blk, :, :])
    slots_tile[blk] = jnp.concatenate([mean, spread], 0)
    swap_tile_sums(mail, place, slots_tile)
    mean, spread, _ = merge(slots_tile, tile_sizes, mid)
    slots_one[batch] = jnp.concatenate([mean, spread], 0)
    swap_sums(mail, place, slots_one, got_spatial.forward)
    keep_stats(slots_one, sizes, stats, 0, mid)
    got_spatial.finish()
    for copy in late:
        copy.wait_recv()
    here_small.wait()
    here_wide.wait()
    here_line.wait()
    mail.close()


def begin(nb, weight, small, spatial, pair, feat, mask, sizes, tile_sizes):
    depth, mid = weight.shape
    tile = feat.shape[0]

    def array(*shape, kind=BF16):
        return jax.ShapeDtypeStruct(shape, kind)

    return pl.pallas_call(
        functools.partial(start_kernel, nb),
        out_shape=(
            array(nb, depth, mid),
            array(nb, *small.shape),
            array(8, 4 * tile, kind=F32),
            array(4 * tile, mid),
            array(9, mid, mid // 4),
            array(tile, mid, kind=F32),
            array(8, mid, kind=F32),
        ),
        in_specs=[ANY] * 4 + [VMEM] * 4,
        out_specs=(VMEM, ANY, ANY, VMEM, VMEM, VMEM, VMEM),
        scratch_shapes=[
            pltpu.VMEM((4, 2, mid), F32),
            pltpu.VMEM((nb, 2, mid), F32),
            DMA((2, 64)),
        ],
        cost_estimate=LONG,
        compiler_params=pltpu.CompilerParams(
            collective_id=21, has_side_effects=True, vmem_limit_bytes=40 * 2**20
        ),
    )(weight, small, spatial, pair, feat, mask, sizes, tile_sizes)


def forward_kernel(
    images,
    early,
    pre_one,
    first_stats,
    spatial,
    wide,
    mask,
    norms,
    sizes,
    last_own,
    shared_own,
    gate_own,
    message_own,
    last,
    shared,
    gate,
    message,
    act_one,
    act_two,
    act_three,
    shared_act,
    pre_two,
    pre_three,
    pre_four,
    stats,
    one_left,
    one_right,
    parts,
    near_in,
    pair,
    far_in,
    slots_two,
    slots_three,
    slots_four,
    sems,
):
    place = Place(images)
    mail = Mail(sems)
    blk, batch = place.blk, place.batch
    tile, total = pre_one.shape[0], mask.shape[0]
    mid = pre_one.shape[1]
    slim = pre_two.shape[1]
    share = last_own.shape[0]
    base = blk * tile
    greet(place.others + place.tiles)

    def rows_of(index):
        return pl.ds(pl.multiple_of(index * share, share), share)

    def slim_lanes(index):
        return pl.ds(pl.multiple_of(index * slim, slim), slim)

    lanes = slim_lanes(blk)
    wide_lanes = pl.ds(pl.multiple_of(blk * mid, mid), mid)
    got_last = Spread(mail, place, last_own.at[:, wide_lanes], lambda index: last.at[rows_of(index), :])
    got_shared = Spread(mail, place, shared_own, lambda index: shared.at[rows_of(index), :])
    got_gate = Spread(mail, place, gate_own.at[blk], lambda index: gate.at[rows_of(index), :])
    got_message = [
        Spread(
            mail,
            place,
            message_own.at[blk, offset],
            lambda index, offset=offset: message.at[offset, rows_of(index), :],
        )
        for offset in range(early)
    ]
    got_last.start()
    got_shared.start()
    stats[...] = first_stats[...]
    clear_ends(act_one, total)
    clear_ends(shared_act, total)
    clear_ends(one_left, total)
    clear_ends(one_right, total)

    def act_first(rows):
        value = (pre_one[rows, :] - stats[0:1, :]) * stats[1:2, :] * norms[0:1, :] + norms[1:2, :]
        value = silu(value) * mask[at_base(base, rows), :]
        act_one[pl.ds(pl.multiple_of(PITCH + base + rows.start, 16), CHUNK), :] = value.astype(BF16)

    share_pieces(
        mail,
        place,
        lambda index, first, size: act_one.at[
            pl.ds(pl.multiple_of(PITCH + index * tile + first, 16), size), :
        ],
        tile,
        lambda first, size: loop(size, CHUNK, act_first, first),
    )
    widen(act_one, one_left, one_right, total)
    got_last.forward()
    got_shared.forward()

    shifted = (one_left, act_one, one_right)

    def conv_two(rows):
        pre_two[rows, :] = conv_rows(
            shifted, rows, lambda offset, window: dot(window, spatial[offset]), False
        )

    loop(total, BLOCK, conv_two)

    def after_two():
        got_gate.start()
        got_message[0].start()
        got_message[1].start()

    batch_norm_stats(mail, place, pre_two, mask, slots_two, sizes, stats, 2, slim, after_two)

    def act_second(rows):
        value = (pre_two[rows, :] - stats[2:3, :slim]) * stats[3:4, :slim]
        value = silu(value * norms[2:3, :slim] + norms[3:4, :slim]) * mask[rows, :]
        act_two[rows, lanes] = value.astype(BF16)

    got_last.finish()

    def expand(rows):
        pre_three[rows, :] = dot(act_two[rows, :], last[...])

    share_pieces(
        mail,
        place,
        lambda index, first, size: act_two.at[pl.ds(first, size), slim_lanes(index)],
        total,
        lambda first, size: loop(size, CHUNK, act_second, first),
        lambda first, size: loop(size, BLOCK, expand, first),
    )
    got_gate.forward()

    def after_three():
        got_message[0].forward()
        got_message[1].forward()
        got_message[2].start()
        got_message[3].start()

    batch_norm_stats(mail, place, pre_three, mask, slots_three, sizes, stats, 4, mid, after_three)
    got_shared.finish()

    def act_third(rows):
        normed = (pre_three[rows, :] - stats[4:5, :]) * stats[5:6, :]
        value = normed * norms[4:5, :] + norms[5:6, :] + wide[rows, :].astype(F32)
        act_three[rows, :] = (silu(value) * mask[rows, :]).astype(BF16)

    loop(total, CHUNK, act_third)

    def reduce(rows):
        parts[rows, :] = dot(act_three[rows, :], shared[...]).astype(BF16)

    sum_over_tiles(
        mail,
        place,
        lambda index: parts.at[:, slim_lanes(index)],
        near_in,
        pair,
        far_in,
        total,
        pre_four,
        None,
        lambda first, size: loop(size, BLOCK, reduce, first),
    )

    def after_four():
        got_message[2].forward()
        got_message[3].forward()
        for later in got_message[4:]:
            later.start()

    batch_norm_stats(mail, place, pre_four, mask, slots_four, sizes, stats, 6, slim, after_four)

    def act_fourth(rows):
        value = (pre_four[rows, :] - stats[6:7, :slim]) * stats[7:8, :slim]
        value = silu(value * norms[6:7, :slim] + norms[7:8, :slim]) * mask[rows, :]
        shared_act[pl.ds(pl.multiple_of(PITCH + rows.start, 16), CHUNK), lanes] = value.astype(BF16)

    share_pieces(
        mail,
        place,
        lambda index, first, size: shared_act.at[pl.ds(PITCH + first, size), slim_lanes(index)],
        total,
        lambda first, size: loop(size, CHUNK, act_fourth, first),
    )
    for later in got_message[4:]:
        later.forward()
    got_gate.finish()
    for one in got_message:
        one.finish()
    mail.close()


def bottleneck(nb, early, pre_one, stats, spatial, wide, mask, norms, sizes, last, shared, gate, message):
    tile, total = pre_one.shape[0], mask.shape[0]
    mid = pre_one.shape[1]
    slim = mid // 4
    padded = total + 2 * PITCH

    def array(*shape, kind=BF16):
        return jax.ShapeDtypeStruct(shape, kind)

    outs = (
        array(mid, mid),
        array(mid, mid),
        array(mid, mid),
        array(early, mid, mid),
        array(padded, mid),
        array(total, mid),
        array(total, mid),
        array(padded, mid),
        array(total, slim, kind=F32),
        array(total, mid, kind=F32),
        array(total, slim, kind=F32),
        array(8, mid, kind=F32),
    )
    return pl.pallas_call(
        functools.partial(forward_kernel, nb, early),
        out_shape=outs,
        in_specs=[VMEM] * 7 + [ANY] * 4,
        out_specs=(VMEM, VMEM, ANY, ANY) + (VMEM,) * 8,
        scratch_shapes=[
            pltpu.VMEM((padded, mid), BF16),
            pltpu.VMEM((padded, mid), BF16),
            pltpu.VMEM((total, mid), BF16),
            pltpu.VMEM((2, total, slim), BF16),
            pltpu.VMEM((total, slim), BF16),
            pltpu.VMEM((total, slim), BF16),
            pltpu.VMEM((nb, 2, slim), F32),
            pltpu.VMEM((nb, 2, mid), F32),
            pltpu.VMEM((nb, 2, slim), F32),
            DMA((2, 128)),
        ],
        cost_estimate=LONG,
        compiler_params=pltpu.CompilerParams(
            collective_id=20, has_side_effects=True, vmem_limit_bytes=60 * 2**20
        ),
    )(pre_one, stats, spatial, wide, mask, norms, sizes, last, shared, gate, message)


class Tiles:
    def __init__(self, mail, place, slot, own=None):
        self.mail, self.place, self.slot, self.own = mail, place, slot, own

    def start(self):
        own, here = self.own, self.slot(self.place.blk)
        if own is None:
            own = here
        else:
            self.mail.open.append(self.mail.local(own, here).wait)
        self.far = self.mail.send(own, here, self.place.across)
        self.near = self.mail.send(own, here, self.place.mate)

    def forward(self):
        self.far.wait_recv()
        passed = self.slot(self.place.blk ^ 2)
        self.last = self.mail.send(passed, passed, self.place.mate)

    def end(self):
        self.near.wait_recv()
        self.last.wait_recv()


class Reduce:
    def __init__(self, mail, place, grad, from_side, summed, from_line, out):
        self.mail, self.place = mail, place
        self.grad, self.from_side, self.summed = grad, from_side, summed
        self.from_line, self.out = from_line, out
        self.side = lax.rem(place.batch, 2)
        self.line = lax.div(place.batch, 2)

    def start(self):
        self.from_x = self.mail.send(self.grad.at[:, 1 - self.side], self.from_side, self.place.side)

    def own_half(self, at):
        return self.grad[at, self.side]

    def add_side(self):
        self.from_x.wait_recv()
        lines = self.from_side.shape[0]
        for at in range(lines):
            self.summed[at] = (self.own_half(at).astype(F32) + self.from_side[at].astype(F32)).astype(BF16)

    def middle(self):
        self.add_side()
        self.send_lines()

    def send_lines(self):
        place = self.place
        lines = self.summed.shape[0]
        self.copies = [
            self.mail.send(
                self.summed.at[self.line ^ mask],
                self.from_line.at[mask - 1],
                (place.blk, place.batch ^ (2 * mask)),
            )
            for mask in range(1, lines)
        ]

    def finish(self):
        total = self.summed[self.line].astype(F32)
        for at, copy in enumerate(self.copies):
            copy.wait_recv()
            total = total + self.from_line[at].astype(F32)
        self.out[...] = total.astype(BF16)


class ReduceFar(Reduce):
    def start(self):
        super().start()
        self.fetch = self.mail.local(self.grad.at[:, self.side], self.summed)

    def own_half(self, at):
        if at == 0:
            self.fetch.wait()
        return self.summed[at]


class Owners:
    def __init__(self, mail, place, result, slots):
        self.mail, self.place, self.result, self.slots = mail, place, result, slots
        self.base = mail.used
        mail.used += 5
        self.owner = 2 * place.blk + lax.div(place.batch, 4)
        self.quarter = lax.rem(place.batch, 4)
        self.at_home = self.owner == place.batch

    def copy(self, mask):
        place, mail = self.place, self.mail
        return pltpu.make_async_remote_copy(
            src_ref=self.result,
            dst_ref=self.slots.at[self.quarter],
            send_sem=mail.sems.at[0, self.base + mask],
            recv_sem=mail.sems.at[1, self.base + self.quarter],
            device_id=(place.blk ^ mask, self.owner),
            device_id_type=MESH,
        )

    def local(self):
        return pltpu.make_async_copy(
            self.result, self.slots.at[self.quarter], self.mail.sems.at[0, self.base + 4]
        )

    def start(self):
        for mask in range(1, 4):
            self.copy(mask).start()

        @pl.when(self.at_home)
        def _():
            self.local().start()

        @pl.when(jnp.logical_not(self.at_home))
        def _():
            self.copy(0).start()

    def forward(self):
        for mask in range(1, 4):
            self.copy(mask).wait_send()

        @pl.when(self.at_home)
        def _():
            self.local().wait()

        @pl.when(jnp.logical_not(self.at_home))
        def _():
            self.copy(0).wait_send()

    def end(self):
        place, mail = self.place, self.mail
        for quarter in range(4):
            source = 4 * lax.rem(place.batch, 2) + quarter
            at_home = (lax.div(place.batch, 2) == place.blk) & (source == place.batch)

            @pl.when(jnp.logical_not(at_home))
            def _():
                pltpu.make_async_remote_copy(
                    src_ref=self.result,
                    dst_ref=self.slots.at[quarter],
                    send_sem=mail.sems.at[0, self.base],
                    recv_sem=mail.sems.at[1, self.base + quarter],
                    device_id=place.mate,
                    device_id_type=MESH,
                ).wait_recv()


def greet_owners(place):
    barrier = pltpu.get_barrier_semaphore()
    regular = [place.mate, place.across]
    for peer in regular:
        pl.semaphore_signal(barrier, inc=1, device_id=peer, device_id_type=MESH)
    for quarter in range(4):
        source = (lax.div(place.batch, 2), 4 * lax.rem(place.batch, 2) + quarter)
        at_home = (source[0] == place.blk) & (source[1] == place.batch)

        @pl.when(jnp.logical_not(at_home))
        def _():
            pl.semaphore_signal(barrier, inc=1, device_id=source, device_id_type=MESH)

    owner = 2 * place.blk + lax.div(place.batch, 4)

    @pl.when(owner == place.batch)
    def _():
        pl.semaphore_wait(barrier, len(regular) + 3)

    @pl.when(owner != place.batch)
    def _():
        pl.semaphore_wait(barrier, len(regular) + 4)


class Job:
    def __init__(self, reduce, tiles):
        self.steps = []
        if reduce is not None:
            self.steps += [reduce.start, reduce.middle, reduce.finish]
        if tiles is not None:
            self.steps += [tiles.start, tiles.forward, tiles.end]


def step(*jobs):
    for job in jobs:
        if job.steps:
            job.steps.pop(0)()


def reduce_scratch(lines, share, columns, own):
    found = [pltpu.VMEM((lines, 2, share, columns), BF16)] if own else []
    return found + [
        pltpu.VMEM((lines, share, columns), BF16),
        pltpu.VMEM((lines, share, columns), BF16),
        pltpu.VMEM((lines - 1, share, columns), BF16),
    ]


def send_sums(mail, place, slots, sums):
    slots[place.batch] = jnp.concatenate(sums, 0)
    own = slots.at[place.batch]
    return [mail.send(own, own, peer) for peer in place.others]


def silu_back(value):
    sigmoid_value = jax.nn.sigmoid(value)
    return sigmoid_value * (1.0 + value * (1.0 - sigmoid_value))


def norm_back(stats, norms, mask, grad, pre, row, channels, lead, offset=None, skip=None, rows_of=None):
    def body(rows):
        normed = (pre[rows, :] - stats[row : row + 1, :channels]) * stats[row + 1 : row + 2, :channels]
        value = normed * norms[row : row + 1, :channels] + norms[row + 1 : row + 2, :channels]
        if skip is not None:
            value = value + skip[rows, :].astype(F32)
        found = lead(rows) * mask[at_base(offset, rows), :] * silu_back(value)
        grad[rows, :] = found
        return found, found * normed

    first, size = (0, pre.shape[0]) if rows_of is None else rows_of
    return loop_sums(size, channels, 2, body, first)


def through(stats, norms, mask, sizes, grad, pre, row, channels, bias_sum, gain_sum, put, offset=None, rows_of=None):
    count = sizes[0, :, :channels]
    for at in range(1, sizes.shape[0]):
        count = count + sizes[at, :, :channels]
    scale = stats[row + 1 : row + 2, :channels] * norms[row : row + 1, :channels]
    bias_part, gain_part = bias_sum / count, gain_sum / count

    def body(rows):
        normed = (pre[rows, :] - stats[row : row + 1, :channels]) * stats[row + 1 : row + 2, :channels]
        found = scale * (grad[rows, :] - bias_part - normed * gain_part)
        put(rows, (found * mask[at_base(offset, rows), :]).astype(BF16))

    first, size = (0, pre.shape[0]) if rows_of is None else rows_of
    loop(size, CHUNK, body, first)


def backward_kernel(
    images,
    back,
    pre_one,
    pre_two,
    pre_three,
    pre_four,
    stats,
    norms,
    mask,
    sizes,
    wide,
    act_one,
    act_two,
    act_three,
    spatial,
    last,
    shared,
    first,
    gate_grads,
    stream_grads,
    message_share,
    head_grads,
    task_sums,
    grad_input,
    share_shared,
    share_first,
    all_last,
    all_spatial,
    all_gates,
    all_stream,
    all_heads,
    all_messages,
    all_sums,
    near_four,
    pair_four,
    far_four,
    grad_four,
    all_four,
    grad_three,
    low_three,
    low_joined,
    joined_rows,
    near_two,
    pair_two,
    far_two,
    grad_two,
    two_left,
    two_here,
    two_right,
    turned,
    strip,
    near_one,
    pair_one,
    far_one,
    grad_one,
    all_one,
    slots_four,
    slots_three,
    slots_two,
    slots_tile,
    slots_one,
    *rest,
):
    place = Place(images)
    sems = rest[-1]
    mail = Mail(sems)
    blk, batch = place.blk, place.batch
    tile, total = pre_one.shape[0], mask.shape[0]
    mid = pre_one.shape[1]
    slim = pre_two.shape[1]
    base = blk * tile
    red_shared = Reduce(mail, place, *rest[0:4], share_shared)
    red_last = Reduce(mail, place, *rest[4:8], all_last.at[blk])
    red_first = Reduce(mail, place, *rest[8:12], share_first)
    red_spatial = Reduce(mail, place, *rest[12:16], all_spatial.at[blk])
    red_gates = Reduce(mail, place, gate_grads, *rest[16:19], all_gates.at[blk])
    red_stream = Reduce(mail, place, stream_grads, *rest[19:22], all_stream.at[blk])
    share = share_shared.shape[0]
    results, sums_out, at = rest[22], rest[23], 24
    heads, messages = [], []

    def tiles_of(slots, first_row, count, own):
        rows_at = pl.ds(first_row, count)
        return Tiles(mail, place, lambda index: slots.at[index, rows_at], own)

    def slots_of(slots):
        return Tiles(mail, place, lambda index: slots.at[index])

    kept = head_grads.shape[0]
    for offset in range(kept):
        result = results.at[offset]
        reduce = ReduceFar(mail, place, head_grads.at[offset], *rest[at : at + 3], result)
        at += 3
        heads.append(Job(reduce, tiles_of(all_heads, offset * share, share, result)))
    heads += [Job(None, None)] * (9 - kept)
    early = message_share.shape[0] // share
    ends = [0, early // 3, 2 * early // 3, early]
    for begin_at, end_at in zip(ends[:-1], ends[1:]):
        count = (end_at - begin_at) * share
        own = message_share.at[pl.ds(begin_at * share, count)]
        messages.append(Job(None, tiles_of(all_messages, begin_at * share, count, own)))
    job_shared, job_first = Job(red_shared, None), Job(red_first, None)
    job_sums = Job(None, Tiles(mail, place, lambda index: all_sums.at[index], sums_out))
    job_last, job_spatial = Job(red_last, slots_of(all_last)), Job(red_spatial, slots_of(all_spatial))
    job_gates, job_stream = Job(red_gates, slots_of(all_gates)), Job(red_stream, slots_of(all_stream))
    greet(place.others + place.tiles)

    def slim_lanes(index):
        return pl.ds(pl.multiple_of(index * slim, slim), slim)

    def tile_rows(index):
        return pl.ds(pl.multiple_of(index * tile, tile), tile)

    def keep(row, bias_sum, gain_sum, channels):
        sums_out[row : row + 1, :channels] = gain_sum
        sums_out[row + 1 : row + 2, :channels] = bias_sum

    sums_out[...] = jnp.zeros_like(sums_out)
    sums_out[8:10, :] = task_sums[0:2, :]
    for cells in (two_left, two_here, two_right):
        clear_ends(cells, total)
    step(heads[0], heads[1], job_gates, job_stream)

    sum_over_tiles(
        mail, place, lambda index: back.at[:, slim_lanes(index)], near_four, pair_four, far_four, total, grad_four
    )
    sums = norm_back(stats, norms, mask, grad_four, pre_four, 6, slim, lambda rows: grad_four[rows, :])
    copies = send_sums(mail, place, slots_four, sums)
    step(heads[0], heads[1], job_gates, job_stream)
    step(heads[2], heads[3], heads[4])
    for offset in range(9):
        turned[offset * slim : (offset + 1) * slim, :] = spatial[offset].T
    for copy in copies:
        copy.wait_recv()
    bias_sum, gain_sum = add_up(slots_four)
    keep(6, bias_sum, gain_sum, slim)
    lanes = slim_lanes(blk)

    def put_four(rows, value):
        all_four[rows, lanes] = value

    def joined_back(rows):
        return dot_t(all_four[rows, :], shared[...])

    sums = []

    def make_four(first, size):
        through(
            stats, norms, mask, sizes, grad_four, pre_four, 6, slim, bias_sum, gain_sum, put_four, None, (first, size)
        )

    def use_four(first, size):
        sums.append(
            norm_back(
                stats, norms, mask, grad_three, pre_three, 4, mid, joined_back, None, wide, (first, size)
            )
        )

    share_pieces(
        mail,
        place,
        lambda index, first, size: all_four.at[pl.ds(first, size), slim_lanes(index)],
        total,
        make_four,
        use_four,
    )
    step(messages[0])
    sums = [sum(one[1:], one[0]) for one in zip(*sums)]
    copies = send_sums(mail, place, slots_three, sums)
    step(heads[2], heads[3], heads[4])
    step(heads[5], heads[6])
    step(heads[0], heads[1], job_gates, job_stream)
    step(messages[0])
    grads, lines = red_shared.grad, red_shared.grad.shape[0]
    grads[...] = t_dot(act_three[...], all_four[...]).astype(BF16).reshape(grads.shape)
    step(job_shared)

    def lower(rows):
        low_joined[rows, :] = grad_three[rows, :].astype(BF16)

    loop(total, CHUNK, lower)
    for copy in copies:
        copy.wait_recv()
    bias_sum, gain_sum = add_up(slots_three)
    keep(4, bias_sum, gain_sum, mid)

    def put_three(rows, value):
        low_three[rows, :] = value

    def two_part(rows):
        all_four[rows, :] = dot_t(low_three[rows, :], last[...]).astype(BF16)

    def make_two(first, size):
        through(
            stats, norms, mask, sizes, grad_three, pre_three, 4, mid, bias_sum, gain_sum, put_three, None, (first, size)
        )
        loop(size, BLOCK, two_part, first)

    sum_over_tiles(
        mail,
        place,
        lambda index: all_four.at[:, slim_lanes(index)],
        near_two,
        pair_two,
        far_two,
        total,
        grad_two,
        None,
        make_two,
    )
    step(messages[1])
    landing = joined_rows.at[:, pl.ds(pl.multiple_of(blk * mid, mid), mid)]
    joined_here = mail.local(low_joined.at[tile_rows(blk)], landing)
    joined_copies = [
        mail.send(low_joined.at[tile_rows(blk ^ mask_t)], landing, (blk ^ mask_t, batch))
        for mask_t in range(1, 4)
    ]
    sums = norm_back(stats, norms, mask, grad_two, pre_two, 2, slim, lambda rows: grad_two[rows, :])
    copies = send_sums(mail, place, slots_two, sums)
    step(heads[5], heads[6], job_shared)
    step(heads[7], heads[8])
    step(heads[2], heads[3], heads[4])
    grads = red_last.grad
    grads[...] = t_dot(act_two[...], low_three[...]).astype(BF16).reshape(grads.shape)
    step(job_last)
    for copy in copies:
        copy.wait_recv()
    bias_sum, gain_sum = add_up(slots_two)
    keep(2, bias_sum, gain_sum, slim)

    def put_two(rows, value):
        two_here[pl.ds(pl.multiple_of(rows.start + PITCH, 16), CHUNK), :] = value

    through(stats, norms, mask, sizes, grad_two, pre_two, 2, slim, bias_sum, gain_sum, put_two)
    widen(two_here, two_left, two_right, total)
    shifted = (two_left, two_here, two_right)

    def one_part(rows):
        for offset in range(9):
            row, col = 2 - offset // 3, 2 - offset % 3
            window = shifted[col][pl.ds(pl.multiple_of(rows.start + PITCH * row, 16), BLOCK), :]
            strip[:, offset * slim : (offset + 1) * slim] = window
        low_three[rows, :] = dot(strip[...], turned[...]).astype(BF16)

    loop(total, BLOCK, one_part)

    def spatial_grads():
        grads = red_spatial.grad
        for offset in range(9):
            row, col = 2 - offset // 3, 2 - offset % 3
            window = shifted[col][PITCH * row : PITCH * row + total, :]
            found = t_dot(act_one[PITCH : PITCH + total, :], window).astype(BF16)
            grads[:, :, :, offset * slim : (offset + 1) * slim] = found.reshape(grads.shape[:3] + (slim,))
        step(job_spatial)

    sum_over_tiles(
        mail,
        place,
        lambda index: low_three.at[tile_rows(index)],
        near_one,
        pair_one,
        far_one,
        tile,
        grad_one,
        spatial_grads,
    )
    step(messages[1])
    step(messages[2])
    step(heads[0], heads[1], job_gates, job_stream)
    sums = norm_back(stats, norms, mask, grad_one, pre_one, 0, mid, lambda rows: grad_one[rows, :], base)
    slots_tile[blk] = jnp.concatenate(sums, 0)
    swap_tile_sums(mail, place, slots_tile)
    copies = send_sums(mail, place, slots_one, list(add_up(slots_tile)))
    step(heads[7], heads[8], job_last, job_spatial)
    step(heads[5], heads[6], job_shared)
    for copy in copies:
        copy.wait_recv()
    bias_sum, gain_sum = add_up(slots_one)
    keep(0, bias_sum, gain_sum, mid)

    def put_one(rows, value):
        all_one[at_base(base, rows), :] = value

    def make_one(first, size):
        through(
            stats, norms, mask, sizes, grad_one, pre_one, 0, mid, bias_sum, gain_sum, put_one, base, (first, size)
        )

    def inputs_back():
        joined_here.wait()
        for copy in joined_copies:
            copy.wait_recv()

        def input_grads(rows):
            own = all_one[pl.ds(pl.multiple_of(base + rows.start, CHUNK), rows.size), :]
            grad_input[rows, :] = dot_t(own, first[...]) + joined_rows[rows, :].astype(F32)

        loop(tile, tile // 3, input_grads)

    share_pieces(
        mail,
        place,
        lambda index, first, size: all_one.at[
            pl.ds(pl.multiple_of(index * tile + first, CHUNK), size), :
        ],
        tile,
        make_one,
        None,
        inputs_back,
    )
    grads = red_first.grad
    grads[...] = t_dot(wide[...], all_one[...]).astype(BF16).reshape(grads.shape)
    step(job_first)
    step(messages[2], job_sums)
    step(heads[0], heads[1], job_gates, job_stream)
    step(heads[2], heads[3], heads[4], heads[5], heads[6])
    step(job_first)
    step(heads[2], heads[3], heads[4], heads[5], heads[6], job_sums)
    step(heads[7], heads[8], job_last, job_spatial)
    step(heads[7], heads[8], job_last, job_spatial)
    step(job_first)
    step(heads[7], heads[8], job_last, job_spatial)
    for job in messages + heads + [job_gates, job_stream, job_last, job_spatial, job_sums]:
        step(job)
    mail.close()


def bottleneck_back(nb, back, pres, stats, norms, mask, sizes, wide, acts, weights, gate_grads, stream_grads, task_grads):
    tile, total = pres[0].shape[0], mask.shape[0]
    mid = pres[0].shape[1]
    slim = mid // 4
    lines, share = nb // 2, mid // nb
    padded = total + 2 * PITCH
    width = weights[3].shape[0]

    def array(*shape, kind=BF16):
        return jax.ShapeDtypeStruct(shape, kind)

    def vmem(*shape, kind=BF16):
        return pltpu.VMEM(shape, kind)

    scratch = [
        vmem(2, total, slim),
        vmem(total, slim),
        vmem(total, slim),
        vmem(total, slim, kind=F32),
        vmem(total, mid),
        vmem(total, mid, kind=F32),
        vmem(total, mid),
        vmem(total, mid),
        vmem(tile, width),
        vmem(2, total, slim),
        vmem(total, slim),
        vmem(total, slim),
        vmem(total, slim, kind=F32),
        vmem(padded, slim),
        vmem(padded, slim),
        vmem(padded, slim),
        vmem(9 * slim, mid),
        vmem(BLOCK, 9 * slim),
        vmem(2, tile, mid),
        vmem(tile, mid),
        vmem(tile, mid),
        vmem(tile, mid, kind=F32),
        vmem(total, mid),
        vmem(nb, 2, slim, kind=F32),
        vmem(nb, 2, mid, kind=F32),
        vmem(nb, 2, slim, kind=F32),
        vmem(4, 2, mid, kind=F32),
        vmem(nb, 2, mid, kind=F32),
    ]
    for columns in (mid, mid, mid, 9 * slim):
        scratch += reduce_scratch(lines, share, columns, True)
    for columns in (mid, LANES):
        scratch += reduce_scratch(lines, share, columns, False)
    message_share, head_grads, task_sums = task_grads
    kept = head_grads.shape[0]
    scratch += [vmem(kept, share, mid), vmem(16, mid, kind=F32)]
    for _ in range(kept):
        scratch += reduce_scratch(lines, share, mid, False)
    scratch.append(DMA((2, 256)))
    return pl.pallas_call(
        functools.partial(backward_kernel, nb),
        out_shape=(
            array(tile, width, kind=F32),
            array(share, mid),
            array(share, mid),
            array(4, share, mid),
            array(4, share, 9 * slim),
            array(4, share, mid),
            array(4, share, LANES),
            array(4, kept * share, mid),
            array(4, message_share.shape[0], mid),
            array(4, 16, mid, kind=F32),
        ),
        in_specs=[VMEM] * 19 + [ANY] * 2 + [VMEM],
        out_specs=(VMEM,) * 7 + (ANY, ANY, VMEM),
        scratch_shapes=scratch,
        cost_estimate=LONG,
        compiler_params=pltpu.CompilerParams(
            collective_id=22, has_side_effects=True, vmem_limit_bytes=62 * 2**20
        ),
    )(
        back,
        *pres,
        stats,
        norms,
        mask,
        sizes,
        wide,
        *acts,
        *weights,
        gate_grads.reshape(lines, 2, share, mid),
        stream_grads.reshape(lines, 2, share, LANES),
        message_share,
        head_grads.reshape(kept, lines, 2, share, mid),
        task_sums,
    )


def finish_kernel(images, first, shared, rest, first_rows, shared_rows, all_rest, sems):
    place = Place(images)
    mail = Mail(sems)
    greet_owners(place)
    jobs = [
        Tiles(mail, place, lambda index: all_rest.at[index], rest),
        Owners(mail, place, first, first_rows),
        Owners(mail, place, shared, shared_rows),
    ]
    for job in jobs:
        job.start()
    for job in jobs:
        job.forward()
    for job in jobs:
        job.end()
    mail.close()


def finish(nb, first, shared, rest):
    share, mid = first.shape
    return pl.pallas_call(
        functools.partial(finish_kernel, nb),
        out_shape=(
            jax.ShapeDtypeStruct((4, share, mid), BF16),
            jax.ShapeDtypeStruct((4, share, mid), BF16),
            jax.ShapeDtypeStruct((4,) + rest.shape, BF16),
        ),
        in_specs=[ANY] * 3,
        out_specs=(ANY,) * 3,
        scratch_shapes=[DMA((2, 32))],
        compiler_params=pltpu.CompilerParams(collective_id=26, has_side_effects=True),
    )(first, shared, rest)


def task_kernel(
    images,
    early,
    shared_act,
    mask,
    mask_line,
    targets,
    sizes,
    norms,
    head,
    message_start,
    gate,
    to_depth,
    to_classes,
    from_gated,
    message_own,
    streams,
    slopes,
    pre_five,
    stats,
    grad_msg,
    grad_gate,
    gate_grads,
    stream_grads,
    message_grads,
    message_rest,
    message_end,
    left,
    right,
    task,
    messages,
    opened,
    gated,
    slots,
    slots_five,
    sems,
):
    place = Place(images)
    mail = Mail(sems)
    total = mask.shape[0]
    mid = pre_five.shape[1]
    is_first, is_last = place.blk == 0, place.blk == 3
    greet(place.others + [place.mate, place.across])
    late = message_end.shape[0]
    share = message_own.shape[2]
    got = [
        Spread(
            mail,
            place,
            message_own.at[place.blk, 9 - late + at],
            lambda index, at=at: message_end.at[at, pl.ds(pl.multiple_of(index * share, share), share), :],
        )
        for at in range(late)
    ]
    for one in got[: late // 2]:
        one.start()
    stats[...] = jnp.zeros_like(stats)
    for cells in (left, right, task, grad_msg):
        clear_ends(cells, total)
    widen(shared_act, left, right, total)

    def heads(rows):
        pre_five[rows, :] = conv_rows(
            (left, shared_act, right), rows, lambda offset, window: dot(window, head[offset]), False
        )

    loop(total, BLOCK, heads)

    def behind():
        for one in got[: late // 2]:
            one.forward()
        for one in got[late // 2 :]:
            one.start()

    batch_norm_stats(mail, place, pre_five, mask, slots_five, sizes, stats, 0, mid, behind)
    for one in got[late // 2 :]:
        one.forward()

    def act_task(rows):
        value = (pre_five[rows, :] - stats[0:1, :]) * stats[1:2, :] * norms[0:1, :] + norms[1:2, :]
        task[pl.ds(pl.multiple_of(PITCH + rows.start, 16), CHUNK), :] = (
            silu(value) * mask[rows, :]
        ).astype(BF16)

    loop(total, CHUNK, act_task)
    widen(task, left, right, total)
    for one in got:
        one.finish()

    def message_weight(offset):
        if offset < early:
            return message_start[offset]
        return head[9 + offset - early] if offset < 9 - late else message_end[offset - 9 + late]

    def here(rows):
        return pl.ds(pl.multiple_of(PITCH + rows.start, 16), rows.size)

    def send_messages(rows):
        messages[rows, :] = conv_rows(
            (left, task, right), rows, lambda offset, window: dot(window, message_weight(offset)), False
        )
        own = task[here(rows), :]
        opened[rows, :] = jax.nn.sigmoid(dot(own, gate[...]))
        part = (opened[rows, :] * messages[rows, :]).astype(BF16)
        gated[rows, :] = part
        depth_part = jnp.where(is_first, own, part)
        sem_part = jnp.where(is_last, own, part)
        slots[place.blk, :, rows] = dot_t(to_depth[...], depth_part) + dot_t(to_classes[...], sem_part)

    loop(total, BLOCK, send_messages)
    share_tiles(mail, place, lambda index: slots.at[index])
    classes = to_depth.shape[0]
    kind = lax.broadcasted_iota(jnp.int32, (classes, 2 * BLOCK), 0)

    def compare(rows):
        value = slots[0, :, rows] + slots[1, :, rows] + slots[2, :, rows] + slots[3, :, rows]
        streams[:, rows] = value
        is_class = (kind >= 1) & (kind <= CLASSES)
        top = jnp.max(jnp.where(is_class, value, -jnp.inf), 0, keepdims=True)
        power = jnp.where(is_class, jnp.exp(value - top), 0.0)
        chance = power / jnp.sum(power, 0, keepdims=True)
        label = targets[1:2, rows]
        chance = chance - jnp.where((kind - 1).astype(F32) == label, 1.0, 0.0)
        slope = jnp.where(kind == 0, value - targets[0:1, rows], jnp.where(is_class, chance, 0.0))
        slopes[:, rows] = (slope * mask_line[0:1, rows]).astype(BF16)

    loop(total, 2 * BLOCK, compare)
    by_part = dot(slopes[...], gated[...])
    by_task = dot(slopes[...], task[PITCH : PITCH + total, :])
    row = lax.broadcasted_iota(jnp.int32, by_part.shape, 0)
    use_task = ((row == 0) & is_first) | ((row > 0) & is_last)
    found = jnp.where(use_task, by_task, by_part)
    found = jnp.concatenate([found, jnp.zeros((LANES - classes, mid), F32)], 0)
    stream_grads[...] = found.T.astype(BF16)

    def grads(rows):
        grad = t_dot(slopes[:, rows], from_gated[...])
        open_part = opened[rows, :]
        grad_msg[here(rows), :] = (grad * open_part).astype(BF16)
        grad_gate[rows, :] = (grad * messages[rows, :] * open_part * (1.0 - open_part)).astype(BF16)

    loop(total, BLOCK, grads)
    gate_grads[...] = t_dot(task[PITCH : PITCH + total, :], grad_gate[...]).astype(BF16)
    widen(grad_msg, left, right, total)
    shifted = (left, grad_msg, right)
    for offset in range(9):
        row, col = 2 - offset // 3, 2 - offset % 3
        window = shifted[col][PITCH * row : PITCH * row + total, :]
        found = t_dot(task[PITCH : PITCH + total, :], window).astype(BF16)
        if offset < early:
            message_grads[offset] = found
        else:
            message_rest[:, (offset - early) * mid : (offset - early + 1) * mid] = found
    mail.close()


CLASSES = 40


def one_task(nb, early, late, shared_act, mask, mask_line, targets, sizes, norms, weights, streams_weights, own):
    total = mask.shape[0]
    padded, mid = shared_act.shape
    lines = streams_weights[0].shape[0]

    def array(*shape, kind=BF16):
        return jax.ShapeDtypeStruct(shape, kind)

    def vmem(*shape, kind=BF16):
        return pltpu.VMEM(shape, kind)

    return pl.pallas_call(
        functools.partial(task_kernel, nb, early),
        out_shape=(
            array(lines, total, kind=F32),
            array(lines, total),
            array(total, mid, kind=F32),
            array(8, mid, kind=F32),
            array(padded, mid),
            array(total, mid),
            array(mid, mid),
            array(mid, LANES),
            array(early, mid, mid),
            array(mid, (9 - early) * mid),
            array(late, mid, mid),
        ),
        in_specs=[VMEM] * 12 + [ANY],
        out_specs=(VMEM,) * 11,
        scratch_shapes=[
            vmem(padded, mid),
            vmem(padded, mid),
            vmem(padded, mid),
            vmem(total, mid, kind=F32),
            vmem(total, mid, kind=F32),
            vmem(total, mid),
            vmem(4, lines, total, kind=F32),
            vmem(nb, 2, mid, kind=F32),
            DMA((2, 64)),
        ],
        cost_estimate=LONG,
        compiler_params=pltpu.CompilerParams(
            collective_id=23, has_side_effects=True, vmem_limit_bytes=60 * 2**20
        ),
    )(shared_act, mask, mask_line, targets, sizes, norms, *weights, *streams_weights, own)


def task_back_kernel(
    images,
    early,
    shared_act,
    mask,
    sizes,
    norms,
    head,
    message_start,
    gate,
    message_end,
    from_direct,
    slopes,
    pre_five,
    stats,
    grad_msg,
    grad_gate,
    message_grads,
    back,
    head_grads,
    head_rest,
    message_done,
    sums_out,
    left,
    right,
    grad_five,
    grad,
    slots_five,
    *rest,
):
    place = Place(images)
    mail = Mail(rest[-1])
    sums_of = [
        Reduce(
            mail,
            place,
            message_grads.at[offset],
            *rest[3 * offset : 3 * offset + 3],
            message_done.at[offset],
        )
        for offset in range(early)
    ]
    total = mask.shape[0]
    late = message_end.shape[0]
    mid = pre_five.shape[1]
    greet(place.others)
    sums_out[...] = jnp.zeros_like(sums_out)
    sums_of[0].start()
    sums_of[1].start()
    for cells in (left, right, grad_five):
        clear_ends(cells, total)
    widen(grad_msg, left, right, total)

    def message_weight(offset):
        if offset < early:
            return message_start[offset]
        return head[9 + offset - early] if offset < 9 - late else message_end[offset - 9 + late]

    def task_grads(rows):
        found = conv_rows(
            (left, grad_msg, right), rows, lambda offset, window: dot_t(window, message_weight(offset)), True
        )
        found = found + dot_t(grad_gate[rows, :], gate[...])
        grad[rows, :] = found + t_dot(slopes[:, rows], from_direct[...])

    loop(total, BLOCK, task_grads)
    sums = norm_back(stats, norms, mask, grad, pre_five, 0, mid, lambda rows: grad[rows, :])
    copies = send_sums(mail, place, slots_five, sums)
    sums_of[0].middle()
    sums_of[1].middle()
    for one in sums_of[2:]:
        one.start()
    for copy in copies:
        copy.wait_recv()
    bias_sum, gain_sum = add_up(slots_five)
    sums_out[0:1, :] = gain_sum
    sums_out[1:2, :] = bias_sum

    def put(rows, value):
        grad_five[pl.ds(pl.multiple_of(PITCH + rows.start, 16), CHUNK), :] = value

    through(stats, norms, mask, sizes, grad, pre_five, 0, mid, bias_sum, gain_sum, put)
    widen(grad_five, left, right, total)
    shifted = (left, grad_five, right)

    def head_back(rows):
        back[rows, :] = conv_rows(
            shifted, rows, lambda offset, window: dot_t(window, head[offset]), True
        ).astype(BF16)

    loop(total, BLOCK, head_back)
    for one in sums_of[2:]:
        one.middle()
    sums_of[0].finish()
    sums_of[1].finish()
    for offset in range(9):
        row, col = 2 - offset // 3, 2 - offset % 3
        window = shifted[col][PITCH * row : PITCH * row + total, :]
        found = t_dot(shared_act[PITCH : PITCH + total, :], window).astype(BF16)
        kept = head_grads.shape[0]
        if offset < kept:
            head_grads[offset] = found
        else:
            head_rest[:, (offset - kept) * mid : (offset - kept + 1) * mid] = found
    for one in sums_of[2:]:
        one.finish()
    mail.close()


def one_task_back(nb, early, kept, shared_act, mask, sizes, norms, weights, from_direct, slopes, rest):
    total = mask.shape[0]
    padded, mid = shared_act.shape
    lines, share = nb // 2, mid // nb

    def array(*shape, kind=BF16):
        return jax.ShapeDtypeStruct(shape, kind)

    def vmem(*shape, kind=BF16):
        return pltpu.VMEM(shape, kind)

    return pl.pallas_call(
        functools.partial(task_back_kernel, nb, early),
        out_shape=(
            array(total, mid),
            array(kept, mid, mid),
            array(mid, (9 - kept) * mid),
            array(early, share, mid),
            array(8, mid, kind=F32),
        ),
        in_specs=[VMEM] * 15,
        out_specs=(VMEM,) * 5,
        scratch_shapes=[
            vmem(padded, mid),
            vmem(padded, mid),
            vmem(padded, mid),
            vmem(total, mid, kind=F32),
            vmem(nb, 2, mid, kind=F32),
        ]
        + early * reduce_scratch(lines, share, mid, False)
        + [DMA((2, 48))],
        cost_estimate=LONG,
        compiler_params=pltpu.CompilerParams(
            collective_id=24, has_side_effects=True, vmem_limit_bytes=60 * 2**20
        ),
    )(shared_act, mask, sizes, norms, *weights, from_direct, slopes, *rest)


def last_kernel(shares, sums, all_shares, all_sums, sems):
    place = Place(2)
    mail = Mail(sems)
    blk = place.blk
    greet([place.mate, place.across])
    here = [mail.local(shares, all_shares.at[blk]), mail.local(sums, all_sums.at[blk])]
    both = []
    for source, slots in ((sums, all_sums), (shares, all_shares)):
        far = mail.send(source, slots.at[blk], place.across)
        near = mail.send(source, slots.at[blk], place.mate)
        both.append((far, near, slots))
    for far, near, slots in both:
        far.wait_recv()
        passed = slots.at[blk ^ 2]
        last = mail.send(passed, passed, place.mate)
        near.wait_recv()
        last.wait_recv()
    for copy in here:
        copy.wait()
    mail.close()


def gather_last(shares, sums):
    return pl.pallas_call(
        last_kernel,
        out_shape=(
            jax.ShapeDtypeStruct((4,) + shares.shape, shares.dtype),
            jax.ShapeDtypeStruct((4,) + sums.shape, sums.dtype),
        ),
        in_specs=[ANY] * 2,
        out_specs=(ANY, ANY),
        scratch_shapes=[DMA((2, 16))],
        compiler_params=pltpu.CompilerParams(collective_id=25, has_side_effects=True),
    )(shares, sums)


def on_device(
    nt,
    nb,
    features,
    crop_rows,
    crop_cols,
    depth_target,
    labels,
    first_weight,
    spatial_weight,
    last_weight,
    shared_weight,
    head_weights,
    message_weights,
    gate_weights,
    depth_weight,
    class_weight,
    mid_gain,
    mid_bias,
    out_gain,
    out_bias,
):
    tile_rows, cols, width = features.shape[1:]
    tile = tile_rows * cols
    rows = tile_rows * nt
    pixels = rows * cols
    tasks = head_weights.shape[0]
    mid = first_weight.shape[1]
    share = mid // nb
    slim = mid // nt
    classes = class_weight.shape[1]
    blk, batch = lax.axis_index("blk"), lax.axis_index("batch")

    image_rows = lax.dynamic_index_in_dim(crop_rows, batch, 0, False)
    image_cols = lax.dynamic_index_in_dim(crop_cols, batch, 0, False)
    row_ids = jnp.arange(rows, dtype=jnp.int32)
    col_ids = jnp.arange(PITCH, dtype=jnp.int32)
    inside_grid = (row_ids[:, None] < image_rows) & (col_ids[None, :] < image_cols)
    inside_grid = inside_grid.astype(F32)
    inside_wide = inside_grid.reshape(rows * PITCH, 1)
    inside = inside_grid[:, :cols].reshape(pixels, 1)
    inside_tile = lax.dynamic_slice_in_dim(inside, blk * tile, tile, 0)
    sizes_flat = (crop_rows * crop_cols).astype(F32)
    valid_count = jnp.sum(sizes_flat)
    sizes = jnp.broadcast_to(sizes_flat[:, None, None], (nb, 1, mid))
    tile_counts = jnp.sum(inside.reshape(nt, tile), 1)
    tile_sizes = jnp.broadcast_to(tile_counts[:, None, None], (nt, 1, mid))
    image_size = jnp.maximum(jnp.sum(inside), 1.0)

    params = jnp.concatenate(
        [
            mid_gain.reshape(-1),
            mid_bias.reshape(-1),
            out_gain,
            out_bias,
            depth_weight,
            class_weight.reshape(-1),
        ]
    )
    room = -(-params.shape[0] // (16 * LANES)) * 16 * LANES
    small = jnp.pad(params, (0, room - params.shape[0])).reshape(-1, LANES)
    feat = jnp.pad(features[0], ((0, 0), (0, PITCH - cols), (0, 0))).reshape(tile_rows * PITCH, width)
    piece = shared_weight.shape[0] // nt
    order = [
        (t * nb + b, (b * nt // nb) * nb + (b % (nb // nt)) * nt + t)
        for t in range(nt)
        for b in range(nb)
    ]
    shared_own = lax.ppermute(
        lax.dynamic_slice_in_dim(shared_weight, blk * piece, piece, 0), ("blk", "batch"), order
    )
    pair = jnp.stack([depth_target[0], labels[0].astype(F32)])
    pair = jnp.pad(pair, ((0, 6), (0, 0), (0, PITCH - cols))).reshape(8, tile_rows * PITCH)
    full_first, smalls, targets, wide_features, spatial, pre_one, stats = begin(
        nb, first_weight, small, spatial_weight, pair, feat, inside_wide, sizes, tile_sizes
    )
    full_first = full_first.reshape(width, mid)
    smalls = smalls.reshape(nb, room)
    at = 0

    def taken(count):
        nonlocal at
        found = smalls[:, at : at + count]
        at += count
        return found

    norms_count = mid_gain.shape[0]
    out_share = out_gain.shape[0]
    gain_mid = taken(norms_count * share).reshape(nb, norms_count, share).swapaxes(0, 1)
    gain_mid = gain_mid.reshape(norms_count, mid).astype(F32)
    bias_mid = taken(norms_count * share).reshape(nb, norms_count, share).swapaxes(0, 1)
    bias_mid = bias_mid.reshape(norms_count, mid).astype(F32)
    gain_out = lax.dynamic_slice_in_dim(taken(out_share).reshape(width), blk * mid, mid, 0).astype(F32)
    bias_out = lax.dynamic_slice_in_dim(taken(out_share).reshape(width), blk * mid, mid, 0).astype(F32)
    full_depth = taken(share).reshape(mid, 1)
    full_classes = taken(share * classes).reshape(mid, classes)

    def slim_of(vector):
        return lax.dynamic_slice_in_dim(vector, blk * slim, slim, 0)

    def filled(vector):
        return jnp.pad(vector, (0, mid - vector.shape[0]))

    gain_two, bias_two = slim_of(gain_mid[1]), slim_of(bias_mid[1])
    gain_four, bias_four = slim_of(gain_mid[2]), slim_of(bias_mid[2])
    norms = jnp.stack(
        [
            gain_mid[0],
            bias_mid[0],
            filled(gain_two),
            filled(bias_two),
            gain_out,
            bias_out,
            filled(gain_four),
            filled(bias_four),
        ]
    )
    early, late = 5, 4
    large = jnp.concatenate(
        [
            lax.dynamic_index_in_dim(head_weights, blk, 0, False),
            lax.dynamic_index_in_dim(message_weights, blk, 0, False)[early : 9 - late],
        ],
        0,
    )
    large, stats = lax.optimization_barrier((large, stats))
    large = lax.all_gather(large, "batch", axis=1, tiled=True)
    (
        last,
        shared,
        gate,
        message_start,
        act_one,
        act_two,
        act_three,
        shared_act,
        pre_two,
        pre_three,
        pre_four,
        stats,
    ) = bottleneck(
        nb,
        early,
        pre_one,
        stats,
        spatial,
        wide_features,
        inside_wide,
        norms,
        sizes,
        last_weight,
        shared_own,
        gate_weights,
        message_weights,
    )

    task_norms = jnp.stack(
        [
            lax.dynamic_index_in_dim(gain_mid, 3 + blk, 0, False),
            lax.dynamic_index_in_dim(bias_mid, 3 + blk, 0, False),
        ]
    )
    task_norms = jnp.pad(task_norms, ((0, 6), (0, 0)))
    lines = -(-(1 + classes) // 16) * 16
    stream_weight = jnp.concatenate([full_depth, full_classes], 1).T
    stream_weight = jnp.pad(stream_weight, ((0, lines - 1 - classes), (0, 0)))
    is_depth = jnp.arange(lines)[:, None] == 0
    none = jnp.zeros((), BF16)
    is_first, is_last = blk == 0, blk == tasks - 1
    own_stream = jnp.where(is_depth, is_first, is_last)
    to_depth = jnp.where(is_depth, stream_weight, none)
    to_classes = jnp.where(is_depth, none, stream_weight)
    from_gated = jnp.where(own_stream, none, stream_weight)
    from_direct = jnp.where(own_stream, stream_weight, none)
    mask_line = jnp.broadcast_to(inside_wide.reshape(1, -1), (8, rows * PITCH))
    weights = (large, message_start, gate)
    (
        streams,
        slopes,
        pre_five,
        task_stats,
        grad_msg,
        grad_gate,
        gate_grads,
        stream_grads,
        message_grads,
        message_rest,
        message_end,
    ) = one_task(
        nb,
        early,
        late,
        shared_act,
        inside_wide,
        mask_line,
        targets,
        sizes,
        task_norms,
        weights,
        (to_depth, to_classes, from_gated),
        message_weights,
    )
    own_streams = lax.dynamic_slice_in_dim(streams, blk * tile_rows * PITCH, tile_rows * PITCH, 1)
    own_streams = own_streams.reshape(lines, tile_rows, PITCH)[:, :, :cols]
    depth_out = own_streams[0]
    logits = own_streams[1 : 1 + classes].transpose(1, 2, 0)
    rest_share = lax.psum_scatter(message_rest, "batch", scatter_dimension=0, tiled=True)
    message_grads = message_grads.reshape(early, nb // 2, 2, share, mid)
    kept = 7
    back, head_grads, head_rest, message_done, task_sums = one_task_back(
        nb,
        early,
        kept,
        shared_act,
        inside_wide,
        sizes,
        task_norms,
        weights + (message_end,),
        from_direct,
        slopes,
        (pre_five, task_stats, grad_msg, grad_gate, message_grads),
    )
    message_share = message_done.reshape(early * share, mid)
    head_share = lax.psum_scatter(head_rest, "batch", scatter_dimension=0, tiled=True)

    (
        grad_input,
        share_shared,
        share_first,
        all_last,
        all_spatial,
        all_gates,
        all_stream,
        all_heads,
        all_messages,
        sums,
    ) = bottleneck_back(
        nb,
        back,
        (pre_one, pre_two, pre_three, pre_four),
        stats,
        norms,
        inside_wide,
        sizes,
        wide_features,
        (act_one, act_two, act_three),
        (spatial, last, shared, full_first),
        gate_grads,
        stream_grads,
        (message_share, head_grads, task_sums),
    )
    grad_input = grad_input.reshape(tile_rows, PITCH, width)[:, :cols]

    rest_share, head_share, share_first = lax.optimization_barrier((rest_share, head_share, share_first))
    rest_share = jnp.concatenate([rest_share, head_share], 1)
    left = 18 - early - kept
    rest_share = rest_share.reshape(share, left, mid).swapaxes(0, 1).reshape(left * share, mid)
    red_first, red_shared, all_rest = finish(nb, share_first, share_shared, rest_share)
    red_first = red_first.astype(F32).reshape(nt * share, mid)
    red_shared = red_shared.astype(F32).reshape(nt * share, mid)
    all_rest = all_rest.reshape(nt, left, share, mid)
    red_messages = jnp.concatenate(
        [all_messages.reshape(nt, early, share, mid), all_rest[:, : 9 - early]], 1
    ).astype(F32)
    red_last = all_last.astype(F32).transpose(1, 0, 2).reshape(share, width)
    red_gates = all_gates.astype(F32)
    red_spatial = all_spatial.astype(F32).reshape(nt, share, 9, slim)
    red_spatial = red_spatial.transpose(2, 1, 0, 3).reshape(9, share, mid)
    streams_red = jnp.sum(all_stream.astype(F32), 0)
    red_depth = streams_red[:, 0]
    red_classes = streams_red[:, 1 : 1 + classes]
    red_heads = jnp.concatenate(
        [all_heads.reshape(nt, kept, share, mid), all_rest[:, 9 - early :]], 1
    ).astype(F32)
    two_gain, two_bias = sums[:, 2, :slim].reshape(1, mid), sums[:, 3, :slim].reshape(1, mid)
    four_gain, four_bias = sums[:, 6, :slim].reshape(1, mid), sums[:, 7, :slim].reshape(1, mid)
    mid_gains = jnp.concatenate([sums[0, 0:1], two_gain, four_gain, sums[:, 8]], 0)
    mid_biases = jnp.concatenate([sums[0, 1:2], two_bias, four_bias, sums[:, 9]], 0)
    grad_mid_gain = lax.dynamic_slice_in_dim(mid_gains, batch * share, share, 1)
    grad_mid_bias = lax.dynamic_slice_in_dim(mid_biases, batch * share, share, 1)
    grad_out_gain = lax.dynamic_slice_in_dim(sums[:, 4].reshape(width), batch * out_share, out_share, 0)
    grad_out_bias = lax.dynamic_slice_in_dim(sums[:, 5].reshape(width), batch * out_share, out_share, 0)
    return (
        depth_out.reshape(1, tile_rows, cols),
        logits.reshape(1, tile_rows, cols, classes),
        grad_input.reshape(1, tile_rows, cols, width),
        red_first,
        red_spatial,
        red_last,
        red_shared,
        red_heads,
        red_messages,
        red_gates,
        red_depth,
        red_classes,
        grad_mid_gain,
        grad_mid_bias,
        grad_out_gain,
        grad_out_bias,
    )


def solution(mesh):
    nt, nb = mesh.shape["blk"], mesh.shape["batch"]
    placed = (
        P("batch", "blk", None, None),
        P(),
        P(),
        P("batch", "blk", None),
        P("batch", "blk", None),
        P("batch", None),
        P(None, "batch", None),
        P("batch", None),
        P("batch", None),
        P(None, None, "batch", None),
        P(None, None, "batch", None),
        P(None, "batch", None),
        P("batch"),
        P("batch", None),
        P(None, "batch"),
        P(None, "batch"),
        P("batch"),
        P("batch"),
    )
    return jax.shard_map(
        functools.partial(on_device if nb == 8 else on_device_any, nt, nb),
        mesh=mesh,
        in_specs=placed,
        out_specs=(
            P("batch", "blk", None),
            P("batch", "blk", None, None),
            P("batch", "blk", None, None),
            P("batch", None),
            P(None, "batch", None),
            P("batch", None),
            P("batch", None),
            P(None, None, "batch", None),
            P(None, None, "batch", None),
            P(None, "batch", None),
            P("batch"),
            P("batch", None),
            P(None, "batch"),
            P(None, "batch"),
            P("batch"),
            P("batch"),
        ),
        check_vma=False,
    )
```

```python
import functools

import jax
import jax.numpy as jnp
from jax import lax
from jax.experimental import pallas as pl
from jax.experimental.pallas import tpu as pltpu
from jax.sharding import PartitionSpec as P

EPSILON = 1e-05
MESH = pl.DeviceIdType.MESH
BF16 = jnp.bfloat16
F32 = jnp.float32
LANES = 128


def greet(peers):
    barrier = pltpu.get_barrier_semaphore()
    for peer in peers:
        pl.semaphore_signal(barrier, inc=1, device_id=peer, device_id_type=MESH)
    pl.semaphore_wait(barrier, len(peers))


def send(src, dst, send_sem, recv_sem, peer):
    copy = pltpu.make_async_remote_copy(
        src_ref=src,
        dst_ref=dst,
        send_sem=send_sem,
        recv_sem=recv_sem,
        device_id=peer,
        device_id_type=MESH,
    )
    copy.start()
    return copy


def first_kernel(images, weight, small, full, smalls, own, zs, xs, cs, ps):
    blk, batch = lax.axis_index("blk"), lax.axis_index("batch")
    half = weight.shape[0] // 2
    rows = pl.ds(pl.multiple_of(lax.rem(blk, 2) * half, half), half)
    side = (blk, batch ^ 1)
    mate = (blk ^ 1, batch)
    lines = range(1, images // 2)
    others = [(blk, batch ^ mask) for mask in range(1, images)]
    greet(others + [mate])
    copies = []
    here = pltpu.make_async_copy(weight, full.at[batch], own.at[0])
    here.start()
    here_small = pltpu.make_async_copy(small, smalls.at[batch], own.at[1])
    here_small.start()
    z_copies = {}
    for mask in lines:
        z_copies[mask] = send(
            weight.at[rows],
            full.at[batch, rows],
            zs.at[0, mask],
            zs.at[1, mask],
            (blk, batch ^ (2 * mask)),
        )
    x_copies = {
        0: send(weight.at[rows], full.at[batch, rows], xs.at[0, 0], xs.at[1, 0], side)
    }
    for place, peer in enumerate(others):
        copies.append(
            send(small, smalls.at[batch], ps.at[0, place], ps.at[1, place], peer)
        )
    core_copies = []

    def hand_over(source, mask):
        block = full.at[source, rows]
        core_copies.append(send(block, block, cs.at[0, mask], cs.at[1, mask], mate))

    for mask in lines:
        z_copies[mask].wait_recv()
        source = batch ^ (2 * mask)
        block = full.at[source, rows]
        x_copies[mask] = send(block, block, xs.at[0, mask], xs.at[1, mask], side)
        hand_over(source, 2 * mask)
    for mask in range(images // 2):
        x_copies[mask].wait_recv()
        hand_over(batch ^ (2 * mask + 1), 2 * mask + 1)
    for copy in core_copies + copies:
        copy.wait()
    for mask in lines:
        z_copies[mask].wait_send()
    for mask in range(images // 2):
        x_copies[mask].wait_send()
    here.wait()
    here_small.wait()


def gather_first(weight, small, images):
    any_place = pl.BlockSpec(memory_space=pl.ANY)
    dma = pltpu.SemaphoreType.DMA
    return pl.pallas_call(
        functools.partial(first_kernel, images),
        out_shape=(
            jax.ShapeDtypeStruct((images,) + weight.shape, weight.dtype),
            jax.ShapeDtypeStruct((images,) + small.shape, small.dtype),
        ),
        in_specs=[any_place] * 2,
        out_specs=(any_place, any_place),
        scratch_shapes=[
            dma((2,)),
            dma((2, images)),
            dma((2, images)),
            dma((2, images)),
            dma((2, images)),
        ],
        compiler_params=pltpu.CompilerParams(collective_id=0, has_side_effects=True),
    )(weight, small)


def tiles_kernel(block, every, own, sems):
    blk, batch = lax.axis_index("blk"), lax.axis_index("batch")
    mate, across = (blk ^ 1, batch), (blk ^ 2, batch)
    greet([mate, across])
    far = send(block, every.at[blk], sems.at[0, 0], sems.at[1, 0], across)
    near = send(block, every.at[blk], sems.at[0, 1], sems.at[1, 1], mate)
    here = pltpu.make_async_copy(block, every.at[blk], own.at[0])
    here.start()
    far.wait_recv()
    passed = every.at[blk ^ 2]
    last = send(passed, passed, sems.at[0, 2], sems.at[1, 2], mate)
    near.wait()
    last.wait()
    far.wait_send()
    here.wait()


def gather_tiles(block, ident):
    any_place = pl.BlockSpec(memory_space=pl.ANY)
    dma = pltpu.SemaphoreType.DMA
    return pl.pallas_call(
        tiles_kernel,
        out_shape=jax.ShapeDtypeStruct((4,) + block.shape, block.dtype),
        in_specs=[any_place],
        out_specs=any_place,
        scratch_shapes=[dma((1,)), dma((2, 3))],
        compiler_params=pltpu.CompilerParams(collective_id=ident, has_side_effects=True),
    )(block)


def sum_kernel(parts, total, near_in, pair, far_in, sems):
    blk, batch = lax.axis_index("blk"), lax.axis_index("batch")
    mate, across = (blk ^ 1, batch), (blk ^ 2, batch)
    greet([mate, across])
    far_first = send(parts.at[blk ^ 3], near_in.at[0], sems.at[0, 0], sems.at[1, 0], mate)
    near_next = send(parts.at[blk ^ 1], near_in.at[1], sems.at[0, 1], sems.at[1, 1], mate)
    far_first.wait_recv()
    pair[...] = (parts[blk ^ 2].astype(F32) + near_in[0].astype(F32)).astype(pair.dtype)
    far = send(pair, far_in, sems.at[0, 2], sems.at[1, 2], across)
    near_next.wait_recv()
    total[...] = parts[blk].astype(F32) + near_in[1].astype(F32)
    far.wait_recv()
    total[...] += far_in[...].astype(F32)
    far_first.wait_send()
    near_next.wait_send()
    far.wait_send()


def sum_tiles(parts, ident):
    dma = pltpu.SemaphoreType.DMA
    block = parts.shape[1:]
    vmem = pl.BlockSpec(memory_space=pltpu.VMEM)
    return pl.pallas_call(
        sum_kernel,
        out_shape=jax.ShapeDtypeStruct(block, F32),
        in_specs=[vmem],
        out_specs=vmem,
        scratch_shapes=[
            pltpu.VMEM((2,) + block, parts.dtype),
            pltpu.VMEM(block, parts.dtype),
            pltpu.VMEM(block, parts.dtype),
            dma((2, 3)),
        ],
        compiler_params=pltpu.CompilerParams(
            collective_id=ident, has_side_effects=True, vmem_limit_bytes=32 * 2**20
        ),
    )(parts)


def combine(slots, weights, half, centred):
    count = slots.shape[0]
    if not centred:
        total = slots[0]
        for at in range(1, count):
            total = total + slots[at]
        return total
    size = weights[0]
    mean = slots[0, :half] * weights[0]
    for at in range(1, count):
        size = size + weights[at]
        mean = mean + slots[at, :half] * weights[at]
    mean = mean / size
    spread = None
    for at in range(count):
        gap = slots[at, :half] - mean
        term = slots[at, half : 2 * half] + weights[at] * gap * gap
        spread = term if spread is None else spread + term
    rest = [jnp.zeros((slots.shape[1] - 2 * half, LANES), F32)] * (slots.shape[1] > 2 * half)
    return jnp.concatenate([mean, spread] + rest, 0)


def sums_kernel(images, half, centred, tiled, own, tile_sizes, sizes, total, *scratch):
    blk, batch = lax.axis_index("blk"), lax.axis_index("batch")
    slots, sems = scratch[0], scratch[1]
    peers = [(blk, batch ^ mask) for mask in range(1, images)]
    mates = [(blk ^ mask, batch) for mask in range(1, 4)] if tiled else []
    greet(peers + mates)
    if tiled:
        tile_slots, tile_sems = scratch[2], scratch[3]
        tile_slots[blk] = own[...]
        copies = [
            send(own, tile_slots.at[blk], tile_sems.at[0, at], tile_sems.at[1, at], peer)
            for at, peer in enumerate(mates)
        ]
        for copy in copies:
            copy.wait()
        slots[batch] = combine(tile_slots, tile_sizes, half, centred)
    else:
        slots[batch] = own[...]
    copies = [
        send(slots.at[batch], slots.at[batch], sems.at[0, at], sems.at[1, at], peer)
        for at, peer in enumerate(peers)
    ]
    for copy in copies:
        copy.wait()
    total[...] = combine(slots, sizes, half, centred)


def all_sums(first, second, tile_sizes, sizes, centred, tiled, ident):
    images = sizes.shape[0]
    channels = first.shape[0]
    half = channels // LANES
    rows = -(-2 * half // 8) * 8
    own = jnp.concatenate(
        [first, second, jnp.zeros(((rows - 2 * half) * LANES,), F32)]
    ).reshape(rows, LANES)
    dma = pltpu.SemaphoreType.DMA
    vmem = pl.BlockSpec(memory_space=pltpu.VMEM)
    scratch = [pltpu.VMEM((images, rows, LANES), F32), dma((2, images))]
    if tiled:
        scratch += [pltpu.VMEM((4, rows, LANES), F32), dma((2, 3))]
    total = pl.pallas_call(
        functools.partial(sums_kernel, images, half, centred, tiled),
        out_shape=jax.ShapeDtypeStruct((rows, LANES), F32),
        in_specs=[vmem] * 3,
        out_specs=vmem,
        scratch_shapes=scratch,
        compiler_params=pltpu.CompilerParams(collective_id=ident, has_side_effects=True),
    )(own, sizes if tile_sizes is None else tile_sizes, sizes)
    flat = total.reshape(-1)
    return flat[:channels], flat[channels : 2 * channels]


def silu_slope(values):
    sigmoid_value = jax.nn.sigmoid(values)
    return sigmoid_value * (1.0 + values * (1.0 - sigmoid_value))


def windows(cells, rows, cols, back):
    channels = cells.shape[1]
    padded = jnp.pad(cells.reshape(rows, cols, channels), ((1, 1), (1, 1), (0, 0)))
    taken = []
    for offset in range(9):
        row, col = offset // 3, offset % 3
        if back:
            row, col = 2 - row, 2 - col
        taken.append(padded[row : row + rows, col : col + cols].reshape(rows * cols, channels))
    return jnp.concatenate(taken, 1)


def dot(left, right):
    return jnp.dot(left, right, preferred_element_type=F32)


def dot_t(left, right):
    return jnp.einsum("pd,cd->pc", left, right, preferred_element_type=F32)


def t_dot(left, right):
    return jnp.einsum("pc,pd->cd", left, right, preferred_element_type=F32)


def on_device_any(
    nt,
    nb,
    features,
    crop_rows,
    crop_cols,
    depth_target,
    labels,
    first_weight,
    spatial_weight,
    last_weight,
    shared_weight,
    head_weights,
    message_weights,
    gate_weights,
    depth_weight,
    class_weight,
    mid_gain,
    mid_bias,
    out_gain,
    out_bias,
):
    tile_rows, cols, width = features.shape[1:]
    tile = tile_rows * cols
    rows = tile_rows * nt
    pixels = rows * cols
    tasks = head_weights.shape[0]
    mid = first_weight.shape[1]
    share = mid // nb
    slim = mid // nt
    piece = width // (nb * nt)
    wide = nb * piece
    classes = class_weight.shape[1]
    blk, batch = lax.axis_index("blk"), lax.axis_index("batch")

    image_rows = lax.dynamic_index_in_dim(crop_rows, batch, 0, False)
    image_cols = lax.dynamic_index_in_dim(crop_cols, batch, 0, False)
    row_ids = jnp.arange(rows, dtype=jnp.int32)
    col_ids = jnp.arange(cols, dtype=jnp.int32)
    inside_grid = (row_ids[:, None] < image_rows) & (col_ids[None, :] < image_cols)
    inside = inside_grid.astype(F32).reshape(pixels, 1)
    inside_tile = lax.dynamic_slice_in_dim(inside, blk * tile, tile, 0)
    sizes_flat = (crop_rows * crop_cols).astype(F32)
    valid_count = jnp.sum(sizes_flat)
    sizes = jnp.broadcast_to(sizes_flat[:, None, None], (nb, 1, LANES))
    tile_counts = jnp.sum(inside.reshape(nt, tile), 1)
    tile_sizes = jnp.broadcast_to(tile_counts[:, None, None], (nt, 1, LANES))
    image_size = jnp.maximum(jnp.sum(inside), 1.0)
    tile_size = jnp.maximum(jnp.sum(inside_tile), 1.0)

    params = jnp.concatenate(
        [
            mid_gain.reshape(-1),
            mid_bias.reshape(-1),
            out_gain,
            out_bias,
            depth_weight,
            class_weight.reshape(-1),
        ]
    )
    room = -(-params.shape[0] // (16 * LANES)) * 16 * LANES
    small = jnp.pad(params, (0, room - params.shape[0])).reshape(-1, LANES)
    full_first, smalls = gather_first(first_weight, small, nb)
    full_first = full_first.reshape(width, mid)
    smalls = smalls.reshape(nb, room)
    at = 0

    def taken(count):
        nonlocal at
        found = smalls[:, at : at + count]
        at += count
        return found

    norms = mid_gain.shape[0]
    gain_mid = taken(norms * share).reshape(nb, norms, share).swapaxes(0, 1)
    gain_mid = gain_mid.reshape(norms, mid).astype(F32)
    bias_mid = taken(norms * share).reshape(nb, norms, share).swapaxes(0, 1)
    bias_mid = bias_mid.reshape(norms, mid).astype(F32)
    gain_out = lax.dynamic_index_in_dim(taken(nt * piece).reshape(nb, nt, piece), blk, 1, False)
    gain_out = gain_out.reshape(wide).astype(F32)
    bias_out = lax.dynamic_index_in_dim(taken(nt * piece).reshape(nb, nt, piece), blk, 1, False)
    bias_out = bias_out.reshape(wide).astype(F32)
    full_depth = taken(share).reshape(mid, 1)
    full_classes = taken(share * classes).reshape(mid, classes)
    stream_weight = jnp.concatenate([full_depth, full_classes], 1)

    spatial = lax.all_gather(
        lax.dynamic_slice_in_dim(spatial_weight, blk * slim, slim, 2), "batch", axis=1, tiled=True
    )
    last = lax.dynamic_index_in_dim(last_weight.reshape(share, nb, nt, piece), blk, 2, False)
    last = lax.all_gather(last.reshape(share, wide), "batch", axis=0, tiled=True)
    shared = lax.dynamic_slice_in_dim(shared_weight, blk * piece, piece, 0)
    shared = lax.all_gather(shared, "batch", axis=0, tiled=True)
    head = lax.all_gather(
        lax.dynamic_index_in_dim(head_weights, blk, 0, False), "batch", axis=1, tiled=True
    )
    message = lax.all_gather(
        lax.dynamic_index_in_dim(message_weights, blk, 0, False), "batch", axis=1, tiled=True
    )
    gate = lax.all_gather(
        lax.dynamic_index_in_dim(gate_weights, blk, 0, False), "batch", axis=0, tiled=True
    )

    flat_features = features.reshape(tile, width)
    cut = flat_features.reshape(tile, nb, nt, piece).transpose(2, 0, 1, 3).reshape(nt, tile, wide)
    wide_features = swap_tiles(cut, blk, nt)

    def slim_of(vector):
        return lax.dynamic_slice_in_dim(vector, blk * slim, slim, 0)

    def normalize(values, mask, local_size, gain, bias, tiled, ident):
        mean = jnp.sum(values * mask, 0) / local_size
        gap = values - mean
        spread = jnp.sum(gap * gap * mask, 0)
        centre, total = all_sums(mean, spread, tile_sizes, sizes, True, tiled, ident)
        inverse = lax.rsqrt(total / valid_count + EPSILON)
        normed = (values - centre) * inverse
        return normed * gain + bias, normed, inverse

    def normalize_back(grad, normed, inverse, gain, mask, tiled, ident):
        bias_sum, gain_sum = all_sums(
            jnp.sum(grad, 0), jnp.sum(grad * normed, 0), tile_sizes, sizes, False, tiled, ident
        )
        back = (
            inverse * gain * (grad - bias_sum / valid_count - normed * gain_sum / valid_count) * mask
        )
        return back.astype(BF16), gain_sum, bias_sum

    def act(values, mask):
        return (jax.nn.silu(values) * mask).astype(BF16)

    def by_rows(blocks):
        return blocks.reshape(pixels, blocks.shape[2])

    def by_channels(blocks):
        return blocks.swapaxes(0, 1).reshape(pixels, nt * blocks.shape[2])

    def cut_channels(values):
        return values.astype(BF16).reshape(pixels, nt, slim).swapaxes(0, 1)

    pre_one = dot(flat_features, full_first)
    norm_one, normed_one, inverse_one = normalize(
        pre_one, inside_tile, tile_size, gain_mid[0], bias_mid[0], True, 1
    )
    act_one = by_rows(gather_tiles(act(norm_one, inside_tile), 2))
    pre_two = dot(windows(act_one, rows, cols, False), spatial.reshape(9 * mid, slim))
    gain_two, bias_two = slim_of(gain_mid[1]), slim_of(bias_mid[1])
    norm_two, normed_two, inverse_two = normalize(
        pre_two, inside, image_size, gain_two, bias_two, False, 3
    )
    act_two = by_channels(gather_tiles(act(norm_two, inside), 4))
    pre_three = dot(act_two, last)
    norm_three, normed_three, inverse_three = normalize(
        pre_three, inside, image_size, gain_out, bias_out, False, 5
    )
    joined = norm_three + wide_features.astype(F32)
    act_three = act(joined, inside)
    pre_four = sum_tiles(cut_channels(dot(act_three, shared)), 6)
    gain_four, bias_four = slim_of(gain_mid[2]), slim_of(bias_mid[2])
    norm_four, normed_four, inverse_four = normalize(
        pre_four, inside, image_size, gain_four, bias_four, False, 3
    )
    shared_act = by_channels(gather_tiles(act(norm_four, inside), 4))

    gain_task = lax.dynamic_index_in_dim(gain_mid, 3 + blk, 0, False)
    bias_task = lax.dynamic_index_in_dim(bias_mid, 3 + blk, 0, False)
    pre_five = dot(windows(shared_act, rows, cols, False), head.reshape(9 * mid, mid))
    norm_five, normed_five, inverse_five = normalize(
        pre_five, inside, image_size, gain_task, bias_task, False, 5
    )
    task_act = act(norm_five, inside)
    messages = dot(windows(task_act, rows, cols, False), message.reshape(9 * mid, mid))
    gate_open = jax.nn.sigmoid(dot(task_act, gate))
    gated = (gate_open * messages).astype(BF16)
    is_first, is_last = blk == 0, blk == tasks - 1
    depth_part = jnp.where(is_first, task_act, gated)
    sem_part = jnp.where(is_last, task_act, gated)
    depth_share = jnp.einsum("pc,co->op", depth_part, full_depth, preferred_element_type=F32)
    class_share = jnp.einsum("pc,co->op", sem_part, full_classes, preferred_element_type=F32)
    lift = -(-(1 + classes) // 8) * 8 - 1 - classes
    shares = jnp.concatenate([depth_share, class_share, jnp.zeros((lift, pixels), F32)], 0)
    streams = jnp.sum(gather_tiles(shares, 7), 0).T
    depth_out = lax.dynamic_slice_in_dim(streams, blk * tile, tile, 0)[:, 0]
    logits = lax.dynamic_slice_in_dim(streams, blk * tile, tile, 0)[:, 1 : 1 + classes]
    targets = by_rows(gather_tiles_pair(depth_target, labels, tile))
    all_depth, all_logits = streams[:, :1], streams[:, 1 : 1 + classes]
    depth_slope = ((all_depth - targets[:, :1]) * inside).astype(BF16)
    onehot = (targets[:, 1:2] == jnp.arange(classes, dtype=jnp.int32)[None, :].astype(F32)).astype(F32)
    logit_slope = ((jax.nn.softmax(all_logits, axis=1) - onehot) * inside).astype(BF16)
    grad_depth = t_dot(depth_part, depth_slope)
    grad_classes = t_dot(sem_part, logit_slope)
    depth_back = depth_slope.astype(F32) * full_depth.astype(F32).reshape(1, mid)
    sem_back = dot_t(logit_slope, full_classes)
    zero = jnp.zeros((), F32)
    grad_gated = jnp.where(is_first, zero, depth_back) + jnp.where(is_last, zero, sem_back)
    grad_direct = jnp.where(is_first, depth_back, zero) + jnp.where(is_last, sem_back, zero)

    grad_msg = (grad_gated * gate_open).astype(BF16)
    grad_gate = (grad_gated * messages * gate_open * (1.0 - gate_open)).astype(BF16)
    msg_windows = windows(grad_msg, rows, cols, True)
    gate_grads = t_dot(task_act, grad_gate).astype(BF16)
    message_grads = t_dot(task_act, msg_windows).astype(BF16)
    share_messages = lax.psum_scatter(message_grads, "batch", scatter_dimension=0, tiled=True)
    task_grad = (
        grad_direct
        + dot_t(grad_gate, gate)
        + dot(msg_windows, message.swapaxes(1, 2).reshape(9 * mid, mid))
    )
    grad_norm_five = task_grad * inside * silu_slope(norm_five)
    grad_pre_five, gain_sum_five, bias_sum_five = normalize_back(
        grad_norm_five, normed_five, inverse_five, gain_task, inside, False, 8
    )
    five_windows = windows(grad_pre_five, rows, cols, True)
    head_grads = t_dot(shared_act, five_windows).astype(BF16)
    share_heads = lax.psum_scatter(head_grads, "batch", scatter_dimension=0, tiled=True)
    shared_back = dot(five_windows, head.swapaxes(1, 2).reshape(9 * mid, mid))
    shared_back = sum_tiles(cut_channels(shared_back), 6)

    grad_norm_four = shared_back * inside * silu_slope(norm_four)
    grad_pre_four, gain_sum_four, bias_sum_four = normalize_back(
        grad_norm_four, normed_four, inverse_four, gain_four, inside, False, 9
    )
    grad_four = by_channels(gather_tiles(grad_pre_four, 4))
    shared_grads = t_dot(act_three, grad_four).astype(BF16)
    grad_joined = dot_t(grad_four, shared) * inside * silu_slope(joined)
    grad_three, gain_sum_three, bias_sum_three = normalize_back(
        grad_joined, normed_three, inverse_three, gain_out, inside, False, 8
    )
    last_grads = t_dot(act_two, grad_three).astype(BF16)
    two_back = sum_tiles(cut_channels(dot_t(grad_three, last)), 6)
    grad_norm_two = two_back * inside * silu_slope(norm_two)
    grad_two, gain_sum_two, bias_sum_two = normalize_back(
        grad_norm_two, normed_two, inverse_two, gain_two, inside, False, 9
    )
    two_windows = windows(grad_two, rows, cols, True)
    spatial_grads = t_dot(act_one, two_windows).astype(BF16)
    one_back = dot(two_windows, spatial.swapaxes(1, 2).reshape(9 * slim, mid))
    one_back = sum_tiles(one_back.astype(BF16).reshape(nt, tile, mid), 10)
    grad_norm_one = one_back * inside_tile * silu_slope(norm_one)
    grad_one, gain_sum_one, bias_sum_one = normalize_back(
        grad_norm_one, normed_one, inverse_one, gain_mid[0], inside_tile, True, 11
    )
    all_one = by_rows(gather_tiles(grad_one, 2))
    first_grads = t_dot(wide_features, all_one).astype(BF16)
    joined_tiles = swap_tiles(grad_joined.astype(BF16).reshape(nt, tile, wide), blk, nt)
    joined_tiles = joined_tiles.reshape(nt, tile, nb, piece).transpose(1, 2, 0, 3).reshape(tile, width)
    grad_input = dot_t(grad_one, full_first) + joined_tiles.astype(F32)

    stream_grads = jnp.concatenate([grad_depth, grad_classes], 1)
    stream_grads = jnp.pad(stream_grads, ((0, 0), (0, LANES - 1 - classes))).astype(BF16)
    late = jnp.concatenate(
        [spatial_grads, shared_grads.reshape(nb, piece, mid).reshape(mid, -1),
         last_grads, first_grads.reshape(mid, -1), gate_grads, stream_grads],
        1,
    )
    late_share = lax.psum_scatter(late, "batch", scatter_dimension=0, tiled=True)
    early_share = jnp.concatenate([share_messages, share_heads], 1)
    early = lax.all_gather(early_share, "blk", axis=0, tiled=False).astype(F32)
    late_all = gather_tiles(late_share, 12).astype(F32)
    early = early.reshape(nt, share, 2, 9, mid).transpose(2, 0, 3, 1, 4)
    red_messages, red_heads = early[0], early[1]
    at = 0

    def part(count):
        nonlocal at
        found = late_all[:, :, at : at + count]
        at += count
        return found

    red_spatial = part(9 * slim).reshape(nt, share, 9, slim).transpose(2, 1, 0, 3).reshape(9, share, mid)
    red_shared = part(wide * mid // mid).reshape(nt * piece, mid)
    red_last = part(wide).reshape(nt, share, nb, piece).transpose(1, 2, 0, 3).reshape(share, width)
    red_first = part(wide * mid // mid).reshape(nt * piece, mid)
    red_gates = part(mid)
    streams_red = jnp.sum(part(LANES), 0)
    red_depth = streams_red[:, 0]
    red_classes = streams_red[:, 1 : 1 + classes]

    sums = jnp.concatenate(
        [
            gain_sum_five,
            bias_sum_five,
            gain_sum_three,
            bias_sum_three,
            gain_sum_two,
            bias_sum_two,
            gain_sum_four,
            bias_sum_four,
        ]
    ).reshape(-1, LANES)
    sums = jnp.pad(sums, ((0, -sums.shape[0] % 8), (0, 0)))
    sums = gather_tiles(sums, 13).reshape(nt, -1)
    five_gain, five_bias = sums[:, :mid], sums[:, mid : 2 * mid]
    at_out = 2 * mid
    three_gain = sums[:, at_out : at_out + wide].reshape(nt, nb, piece)
    three_bias = sums[:, at_out + wide : at_out + 2 * wide].reshape(nt, nb, piece)
    at_slim = at_out + 2 * wide
    slims = [
        sums[:, at_slim + i * slim : at_slim + (i + 1) * slim].reshape(1, mid) for i in range(4)
    ]
    mid_gains = jnp.concatenate([gain_sum_one[None], slims[0], slims[2], five_gain], 0)
    mid_biases = jnp.concatenate([bias_sum_one[None], slims[1], slims[3], five_bias], 0)
    grad_mid_gain = lax.dynamic_slice_in_dim(mid_gains, batch * share, share, 1)
    grad_mid_bias = lax.dynamic_slice_in_dim(mid_biases, batch * share, share, 1)
    grad_out_gain = lax.dynamic_index_in_dim(three_gain, batch, 1, False).reshape(nt * piece)
    grad_out_bias = lax.dynamic_index_in_dim(three_bias, batch, 1, False).reshape(nt * piece)
    return (
        depth_out.reshape(1, tile_rows, cols),
        logits.reshape(1, tile_rows, cols, classes),
        grad_input.reshape(1, tile_rows, cols, width),
        red_first,
        red_spatial,
        red_last,
        red_shared,
        red_heads,
        red_messages,
        red_gates,
        red_depth,
        red_classes,
        grad_mid_gain,
        grad_mid_bias,
        grad_out_gain,
        grad_out_bias,
    )


def swap_tiles(blocks, blk, nt):
    out = jnp.zeros_like(blocks)
    out = lax.dynamic_update_index_in_dim(
        out, lax.dynamic_index_in_dim(blocks, blk, 0, False), blk, 0
    )
    for mask in range(1, nt):
        sent = lax.dynamic_index_in_dim(blocks, blk ^ mask, 0, False)
        came = lax.ppermute(sent, "blk", [(i, i ^ mask) for i in range(nt)])
        out = lax.dynamic_update_index_in_dim(out, came, blk ^ mask, 0)
    return out.reshape(-1, blocks.shape[2])


def gather_tiles_pair(depth_target, labels, tile):
    pair = jnp.stack([depth_target.reshape(tile), labels.reshape(tile).astype(F32)], 0)
    pair = jnp.pad(pair, ((0, 6), (0, 0)))
    return gather_tiles(pair, 14).swapaxes(1, 2)


PITCH = 48
CHUNK = 64
BLOCK = 256
ANY = pl.BlockSpec(memory_space=pl.ANY)
VMEM = pl.BlockSpec(memory_space=pltpu.VMEM)
DMA = pltpu.SemaphoreType.DMA
LONG = pl.CostEstimate(flops=80_000_000_000, bytes_accessed=30_000_000, transcendentals=2_000_000)


class Mail:
    def __init__(self, sems):
        self.sems, self.used, self.open = sems, 0, []

    def send(self, src, dst, peer, keep=True):
        copy = send(src, dst, self.sems.at[0, self.used], self.sems.at[1, self.used], peer)
        self.used += 1
        if keep:
            self.open.append(copy.wait_send)
        return copy

    def local(self, src, dst):
        copy = pltpu.make_async_copy(src, dst, self.sems.at[0, self.used])
        copy.start()
        self.used += 1
        return copy

    def close(self):
        for wait in self.open:
            wait()
        self.open = []


class Place:
    def __init__(self, images):
        self.blk, self.batch = lax.axis_index("blk"), lax.axis_index("batch")
        self.images = images
        self.mate = (self.blk ^ 1, self.batch)
        self.across = (self.blk ^ 2, self.batch)
        self.tiles = [(self.blk ^ mask, self.batch) for mask in range(1, 4)]
        self.others = [(self.blk, self.batch ^ mask) for mask in range(1, images)]
        self.side = (self.blk, self.batch ^ 1)


class Spread:
    def __init__(self, mail, place, own, slot):
        self.mail, self.place, self.own, self.slot = mail, place, own, slot
        self.z_copies, self.x_copies = [], []

    def start(self):
        place, here = self.place, self.slot(self.place.batch)
        self.here = self.mail.local(self.own, here)
        for mask in range(1, place.images // 2):
            peer = (place.blk, place.batch ^ (2 * mask))
            self.z_copies.append(self.mail.send(self.own, here, peer))
        self.x_copies.append(self.mail.send(self.own, here, place.side))
        return self

    def forward(self):
        for mask, copy in enumerate(self.z_copies, 1):
            copy.wait_recv()
            block = self.slot(self.place.batch ^ (2 * mask))
            self.x_copies.append(self.mail.send(block, block, self.place.side))

    def finish(self):
        self.here.wait()
        for copy in self.x_copies:
            copy.wait_recv()


def share_tiles(mail, place, slot):
    own = slot(place.blk)
    far = mail.send(own, own, place.across, False)
    near = mail.send(own, own, place.mate, False)
    far.wait_recv()
    passed = slot(place.blk ^ 2)
    last = mail.send(passed, passed, place.mate, False)
    near.wait()
    last.wait()
    far.wait_send()


def loop(total, step, body, base=0):
    def run(at, carry):
        body(pl.ds(pl.multiple_of(base + at * step, step), step))
        return carry

    lax.fori_loop(0, total // step, run, 0)


PIECES = 3


def pieces_of(total):
    size = total // PIECES
    return [(at * size, size) for at in range(PIECES)]


def share_pieces(mail, place, slot, total, produce=None, consume=None, meanwhile=None):
    pieces = pieces_of(total)
    far, near, last = [], [], []
    for first, size in pieces:
        if produce is not None:
            produce(first, size)
        own = slot(place.blk, first, size)
        far.append(mail.send(own, own, place.across, False))
        near.append(mail.send(own, own, place.mate, False))
    if meanwhile is not None:
        meanwhile()

    def use(at):
        near[at].wait_recv()
        last[at].wait_recv()
        if consume is not None:
            consume(*pieces[at])

    for at, (first, size) in enumerate(pieces):
        far[at].wait_recv()
        passed = slot(place.blk ^ 2, first, size)
        last.append(mail.send(passed, passed, place.mate, False))
        if at > 0:
            use(at - 1)
    use(len(pieces) - 1)
    for copy in far + near + last:
        copy.wait_send()


def folded(values):
    return jnp.sum(values.reshape(values.shape[0] // 8, 8, values.shape[1]), 0)


def loop_sums(total, channels, count, body, base=0):
    def run(at, carry):
        found = body(pl.ds(pl.multiple_of(base + at * CHUNK, CHUNK), CHUNK))
        return tuple(kept + folded(one) for kept, one in zip(carry, found))

    start = tuple(jnp.zeros((8, channels), F32) for _ in range(count))
    return [jnp.sum(one, 0, keepdims=True) for one in lax.fori_loop(0, total // CHUNK, run, start)]


def merge(slots, sizes, channels):
    count = slots.shape[0]
    size, mean = None, None
    for at in range(count):
        weight = sizes[at, :, :channels]
        term = slots[at, 0:1, :] * weight
        size = weight if size is None else size + weight
        mean = term if mean is None else mean + term
    mean = mean / size
    spread = None
    for at in range(count):
        gap = slots[at, 0:1, :] - mean
        term = slots[at, 1:2, :] + sizes[at, :, :channels] * gap * gap
        spread = term if spread is None else spread + term
    return mean, spread, size


def add_up(slots):
    total = slots[0]
    for at in range(1, slots.shape[0]):
        total = total + slots[at]
    return total[0:1, :], total[1:2, :]


def swap_sums(mail, place, slots, meanwhile=None):
    own = slots.at[place.batch]
    copies = [mail.send(own, own, peer) for peer in place.others]
    if meanwhile is not None:
        meanwhile()
    for copy in copies:
        copy.wait_recv()


def swap_tile_sums(mail, place, slots):
    own = slots.at[place.blk]
    copies = [mail.send(own, own, peer) for peer in place.tiles]
    for copy in copies:
        copy.wait_recv()


def local_stats(pre, mask, base, total, channels, size):
    def first(rows):
        return (pre[rows, :] * mask[at_base(base, rows), :],)

    (summed,) = loop_sums(total, channels, 1, first)
    mean = summed / jnp.maximum(size, 1.0)

    def second(rows):
        gap = pre[rows, :] - mean
        return (gap * gap * mask[at_base(base, rows), :],)

    (spread,) = loop_sums(total, channels, 1, second)
    return mean, spread


def at_base(base, rows):
    if base is None:
        return rows
    return pl.ds(pl.multiple_of(base + rows.start, CHUNK), rows.size)


def batch_norm_stats(mail, place, pre, mask, slots, sizes, stats, row, channels, meanwhile=None):
    total = pre.shape[0]
    mean, spread = local_stats(pre, mask, None, total, channels, sizes[place.batch, :, :channels])
    slots[place.batch] = jnp.concatenate([mean, spread], 0)
    swap_sums(mail, place, slots, meanwhile)
    keep_stats(slots, sizes, stats, row, channels)


def keep_stats(slots, sizes, stats, row, channels):
    mean, spread, size = merge(slots, sizes, channels)
    stats[row : row + 1, :channels] = mean
    stats[row + 1 : row + 2, :channels] = lax.rsqrt(spread / size + EPSILON)


def silu(values):
    return values * jax.nn.sigmoid(values)


def widen(cells, left, right, total):
    def body(rows):
        seen = cells[pl.ds(pl.multiple_of(rows.start + PITCH - 16, 16), CHUNK + 32), :].astype(F32)
        here = pl.ds(pl.multiple_of(rows.start + PITCH, 16), CHUNK)
        left[here, :] = seen[15 : 15 + CHUNK].astype(BF16)
        right[here, :] = seen[17 : 17 + CHUNK].astype(BF16)

    loop(total, CHUNK, body)


def clear_ends(cells, total):
    zeros = jnp.zeros((PITCH, cells.shape[1]), cells.dtype)
    cells[0:PITCH, :] = zeros
    cells[PITCH + total : 2 * PITCH + total, :] = zeros


def conv_rows(shifted, rows, weight, back):
    total = None
    for offset in range(9):
        row, col = offset // 3, offset % 3
        if back:
            row, col = 2 - row, 2 - col
        window = shifted[col][pl.ds(pl.multiple_of(rows.start + PITCH * row, 16), rows.size), :]
        product = weight(offset, window)
        total = product if total is None else total + product
    return total


def sum_over_tiles(mail, place, part, near_in, pair, far_in, total, out, meanwhile=None, produce=None):
    mine_far, mine = part(place.blk ^ 2), part(place.blk)
    pieces = pieces_of(total)
    near_far, near_own, far = [], [], []

    def pairs(rows):
        pair[rows, :] = (mine_far[rows, :].astype(F32) + near_in[0, rows, :].astype(F32)).astype(BF16)

    def pass_on(at):
        first, size = pieces[at]
        near_far[at].wait_recv()
        loop(size, CHUNK, pairs, first)
        here = pl.ds(first, size)
        far.append(mail.send(pair.at[here], far_in.at[here], place.across))

    for at, (first, size) in enumerate(pieces):
        if produce is not None:
            produce(first, size)
        here = pl.ds(first, size)
        near_far.append(mail.send(part(place.blk ^ 3).at[here], near_in.at[0, here], place.mate))
        near_own.append(mail.send(part(place.blk ^ 1).at[here], near_in.at[1, here], place.mate))
        if at > 0:
            pass_on(at - 1)
    pass_on(len(pieces) - 1)
    if meanwhile is not None:
        meanwhile()

    def finish(rows):
        out[rows, :] = (
            mine[rows, :].astype(F32) + near_in[1, rows, :].astype(F32) + far_in[rows, :].astype(F32)
        )

    for at, (first, size) in enumerate(pieces):
        near_own[at].wait_recv()
        far[at].wait_recv()
        loop(size, CHUNK, finish, first)


def start_kernel(
    images,
    weight,
    small,
    spatial_own,
    pair,
    head_all,
    feat,
    mask,
    sizes,
    tile_sizes,
    full,
    smalls,
    targets,
    wide,
    spatial,
    pre_one,
    stats,
    head_own,
    slots_tile,
    slots_one,
    sems,
):
    place = Place(images)
    mail = Mail(sems)
    blk, batch = place.blk, place.batch
    depth = weight.shape[0]
    half = depth // 2
    mid = weight.shape[1]
    tile = feat.shape[0]
    slim = mid // 4
    share = spatial_own.shape[1]
    mine = pl.ds(pl.multiple_of(lax.rem(blk, 2) * half, half), half)
    greet(place.others + place.tiles)
    here = mail.local(weight, full.at[batch])
    here_small = mail.local(small, smalls.at[batch])
    here_head = mail.local(head_all.at[blk], head_own)
    z_copies, x_copies, arrived, late = {}, [], [], []
    for peer in place.others:
        late.append(mail.send(small, smalls.at[batch], peer))
    for mask_z in range(1, images // 2):
        z_copies[mask_z] = mail.send(
            weight.at[mine], full.at[batch, mine], (blk, batch ^ (2 * mask_z))
        )
    x_copies.append(mail.send(weight.at[mine], full.at[batch, mine], place.side))
    lanes = pl.ds(pl.multiple_of(blk * slim, slim), slim)
    got_spatial = Spread(
        mail,
        place,
        spatial_own.at[:, :, lanes],
        lambda index: spatial.at[:, pl.ds(pl.multiple_of(index * share, share), share), :],
    ).start()

    def columns(index):
        return feat.at[:, pl.ds(pl.multiple_of(index * mid, mid), mid)]

    landing = wide.at[pl.ds(pl.multiple_of(blk * tile, tile), tile), :]
    here_wide = mail.local(columns(blk), landing)
    line = targets.at[:, pl.ds(pl.multiple_of(blk * tile, tile), tile)]
    here_line = mail.local(pair, line)
    for mask_t in range(1, 4):
        late.append(mail.send(pair, line, (blk ^ mask_t, batch)))
        late.append(mail.send(columns(blk ^ mask_t), landing, (blk ^ mask_t, batch)))

    def hand_over(source):
        block = full.at[source, mine]
        arrived.append(mail.send(block, block, place.mate))

    for mask_z in range(1, images // 2):
        z_copies[mask_z].wait_recv()
        source = batch ^ (2 * mask_z)
        block = full.at[source, mine]
        x_copies.append(mail.send(block, block, place.side))
        hand_over(source)
    for mask_z in range(images // 2):
        x_copies[mask_z].wait_recv()
        hand_over(batch ^ (2 * mask_z + 1))
    stats[...] = jnp.zeros_like(stats)
    here.wait()
    for copy in arrived:
        copy.wait_recv()

    def reduce(rows):
        total = None
        for index in range(images):
            product = dot(feat[rows, index * depth : (index + 1) * depth], full[index])
            total = product if total is None else total + product
        pre_one[rows, :] = total

    loop(tile, tile // 2, reduce)
    base = blk * tile
    mean, spread = local_stats(pre_one, mask, base, tile, mid, tile_sizes[blk, :, :])
    slots_tile[blk] = jnp.concatenate([mean, spread], 0)
    swap_tile_sums(mail, place, slots_tile)
    mean, spread, _ = merge(slots_tile, tile_sizes, mid)
    slots_one[batch] = jnp.concatenate([mean, spread], 0)
    swap_sums(mail, place, slots_one, got_spatial.forward)
    keep_stats(slots_one, sizes, stats, 0, mid)
    got_spatial.finish()
    for copy in late:
        copy.wait_recv()
    here_small.wait()
    here_wide.wait()
    here_line.wait()
    here_head.wait()
    mail.close()


def begin(nb, weight, small, spatial, pair, heads, feat, mask, sizes, tile_sizes):
    depth, mid = weight.shape
    tile = feat.shape[0]

    def array(*shape, kind=BF16):
        return jax.ShapeDtypeStruct(shape, kind)

    return pl.pallas_call(
        functools.partial(start_kernel, nb),
        out_shape=(
            array(nb, depth, mid),
            array(nb, *small.shape),
            array(8, 4 * tile, kind=F32),
            array(4 * tile, mid),
            array(9, mid, mid // 4),
            array(tile, mid, kind=F32),
            array(8, mid, kind=F32),
            array(*heads.shape[1:]),
        ),
        in_specs=[ANY] * 5 + [VMEM] * 4,
        out_specs=(VMEM, ANY, ANY, VMEM, VMEM, VMEM, VMEM, ANY),
        scratch_shapes=[
            pltpu.VMEM((4, 2, mid), F32),
            pltpu.VMEM((nb, 2, mid), F32),
            DMA((2, 64)),
        ],
        cost_estimate=LONG,
        compiler_params=pltpu.CompilerParams(
            collective_id=21, has_side_effects=True, vmem_limit_bytes=40 * 2**20
        ),
    )(weight, small, spatial, pair, heads, feat, mask, sizes, tile_sizes)


def forward_kernel(
    images,
    early,
    pre_one,
    first_stats,
    spatial,
    wide,
    mask,
    norms,
    sizes,
    last_own,
    shared_own,
    gate_own,
    message_own,
    last,
    shared,
    gate,
    message,
    act_one,
    act_two,
    act_three,
    shared_act,
    pre_two,
    pre_three,
    pre_four,
    stats,
    one_left,
    one_right,
    parts,
    near_in,
    pair,
    far_in,
    slots_two,
    slots_three,
    slots_four,
    sems,
):
    place = Place(images)
    mail = Mail(sems)
    blk, batch = place.blk, place.batch
    tile, total = pre_one.shape[0], mask.shape[0]
    mid = pre_one.shape[1]
    slim = pre_two.shape[1]
    share = last_own.shape[0]
    base = blk * tile
    greet(place.others + place.tiles)

    def rows_of(index):
        return pl.ds(pl.multiple_of(index * share, share), share)

    def slim_lanes(index):
        return pl.ds(pl.multiple_of(index * slim, slim), slim)

    lanes = slim_lanes(blk)
    wide_lanes = pl.ds(pl.multiple_of(blk * mid, mid), mid)
    got_last = Spread(mail, place, last_own.at[:, wide_lanes], lambda index: last.at[rows_of(index), :])
    got_shared = Spread(mail, place, shared_own, lambda index: shared.at[rows_of(index), :])
    got_gate = Spread(mail, place, gate_own.at[blk], lambda index: gate.at[rows_of(index), :])
    got_message = [
        Spread(
            mail,
            place,
            message_own.at[blk, offset],
            lambda index, offset=offset: message.at[offset, rows_of(index), :],
        )
        for offset in range(early)
    ]
    got_last.start()
    got_shared.start()
    stats[...] = first_stats[...]
    clear_ends(act_one, total)
    clear_ends(shared_act, total)
    clear_ends(one_left, total)
    clear_ends(one_right, total)

    def act_first(rows):
        value = (pre_one[rows, :] - stats[0:1, :]) * stats[1:2, :] * norms[0:1, :] + norms[1:2, :]
        value = silu(value) * mask[at_base(base, rows), :]
        act_one[pl.ds(pl.multiple_of(PITCH + base + rows.start, 16), CHUNK), :] = value.astype(BF16)

    share_pieces(
        mail,
        place,
        lambda index, first, size: act_one.at[
            pl.ds(pl.multiple_of(PITCH + index * tile + first, 16), size), :
        ],
        tile,
        lambda first, size: loop(size, CHUNK, act_first, first),
    )
    widen(act_one, one_left, one_right, total)
    got_last.forward()
    got_shared.forward()

    shifted = (one_left, act_one, one_right)

    def conv_two(rows):
        pre_two[rows, :] = conv_rows(
            shifted, rows, lambda offset, window: dot(window, spatial[offset]), False
        )

    loop(total, BLOCK, conv_two)

    def after_two():
        got_gate.start()
        got_message[0].start()
        got_message[1].start()

    batch_norm_stats(mail, place, pre_two, mask, slots_two, sizes, stats, 2, slim, after_two)

    def act_second(rows):
        value = (pre_two[rows, :] - stats[2:3, :slim]) * stats[3:4, :slim]
        value = silu(value * norms[2:3, :slim] + norms[3:4, :slim]) * mask[rows, :]
        act_two[rows, lanes] = value.astype(BF16)

    got_last.finish()

    def expand(rows):
        pre_three[rows, :] = dot(act_two[rows, :], last[...])

    share_pieces(
        mail,
        place,
        lambda index, first, size: act_two.at[pl.ds(first, size), slim_lanes(index)],
        total,
        lambda first, size: loop(size, CHUNK, act_second, first),
        lambda first, size: loop(size, BLOCK, expand, first),
    )
    got_gate.forward()

    def after_three():
        got_message[0].forward()
        got_message[1].forward()
        got_message[2].start()
        got_message[3].start()

    batch_norm_stats(mail, place, pre_three, mask, slots_three, sizes, stats, 4, mid, after_three)
    got_shared.finish()

    def act_third(rows):
        normed = (pre_three[rows, :] - stats[4:5, :]) * stats[5:6, :]
        value = normed * norms[4:5, :] + norms[5:6, :] + wide[rows, :].astype(F32)
        act_three[rows, :] = (silu(value) * mask[rows, :]).astype(BF16)

    loop(total, CHUNK, act_third)

    def reduce(rows):
        parts[rows, :] = dot(act_three[rows, :], shared[...]).astype(BF16)

    sum_over_tiles(
        mail,
        place,
        lambda index: parts.at[:, slim_lanes(index)],
        near_in,
        pair,
        far_in,
        total,
        pre_four,
        None,
        lambda first, size: loop(size, BLOCK, reduce, first),
    )

    def after_four():
        got_message[2].forward()
        got_message[3].forward()
        for later in got_message[4:]:
            later.start()

    batch_norm_stats(mail, place, pre_four, mask, slots_four, sizes, stats, 6, slim, after_four)

    def act_fourth(rows):
        value = (pre_four[rows, :] - stats[6:7, :slim]) * stats[7:8, :slim]
        value = silu(value * norms[6:7, :slim] + norms[7:8, :slim]) * mask[rows, :]
        shared_act[pl.ds(pl.multiple_of(PITCH + rows.start, 16), CHUNK), lanes] = value.astype(BF16)

    share_pieces(
        mail,
        place,
        lambda index, first, size: shared_act.at[pl.ds(PITCH + first, size), slim_lanes(index)],
        total,
        lambda first, size: loop(size, CHUNK, act_fourth, first),
    )
    for later in got_message[4:]:
        later.forward()
    got_gate.finish()
    for one in got_message:
        one.finish()
    mail.close()


def bottleneck(nb, early, pre_one, stats, spatial, wide, mask, norms, sizes, last, shared, gate, message):
    tile, total = pre_one.shape[0], mask.shape[0]
    mid = pre_one.shape[1]
    slim = mid // 4
    padded = total + 2 * PITCH

    def array(*shape, kind=BF16):
        return jax.ShapeDtypeStruct(shape, kind)

    outs = (
        array(mid, mid),
        array(mid, mid),
        array(mid, mid),
        array(early, mid, mid),
        array(padded, mid),
        array(total, mid),
        array(total, mid),
        array(padded, mid),
        array(total, slim, kind=F32),
        array(total, mid, kind=F32),
        array(total, slim, kind=F32),
        array(8, mid, kind=F32),
    )
    return pl.pallas_call(
        functools.partial(forward_kernel, nb, early),
        out_shape=outs,
        in_specs=[VMEM] * 7 + [ANY] * 4,
        out_specs=(VMEM, VMEM, ANY, ANY) + (VMEM,) * 8,
        scratch_shapes=[
            pltpu.VMEM((padded, mid), BF16),
            pltpu.VMEM((padded, mid), BF16),
            pltpu.VMEM((total, mid), BF16),
            pltpu.VMEM((2, total, slim), BF16),
            pltpu.VMEM((total, slim), BF16),
            pltpu.VMEM((total, slim), BF16),
            pltpu.VMEM((nb, 2, slim), F32),
            pltpu.VMEM((nb, 2, mid), F32),
            pltpu.VMEM((nb, 2, slim), F32),
            DMA((2, 192)),
        ],
        cost_estimate=LONG,
        compiler_params=pltpu.CompilerParams(
            collective_id=20, has_side_effects=True, vmem_limit_bytes=60 * 2**20
        ),
    )(pre_one, stats, spatial, wide, mask, norms, sizes, last, shared, gate, message)


class Tiles:
    def __init__(self, mail, place, slot, own=None):
        self.mail, self.place, self.slot, self.own = mail, place, slot, own

    def start(self):
        own, here = self.own, self.slot(self.place.blk)
        if own is None:
            own = here
        else:
            self.mail.open.append(self.mail.local(own, here).wait)
        self.far = self.mail.send(own, here, self.place.across)
        self.near = self.mail.send(own, here, self.place.mate)

    def forward(self):
        self.far.wait_recv()
        passed = self.slot(self.place.blk ^ 2)
        self.last = self.mail.send(passed, passed, self.place.mate)

    def end(self):
        self.near.wait_recv()
        self.last.wait_recv()


class Reduce:
    def __init__(self, mail, place, grad, from_side, summed, from_line, out):
        self.mail, self.place = mail, place
        self.grad, self.from_side, self.summed = grad, from_side, summed
        self.from_line, self.out = from_line, out
        self.side = lax.rem(place.batch, 2)
        self.line = lax.div(place.batch, 2)

    def start(self):
        self.from_x = self.mail.send(self.grad.at[:, 1 - self.side], self.from_side, self.place.side)

    def own_half(self, at):
        return self.grad[at, self.side]

    def add_side(self):
        self.from_x.wait_recv()
        lines = self.from_side.shape[0]
        for at in range(lines):
            self.summed[at] = (self.own_half(at).astype(F32) + self.from_side[at].astype(F32)).astype(BF16)

    def middle(self):
        self.add_side()
        self.send_lines()

    def send_lines(self):
        place = self.place
        lines = self.summed.shape[0]
        self.copies = [
            self.mail.send(
                self.summed.at[self.line ^ mask],
                self.from_line.at[mask - 1],
                (place.blk, place.batch ^ (2 * mask)),
            )
            for mask in range(1, lines)
        ]

    def finish(self):
        total = self.summed[self.line].astype(F32)
        for at, copy in enumerate(self.copies):
            copy.wait_recv()
            total = total + self.from_line[at].astype(F32)
        self.out[...] = total.astype(BF16)


class ReduceFar(Reduce):
    def start(self):
        super().start()
        self.fetch = self.mail.local(self.grad.at[:, self.side], self.summed)

    def own_half(self, at):
        if at == 0:
            self.fetch.wait()
        return self.summed[at]


class Job:
    def __init__(self, reduce, tiles):
        self.steps = []
        if reduce is not None:
            self.steps += [reduce.start, reduce.middle, reduce.finish]
        if tiles is not None:
            self.steps += [tiles.start, tiles.forward, tiles.end]


def step(*jobs):
    for job in jobs:
        if job.steps:
            job.steps.pop(0)()


def reduce_scratch(lines, share, columns, own):
    found = [pltpu.VMEM((lines, 2, share, columns), BF16)] if own else []
    return found + [
        pltpu.VMEM((lines, share, columns), BF16),
        pltpu.VMEM((lines, share, columns), BF16),
        pltpu.VMEM((lines - 1, share, columns), BF16),
    ]


def send_sums(mail, place, slots, sums):
    slots[place.batch] = jnp.concatenate(sums, 0)
    own = slots.at[place.batch]
    return [mail.send(own, own, peer) for peer in place.others]


def silu_back(value):
    sigmoid_value = jax.nn.sigmoid(value)
    return sigmoid_value * (1.0 + value * (1.0 - sigmoid_value))


def norm_back(stats, norms, mask, grad, pre, row, channels, lead, offset=None, skip=None, rows_of=None):
    def body(rows):
        normed = (pre[rows, :] - stats[row : row + 1, :channels]) * stats[row + 1 : row + 2, :channels]
        value = normed * norms[row : row + 1, :channels] + norms[row + 1 : row + 2, :channels]
        if skip is not None:
            value = value + skip[rows, :].astype(F32)
        found = lead(rows) * mask[at_base(offset, rows), :] * silu_back(value)
        grad[rows, :] = found
        return found, found * normed

    first, size = (0, pre.shape[0]) if rows_of is None else rows_of
    return loop_sums(size, channels, 2, body, first)


def through(stats, norms, mask, sizes, grad, pre, row, channels, bias_sum, gain_sum, put, offset=None, rows_of=None):
    count = sizes[0, :, :channels]
    for at in range(1, sizes.shape[0]):
        count = count + sizes[at, :, :channels]
    scale = stats[row + 1 : row + 2, :channels] * norms[row : row + 1, :channels]
    bias_part, gain_part = bias_sum / count, gain_sum / count

    def body(rows):
        normed = (pre[rows, :] - stats[row : row + 1, :channels]) * stats[row + 1 : row + 2, :channels]
        found = scale * (grad[rows, :] - bias_part - normed * gain_part)
        put(rows, (found * mask[at_base(offset, rows), :]).astype(BF16))

    first, size = (0, pre.shape[0]) if rows_of is None else rows_of
    loop(size, CHUNK, body, first)


def backward_kernel(
    images,
    back,
    pre_one,
    pre_two,
    pre_three,
    pre_four,
    stats,
    norms,
    mask,
    sizes,
    wide,
    act_one,
    act_two,
    act_three,
    spatial,
    last,
    shared,
    first,
    gate_grads,
    stream_grads,
    message_share,
    head_grads,
    task_sums,
    grad_input,
    share_shared,
    share_first,
    all_last,
    all_spatial,
    all_gates,
    all_stream,
    all_heads,
    all_messages,
    all_sums,
    near_four,
    pair_four,
    far_four,
    grad_four,
    all_four,
    grad_three,
    low_three,
    low_joined,
    joined_rows,
    near_two,
    pair_two,
    far_two,
    grad_two,
    two_left,
    two_here,
    two_right,
    turned,
    strip,
    near_one,
    pair_one,
    far_one,
    grad_one,
    all_one,
    slots_four,
    slots_three,
    slots_two,
    slots_tile,
    slots_one,
    *rest,
):
    place = Place(images)
    sems = rest[-1]
    mail = Mail(sems)
    blk, batch = place.blk, place.batch
    tile, total = pre_one.shape[0], mask.shape[0]
    mid = pre_one.shape[1]
    slim = pre_two.shape[1]
    base = blk * tile
    red_shared = Reduce(mail, place, *rest[0:4], share_shared)
    red_last = Reduce(mail, place, *rest[4:8], all_last.at[blk])
    red_first = Reduce(mail, place, *rest[8:12], share_first)
    red_spatial = Reduce(mail, place, *rest[12:16], all_spatial.at[blk])
    red_gates = Reduce(mail, place, gate_grads, *rest[16:19], all_gates.at[blk])
    red_stream = Reduce(mail, place, stream_grads, *rest[19:22], all_stream.at[blk])
    share = share_shared.shape[0]
    results, sums_out, at = rest[22], rest[23], 24
    heads, messages = [], []

    def tiles_of(slots, first_row, count, own):
        rows_at = pl.ds(first_row, count)
        return Tiles(mail, place, lambda index: slots.at[index, rows_at], own)

    def slots_of(slots):
        return Tiles(mail, place, lambda index: slots.at[index])

    kept = head_grads.shape[0]
    for offset in range(kept):
        result = results.at[offset]
        reduce = ReduceFar(mail, place, head_grads.at[offset], *rest[at : at + 3], result)
        at += 3
        heads.append(Job(reduce, tiles_of(all_heads, offset * share, share, result)))
    heads += [Job(None, None)] * (9 - kept)
    early = message_share.shape[0] // share
    ends = [0, early // 3, 2 * early // 3, early]
    for begin_at, end_at in zip(ends[:-1], ends[1:]):
        count = (end_at - begin_at) * share
        own = message_share.at[pl.ds(begin_at * share, count)]
        messages.append(Job(None, tiles_of(all_messages, begin_at * share, count, own)))
    job_shared, job_first = Job(red_shared, None), Job(red_first, None)
    job_sums = Job(None, Tiles(mail, place, lambda index: all_sums.at[index], sums_out))
    job_last, job_spatial = Job(red_last, slots_of(all_last)), Job(red_spatial, slots_of(all_spatial))
    job_gates, job_stream = Job(red_gates, slots_of(all_gates)), Job(red_stream, slots_of(all_stream))
    greet(place.others + place.tiles)

    def slim_lanes(index):
        return pl.ds(pl.multiple_of(index * slim, slim), slim)

    def tile_rows(index):
        return pl.ds(pl.multiple_of(index * tile, tile), tile)

    def keep(row, bias_sum, gain_sum, channels):
        sums_out[row : row + 1, :channels] = gain_sum
        sums_out[row + 1 : row + 2, :channels] = bias_sum

    sums_out[...] = jnp.zeros_like(sums_out)
    sums_out[8:10, :] = task_sums[0:2, :]
    for cells in (two_left, two_here, two_right):
        clear_ends(cells, total)
    step(heads[0], heads[1], job_gates, job_stream)

    sum_over_tiles(
        mail, place, lambda index: back.at[:, slim_lanes(index)], near_four, pair_four, far_four, total, grad_four
    )
    sums = norm_back(stats, norms, mask, grad_four, pre_four, 6, slim, lambda rows: grad_four[rows, :])
    copies = send_sums(mail, place, slots_four, sums)
    step(heads[0], heads[1], job_gates, job_stream)
    step(heads[2], heads[3], heads[4])
    for offset in range(9):
        turned[offset * slim : (offset + 1) * slim, :] = spatial[offset].T
    for copy in copies:
        copy.wait_recv()
    bias_sum, gain_sum = add_up(slots_four)
    keep(6, bias_sum, gain_sum, slim)
    lanes = slim_lanes(blk)

    def put_four(rows, value):
        all_four[rows, lanes] = value

    def joined_back(rows):
        return dot_t(all_four[rows, :], shared[...])

    sums = []

    def make_four(first, size):
        through(
            stats, norms, mask, sizes, grad_four, pre_four, 6, slim, bias_sum, gain_sum, put_four, None, (first, size)
        )

    def use_four(first, size):
        sums.append(
            norm_back(
                stats, norms, mask, grad_three, pre_three, 4, mid, joined_back, None, wide, (first, size)
            )
        )

    share_pieces(
        mail,
        place,
        lambda index, first, size: all_four.at[pl.ds(first, size), slim_lanes(index)],
        total,
        make_four,
        use_four,
    )
    step(messages[0])
    sums = [sum(one[1:], one[0]) for one in zip(*sums)]
    copies = send_sums(mail, place, slots_three, sums)
    step(heads[2], heads[3], heads[4])
    step(heads[5], heads[6])
    step(heads[0], heads[1], job_gates, job_stream)
    step(messages[0])
    grads, lines = red_shared.grad, red_shared.grad.shape[0]
    grads[...] = t_dot(act_three[...], all_four[...]).astype(BF16).reshape(grads.shape)
    step(job_shared)

    def lower(rows):
        low_joined[rows, :] = grad_three[rows, :].astype(BF16)

    loop(total, CHUNK, lower)
    for copy in copies:
        copy.wait_recv()
    bias_sum, gain_sum = add_up(slots_three)
    keep(4, bias_sum, gain_sum, mid)

    def put_three(rows, value):
        low_three[rows, :] = value

    def two_part(rows):
        all_four[rows, :] = dot_t(low_three[rows, :], last[...]).astype(BF16)

    def make_two(first, size):
        through(
            stats, norms, mask, sizes, grad_three, pre_three, 4, mid, bias_sum, gain_sum, put_three, None, (first, size)
        )
        loop(size, BLOCK, two_part, first)

    sum_over_tiles(
        mail,
        place,
        lambda index: all_four.at[:, slim_lanes(index)],
        near_two,
        pair_two,
        far_two,
        total,
        grad_two,
        None,
        make_two,
    )
    step(messages[1])
    landing = joined_rows.at[:, pl.ds(pl.multiple_of(blk * mid, mid), mid)]
    joined_here = mail.local(low_joined.at[tile_rows(blk)], landing)
    joined_copies = [
        mail.send(low_joined.at[tile_rows(blk ^ mask_t)], landing, (blk ^ mask_t, batch))
        for mask_t in range(1, 4)
    ]
    sums = norm_back(stats, norms, mask, grad_two, pre_two, 2, slim, lambda rows: grad_two[rows, :])
    copies = send_sums(mail, place, slots_two, sums)
    step(heads[5], heads[6], job_shared)
    step(heads[7], heads[8])
    step(heads[2], heads[3], heads[4])
    grads = red_last.grad
    grads[...] = t_dot(act_two[...], low_three[...]).astype(BF16).reshape(grads.shape)
    step(job_last)
    for copy in copies:
        copy.wait_recv()
    bias_sum, gain_sum = add_up(slots_two)
    keep(2, bias_sum, gain_sum, slim)

    def put_two(rows, value):
        two_here[pl.ds(pl.multiple_of(rows.start + PITCH, 16), CHUNK), :] = value

    through(stats, norms, mask, sizes, grad_two, pre_two, 2, slim, bias_sum, gain_sum, put_two)
    widen(two_here, two_left, two_right, total)
    shifted = (two_left, two_here, two_right)

    def one_part(rows):
        for offset in range(9):
            row, col = 2 - offset // 3, 2 - offset % 3
            window = shifted[col][pl.ds(pl.multiple_of(rows.start + PITCH * row, 16), BLOCK), :]
            strip[:, offset * slim : (offset + 1) * slim] = window
        low_three[rows, :] = dot(strip[...], turned[...]).astype(BF16)

    loop(total, BLOCK, one_part)

    def spatial_grads():
        grads = red_spatial.grad
        for offset in range(9):
            row, col = 2 - offset // 3, 2 - offset % 3
            window = shifted[col][PITCH * row : PITCH * row + total, :]
            found = t_dot(act_one[PITCH : PITCH + total, :], window).astype(BF16)
            grads[:, :, :, offset * slim : (offset + 1) * slim] = found.reshape(grads.shape[:3] + (slim,))
        step(job_spatial)

    sum_over_tiles(
        mail,
        place,
        lambda index: low_three.at[tile_rows(index)],
        near_one,
        pair_one,
        far_one,
        tile,
        grad_one,
        spatial_grads,
    )
    step(messages[1])
    step(messages[2])
    step(heads[0], heads[1], job_gates, job_stream)
    sums = norm_back(stats, norms, mask, grad_one, pre_one, 0, mid, lambda rows: grad_one[rows, :], base)
    slots_tile[blk] = jnp.concatenate(sums, 0)
    swap_tile_sums(mail, place, slots_tile)
    copies = send_sums(mail, place, slots_one, list(add_up(slots_tile)))
    step(heads[7], heads[8], job_last, job_spatial)
    step(heads[5], heads[6], job_shared)
    for copy in copies:
        copy.wait_recv()
    bias_sum, gain_sum = add_up(slots_one)
    keep(0, bias_sum, gain_sum, mid)

    def put_one(rows, value):
        all_one[at_base(base, rows), :] = value

    def make_one(first, size):
        through(
            stats, norms, mask, sizes, grad_one, pre_one, 0, mid, bias_sum, gain_sum, put_one, base, (first, size)
        )

    def inputs_back():
        joined_here.wait()
        for copy in joined_copies:
            copy.wait_recv()

        def input_grads(rows):
            own = all_one[pl.ds(pl.multiple_of(base + rows.start, CHUNK), rows.size), :]
            grad_input[rows, :] = dot_t(own, first[...]) + joined_rows[rows, :].astype(F32)

        loop(tile, tile // 3, input_grads)

    share_pieces(
        mail,
        place,
        lambda index, first, size: all_one.at[
            pl.ds(pl.multiple_of(index * tile + first, CHUNK), size), :
        ],
        tile,
        make_one,
        None,
        inputs_back,
    )
    grads = red_first.grad
    grads[...] = t_dot(wide[...], all_one[...]).astype(BF16).reshape(grads.shape)
    step(job_first)
    step(messages[2], job_sums)
    step(heads[0], heads[1], job_gates, job_stream)
    step(heads[2], heads[3], heads[4], heads[5], heads[6])
    step(job_first)
    step(heads[2], heads[3], heads[4], heads[5], heads[6], job_sums)
    step(heads[7], heads[8], job_last, job_spatial)
    step(heads[7], heads[8], job_last, job_spatial)
    step(job_first)
    step(heads[7], heads[8], job_last, job_spatial)
    for job in messages + heads + [job_gates, job_stream, job_last, job_spatial, job_sums]:
        step(job)
    mail.close()


def bottleneck_back(nb, back, pres, stats, norms, mask, sizes, wide, acts, weights, gate_grads, stream_grads, task_grads):
    tile, total = pres[0].shape[0], mask.shape[0]
    mid = pres[0].shape[1]
    slim = mid // 4
    lines, share = nb // 2, mid // nb
    padded = total + 2 * PITCH
    width = weights[3].shape[0]

    def array(*shape, kind=BF16):
        return jax.ShapeDtypeStruct(shape, kind)

    def vmem(*shape, kind=BF16):
        return pltpu.VMEM(shape, kind)

    scratch = [
        vmem(2, total, slim),
        vmem(total, slim),
        vmem(total, slim),
        vmem(total, slim, kind=F32),
        vmem(total, mid),
        vmem(total, mid, kind=F32),
        vmem(total, mid),
        vmem(total, mid),
        vmem(tile, width),
        vmem(2, total, slim),
        vmem(total, slim),
        vmem(total, slim),
        vmem(total, slim, kind=F32),
        vmem(padded, slim),
        vmem(padded, slim),
        vmem(padded, slim),
        vmem(9 * slim, mid),
        vmem(BLOCK, 9 * slim),
        vmem(2, tile, mid),
        vmem(tile, mid),
        vmem(tile, mid),
        vmem(tile, mid, kind=F32),
        vmem(total, mid),
        vmem(nb, 2, slim, kind=F32),
        vmem(nb, 2, mid, kind=F32),
        vmem(nb, 2, slim, kind=F32),
        vmem(4, 2, mid, kind=F32),
        vmem(nb, 2, mid, kind=F32),
    ]
    for columns in (mid, mid, mid, 9 * slim):
        scratch += reduce_scratch(lines, share, columns, True)
    for columns in (mid, LANES):
        scratch += reduce_scratch(lines, share, columns, False)
    message_share, head_grads, task_sums = task_grads
    kept = head_grads.shape[0]
    scratch += [vmem(kept, share, mid), vmem(16, mid, kind=F32)]
    for _ in range(kept):
        scratch += reduce_scratch(lines, share, mid, False)
    scratch.append(DMA((2, 256)))
    return pl.pallas_call(
        functools.partial(backward_kernel, nb),
        out_shape=(
            array(tile, width, kind=F32),
            array(share, mid),
            array(share, mid),
            array(4, share, mid),
            array(4, share, 9 * slim),
            array(4, share, mid),
            array(4, share, LANES),
            array(4, kept * share, mid),
            array(4, message_share.shape[0], mid),
            array(4, 16, mid, kind=F32),
        ),
        in_specs=[VMEM] * 19 + [ANY] * 2 + [VMEM],
        out_specs=(VMEM,) * 7 + (ANY, ANY, VMEM),
        scratch_shapes=scratch,
        cost_estimate=LONG,
        compiler_params=pltpu.CompilerParams(
            collective_id=22, has_side_effects=True, vmem_limit_bytes=62 * 2**20
        ),
    )(
        back,
        *pres,
        stats,
        norms,
        mask,
        sizes,
        wide,
        *acts,
        *weights,
        gate_grads.reshape(lines, 2, share, mid),
        stream_grads.reshape(lines, 2, share, LANES),
        message_share,
        head_grads.reshape(kept, lines, 2, share, mid),
        task_sums,
    )


def finish_kernel(images, first, shared, rest, first_rows, shared_rows, all_rest, sems):
    place = Place(images)
    mail = Mail(sems)
    blk, batch = place.blk, place.batch
    target = (lax.rem(batch, 4), 2 * blk + lax.div(batch, 4))
    source = (lax.div(batch, 2), 4 * lax.rem(batch, 2) + blk)
    stays = (target[0] == blk) & (target[1] == batch)
    moves = jnp.logical_not(stays)
    barrier = pltpu.get_barrier_semaphore()
    for peer in (place.mate, place.across):
        pl.semaphore_signal(barrier, inc=1, device_id=peer, device_id_type=MESH)

    @pl.when(moves)
    def _():
        pl.semaphore_signal(barrier, inc=1, device_id=source, device_id_type=MESH)
        pl.semaphore_wait(barrier, 3)

    @pl.when(stays)
    def _():
        pl.semaphore_wait(barrier, 2)

    def hop(at, own, slots):
        return pltpu.make_async_remote_copy(
            src_ref=own,
            dst_ref=slots.at[target[0]],
            send_sem=sems.at[0, at],
            recv_sem=sems.at[1, at],
            device_id=target,
            device_id_type=MESH,
        )

    def stay(at, own, slots):
        return pltpu.make_async_copy(own, slots.at[blk], sems.at[0, at])

    mail.used = 2
    pairs = [(0, first, first_rows), (1, shared, shared_rows)]

    @pl.when(moves)
    def _():
        for pair in pairs:
            hop(*pair).start()

    @pl.when(stays)
    def _():
        for pair in pairs:
            stay(*pair).start()

    tiles = Tiles(mail, place, lambda index: all_rest.at[index], rest)
    tiles.start()
    jobs = [Tiles(mail, place, lambda index, slots=slots: slots.at[index]) for _, _, slots in pairs]

    @pl.when(moves)
    def _():
        for pair in pairs:
            hop(*pair).wait()

    @pl.when(stays)
    def _():
        for pair in pairs:
            stay(*pair).wait()

    for job in jobs:
        job.start()
    for job in [tiles] + jobs:
        job.forward()
    for job in [tiles] + jobs:
        job.end()
    mail.close()


def finish(nb, first, shared, rest):
    share, mid = first.shape
    return pl.pallas_call(
        functools.partial(finish_kernel, nb),
        out_shape=(
            jax.ShapeDtypeStruct((4, share, mid), BF16),
            jax.ShapeDtypeStruct((4, share, mid), BF16),
            jax.ShapeDtypeStruct((4,) + rest.shape, BF16),
        ),
        in_specs=[ANY] * 3,
        out_specs=(ANY,) * 3,
        scratch_shapes=[DMA((2, 32))],
        compiler_params=pltpu.CompilerParams(collective_id=26, has_side_effects=True),
    )(first, shared, rest)


def task_kernel(
    images,
    early,
    shared_act,
    mask,
    mask_line,
    targets,
    sizes,
    norms,
    head,
    message_start,
    gate,
    to_depth,
    to_classes,
    from_gated,
    message_own,
    streams,
    slopes,
    pre_five,
    stats,
    grad_msg,
    grad_gate,
    gate_grads,
    stream_grads,
    message_grads,
    message_rest,
    message_end,
    left,
    right,
    task,
    messages,
    opened,
    gated,
    slots,
    slots_five,
    sems,
):
    place = Place(images)
    mail = Mail(sems)
    total = mask.shape[0]
    mid = pre_five.shape[1]
    is_first, is_last = place.blk == 0, place.blk == 3
    greet(place.others + [place.mate, place.across])
    late = message_end.shape[0]
    share = message_own.shape[2]
    got = [
        Spread(
            mail,
            place,
            message_own.at[place.blk, 9 - late + at],
            lambda index, at=at: message_end.at[at, pl.ds(pl.multiple_of(index * share, share), share), :],
        )
        for at in range(late)
    ]
    for one in got[: (late + 1) // 2]:
        one.start()
    stats[...] = jnp.zeros_like(stats)
    for cells in (left, right, task, grad_msg):
        clear_ends(cells, total)
    widen(shared_act, left, right, total)

    def heads(rows):
        pre_five[rows, :] = conv_rows(
            (left, shared_act, right), rows, lambda offset, window: dot(window, head[offset]), False
        )

    loop(total, BLOCK, heads)

    def behind():
        for one in got[: (late + 1) // 2]:
            one.forward()
        for one in got[(late + 1) // 2 :]:
            one.start()

    batch_norm_stats(mail, place, pre_five, mask, slots_five, sizes, stats, 0, mid, behind)
    for one in got[(late + 1) // 2 :]:
        one.forward()

    def act_task(rows):
        value = (pre_five[rows, :] - stats[0:1, :]) * stats[1:2, :] * norms[0:1, :] + norms[1:2, :]
        task[pl.ds(pl.multiple_of(PITCH + rows.start, 16), CHUNK), :] = (
            silu(value) * mask[rows, :]
        ).astype(BF16)

    loop(total, CHUNK, act_task)
    widen(task, left, right, total)
    for one in got:
        one.finish()

    def message_weight(offset):
        if offset < early:
            return message_start[offset]
        return head[9 + offset - early] if offset < 9 - late else message_end[offset - 9 + late]

    def here(rows):
        return pl.ds(pl.multiple_of(PITCH + rows.start, 16), rows.size)

    def send_messages(rows):
        messages[rows, :] = conv_rows(
            (left, task, right), rows, lambda offset, window: dot(window, message_weight(offset)), False
        )
        own = task[here(rows), :]
        opened[rows, :] = jax.nn.sigmoid(dot(own, gate[...]))
        part = (opened[rows, :] * messages[rows, :]).astype(BF16)
        gated[rows, :] = part
        depth_part = jnp.where(is_first, own, part)
        sem_part = jnp.where(is_last, own, part)
        slots[place.blk, :, rows] = dot_t(to_depth[...], depth_part) + dot_t(to_classes[...], sem_part)

    loop(total, BLOCK, send_messages)
    share_tiles(mail, place, lambda index: slots.at[index])
    classes = to_depth.shape[0]
    kind = lax.broadcasted_iota(jnp.int32, (classes, 2 * BLOCK), 0)

    def compare(rows):
        value = slots[0, :, rows] + slots[1, :, rows] + slots[2, :, rows] + slots[3, :, rows]
        streams[:, rows] = value
        is_class = (kind >= 1) & (kind <= CLASSES)
        top = jnp.max(jnp.where(is_class, value, -jnp.inf), 0, keepdims=True)
        power = jnp.where(is_class, jnp.exp(value - top), 0.0)
        chance = power / jnp.sum(power, 0, keepdims=True)
        label = targets[1:2, rows]
        chance = chance - jnp.where((kind - 1).astype(F32) == label, 1.0, 0.0)
        slope = jnp.where(kind == 0, value - targets[0:1, rows], jnp.where(is_class, chance, 0.0))
        slopes[:, rows] = (slope * mask_line[0:1, rows]).astype(BF16)

    loop(total, 2 * BLOCK, compare)
    by_part = dot(slopes[...], gated[...])
    by_task = dot(slopes[...], task[PITCH : PITCH + total, :])
    row = lax.broadcasted_iota(jnp.int32, by_part.shape, 0)
    use_task = ((row == 0) & is_first) | ((row > 0) & is_last)
    found = jnp.where(use_task, by_task, by_part)
    found = jnp.concatenate([found, jnp.zeros((LANES - classes, mid), F32)], 0)
    stream_grads[...] = found.T.astype(BF16)

    def grads(rows):
        grad = t_dot(slopes[:, rows], from_gated[...])
        open_part = opened[rows, :]
        grad_msg[here(rows), :] = (grad * open_part).astype(BF16)
        grad_gate[rows, :] = (grad * messages[rows, :] * open_part * (1.0 - open_part)).astype(BF16)

    loop(total, BLOCK, grads)
    gate_grads[...] = t_dot(task[PITCH : PITCH + total, :], grad_gate[...]).astype(BF16)
    widen(grad_msg, left, right, total)
    shifted = (left, grad_msg, right)
    for offset in range(9):
        row, col = 2 - offset // 3, 2 - offset % 3
        window = shifted[col][PITCH * row : PITCH * row + total, :]
        found = t_dot(task[PITCH : PITCH + total, :], window).astype(BF16)
        if offset < early:
            message_grads[offset] = found
        else:
            message_rest[:, (offset - early) * mid : (offset - early + 1) * mid] = found
    mail.close()


CLASSES = 40


def one_task(nb, early, late, shared_act, mask, mask_line, targets, sizes, norms, weights, streams_weights, own):
    total = mask.shape[0]
    padded, mid = shared_act.shape
    lines = streams_weights[0].shape[0]

    def array(*shape, kind=BF16):
        return jax.ShapeDtypeStruct(shape, kind)

    def vmem(*shape, kind=BF16):
        return pltpu.VMEM(shape, kind)

    return pl.pallas_call(
        functools.partial(task_kernel, nb, early),
        out_shape=(
            array(lines, total, kind=F32),
            array(lines, total),
            array(total, mid, kind=F32),
            array(8, mid, kind=F32),
            array(padded, mid),
            array(total, mid),
            array(mid, mid),
            array(mid, LANES),
            array(early, mid, mid),
            array(mid, (9 - early) * mid),
            array(late, mid, mid),
        ),
        in_specs=[VMEM] * 12 + [ANY],
        out_specs=(VMEM,) * 11,
        scratch_shapes=[
            vmem(padded, mid),
            vmem(padded, mid),
            vmem(padded, mid),
            vmem(total, mid, kind=F32),
            vmem(total, mid, kind=F32),
            vmem(total, mid),
            vmem(4, lines, total, kind=F32),
            vmem(nb, 2, mid, kind=F32),
            DMA((2, 64)),
        ],
        cost_estimate=LONG,
        compiler_params=pltpu.CompilerParams(
            collective_id=23, has_side_effects=True, vmem_limit_bytes=60 * 2**20
        ),
    )(shared_act, mask, mask_line, targets, sizes, norms, *weights, *streams_weights, own)


def task_back_kernel(
    images,
    early,
    shared_act,
    mask,
    sizes,
    norms,
    head,
    message_start,
    gate,
    message_end,
    from_direct,
    slopes,
    pre_five,
    stats,
    grad_msg,
    grad_gate,
    message_grads,
    back,
    head_grads,
    head_rest,
    message_done,
    sums_out,
    left,
    right,
    grad_five,
    grad,
    slots_five,
    *rest,
):
    place = Place(images)
    mail = Mail(rest[-1])
    sums_of = [
        Reduce(
            mail,
            place,
            message_grads.at[offset],
            *rest[3 * offset : 3 * offset + 3],
            message_done.at[offset],
        )
        for offset in range(early)
    ]
    total = mask.shape[0]
    late = message_end.shape[0]
    mid = pre_five.shape[1]
    greet(place.others)
    sums_out[...] = jnp.zeros_like(sums_out)
    sums_of[0].start()
    sums_of[1].start()
    for cells in (left, right, grad_five):
        clear_ends(cells, total)
    widen(grad_msg, left, right, total)

    def message_weight(offset):
        if offset < early:
            return message_start[offset]
        return head[9 + offset - early] if offset < 9 - late else message_end[offset - 9 + late]

    def task_grads(rows):
        found = conv_rows(
            (left, grad_msg, right), rows, lambda offset, window: dot_t(window, message_weight(offset)), True
        )
        found = found + dot_t(grad_gate[rows, :], gate[...])
        grad[rows, :] = found + t_dot(slopes[:, rows], from_direct[...])

    loop(total, BLOCK, task_grads)
    sums = norm_back(stats, norms, mask, grad, pre_five, 0, mid, lambda rows: grad[rows, :])
    copies = send_sums(mail, place, slots_five, sums)
    sums_of[0].middle()
    sums_of[1].middle()
    for one in sums_of[2:]:
        one.start()
    for copy in copies:
        copy.wait_recv()
    bias_sum, gain_sum = add_up(slots_five)
    sums_out[0:1, :] = gain_sum
    sums_out[1:2, :] = bias_sum

    def put(rows, value):
        grad_five[pl.ds(pl.multiple_of(PITCH + rows.start, 16), CHUNK), :] = value

    through(stats, norms, mask, sizes, grad, pre_five, 0, mid, bias_sum, gain_sum, put)
    widen(grad_five, left, right, total)
    shifted = (left, grad_five, right)

    def head_back(rows):
        back[rows, :] = conv_rows(
            shifted, rows, lambda offset, window: dot_t(window, head[offset]), True
        ).astype(BF16)

    loop(total, BLOCK, head_back)
    for one in sums_of[2:]:
        one.middle()
    sums_of[0].finish()
    sums_of[1].finish()
    for offset in range(9):
        row, col = 2 - offset // 3, 2 - offset % 3
        window = shifted[col][PITCH * row : PITCH * row + total, :]
        found = t_dot(shared_act[PITCH : PITCH + total, :], window).astype(BF16)
        kept = head_grads.shape[0]
        if offset < kept:
            head_grads[offset] = found
        else:
            head_rest[:, (offset - kept) * mid : (offset - kept + 1) * mid] = found
    for one in sums_of[2:]:
        one.finish()
    mail.close()


def one_task_back(nb, early, kept, shared_act, mask, sizes, norms, weights, from_direct, slopes, rest):
    total = mask.shape[0]
    padded, mid = shared_act.shape
    lines, share = nb // 2, mid // nb

    def array(*shape, kind=BF16):
        return jax.ShapeDtypeStruct(shape, kind)

    def vmem(*shape, kind=BF16):
        return pltpu.VMEM(shape, kind)

    return pl.pallas_call(
        functools.partial(task_back_kernel, nb, early),
        out_shape=(
            array(total, mid),
            array(kept, mid, mid),
            array(mid, (9 - kept) * mid),
            array(early, share, mid),
            array(8, mid, kind=F32),
        ),
        in_specs=[VMEM] * 15,
        out_specs=(VMEM,) * 5,
        scratch_shapes=[
            vmem(padded, mid),
            vmem(padded, mid),
            vmem(padded, mid),
            vmem(total, mid, kind=F32),
            vmem(nb, 2, mid, kind=F32),
        ]
        + early * reduce_scratch(lines, share, mid, False)
        + [DMA((2, 48))],
        cost_estimate=LONG,
        compiler_params=pltpu.CompilerParams(
            collective_id=24, has_side_effects=True, vmem_limit_bytes=60 * 2**20
        ),
    )(shared_act, mask, sizes, norms, *weights, from_direct, slopes, *rest)


def last_kernel(shares, sums, all_shares, all_sums, sems):
    place = Place(2)
    mail = Mail(sems)
    blk = place.blk
    greet([place.mate, place.across])
    here = [mail.local(shares, all_shares.at[blk]), mail.local(sums, all_sums.at[blk])]
    both = []
    for source, slots in ((sums, all_sums), (shares, all_shares)):
        far = mail.send(source, slots.at[blk], place.across)
        near = mail.send(source, slots.at[blk], place.mate)
        both.append((far, near, slots))
    for far, near, slots in both:
        far.wait_recv()
        passed = slots.at[blk ^ 2]
        last = mail.send(passed, passed, place.mate)
        near.wait_recv()
        last.wait_recv()
    for copy in here:
        copy.wait()
    mail.close()


def gather_last(shares, sums):
    return pl.pallas_call(
        last_kernel,
        out_shape=(
            jax.ShapeDtypeStruct((4,) + shares.shape, shares.dtype),
            jax.ShapeDtypeStruct((4,) + sums.shape, sums.dtype),
        ),
        in_specs=[ANY] * 2,
        out_specs=(ANY, ANY),
        scratch_shapes=[DMA((2, 16))],
        compiler_params=pltpu.CompilerParams(collective_id=25, has_side_effects=True),
    )(shares, sums)


def on_device(
    nt,
    nb,
    features,
    crop_rows,
    crop_cols,
    depth_target,
    labels,
    first_weight,
    spatial_weight,
    last_weight,
    shared_weight,
    head_weights,
    message_weights,
    gate_weights,
    depth_weight,
    class_weight,
    mid_gain,
    mid_bias,
    out_gain,
    out_bias,
):
    tile_rows, cols, width = features.shape[1:]
    tile = tile_rows * cols
    rows = tile_rows * nt
    pixels = rows * cols
    tasks = head_weights.shape[0]
    mid = first_weight.shape[1]
    share = mid // nb
    slim = mid // nt
    classes = class_weight.shape[1]
    blk, batch = lax.axis_index("blk"), lax.axis_index("batch")

    image_rows = lax.dynamic_index_in_dim(crop_rows, batch, 0, False)
    image_cols = lax.dynamic_index_in_dim(crop_cols, batch, 0, False)
    row_ids = jnp.arange(rows, dtype=jnp.int32)
    col_ids = jnp.arange(PITCH, dtype=jnp.int32)
    inside_grid = (row_ids[:, None] < image_rows) & (col_ids[None, :] < image_cols)
    inside_grid = inside_grid.astype(F32)
    inside_wide = inside_grid.reshape(rows * PITCH, 1)
    inside = inside_grid[:, :cols].reshape(pixels, 1)
    inside_tile = lax.dynamic_slice_in_dim(inside, blk * tile, tile, 0)
    sizes_flat = (crop_rows * crop_cols).astype(F32)
    valid_count = jnp.sum(sizes_flat)
    sizes = jnp.broadcast_to(sizes_flat[:, None, None], (nb, 1, mid))
    tile_counts = jnp.sum(inside.reshape(nt, tile), 1)
    tile_sizes = jnp.broadcast_to(tile_counts[:, None, None], (nt, 1, mid))
    image_size = jnp.maximum(jnp.sum(inside), 1.0)

    params = jnp.concatenate(
        [
            mid_gain.reshape(-1),
            mid_bias.reshape(-1),
            out_gain,
            out_bias,
            depth_weight,
            class_weight.reshape(-1),
        ]
    )
    room = -(-params.shape[0] // (16 * LANES)) * 16 * LANES
    small = jnp.pad(params, (0, room - params.shape[0])).reshape(-1, LANES)
    feat = jnp.pad(features[0], ((0, 0), (0, PITCH - cols), (0, 0))).reshape(tile_rows * PITCH, width)
    piece = shared_weight.shape[0] // nt
    order = [
        (t * nb + b, (b * nt // nb) * nb + (b % (nb // nt)) * nt + t)
        for t in range(nt)
        for b in range(nb)
    ]
    shared_own = lax.ppermute(
        lax.dynamic_slice_in_dim(shared_weight, blk * piece, piece, 0), ("blk", "batch"), order
    )
    pair = jnp.stack([depth_target[0], labels[0].astype(F32)])
    pair = jnp.pad(pair, ((0, 6), (0, 0), (0, PITCH - cols))).reshape(8, tile_rows * PITCH)
    full_first, smalls, targets, wide_features, spatial, pre_one, stats, large = begin(
        nb, first_weight, small, spatial_weight, pair, head_weights, feat, inside_wide, sizes, tile_sizes
    )
    full_first = full_first.reshape(width, mid)
    smalls = smalls.reshape(nb, room)
    at = 0

    def taken(count):
        nonlocal at
        found = smalls[:, at : at + count]
        at += count
        return found

    norms_count = mid_gain.shape[0]
    out_share = out_gain.shape[0]
    gain_mid = taken(norms_count * share).reshape(nb, norms_count, share).swapaxes(0, 1)
    gain_mid = gain_mid.reshape(norms_count, mid).astype(F32)
    bias_mid = taken(norms_count * share).reshape(nb, norms_count, share).swapaxes(0, 1)
    bias_mid = bias_mid.reshape(norms_count, mid).astype(F32)
    gain_out = lax.dynamic_slice_in_dim(taken(out_share).reshape(width), blk * mid, mid, 0).astype(F32)
    bias_out = lax.dynamic_slice_in_dim(taken(out_share).reshape(width), blk * mid, mid, 0).astype(F32)
    full_depth = taken(share).reshape(mid, 1)
    full_classes = taken(share * classes).reshape(mid, classes)

    def slim_of(vector):
        return lax.dynamic_slice_in_dim(vector, blk * slim, slim, 0)

    def filled(vector):
        return jnp.pad(vector, (0, mid - vector.shape[0]))

    gain_two, bias_two = slim_of(gain_mid[1]), slim_of(bias_mid[1])
    gain_four, bias_four = slim_of(gain_mid[2]), slim_of(bias_mid[2])
    norms = jnp.stack(
        [
            gain_mid[0],
            bias_mid[0],
            filled(gain_two),
            filled(bias_two),
            gain_out,
            bias_out,
            filled(gain_four),
            filled(bias_four),
        ]
    )
    early, late = 4, 5
    large = lax.all_gather(large, "batch", axis=1, tiled=True)
    (
        last,
        shared,
        gate,
        message_start,
        act_one,
        act_two,
        act_three,
        shared_act,
        pre_two,
        pre_three,
        pre_four,
        stats,
    ) = bottleneck(
        nb,
        early,
        pre_one,
        stats,
        spatial,
        wide_features,
        inside_wide,
        norms,
        sizes,
        last_weight,
        shared_own,
        gate_weights,
        message_weights,
    )

    task_norms = jnp.stack(
        [
            lax.dynamic_index_in_dim(gain_mid, 3 + blk, 0, False),
            lax.dynamic_index_in_dim(bias_mid, 3 + blk, 0, False),
        ]
    )
    task_norms = jnp.pad(task_norms, ((0, 6), (0, 0)))
    lines = -(-(1 + classes) // 16) * 16
    stream_weight = jnp.concatenate([full_depth, full_classes], 1).T
    stream_weight = jnp.pad(stream_weight, ((0, lines - 1 - classes), (0, 0)))
    is_depth = jnp.arange(lines)[:, None] == 0
    none = jnp.zeros((), BF16)
    is_first, is_last = blk == 0, blk == tasks - 1
    own_stream = jnp.where(is_depth, is_first, is_last)
    to_depth = jnp.where(is_depth, stream_weight, none)
    to_classes = jnp.where(is_depth, none, stream_weight)
    from_gated = jnp.where(own_stream, none, stream_weight)
    from_direct = jnp.where(own_stream, stream_weight, none)
    mask_line = jnp.broadcast_to(inside_wide.reshape(1, -1), (8, rows * PITCH))
    weights = (large, message_start, gate)
    (
        streams,
        slopes,
        pre_five,
        task_stats,
        grad_msg,
        grad_gate,
        gate_grads,
        stream_grads,
        message_grads,
        message_rest,
        message_end,
    ) = one_task(
        nb,
        early,
        late,
        shared_act,
        inside_wide,
        mask_line,
        targets,
        sizes,
        task_norms,
        weights,
        (to_depth, to_classes, from_gated),
        message_weights,
    )
    own_streams = lax.dynamic_slice_in_dim(streams, blk * tile_rows * PITCH, tile_rows * PITCH, 1)
    own_streams = own_streams.reshape(lines, tile_rows, PITCH)[:, :, :cols]
    depth_out = own_streams[0]
    logits = own_streams[1 : 1 + classes].transpose(1, 2, 0)
    rest_share = lax.psum_scatter(message_rest, "batch", scatter_dimension=0, tiled=True)
    message_grads = message_grads.reshape(early, nb // 2, 2, share, mid)
    kept = 7
    back, head_grads, head_rest, message_done, task_sums = one_task_back(
        nb,
        early,
        kept,
        shared_act,
        inside_wide,
        sizes,
        task_norms,
        weights + (message_end,),
        from_direct,
        slopes,
        (pre_five, task_stats, grad_msg, grad_gate, message_grads),
    )
    message_share = message_done.reshape(early * share, mid)
    head_share = lax.psum_scatter(head_rest, "batch", scatter_dimension=0, tiled=True)

    (
        grad_input,
        share_shared,
        share_first,
        all_last,
        all_spatial,
        all_gates,
        all_stream,
        all_heads,
        all_messages,
        sums,
    ) = bottleneck_back(
        nb,
        back,
        (pre_one, pre_two, pre_three, pre_four),
        stats,
        norms,
        inside_wide,
        sizes,
        wide_features,
        (act_one, act_two, act_three),
        (spatial, last, shared, full_first),
        gate_grads,
        stream_grads,
        (message_share, head_grads, task_sums),
    )
    grad_input = grad_input.reshape(tile_rows, PITCH, width)[:, :cols]

    rest_share, head_share, share_first = lax.optimization_barrier((rest_share, head_share, share_first))
    rest_share = jnp.concatenate([rest_share, head_share], 1)
    left = 18 - early - kept
    rest_share = rest_share.reshape(share, left, mid).swapaxes(0, 1).reshape(left * share, mid)
    red_first, red_shared, all_rest = finish(nb, share_first, share_shared, rest_share)
    red_first = red_first.astype(F32).reshape(nt * share, mid)
    red_shared = red_shared.astype(F32).reshape(nt * share, mid)
    all_rest = all_rest.reshape(nt, left, share, mid)
    red_messages = jnp.concatenate(
        [all_messages.reshape(nt, early, share, mid), all_rest[:, : 9 - early]], 1
    ).astype(F32)
    red_last = all_last.astype(F32).transpose(1, 0, 2).reshape(share, width)
    red_gates = all_gates.astype(F32)
    red_spatial = all_spatial.astype(F32).reshape(nt, share, 9, slim)
    red_spatial = red_spatial.transpose(2, 1, 0, 3).reshape(9, share, mid)
    streams_red = jnp.sum(all_stream.astype(F32), 0)
    red_depth = streams_red[:, 0]
    red_classes = streams_red[:, 1 : 1 + classes]
    red_heads = jnp.concatenate(
        [all_heads.reshape(nt, kept, share, mid), all_rest[:, 9 - early :]], 1
    ).astype(F32)
    two_gain, two_bias = sums[:, 2, :slim].reshape(1, mid), sums[:, 3, :slim].reshape(1, mid)
    four_gain, four_bias = sums[:, 6, :slim].reshape(1, mid), sums[:, 7, :slim].reshape(1, mid)
    mid_gains = jnp.concatenate([sums[0, 0:1], two_gain, four_gain, sums[:, 8]], 0)
    mid_biases = jnp.concatenate([sums[0, 1:2], two_bias, four_bias, sums[:, 9]], 0)
    grad_mid_gain = lax.dynamic_slice_in_dim(mid_gains, batch * share, share, 1)
    grad_mid_bias = lax.dynamic_slice_in_dim(mid_biases, batch * share, share, 1)
    grad_out_gain = lax.dynamic_slice_in_dim(sums[:, 4].reshape(width), batch * out_share, out_share, 0)
    grad_out_bias = lax.dynamic_slice_in_dim(sums[:, 5].reshape(width), batch * out_share, out_share, 0)
    return (
        depth_out.reshape(1, tile_rows, cols),
        logits.reshape(1, tile_rows, cols, classes),
        grad_input.reshape(1, tile_rows, cols, width),
        red_first,
        red_spatial,
        red_last,
        red_shared,
        red_heads,
        red_messages,
        red_gates,
        red_depth,
        red_classes,
        grad_mid_gain,
        grad_mid_bias,
        grad_out_gain,
        grad_out_bias,
    )


def solution(mesh):
    nt, nb = mesh.shape["blk"], mesh.shape["batch"]
    placed = (
        P("batch", "blk", None, None),
        P(),
        P(),
        P("batch", "blk", None),
        P("batch", "blk", None),
        P("batch", None),
        P(None, "batch", None),
        P("batch", None),
        P("batch", None),
        P(None, None, "batch", None),
        P(None, None, "batch", None),
        P(None, "batch", None),
        P("batch"),
        P("batch", None),
        P(None, "batch"),
        P(None, "batch"),
        P("batch"),
        P("batch"),
    )
    return jax.shard_map(
        functools.partial(on_device if nb == 8 else on_device_any, nt, nb),
        mesh=mesh,
        in_specs=placed,
        out_specs=(
            P("batch", "blk", None),
            P("batch", "blk", None, None),
            P("batch", "blk", None, None),
            P("batch", None),
            P(None, "batch", None),
            P("batch", None),
            P("batch", None),
            P(None, None, "batch", None),
            P(None, None, "batch", None),
            P(None, "batch", None),
            P("batch"),
            P("batch", None),
            P(None, "batch"),
            P(None, "batch"),
            P("batch"),
            P("batch"),
        ),
        check_vma=False,
    )
```

```python
import functools

import jax
import jax.numpy as jnp
from jax import lax
from jax.experimental import pallas as pl
from jax.experimental.pallas import tpu as pltpu
from jax.sharding import PartitionSpec as P

EPSILON = 1e-05
MESH = pl.DeviceIdType.MESH
BF16 = jnp.bfloat16
F32 = jnp.float32
LANES = 128


def greet(peers):
    barrier = pltpu.get_barrier_semaphore()
    for peer in peers:
        pl.semaphore_signal(barrier, inc=1, device_id=peer, device_id_type=MESH)
    pl.semaphore_wait(barrier, len(peers))


def send(src, dst, send_sem, recv_sem, peer):
    copy = pltpu.make_async_remote_copy(
        src_ref=src,
        dst_ref=dst,
        send_sem=send_sem,
        recv_sem=recv_sem,
        device_id=peer,
        device_id_type=MESH,
    )
    copy.start()
    return copy


def first_kernel(images, weight, small, full, smalls, own, zs, xs, cs, ps):
    blk, batch = lax.axis_index("blk"), lax.axis_index("batch")
    half = weight.shape[0] // 2
    rows = pl.ds(pl.multiple_of(lax.rem(blk, 2) * half, half), half)
    side = (blk, batch ^ 1)
    mate = (blk ^ 1, batch)
    lines = range(1, images // 2)
    others = [(blk, batch ^ mask) for mask in range(1, images)]
    greet(others + [mate])
    copies = []
    here = pltpu.make_async_copy(weight, full.at[batch], own.at[0])
    here.start()
    here_small = pltpu.make_async_copy(small, smalls.at[batch], own.at[1])
    here_small.start()
    z_copies = {}
    for mask in lines:
        z_copies[mask] = send(
            weight.at[rows],
            full.at[batch, rows],
            zs.at[0, mask],
            zs.at[1, mask],
            (blk, batch ^ (2 * mask)),
        )
    x_copies = {
        0: send(weight.at[rows], full.at[batch, rows], xs.at[0, 0], xs.at[1, 0], side)
    }
    for place, peer in enumerate(others):
        copies.append(
            send(small, smalls.at[batch], ps.at[0, place], ps.at[1, place], peer)
        )
    core_copies = []

    def hand_over(source, mask):
        block = full.at[source, rows]
        core_copies.append(send(block, block, cs.at[0, mask], cs.at[1, mask], mate))

    for mask in lines:
        z_copies[mask].wait_recv()
        source = batch ^ (2 * mask)
        block = full.at[source, rows]
        x_copies[mask] = send(block, block, xs.at[0, mask], xs.at[1, mask], side)
        hand_over(source, 2 * mask)
    for mask in range(images // 2):
        x_copies[mask].wait_recv()
        hand_over(batch ^ (2 * mask + 1), 2 * mask + 1)
    for copy in core_copies + copies:
        copy.wait()
    for mask in lines:
        z_copies[mask].wait_send()
    for mask in range(images // 2):
        x_copies[mask].wait_send()
    here.wait()
    here_small.wait()


def gather_first(weight, small, images):
    any_place = pl.BlockSpec(memory_space=pl.ANY)
    dma = pltpu.SemaphoreType.DMA
    return pl.pallas_call(
        functools.partial(first_kernel, images),
        out_shape=(
            jax.ShapeDtypeStruct((images,) + weight.shape, weight.dtype),
            jax.ShapeDtypeStruct((images,) + small.shape, small.dtype),
        ),
        in_specs=[any_place] * 2,
        out_specs=(any_place, any_place),
        scratch_shapes=[
            dma((2,)),
            dma((2, images)),
            dma((2, images)),
            dma((2, images)),
            dma((2, images)),
        ],
        compiler_params=pltpu.CompilerParams(collective_id=0, has_side_effects=True),
    )(weight, small)


def tiles_kernel(block, every, own, sems):
    blk, batch = lax.axis_index("blk"), lax.axis_index("batch")
    mate, across = (blk ^ 1, batch), (blk ^ 2, batch)
    greet([mate, across])
    far = send(block, every.at[blk], sems.at[0, 0], sems.at[1, 0], across)
    near = send(block, every.at[blk], sems.at[0, 1], sems.at[1, 1], mate)
    here = pltpu.make_async_copy(block, every.at[blk], own.at[0])
    here.start()
    far.wait_recv()
    passed = every.at[blk ^ 2]
    last = send(passed, passed, sems.at[0, 2], sems.at[1, 2], mate)
    near.wait()
    last.wait()
    far.wait_send()
    here.wait()


def gather_tiles(block, ident):
    any_place = pl.BlockSpec(memory_space=pl.ANY)
    dma = pltpu.SemaphoreType.DMA
    return pl.pallas_call(
        tiles_kernel,
        out_shape=jax.ShapeDtypeStruct((4,) + block.shape, block.dtype),
        in_specs=[any_place],
        out_specs=any_place,
        scratch_shapes=[dma((1,)), dma((2, 3))],
        compiler_params=pltpu.CompilerParams(collective_id=ident, has_side_effects=True),
    )(block)


def sum_kernel(parts, total, near_in, pair, far_in, sems):
    blk, batch = lax.axis_index("blk"), lax.axis_index("batch")
    mate, across = (blk ^ 1, batch), (blk ^ 2, batch)
    greet([mate, across])
    far_first = send(parts.at[blk ^ 3], near_in.at[0], sems.at[0, 0], sems.at[1, 0], mate)
    near_next = send(parts.at[blk ^ 1], near_in.at[1], sems.at[0, 1], sems.at[1, 1], mate)
    far_first.wait_recv()
    pair[...] = (parts[blk ^ 2].astype(F32) + near_in[0].astype(F32)).astype(pair.dtype)
    far = send(pair, far_in, sems.at[0, 2], sems.at[1, 2], across)
    near_next.wait_recv()
    total[...] = parts[blk].astype(F32) + near_in[1].astype(F32)
    far.wait_recv()
    total[...] += far_in[...].astype(F32)
    far_first.wait_send()
    near_next.wait_send()
    far.wait_send()


def sum_tiles(parts, ident):
    dma = pltpu.SemaphoreType.DMA
    block = parts.shape[1:]
    vmem = pl.BlockSpec(memory_space=pltpu.VMEM)
    return pl.pallas_call(
        sum_kernel,
        out_shape=jax.ShapeDtypeStruct(block, F32),
        in_specs=[vmem],
        out_specs=vmem,
        scratch_shapes=[
            pltpu.VMEM((2,) + block, parts.dtype),
            pltpu.VMEM(block, parts.dtype),
            pltpu.VMEM(block, parts.dtype),
            dma((2, 3)),
        ],
        compiler_params=pltpu.CompilerParams(
            collective_id=ident, has_side_effects=True, vmem_limit_bytes=32 * 2**20
        ),
    )(parts)


def combine(slots, weights, half, centred):
    count = slots.shape[0]
    if not centred:
        total = slots[0]
        for at in range(1, count):
            total = total + slots[at]
        return total
    size = weights[0]
    mean = slots[0, :half] * weights[0]
    for at in range(1, count):
        size = size + weights[at]
        mean = mean + slots[at, :half] * weights[at]
    mean = mean / size
    spread = None
    for at in range(count):
        gap = slots[at, :half] - mean
        term = slots[at, half : 2 * half] + weights[at] * gap * gap
        spread = term if spread is None else spread + term
    rest = [jnp.zeros((slots.shape[1] - 2 * half, LANES), F32)] * (slots.shape[1] > 2 * half)
    return jnp.concatenate([mean, spread] + rest, 0)


def sums_kernel(images, half, centred, tiled, own, tile_sizes, sizes, total, *scratch):
    blk, batch = lax.axis_index("blk"), lax.axis_index("batch")
    slots, sems = scratch[0], scratch[1]
    peers = [(blk, batch ^ mask) for mask in range(1, images)]
    mates = [(blk ^ mask, batch) for mask in range(1, 4)] if tiled else []
    greet(peers + mates)
    if tiled:
        tile_slots, tile_sems = scratch[2], scratch[3]
        tile_slots[blk] = own[...]
        copies = [
            send(own, tile_slots.at[blk], tile_sems.at[0, at], tile_sems.at[1, at], peer)
            for at, peer in enumerate(mates)
        ]
        for copy in copies:
            copy.wait()
        slots[batch] = combine(tile_slots, tile_sizes, half, centred)
    else:
        slots[batch] = own[...]
    copies = [
        send(slots.at[batch], slots.at[batch], sems.at[0, at], sems.at[1, at], peer)
        for at, peer in enumerate(peers)
    ]
    for copy in copies:
        copy.wait()
    total[...] = combine(slots, sizes, half, centred)


def all_sums(first, second, tile_sizes, sizes, centred, tiled, ident):
    images = sizes.shape[0]
    channels = first.shape[0]
    half = channels // LANES
    rows = -(-2 * half // 8) * 8
    own = jnp.concatenate(
        [first, second, jnp.zeros(((rows - 2 * half) * LANES,), F32)]
    ).reshape(rows, LANES)
    dma = pltpu.SemaphoreType.DMA
    vmem = pl.BlockSpec(memory_space=pltpu.VMEM)
    scratch = [pltpu.VMEM((images, rows, LANES), F32), dma((2, images))]
    if tiled:
        scratch += [pltpu.VMEM((4, rows, LANES), F32), dma((2, 3))]
    total = pl.pallas_call(
        functools.partial(sums_kernel, images, half, centred, tiled),
        out_shape=jax.ShapeDtypeStruct((rows, LANES), F32),
        in_specs=[vmem] * 3,
        out_specs=vmem,
        scratch_shapes=scratch,
        compiler_params=pltpu.CompilerParams(collective_id=ident, has_side_effects=True),
    )(own, sizes if tile_sizes is None else tile_sizes, sizes)
    flat = total.reshape(-1)
    return flat[:channels], flat[channels : 2 * channels]


def silu_slope(values):
    sigmoid_value = jax.nn.sigmoid(values)
    return sigmoid_value * (1.0 + values * (1.0 - sigmoid_value))


def windows(cells, rows, cols, back):
    channels = cells.shape[1]
    padded = jnp.pad(cells.reshape(rows, cols, channels), ((1, 1), (1, 1), (0, 0)))
    taken = []
    for offset in range(9):
        row, col = offset // 3, offset % 3
        if back:
            row, col = 2 - row, 2 - col
        taken.append(padded[row : row + rows, col : col + cols].reshape(rows * cols, channels))
    return jnp.concatenate(taken, 1)


def dot(left, right):
    return jnp.dot(left, right, preferred_element_type=F32)


def dot_t(left, right):
    return jnp.einsum("pd,cd->pc", left, right, preferred_element_type=F32)


def t_dot(left, right):
    return jnp.einsum("pc,pd->cd", left, right, preferred_element_type=F32)


def on_device_any(
    nt,
    nb,
    features,
    crop_rows,
    crop_cols,
    depth_target,
    labels,
    first_weight,
    spatial_weight,
    last_weight,
    shared_weight,
    head_weights,
    message_weights,
    gate_weights,
    depth_weight,
    class_weight,
    mid_gain,
    mid_bias,
    out_gain,
    out_bias,
):
    tile_rows, cols, width = features.shape[1:]
    tile = tile_rows * cols
    rows = tile_rows * nt
    pixels = rows * cols
    tasks = head_weights.shape[0]
    mid = first_weight.shape[1]
    share = mid // nb
    slim = mid // nt
    piece = width // (nb * nt)
    wide = nb * piece
    classes = class_weight.shape[1]
    blk, batch = lax.axis_index("blk"), lax.axis_index("batch")

    image_rows = lax.dynamic_index_in_dim(crop_rows, batch, 0, False)
    image_cols = lax.dynamic_index_in_dim(crop_cols, batch, 0, False)
    row_ids = jnp.arange(rows, dtype=jnp.int32)
    col_ids = jnp.arange(cols, dtype=jnp.int32)
    inside_grid = (row_ids[:, None] < image_rows) & (col_ids[None, :] < image_cols)
    inside = inside_grid.astype(F32).reshape(pixels, 1)
    inside_tile = lax.dynamic_slice_in_dim(inside, blk * tile, tile, 0)
    sizes_flat = (crop_rows * crop_cols).astype(F32)
    valid_count = jnp.sum(sizes_flat)
    sizes = jnp.broadcast_to(sizes_flat[:, None, None], (nb, 1, LANES))
    tile_counts = jnp.sum(inside.reshape(nt, tile), 1)
    tile_sizes = jnp.broadcast_to(tile_counts[:, None, None], (nt, 1, LANES))
    image_size = jnp.maximum(jnp.sum(inside), 1.0)
    tile_size = jnp.maximum(jnp.sum(inside_tile), 1.0)

    params = jnp.concatenate(
        [
            mid_gain.reshape(-1),
            mid_bias.reshape(-1),
            out_gain,
            out_bias,
            depth_weight,
            class_weight.reshape(-1),
        ]
    )
    room = -(-params.shape[0] // (16 * LANES)) * 16 * LANES
    small = jnp.pad(params, (0, room - params.shape[0])).reshape(-1, LANES)
    full_first, smalls = gather_first(first_weight, small, nb)
    full_first = full_first.reshape(width, mid)
    smalls = smalls.reshape(nb, room)
    at = 0

    def taken(count):
        nonlocal at
        found = smalls[:, at : at + count]
        at += count
        return found

    norms = mid_gain.shape[0]
    gain_mid = taken(norms * share).reshape(nb, norms, share).swapaxes(0, 1)
    gain_mid = gain_mid.reshape(norms, mid).astype(F32)
    bias_mid = taken(norms * share).reshape(nb, norms, share).swapaxes(0, 1)
    bias_mid = bias_mid.reshape(norms, mid).astype(F32)
    gain_out = lax.dynamic_index_in_dim(taken(nt * piece).reshape(nb, nt, piece), blk, 1, False)
    gain_out = gain_out.reshape(wide).astype(F32)
    bias_out = lax.dynamic_index_in_dim(taken(nt * piece).reshape(nb, nt, piece), blk, 1, False)
    bias_out = bias_out.reshape(wide).astype(F32)
    full_depth = taken(share).reshape(mid, 1)
    full_classes = taken(share * classes).reshape(mid, classes)
    stream_weight = jnp.concatenate([full_depth, full_classes], 1)

    spatial = lax.all_gather(
        lax.dynamic_slice_in_dim(spatial_weight, blk * slim, slim, 2), "batch", axis=1, tiled=True
    )
    last = lax.dynamic_index_in_dim(last_weight.reshape(share, nb, nt, piece), blk, 2, False)
    last = lax.all_gather(last.reshape(share, wide), "batch", axis=0, tiled=True)
    shared = lax.dynamic_slice_in_dim(shared_weight, blk * piece, piece, 0)
    shared = lax.all_gather(shared, "batch", axis=0, tiled=True)
    head = lax.all_gather(
        lax.dynamic_index_in_dim(head_weights, blk, 0, False), "batch", axis=1, tiled=True
    )
    message = lax.all_gather(
        lax.dynamic_index_in_dim(message_weights, blk, 0, False), "batch", axis=1, tiled=True
    )
    gate = lax.all_gather(
        lax.dynamic_index_in_dim(gate_weights, blk, 0, False), "batch", axis=0, tiled=True
    )

    flat_features = features.reshape(tile, width)
    cut = flat_features.reshape(tile, nb, nt, piece).transpose(2, 0, 1, 3).reshape(nt, tile, wide)
    wide_features = swap_tiles(cut, blk, nt)

    def slim_of(vector):
        return lax.dynamic_slice_in_dim(vector, blk * slim, slim, 0)

    def normalize(values, mask, local_size, gain, bias, tiled, ident):
        mean = jnp.sum(values * mask, 0) / local_size
        gap = values - mean
        spread = jnp.sum(gap * gap * mask, 0)
        centre, total = all_sums(mean, spread, tile_sizes, sizes, True, tiled, ident)
        inverse = lax.rsqrt(total / valid_count + EPSILON)
        normed = (values - centre) * inverse
        return normed * gain + bias, normed, inverse

    def normalize_back(grad, normed, inverse, gain, mask, tiled, ident):
        bias_sum, gain_sum = all_sums(
            jnp.sum(grad, 0), jnp.sum(grad * normed, 0), tile_sizes, sizes, False, tiled, ident
        )
        back = (
            inverse * gain * (grad - bias_sum / valid_count - normed * gain_sum / valid_count) * mask
        )
        return back.astype(BF16), gain_sum, bias_sum

    def act(values, mask):
        return (jax.nn.silu(values) * mask).astype(BF16)

    def by_rows(blocks):
        return blocks.reshape(pixels, blocks.shape[2])

    def by_channels(blocks):
        return blocks.swapaxes(0, 1).reshape(pixels, nt * blocks.shape[2])

    def cut_channels(values):
        return values.astype(BF16).reshape(pixels, nt, slim).swapaxes(0, 1)

    pre_one = dot(flat_features, full_first)
    norm_one, normed_one, inverse_one = normalize(
        pre_one, inside_tile, tile_size, gain_mid[0], bias_mid[0], True, 1
    )
    act_one = by_rows(gather_tiles(act(norm_one, inside_tile), 2))
    pre_two = dot(windows(act_one, rows, cols, False), spatial.reshape(9 * mid, slim))
    gain_two, bias_two = slim_of(gain_mid[1]), slim_of(bias_mid[1])
    norm_two, normed_two, inverse_two = normalize(
        pre_two, inside, image_size, gain_two, bias_two, False, 3
    )
    act_two = by_channels(gather_tiles(act(norm_two, inside), 4))
    pre_three = dot(act_two, last)
    norm_three, normed_three, inverse_three = normalize(
        pre_three, inside, image_size, gain_out, bias_out, False, 5
    )
    joined = norm_three + wide_features.astype(F32)
    act_three = act(joined, inside)
    pre_four = sum_tiles(cut_channels(dot(act_three, shared)), 6)
    gain_four, bias_four = slim_of(gain_mid[2]), slim_of(bias_mid[2])
    norm_four, normed_four, inverse_four = normalize(
        pre_four, inside, image_size, gain_four, bias_four, False, 3
    )
    shared_act = by_channels(gather_tiles(act(norm_four, inside), 4))

    gain_task = lax.dynamic_index_in_dim(gain_mid, 3 + blk, 0, False)
    bias_task = lax.dynamic_index_in_dim(bias_mid, 3 + blk, 0, False)
    pre_five = dot(windows(shared_act, rows, cols, False), head.reshape(9 * mid, mid))
    norm_five, normed_five, inverse_five = normalize(
        pre_five, inside, image_size, gain_task, bias_task, False, 5
    )
    task_act = act(norm_five, inside)
    messages = dot(windows(task_act, rows, cols, False), message.reshape(9 * mid, mid))
    gate_open = jax.nn.sigmoid(dot(task_act, gate))
    gated = (gate_open * messages).astype(BF16)
    is_first, is_last = blk == 0, blk == tasks - 1
    depth_part = jnp.where(is_first, task_act, gated)
    sem_part = jnp.where(is_last, task_act, gated)
    depth_share = jnp.einsum("pc,co->op", depth_part, full_depth, preferred_element_type=F32)
    class_share = jnp.einsum("pc,co->op", sem_part, full_classes, preferred_element_type=F32)
    lift = -(-(1 + classes) // 8) * 8 - 1 - classes
    shares = jnp.concatenate([depth_share, class_share, jnp.zeros((lift, pixels), F32)], 0)
    streams = jnp.sum(gather_tiles(shares, 7), 0).T
    depth_out = lax.dynamic_slice_in_dim(streams, blk * tile, tile, 0)[:, 0]
    logits = lax.dynamic_slice_in_dim(streams, blk * tile, tile, 0)[:, 1 : 1 + classes]
    targets = by_rows(gather_tiles_pair(depth_target, labels, tile))
    all_depth, all_logits = streams[:, :1], streams[:, 1 : 1 + classes]
    depth_slope = ((all_depth - targets[:, :1]) * inside).astype(BF16)
    onehot = (targets[:, 1:2] == jnp.arange(classes, dtype=jnp.int32)[None, :].astype(F32)).astype(F32)
    logit_slope = ((jax.nn.softmax(all_logits, axis=1) - onehot) * inside).astype(BF16)
    grad_depth = t_dot(depth_part, depth_slope)
    grad_classes = t_dot(sem_part, logit_slope)
    depth_back = depth_slope.astype(F32) * full_depth.astype(F32).reshape(1, mid)
    sem_back = dot_t(logit_slope, full_classes)
    zero = jnp.zeros((), F32)
    grad_gated = jnp.where(is_first, zero, depth_back) + jnp.where(is_last, zero, sem_back)
    grad_direct = jnp.where(is_first, depth_back, zero) + jnp.where(is_last, sem_back, zero)

    grad_msg = (grad_gated * gate_open).astype(BF16)
    grad_gate = (grad_gated * messages * gate_open * (1.0 - gate_open)).astype(BF16)
    msg_windows = windows(grad_msg, rows, cols, True)
    gate_grads = t_dot(task_act, grad_gate).astype(BF16)
    message_grads = t_dot(task_act, msg_windows).astype(BF16)
    share_messages = lax.psum_scatter(message_grads, "batch", scatter_dimension=0, tiled=True)
    task_grad = (
        grad_direct
        + dot_t(grad_gate, gate)
        + dot(msg_windows, message.swapaxes(1, 2).reshape(9 * mid, mid))
    )
    grad_norm_five = task_grad * inside * silu_slope(norm_five)
    grad_pre_five, gain_sum_five, bias_sum_five = normalize_back(
        grad_norm_five, normed_five, inverse_five, gain_task, inside, False, 8
    )
    five_windows = windows(grad_pre_five, rows, cols, True)
    head_grads = t_dot(shared_act, five_windows).astype(BF16)
    share_heads = lax.psum_scatter(head_grads, "batch", scatter_dimension=0, tiled=True)
    shared_back = dot(five_windows, head.swapaxes(1, 2).reshape(9 * mid, mid))
    shared_back = sum_tiles(cut_channels(shared_back), 6)

    grad_norm_four = shared_back * inside * silu_slope(norm_four)
    grad_pre_four, gain_sum_four, bias_sum_four = normalize_back(
        grad_norm_four, normed_four, inverse_four, gain_four, inside, False, 9
    )
    grad_four = by_channels(gather_tiles(grad_pre_four, 4))
    shared_grads = t_dot(act_three, grad_four).astype(BF16)
    grad_joined = dot_t(grad_four, shared) * inside * silu_slope(joined)
    grad_three, gain_sum_three, bias_sum_three = normalize_back(
        grad_joined, normed_three, inverse_three, gain_out, inside, False, 8
    )
    last_grads = t_dot(act_two, grad_three).astype(BF16)
    two_back = sum_tiles(cut_channels(dot_t(grad_three, last)), 6)
    grad_norm_two = two_back * inside * silu_slope(norm_two)
    grad_two, gain_sum_two, bias_sum_two = normalize_back(
        grad_norm_two, normed_two, inverse_two, gain_two, inside, False, 9
    )
    two_windows = windows(grad_two, rows, cols, True)
    spatial_grads = t_dot(act_one, two_windows).astype(BF16)
    one_back = dot(two_windows, spatial.swapaxes(1, 2).reshape(9 * slim, mid))
    one_back = sum_tiles(one_back.astype(BF16).reshape(nt, tile, mid), 10)
    grad_norm_one = one_back * inside_tile * silu_slope(norm_one)
    grad_one, gain_sum_one, bias_sum_one = normalize_back(
        grad_norm_one, normed_one, inverse_one, gain_mid[0], inside_tile, True, 11
    )
    all_one = by_rows(gather_tiles(grad_one, 2))
    first_grads = t_dot(wide_features, all_one).astype(BF16)
    joined_tiles = swap_tiles(grad_joined.astype(BF16).reshape(nt, tile, wide), blk, nt)
    joined_tiles = joined_tiles.reshape(nt, tile, nb, piece).transpose(1, 2, 0, 3).reshape(tile, width)
    grad_input = dot_t(grad_one, full_first) + joined_tiles.astype(F32)

    stream_grads = jnp.concatenate([grad_depth, grad_classes], 1)
    stream_grads = jnp.pad(stream_grads, ((0, 0), (0, LANES - 1 - classes))).astype(BF16)
    late = jnp.concatenate(
        [spatial_grads, shared_grads.reshape(nb, piece, mid).reshape(mid, -1),
         last_grads, first_grads.reshape(mid, -1), gate_grads, stream_grads],
        1,
    )
    late_share = lax.psum_scatter(late, "batch", scatter_dimension=0, tiled=True)
    early_share = jnp.concatenate([share_messages, share_heads], 1)
    early = lax.all_gather(early_share, "blk", axis=0, tiled=False).astype(F32)
    late_all = gather_tiles(late_share, 12).astype(F32)
    early = early.reshape(nt, share, 2, 9, mid).transpose(2, 0, 3, 1, 4)
    red_messages, red_heads = early[0], early[1]
    at = 0

    def part(count):
        nonlocal at
        found = late_all[:, :, at : at + count]
        at += count
        return found

    red_spatial = part(9 * slim).reshape(nt, share, 9, slim).transpose(2, 1, 0, 3).reshape(9, share, mid)
    red_shared = part(wide * mid // mid).reshape(nt * piece, mid)
    red_last = part(wide).reshape(nt, share, nb, piece).transpose(1, 2, 0, 3).reshape(share, width)
    red_first = part(wide * mid // mid).reshape(nt * piece, mid)
    red_gates = part(mid)
    streams_red = jnp.sum(part(LANES), 0)
    red_depth = streams_red[:, 0]
    red_classes = streams_red[:, 1 : 1 + classes]

    sums = jnp.concatenate(
        [
            gain_sum_five,
            bias_sum_five,
            gain_sum_three,
            bias_sum_three,
            gain_sum_two,
            bias_sum_two,
            gain_sum_four,
            bias_sum_four,
        ]
    ).reshape(-1, LANES)
    sums = jnp.pad(sums, ((0, -sums.shape[0] % 8), (0, 0)))
    sums = gather_tiles(sums, 13).reshape(nt, -1)
    five_gain, five_bias = sums[:, :mid], sums[:, mid : 2 * mid]
    at_out = 2 * mid
    three_gain = sums[:, at_out : at_out + wide].reshape(nt, nb, piece)
    three_bias = sums[:, at_out + wide : at_out + 2 * wide].reshape(nt, nb, piece)
    at_slim = at_out + 2 * wide
    slims = [
        sums[:, at_slim + i * slim : at_slim + (i + 1) * slim].reshape(1, mid) for i in range(4)
    ]
    mid_gains = jnp.concatenate([gain_sum_one[None], slims[0], slims[2], five_gain], 0)
    mid_biases = jnp.concatenate([bias_sum_one[None], slims[1], slims[3], five_bias], 0)
    grad_mid_gain = lax.dynamic_slice_in_dim(mid_gains, batch * share, share, 1)
    grad_mid_bias = lax.dynamic_slice_in_dim(mid_biases, batch * share, share, 1)
    grad_out_gain = lax.dynamic_index_in_dim(three_gain, batch, 1, False).reshape(nt * piece)
    grad_out_bias = lax.dynamic_index_in_dim(three_bias, batch, 1, False).reshape(nt * piece)
    return (
        depth_out.reshape(1, tile_rows, cols),
        logits.reshape(1, tile_rows, cols, classes),
        grad_input.reshape(1, tile_rows, cols, width),
        red_first,
        red_spatial,
        red_last,
        red_shared,
        red_heads,
        red_messages,
        red_gates,
        red_depth,
        red_classes,
        grad_mid_gain,
        grad_mid_bias,
        grad_out_gain,
        grad_out_bias,
    )


def swap_tiles(blocks, blk, nt):
    out = jnp.zeros_like(blocks)
    out = lax.dynamic_update_index_in_dim(
        out, lax.dynamic_index_in_dim(blocks, blk, 0, False), blk, 0
    )
    for mask in range(1, nt):
        sent = lax.dynamic_index_in_dim(blocks, blk ^ mask, 0, False)
        came = lax.ppermute(sent, "blk", [(i, i ^ mask) for i in range(nt)])
        out = lax.dynamic_update_index_in_dim(out, came, blk ^ mask, 0)
    return out.reshape(-1, blocks.shape[2])


def gather_tiles_pair(depth_target, labels, tile):
    pair = jnp.stack([depth_target.reshape(tile), labels.reshape(tile).astype(F32)], 0)
    pair = jnp.pad(pair, ((0, 6), (0, 0)))
    return gather_tiles(pair, 14).swapaxes(1, 2)


PITCH = 48
CHUNK = 64
BLOCK = 256
ANY = pl.BlockSpec(memory_space=pl.ANY)
VMEM = pl.BlockSpec(memory_space=pltpu.VMEM)
DMA = pltpu.SemaphoreType.DMA
LONG = pl.CostEstimate(flops=80_000_000_000, bytes_accessed=30_000_000, transcendentals=2_000_000)


class Mail:
    def __init__(self, sems):
        self.sems, self.used, self.open = sems, 0, []

    def send(self, src, dst, peer, keep=True):
        copy = send(src, dst, self.sems.at[0, self.used], self.sems.at[1, self.used], peer)
        self.used += 1
        if keep:
            self.open.append(copy.wait_send)
        return copy

    def local(self, src, dst):
        copy = pltpu.make_async_copy(src, dst, self.sems.at[0, self.used])
        copy.start()
        self.used += 1
        return copy

    def close(self):
        for wait in self.open:
            wait()
        self.open = []


class Place:
    def __init__(self, images):
        self.blk, self.batch = lax.axis_index("blk"), lax.axis_index("batch")
        self.images = images
        self.mate = (self.blk ^ 1, self.batch)
        self.across = (self.blk ^ 2, self.batch)
        self.tiles = [(self.blk ^ mask, self.batch) for mask in range(1, 4)]
        self.others = [(self.blk, self.batch ^ mask) for mask in range(1, images)]
        self.side = (self.blk, self.batch ^ 1)


class Spread:
    def __init__(self, mail, place, own, slot):
        self.mail, self.place, self.own, self.slot = mail, place, own, slot
        self.z_copies, self.x_copies = [], []

    def start(self):
        place, here = self.place, self.slot(self.place.batch)
        self.here = self.mail.local(self.own, here)
        for mask in range(1, place.images // 2):
            peer = (place.blk, place.batch ^ (2 * mask))
            self.z_copies.append(self.mail.send(self.own, here, peer))
        self.x_copies.append(self.mail.send(self.own, here, place.side))
        return self

    def forward(self):
        for mask, copy in enumerate(self.z_copies, 1):
            copy.wait_recv()
            block = self.slot(self.place.batch ^ (2 * mask))
            self.x_copies.append(self.mail.send(block, block, self.place.side))

    def finish(self):
        self.here.wait()
        for copy in self.x_copies:
            copy.wait_recv()


def share_tiles(mail, place, slot):
    own = slot(place.blk)
    far = mail.send(own, own, place.across, False)
    near = mail.send(own, own, place.mate, False)
    far.wait_recv()
    passed = slot(place.blk ^ 2)
    last = mail.send(passed, passed, place.mate, False)
    near.wait()
    last.wait()
    far.wait_send()


def loop(total, step, body, base=0):
    def run(at, carry):
        body(pl.ds(pl.multiple_of(base + at * step, step), step))
        return carry

    lax.fori_loop(0, total // step, run, 0)


PIECES = 3


def pieces_of(total):
    size = total // PIECES
    return [(at * size, size) for at in range(PIECES)]


def share_pieces(mail, place, slot, total, produce=None, consume=None, meanwhile=None):
    pieces = pieces_of(total)
    far, near, last = [], [], []
    for first, size in pieces:
        if produce is not None:
            produce(first, size)
        own = slot(place.blk, first, size)
        far.append(mail.send(own, own, place.across, False))
        near.append(mail.send(own, own, place.mate, False))
    if meanwhile is not None:
        meanwhile()

    def use(at):
        near[at].wait_recv()
        last[at].wait_recv()
        if consume is not None:
            consume(*pieces[at])

    for at, (first, size) in enumerate(pieces):
        far[at].wait_recv()
        passed = slot(place.blk ^ 2, first, size)
        last.append(mail.send(passed, passed, place.mate, False))
        if at > 0:
            use(at - 1)
    use(len(pieces) - 1)
    for copy in far + near + last:
        copy.wait_send()


def folded(values):
    return jnp.sum(values.reshape(values.shape[0] // 8, 8, values.shape[1]), 0)


def loop_sums(total, channels, count, body, base=0):
    def run(at, carry):
        found = body(pl.ds(pl.multiple_of(base + at * CHUNK, CHUNK), CHUNK))
        return tuple(kept + folded(one) for kept, one in zip(carry, found))

    start = tuple(jnp.zeros((8, channels), F32) for _ in range(count))
    return [jnp.sum(one, 0, keepdims=True) for one in lax.fori_loop(0, total // CHUNK, run, start)]


def merge(slots, sizes, channels):
    count = slots.shape[0]
    size, mean = None, None
    for at in range(count):
        weight = sizes[at, :, :channels]
        term = slots[at, 0:1, :] * weight
        size = weight if size is None else size + weight
        mean = term if mean is None else mean + term
    mean = mean / size
    spread = None
    for at in range(count):
        gap = slots[at, 0:1, :] - mean
        term = slots[at, 1:2, :] + sizes[at, :, :channels] * gap * gap
        spread = term if spread is None else spread + term
    return mean, spread, size


def add_up(slots):
    total = slots[0]
    for at in range(1, slots.shape[0]):
        total = total + slots[at]
    return total[0:1, :], total[1:2, :]


def swap_sums(mail, place, slots, meanwhile=None):
    own = slots.at[place.batch]
    copies = [mail.send(own, own, peer) for peer in place.others]
    if meanwhile is not None:
        meanwhile()
    for copy in copies:
        copy.wait_recv()


def swap_tile_sums(mail, place, slots):
    own = slots.at[place.blk]
    copies = [mail.send(own, own, peer) for peer in place.tiles]
    for copy in copies:
        copy.wait_recv()


def local_stats(pre, mask, base, total, channels, size):
    def first(rows):
        return (pre[rows, :] * mask[at_base(base, rows), :],)

    (summed,) = loop_sums(total, channels, 1, first)
    mean = summed / jnp.maximum(size, 1.0)

    def second(rows):
        gap = pre[rows, :] - mean
        return (gap * gap * mask[at_base(base, rows), :],)

    (spread,) = loop_sums(total, channels, 1, second)
    return mean, spread


def at_base(base, rows):
    if base is None:
        return rows
    return pl.ds(pl.multiple_of(base + rows.start, CHUNK), rows.size)


def batch_norm_stats(mail, place, pre, mask, slots, sizes, stats, row, channels, meanwhile=None):
    total = pre.shape[0]
    mean, spread = local_stats(pre, mask, None, total, channels, sizes[place.batch, :, :channels])
    slots[place.batch] = jnp.concatenate([mean, spread], 0)
    swap_sums(mail, place, slots, meanwhile)
    keep_stats(slots, sizes, stats, row, channels)


def keep_stats(slots, sizes, stats, row, channels):
    mean, spread, size = merge(slots, sizes, channels)
    stats[row : row + 1, :channels] = mean
    stats[row + 1 : row + 2, :channels] = lax.rsqrt(spread / size + EPSILON)


def silu(values):
    return values * jax.nn.sigmoid(values)


def widen(cells, left, right, total):
    def body(rows):
        seen = cells[pl.ds(pl.multiple_of(rows.start + PITCH - 16, 16), CHUNK + 32), :].astype(F32)
        here = pl.ds(pl.multiple_of(rows.start + PITCH, 16), CHUNK)
        left[here, :] = seen[15 : 15 + CHUNK].astype(BF16)
        right[here, :] = seen[17 : 17 + CHUNK].astype(BF16)

    loop(total, CHUNK, body)


def clear_ends(cells, total):
    zeros = jnp.zeros((PITCH, cells.shape[1]), cells.dtype)
    cells[0:PITCH, :] = zeros
    cells[PITCH + total : 2 * PITCH + total, :] = zeros


def conv_rows(shifted, rows, weight, back, offsets=range(9)):
    total = None
    for offset in offsets:
        row, col = offset // 3, offset % 3
        if back:
            row, col = 2 - row, 2 - col
        window = shifted[col][pl.ds(pl.multiple_of(rows.start + PITCH * row, 16), rows.size), :]
        product = weight(offset, window)
        total = product if total is None else total + product
    return total


def sum_over_tiles(mail, place, part, near_in, pair, far_in, total, out, meanwhile=None, produce=None):
    mine_far, mine = part(place.blk ^ 2), part(place.blk)
    pieces = pieces_of(total)
    near_far, near_own, far = [], [], []

    def pairs(rows):
        pair[rows, :] = (mine_far[rows, :].astype(F32) + near_in[0, rows, :].astype(F32)).astype(BF16)

    def pass_on(at):
        first, size = pieces[at]
        near_far[at].wait_recv()
        loop(size, CHUNK, pairs, first)
        here = pl.ds(first, size)
        far.append(mail.send(pair.at[here], far_in.at[here], place.across))

    for at, (first, size) in enumerate(pieces):
        if produce is not None:
            produce(first, size)
        here = pl.ds(first, size)
        near_far.append(mail.send(part(place.blk ^ 3).at[here], near_in.at[0, here], place.mate))
        near_own.append(mail.send(part(place.blk ^ 1).at[here], near_in.at[1, here], place.mate))
        if at > 0:
            pass_on(at - 1)
    pass_on(len(pieces) - 1)
    if meanwhile is not None:
        meanwhile()

    def finish(rows):
        out[rows, :] = (
            mine[rows, :].astype(F32) + near_in[1, rows, :].astype(F32) + far_in[rows, :].astype(F32)
        )

    for at, (first, size) in enumerate(pieces):
        near_own[at].wait_recv()
        far[at].wait_recv()
        loop(size, CHUNK, finish, first)


def start_kernel(
    images,
    weight,
    small,
    spatial_own,
    pair,
    head_all,
    feat,
    mask,
    sizes,
    tile_sizes,
    full,
    smalls,
    targets,
    wide,
    spatial,
    pre_one,
    stats,
    head_own,
    slots_tile,
    slots_one,
    sems,
):
    place = Place(images)
    mail = Mail(sems)
    blk, batch = place.blk, place.batch
    depth = weight.shape[0]
    half = depth // 2
    mid = weight.shape[1]
    tile = feat.shape[0]
    slim = mid // 4
    share = spatial_own.shape[1]
    mine = pl.ds(pl.multiple_of(lax.rem(blk, 2) * half, half), half)
    greet(place.others + place.tiles)
    here = mail.local(weight, full.at[batch])
    here_small = mail.local(small, smalls.at[batch])
    here_head = mail.local(head_all.at[blk], head_own)
    z_copies, x_copies, arrived, late = {}, [], [], []
    for peer in place.others:
        late.append(mail.send(small, smalls.at[batch], peer))
    for mask_z in range(1, images // 2):
        z_copies[mask_z] = mail.send(
            weight.at[mine], full.at[batch, mine], (blk, batch ^ (2 * mask_z))
        )
    x_copies.append(mail.send(weight.at[mine], full.at[batch, mine], place.side))
    lanes = pl.ds(pl.multiple_of(blk * slim, slim), slim)
    got_spatial = Spread(
        mail,
        place,
        spatial_own.at[:, :, lanes],
        lambda index: spatial.at[:, pl.ds(pl.multiple_of(index * share, share), share), :],
    ).start()

    def columns(index):
        return feat.at[:, pl.ds(pl.multiple_of(index * mid, mid), mid)]

    landing = wide.at[pl.ds(pl.multiple_of(blk * tile, tile), tile), :]
    here_wide = mail.local(columns(blk), landing)
    line = targets.at[:, pl.ds(pl.multiple_of(blk * tile, tile), tile)]
    here_line = mail.local(pair, line)
    for mask_t in range(1, 4):
        late.append(mail.send(pair, line, (blk ^ mask_t, batch)))
        late.append(mail.send(columns(blk ^ mask_t), landing, (blk ^ mask_t, batch)))

    def hand_over(source):
        block = full.at[source, mine]
        arrived.append(mail.send(block, block, place.mate))

    for mask_z in range(1, images // 2):
        z_copies[mask_z].wait_recv()
        source = batch ^ (2 * mask_z)
        block = full.at[source, mine]
        x_copies.append(mail.send(block, block, place.side))
        hand_over(source)
    for mask_z in range(images // 2):
        x_copies[mask_z].wait_recv()
        hand_over(batch ^ (2 * mask_z + 1))
    stats[...] = jnp.zeros_like(stats)
    here.wait()
    for copy in arrived:
        copy.wait_recv()

    def reduce(rows):
        total = None
        for index in range(images):
            product = dot(feat[rows, index * depth : (index + 1) * depth], full[index])
            total = product if total is None else total + product
        pre_one[rows, :] = total

    loop(tile, tile // 2, reduce)
    base = blk * tile
    mean, spread = local_stats(pre_one, mask, base, tile, mid, tile_sizes[blk, :, :])
    slots_tile[blk] = jnp.concatenate([mean, spread], 0)
    swap_tile_sums(mail, place, slots_tile)
    mean, spread, _ = merge(slots_tile, tile_sizes, mid)
    slots_one[batch] = jnp.concatenate([mean, spread], 0)
    swap_sums(mail, place, slots_one, got_spatial.forward)
    keep_stats(slots_one, sizes, stats, 0, mid)
    got_spatial.finish()
    for copy in late:
        copy.wait_recv()
    here_small.wait()
    here_wide.wait()
    here_line.wait()
    here_head.wait()
    mail.close()


def begin(nb, weight, small, spatial, pair, heads, feat, mask, sizes, tile_sizes):
    depth, mid = weight.shape
    tile = feat.shape[0]

    def array(*shape, kind=BF16):
        return jax.ShapeDtypeStruct(shape, kind)

    return pl.pallas_call(
        functools.partial(start_kernel, nb),
        out_shape=(
            array(nb, depth, mid),
            array(nb, *small.shape),
            array(8, 4 * tile, kind=F32),
            array(4 * tile, mid),
            array(9, mid, mid // 4),
            array(tile, mid, kind=F32),
            array(8, mid, kind=F32),
            array(*heads.shape[1:]),
        ),
        in_specs=[ANY] * 5 + [VMEM] * 4,
        out_specs=(VMEM, ANY, ANY, VMEM, VMEM, VMEM, VMEM, ANY),
        scratch_shapes=[
            pltpu.VMEM((4, 2, mid), F32),
            pltpu.VMEM((nb, 2, mid), F32),
            DMA((2, 64)),
        ],
        cost_estimate=LONG,
        compiler_params=pltpu.CompilerParams(
            collective_id=21, has_side_effects=True, vmem_limit_bytes=40 * 2**20
        ),
    )(weight, small, spatial, pair, heads, feat, mask, sizes, tile_sizes)


def forward_kernel(
    images,
    early,
    pre_one,
    first_stats,
    spatial,
    wide,
    mask,
    norms,
    sizes,
    last_own,
    shared_own,
    gate_own,
    message_own,
    last,
    shared,
    gate,
    message,
    act_one,
    act_two,
    act_three,
    shared_act,
    pre_two,
    pre_three,
    pre_four,
    stats,
    one_left,
    one_right,
    parts,
    near_in,
    pair,
    far_in,
    slots_two,
    slots_three,
    slots_four,
    sems,
):
    place = Place(images)
    mail = Mail(sems)
    blk, batch = place.blk, place.batch
    tile, total = pre_one.shape[0], mask.shape[0]
    mid = pre_one.shape[1]
    slim = pre_two.shape[1]
    share = last_own.shape[0]
    base = blk * tile
    greet(place.others + place.tiles)

    def rows_of(index):
        return pl.ds(pl.multiple_of(index * share, share), share)

    def slim_lanes(index):
        return pl.ds(pl.multiple_of(index * slim, slim), slim)

    lanes = slim_lanes(blk)
    wide_lanes = pl.ds(pl.multiple_of(blk * mid, mid), mid)
    got_last = Spread(mail, place, last_own.at[:, wide_lanes], lambda index: last.at[rows_of(index), :])
    got_shared = Spread(mail, place, shared_own, lambda index: shared.at[rows_of(index), :])
    got_gate = Spread(mail, place, gate_own.at[blk], lambda index: gate.at[rows_of(index), :])
    got_message = [
        Spread(
            mail,
            place,
            message_own.at[blk, offset],
            lambda index, offset=offset: message.at[offset, rows_of(index), :],
        )
        for offset in range(early)
    ]
    got_last.start()
    got_shared.start()
    stats[...] = first_stats[...]
    clear_ends(act_one, total)
    clear_ends(shared_act, total)
    clear_ends(one_left, total)
    clear_ends(one_right, total)

    def act_first(rows):
        value = (pre_one[rows, :] - stats[0:1, :]) * stats[1:2, :] * norms[0:1, :] + norms[1:2, :]
        value = silu(value) * mask[at_base(base, rows), :]
        act_one[pl.ds(pl.multiple_of(PITCH + base + rows.start, 16), CHUNK), :] = value.astype(BF16)

    share_pieces(
        mail,
        place,
        lambda index, first, size: act_one.at[
            pl.ds(pl.multiple_of(PITCH + index * tile + first, 16), size), :
        ],
        tile,
        lambda first, size: loop(size, CHUNK, act_first, first),
    )
    widen(act_one, one_left, one_right, total)
    got_last.forward()
    got_shared.forward()

    shifted = (one_left, act_one, one_right)

    def conv_two(rows):
        pre_two[rows, :] = conv_rows(
            shifted, rows, lambda offset, window: dot(window, spatial[offset]), False
        )

    loop(total, BLOCK, conv_two)

    def after_two():
        got_gate.start()
        got_message[0].start()
        got_message[1].start()

    batch_norm_stats(mail, place, pre_two, mask, slots_two, sizes, stats, 2, slim, after_two)

    def act_second(rows):
        value = (pre_two[rows, :] - stats[2:3, :slim]) * stats[3:4, :slim]
        value = silu(value * norms[2:3, :slim] + norms[3:4, :slim]) * mask[rows, :]
        act_two[rows, lanes] = value.astype(BF16)

    got_last.finish()

    def expand(rows):
        pre_three[rows, :] = dot(act_two[rows, :], last[...])

    share_pieces(
        mail,
        place,
        lambda index, first, size: act_two.at[pl.ds(first, size), slim_lanes(index)],
        total,
        lambda first, size: loop(size, CHUNK, act_second, first),
        lambda first, size: loop(size, BLOCK, expand, first),
    )
    got_gate.forward()

    def after_three():
        got_message[0].forward()
        got_message[1].forward()
        got_message[2].start()
        got_message[3].start()

    batch_norm_stats(mail, place, pre_three, mask, slots_three, sizes, stats, 4, mid, after_three)
    got_shared.finish()

    def act_third(rows):
        normed = (pre_three[rows, :] - stats[4:5, :]) * stats[5:6, :]
        value = normed * norms[4:5, :] + norms[5:6, :] + wide[rows, :].astype(F32)
        act_three[rows, :] = (silu(value) * mask[rows, :]).astype(BF16)

    loop(total, CHUNK, act_third)

    def reduce(rows):
        parts[rows, :] = dot(act_three[rows, :], shared[...]).astype(BF16)

    sum_over_tiles(
        mail,
        place,
        lambda index: parts.at[:, slim_lanes(index)],
        near_in,
        pair,
        far_in,
        total,
        pre_four,
        None,
        lambda first, size: loop(size, BLOCK, reduce, first),
    )

    def after_four():
        got_message[2].forward()
        got_message[3].forward()
        for later in got_message[4:]:
            later.start()

    batch_norm_stats(mail, place, pre_four, mask, slots_four, sizes, stats, 6, slim, after_four)

    def act_fourth(rows):
        value = (pre_four[rows, :] - stats[6:7, :slim]) * stats[7:8, :slim]
        value = silu(value * norms[6:7, :slim] + norms[7:8, :slim]) * mask[rows, :]
        shared_act[pl.ds(pl.multiple_of(PITCH + rows.start, 16), CHUNK), lanes] = value.astype(BF16)

    share_pieces(
        mail,
        place,
        lambda index, first, size: shared_act.at[pl.ds(PITCH + first, size), slim_lanes(index)],
        total,
        lambda first, size: loop(size, CHUNK, act_fourth, first),
    )
    for later in got_message[4:]:
        later.forward()
    got_gate.finish()
    for one in got_message:
        one.finish()
    mail.close()


def bottleneck(nb, early, pre_one, stats, spatial, wide, mask, norms, sizes, last, shared, gate, message):
    tile, total = pre_one.shape[0], mask.shape[0]
    mid = pre_one.shape[1]
    slim = mid // 4
    padded = total + 2 * PITCH

    def array(*shape, kind=BF16):
        return jax.ShapeDtypeStruct(shape, kind)

    outs = (
        array(mid, mid),
        array(mid, mid),
        array(mid, mid),
        array(early, mid, mid),
        array(padded, mid),
        array(total, mid),
        array(total, mid),
        array(padded, mid),
        array(total, slim, kind=F32),
        array(total, mid, kind=F32),
        array(total, slim, kind=F32),
        array(8, mid, kind=F32),
    )
    return pl.pallas_call(
        functools.partial(forward_kernel, nb, early),
        out_shape=outs,
        in_specs=[VMEM] * 7 + [ANY] * 4,
        out_specs=(VMEM, VMEM, ANY, ANY) + (VMEM,) * 8,
        scratch_shapes=[
            pltpu.VMEM((padded, mid), BF16),
            pltpu.VMEM((padded, mid), BF16),
            pltpu.VMEM((total, mid), BF16),
            pltpu.VMEM((2, total, slim), BF16),
            pltpu.VMEM((total, slim), BF16),
            pltpu.VMEM((total, slim), BF16),
            pltpu.VMEM((nb, 2, slim), F32),
            pltpu.VMEM((nb, 2, mid), F32),
            pltpu.VMEM((nb, 2, slim), F32),
            DMA((2, 192)),
        ],
        cost_estimate=LONG,
        compiler_params=pltpu.CompilerParams(
            collective_id=20, has_side_effects=True, vmem_limit_bytes=60 * 2**20
        ),
    )(pre_one, stats, spatial, wide, mask, norms, sizes, last, shared, gate, message)


class Tiles:
    def __init__(self, mail, place, slot, own=None):
        self.mail, self.place, self.slot, self.own = mail, place, slot, own

    def start(self):
        own, here = self.own, self.slot(self.place.blk)
        if own is None:
            own = here
        else:
            self.mail.open.append(self.mail.local(own, here).wait)
        self.far = self.mail.send(own, here, self.place.across)
        self.near = self.mail.send(own, here, self.place.mate)

    def forward(self):
        self.far.wait_recv()
        passed = self.slot(self.place.blk ^ 2)
        self.last = self.mail.send(passed, passed, self.place.mate)

    def end(self):
        self.near.wait_recv()
        self.last.wait_recv()


class Reduce:
    def __init__(self, mail, place, grad, from_side, summed, from_line, out):
        self.mail, self.place = mail, place
        self.grad, self.from_side, self.summed = grad, from_side, summed
        self.from_line, self.out = from_line, out
        self.side = lax.rem(place.batch, 2)
        self.line = lax.div(place.batch, 2)

    def start(self):
        self.from_x = self.mail.send(self.grad.at[:, 1 - self.side], self.from_side, self.place.side)

    def own_half(self, at):
        return self.grad[at, self.side]

    def add_side(self):
        self.from_x.wait_recv()
        lines = self.from_side.shape[0]
        for at in range(lines):
            self.summed[at] = (self.own_half(at).astype(F32) + self.from_side[at].astype(F32)).astype(BF16)

    def middle(self):
        self.add_side()
        self.send_lines()

    def send_lines(self):
        place = self.place
        lines = self.summed.shape[0]
        self.copies = [
            self.mail.send(
                self.summed.at[self.line ^ mask],
                self.from_line.at[mask - 1],
                (place.blk, place.batch ^ (2 * mask)),
            )
            for mask in range(1, lines)
        ]

    def finish(self):
        total = self.summed[self.line].astype(F32)
        for at, copy in enumerate(self.copies):
            copy.wait_recv()
            total = total + self.from_line[at].astype(F32)
        self.out[...] = total.astype(BF16)


class ReduceFar(Reduce):
    def start(self):
        super().start()
        self.fetch = self.mail.local(self.grad.at[:, self.side], self.summed)

    def own_half(self, at):
        if at == 0:
            self.fetch.wait()
        return self.summed[at]


class Job:
    def __init__(self, reduce, tiles):
        self.steps = []
        if reduce is not None:
            self.steps += [reduce.start, reduce.middle, reduce.finish]
        if tiles is not None:
            self.steps += [tiles.start, tiles.forward, tiles.end]


def step(*jobs):
    for job in jobs:
        if job.steps:
            job.steps.pop(0)()


def reduce_scratch(lines, share, columns, own):
    found = [pltpu.VMEM((lines, 2, share, columns), BF16)] if own else []
    return found + [
        pltpu.VMEM((lines, share, columns), BF16),
        pltpu.VMEM((lines, share, columns), BF16),
        pltpu.VMEM((lines - 1, share, columns), BF16),
    ]


def send_sums(mail, place, slots, sums):
    slots[place.batch] = jnp.concatenate(sums, 0)
    own = slots.at[place.batch]
    return [mail.send(own, own, peer) for peer in place.others]


def silu_back(value):
    sigmoid_value = jax.nn.sigmoid(value)
    return sigmoid_value * (1.0 + value * (1.0 - sigmoid_value))


def norm_back(stats, norms, mask, grad, pre, row, channels, lead, offset=None, skip=None, rows_of=None):
    def body(rows):
        normed = (pre[rows, :] - stats[row : row + 1, :channels]) * stats[row + 1 : row + 2, :channels]
        value = normed * norms[row : row + 1, :channels] + norms[row + 1 : row + 2, :channels]
        if skip is not None:
            value = value + skip[rows, :].astype(F32)
        found = lead(rows) * mask[at_base(offset, rows), :] * silu_back(value)
        grad[rows, :] = found
        return found, found * normed

    first, size = (0, pre.shape[0]) if rows_of is None else rows_of
    return loop_sums(size, channels, 2, body, first)


def through(stats, norms, mask, sizes, grad, pre, row, channels, bias_sum, gain_sum, put, offset=None, rows_of=None):
    count = sizes[0, :, :channels]
    for at in range(1, sizes.shape[0]):
        count = count + sizes[at, :, :channels]
    scale = stats[row + 1 : row + 2, :channels] * norms[row : row + 1, :channels]
    bias_part, gain_part = bias_sum / count, gain_sum / count

    def body(rows):
        normed = (pre[rows, :] - stats[row : row + 1, :channels]) * stats[row + 1 : row + 2, :channels]
        found = scale * (grad[rows, :] - bias_part - normed * gain_part)
        put(rows, (found * mask[at_base(offset, rows), :]).astype(BF16))

    first, size = (0, pre.shape[0]) if rows_of is None else rows_of
    loop(size, CHUNK, body, first)


def backward_kernel(
    images,
    back,
    pre_one,
    pre_two,
    pre_three,
    pre_four,
    stats,
    norms,
    mask,
    sizes,
    wide,
    act_one,
    act_two,
    act_three,
    spatial,
    last,
    shared,
    first,
    gate_grads,
    stream_grads,
    message_share,
    head_grads,
    task_sums,
    grad_input,
    share_shared,
    share_first,
    all_last,
    all_spatial,
    all_gates,
    all_stream,
    all_heads,
    all_messages,
    all_sums,
    near_four,
    pair_four,
    far_four,
    grad_four,
    all_four,
    grad_three,
    low_three,
    low_joined,
    joined_rows,
    near_two,
    pair_two,
    far_two,
    grad_two,
    two_left,
    two_here,
    two_right,
    turned,
    strip,
    near_one,
    pair_one,
    far_one,
    grad_one,
    all_one,
    slots_four,
    slots_three,
    slots_two,
    slots_tile,
    slots_one,
    *rest,
):
    place = Place(images)
    sems = rest[-1]
    mail = Mail(sems)
    blk, batch = place.blk, place.batch
    tile, total = pre_one.shape[0], mask.shape[0]
    mid = pre_one.shape[1]
    slim = pre_two.shape[1]
    base = blk * tile
    red_shared = Reduce(mail, place, *rest[0:4], share_shared)
    red_last = Reduce(mail, place, *rest[4:8], all_last.at[blk])
    red_first = Reduce(mail, place, *rest[8:12], share_first)
    red_spatial = Reduce(mail, place, *rest[12:16], all_spatial.at[blk])
    red_gates = Reduce(mail, place, gate_grads, *rest[16:19], all_gates.at[blk])
    red_stream = Reduce(mail, place, stream_grads, *rest[19:22], all_stream.at[blk])
    share = share_shared.shape[0]
    results, sums_out, at = rest[22], rest[23], 24
    heads, messages = [], []

    def tiles_of(slots, first_row, count, own):
        rows_at = pl.ds(first_row, count)
        return Tiles(mail, place, lambda index: slots.at[index, rows_at], own)

    def slots_of(slots):
        return Tiles(mail, place, lambda index: slots.at[index])

    kept = head_grads.shape[0]
    for offset in range(kept):
        result = results.at[offset]
        reduce = ReduceFar(mail, place, head_grads.at[offset], *rest[at : at + 3], result)
        at += 3
        heads.append(Job(reduce, tiles_of(all_heads, offset * share, share, result)))
    heads += [Job(None, None)] * (9 - kept)
    early = message_share.shape[0] // share
    ends = [0, early // 3, 2 * early // 3, early]
    for begin_at, end_at in zip(ends[:-1], ends[1:]):
        count = (end_at - begin_at) * share
        own = message_share.at[pl.ds(begin_at * share, count)]
        messages.append(Job(None, tiles_of(all_messages, begin_at * share, count, own)))
    job_shared, job_first = Job(red_shared, None), Job(red_first, None)
    job_sums = Job(None, Tiles(mail, place, lambda index: all_sums.at[index], sums_out))
    job_last, job_spatial = Job(red_last, slots_of(all_last)), Job(red_spatial, slots_of(all_spatial))
    job_gates, job_stream = Job(red_gates, slots_of(all_gates)), Job(red_stream, slots_of(all_stream))
    greet(place.others + place.tiles)

    def slim_lanes(index):
        return pl.ds(pl.multiple_of(index * slim, slim), slim)

    def tile_rows(index):
        return pl.ds(pl.multiple_of(index * tile, tile), tile)

    def keep(row, bias_sum, gain_sum, channels):
        sums_out[row : row + 1, :channels] = gain_sum
        sums_out[row + 1 : row + 2, :channels] = bias_sum

    sums_out[...] = jnp.zeros_like(sums_out)
    sums_out[8:10, :] = task_sums[0:2, :]
    for cells in (two_left, two_here, two_right):
        clear_ends(cells, total)
    step(heads[0], heads[1], job_gates, job_stream)

    sum_over_tiles(
        mail, place, lambda index: back.at[:, slim_lanes(index)], near_four, pair_four, far_four, total, grad_four
    )
    sums = norm_back(stats, norms, mask, grad_four, pre_four, 6, slim, lambda rows: grad_four[rows, :])
    copies = send_sums(mail, place, slots_four, sums)
    step(heads[0], heads[1], job_gates, job_stream)
    step(heads[2], heads[3], heads[4])
    for offset in range(9):
        turned[offset * slim : (offset + 1) * slim, :] = spatial[offset].T
    for copy in copies:
        copy.wait_recv()
    bias_sum, gain_sum = add_up(slots_four)
    keep(6, bias_sum, gain_sum, slim)
    lanes = slim_lanes(blk)

    def put_four(rows, value):
        all_four[rows, lanes] = value

    def joined_back(rows):
        return dot_t(all_four[rows, :], shared[...])

    sums = []

    def make_four(first, size):
        through(
            stats, norms, mask, sizes, grad_four, pre_four, 6, slim, bias_sum, gain_sum, put_four, None, (first, size)
        )

    def use_four(first, size):
        sums.append(
            norm_back(
                stats, norms, mask, grad_three, pre_three, 4, mid, joined_back, None, wide, (first, size)
            )
        )

    share_pieces(
        mail,
        place,
        lambda index, first, size: all_four.at[pl.ds(first, size), slim_lanes(index)],
        total,
        make_four,
        use_four,
    )
    step(messages[0])
    sums = [sum(one[1:], one[0]) for one in zip(*sums)]
    copies = send_sums(mail, place, slots_three, sums)
    step(heads[2], heads[3], heads[4])
    step(heads[5], heads[6])
    step(heads[0], heads[1], job_gates, job_stream)
    step(messages[0])
    grads, lines = red_shared.grad, red_shared.grad.shape[0]
    grads[...] = t_dot(act_three[...], all_four[...]).astype(BF16).reshape(grads.shape)
    step(job_shared)

    def lower(rows):
        low_joined[rows, :] = grad_three[rows, :].astype(BF16)

    loop(total, CHUNK, lower)
    for copy in copies:
        copy.wait_recv()
    bias_sum, gain_sum = add_up(slots_three)
    keep(4, bias_sum, gain_sum, mid)

    def put_three(rows, value):
        low_three[rows, :] = value

    def two_part(rows):
        all_four[rows, :] = dot_t(low_three[rows, :], last[...]).astype(BF16)

    def make_two(first, size):
        through(
            stats, norms, mask, sizes, grad_three, pre_three, 4, mid, bias_sum, gain_sum, put_three, None, (first, size)
        )
        loop(size, BLOCK, two_part, first)

    sum_over_tiles(
        mail,
        place,
        lambda index: all_four.at[:, slim_lanes(index)],
        near_two,
        pair_two,
        far_two,
        total,
        grad_two,
        None,
        make_two,
    )
    step(messages[1])
    landing = joined_rows.at[:, pl.ds(pl.multiple_of(blk * mid, mid), mid)]
    joined_here = mail.local(low_joined.at[tile_rows(blk)], landing)
    joined_copies = [
        mail.send(low_joined.at[tile_rows(blk ^ mask_t)], landing, (blk ^ mask_t, batch))
        for mask_t in range(1, 4)
    ]
    sums = norm_back(stats, norms, mask, grad_two, pre_two, 2, slim, lambda rows: grad_two[rows, :])
    copies = send_sums(mail, place, slots_two, sums)
    step(heads[5], heads[6], job_shared)
    step(heads[7], heads[8])
    step(heads[2], heads[3], heads[4])
    grads = red_last.grad
    grads[...] = t_dot(act_two[...], low_three[...]).astype(BF16).reshape(grads.shape)
    step(job_last)
    for copy in copies:
        copy.wait_recv()
    bias_sum, gain_sum = add_up(slots_two)
    keep(2, bias_sum, gain_sum, slim)

    def put_two(rows, value):
        two_here[pl.ds(pl.multiple_of(rows.start + PITCH, 16), CHUNK), :] = value

    through(stats, norms, mask, sizes, grad_two, pre_two, 2, slim, bias_sum, gain_sum, put_two)
    widen(two_here, two_left, two_right, total)
    shifted = (two_left, two_here, two_right)

    def one_part(rows):
        for offset in range(9):
            row, col = 2 - offset // 3, 2 - offset % 3
            window = shifted[col][pl.ds(pl.multiple_of(rows.start + PITCH * row, 16), BLOCK), :]
            strip[:, offset * slim : (offset + 1) * slim] = window
        low_three[rows, :] = dot(strip[...], turned[...]).astype(BF16)

    loop(total, BLOCK, one_part)

    def spatial_grads():
        grads = red_spatial.grad
        for offset in range(9):
            row, col = 2 - offset // 3, 2 - offset % 3
            window = shifted[col][PITCH * row : PITCH * row + total, :]
            found = t_dot(act_one[PITCH : PITCH + total, :], window).astype(BF16)
            grads[:, :, :, offset * slim : (offset + 1) * slim] = found.reshape(grads.shape[:3] + (slim,))
        step(job_spatial)

    sum_over_tiles(
        mail,
        place,
        lambda index: low_three.at[tile_rows(index)],
        near_one,
        pair_one,
        far_one,
        tile,
        grad_one,
        spatial_grads,
    )
    step(messages[1])
    step(messages[2])
    step(heads[0], heads[1], job_gates, job_stream)
    sums = norm_back(stats, norms, mask, grad_one, pre_one, 0, mid, lambda rows: grad_one[rows, :], base)
    slots_tile[blk] = jnp.concatenate(sums, 0)
    swap_tile_sums(mail, place, slots_tile)
    copies = send_sums(mail, place, slots_one, list(add_up(slots_tile)))
    step(heads[7], heads[8], job_last, job_spatial)
    step(heads[5], heads[6], job_shared)
    for copy in copies:
        copy.wait_recv()
    bias_sum, gain_sum = add_up(slots_one)
    keep(0, bias_sum, gain_sum, mid)

    def put_one(rows, value):
        all_one[at_base(base, rows), :] = value

    def make_one(first, size):
        through(
            stats, norms, mask, sizes, grad_one, pre_one, 0, mid, bias_sum, gain_sum, put_one, base, (first, size)
        )

    def inputs_back():
        joined_here.wait()
        for copy in joined_copies:
            copy.wait_recv()

        def input_grads(rows):
            own = all_one[pl.ds(pl.multiple_of(base + rows.start, CHUNK), rows.size), :]
            grad_input[rows, :] = dot_t(own, first[...]) + joined_rows[rows, :].astype(F32)

        loop(tile, tile // 3, input_grads)

    share_pieces(
        mail,
        place,
        lambda index, first, size: all_one.at[
            pl.ds(pl.multiple_of(index * tile + first, CHUNK), size), :
        ],
        tile,
        make_one,
        None,
        inputs_back,
    )
    grads = red_first.grad
    grads[...] = t_dot(wide[...], all_one[...]).astype(BF16).reshape(grads.shape)
    step(job_first)
    step(messages[2], job_sums)
    step(heads[0], heads[1], job_gates, job_stream)
    step(heads[2], heads[3], heads[4], heads[5], heads[6])
    step(job_first)
    step(heads[2], heads[3], heads[4], heads[5], heads[6], job_sums)
    step(heads[7], heads[8], job_last, job_spatial)
    step(heads[7], heads[8], job_last, job_spatial)
    step(job_first)
    step(heads[7], heads[8], job_last, job_spatial)
    for job in messages + heads + [job_gates, job_stream, job_last, job_spatial, job_sums]:
        step(job)
    mail.close()


def bottleneck_back(nb, back, pres, stats, norms, mask, sizes, wide, acts, weights, gate_grads, stream_grads, task_grads):
    tile, total = pres[0].shape[0], mask.shape[0]
    mid = pres[0].shape[1]
    slim = mid // 4
    lines, share = nb // 2, mid // nb
    padded = total + 2 * PITCH
    width = weights[3].shape[0]

    def array(*shape, kind=BF16):
        return jax.ShapeDtypeStruct(shape, kind)

    def vmem(*shape, kind=BF16):
        return pltpu.VMEM(shape, kind)

    scratch = [
        vmem(2, total, slim),
        vmem(total, slim),
        vmem(total, slim),
        vmem(total, slim, kind=F32),
        vmem(total, mid),
        vmem(total, mid, kind=F32),
        vmem(total, mid),
        vmem(total, mid),
        vmem(tile, width),
        vmem(2, total, slim),
        vmem(total, slim),
        vmem(total, slim),
        vmem(total, slim, kind=F32),
        vmem(padded, slim),
        vmem(padded, slim),
        vmem(padded, slim),
        vmem(9 * slim, mid),
        vmem(BLOCK, 9 * slim),
        vmem(2, tile, mid),
        vmem(tile, mid),
        vmem(tile, mid),
        vmem(tile, mid, kind=F32),
        vmem(total, mid),
        vmem(nb, 2, slim, kind=F32),
        vmem(nb, 2, mid, kind=F32),
        vmem(nb, 2, slim, kind=F32),
        vmem(4, 2, mid, kind=F32),
        vmem(nb, 2, mid, kind=F32),
    ]
    for columns in (mid, mid, mid, 9 * slim):
        scratch += reduce_scratch(lines, share, columns, True)
    for columns in (mid, LANES):
        scratch += reduce_scratch(lines, share, columns, False)
    message_share, head_grads, task_sums = task_grads
    kept = head_grads.shape[0]
    scratch += [vmem(kept, share, mid), vmem(16, mid, kind=F32)]
    for _ in range(kept):
        scratch += reduce_scratch(lines, share, mid, False)
    scratch.append(DMA((2, 256)))
    return pl.pallas_call(
        functools.partial(backward_kernel, nb),
        out_shape=(
            array(tile, width, kind=F32),
            array(share, mid),
            array(share, mid),
            array(4, share, mid),
            array(4, share, 9 * slim),
            array(4, share, mid),
            array(4, share, LANES),
            array(4, kept * share, mid),
            array(4, message_share.shape[0], mid),
            array(4, 16, mid, kind=F32),
        ),
        in_specs=[VMEM] * 19 + [ANY] * 2 + [VMEM],
        out_specs=(VMEM,) * 7 + (ANY, ANY, VMEM),
        scratch_shapes=scratch,
        cost_estimate=LONG,
        compiler_params=pltpu.CompilerParams(
            collective_id=22, has_side_effects=True, vmem_limit_bytes=62 * 2**20
        ),
    )(
        back,
        *pres,
        stats,
        norms,
        mask,
        sizes,
        wide,
        *acts,
        *weights,
        gate_grads.reshape(lines, 2, share, mid),
        stream_grads.reshape(lines, 2, share, LANES),
        message_share,
        head_grads.reshape(kept, lines, 2, share, mid),
        task_sums,
    )


def finish_kernel(images, first, shared, rest, first_rows, shared_rows, all_rest, sems):
    place = Place(images)
    mail = Mail(sems)
    blk, batch = place.blk, place.batch
    target = (lax.rem(batch, 4), 2 * blk + lax.div(batch, 4))
    source = (lax.div(batch, 2), 4 * lax.rem(batch, 2) + blk)
    stays = (target[0] == blk) & (target[1] == batch)
    moves = jnp.logical_not(stays)
    barrier = pltpu.get_barrier_semaphore()
    for peer in (place.mate, place.across):
        pl.semaphore_signal(barrier, inc=1, device_id=peer, device_id_type=MESH)

    @pl.when(moves)
    def _():
        pl.semaphore_signal(barrier, inc=1, device_id=source, device_id_type=MESH)
        pl.semaphore_wait(barrier, 3)

    @pl.when(stays)
    def _():
        pl.semaphore_wait(barrier, 2)

    def hop(at, own, slots):
        return pltpu.make_async_remote_copy(
            src_ref=own,
            dst_ref=slots.at[target[0]],
            send_sem=sems.at[0, at],
            recv_sem=sems.at[1, at],
            device_id=target,
            device_id_type=MESH,
        )

    def stay(at, own, slots):
        return pltpu.make_async_copy(own, slots.at[blk], sems.at[0, at])

    mail.used = 2
    pairs = [(0, first, first_rows), (1, shared, shared_rows)]

    @pl.when(moves)
    def _():
        for pair in pairs:
            hop(*pair).start()

    @pl.when(stays)
    def _():
        for pair in pairs:
            stay(*pair).start()

    tiles = Tiles(mail, place, lambda index: all_rest.at[index], rest)
    tiles.start()
    jobs = [Tiles(mail, place, lambda index, slots=slots: slots.at[index]) for _, _, slots in pairs]

    @pl.when(moves)
    def _():
        for pair in pairs:
            hop(*pair).wait()

    @pl.when(stays)
    def _():
        for pair in pairs:
            stay(*pair).wait()

    for job in jobs:
        job.start()
    for job in [tiles] + jobs:
        job.forward()
    for job in [tiles] + jobs:
        job.end()
    mail.close()


def finish(nb, first, shared, rest):
    share, mid = first.shape
    return pl.pallas_call(
        functools.partial(finish_kernel, nb),
        out_shape=(
            jax.ShapeDtypeStruct((4, share, mid), BF16),
            jax.ShapeDtypeStruct((4, share, mid), BF16),
            jax.ShapeDtypeStruct((4,) + rest.shape, BF16),
        ),
        in_specs=[ANY] * 3,
        out_specs=(ANY,) * 3,
        scratch_shapes=[DMA((2, 32))],
        compiler_params=pltpu.CompilerParams(collective_id=26, has_side_effects=True),
    )(first, shared, rest)


def task_kernel(
    images,
    early,
    shared_act,
    mask,
    mask_line,
    targets,
    sizes,
    norms,
    head,
    message_start,
    gate,
    to_depth,
    to_classes,
    from_gated,
    message_own,
    streams,
    slopes,
    pre_five,
    stats,
    grad_msg,
    grad_gate,
    gate_grads,
    stream_grads,
    message_grads,
    message_rest,
    message_end,
    left,
    right,
    task,
    messages,
    opened,
    gated,
    slots,
    slots_five,
    sems,
):
    place = Place(images)
    mail = Mail(sems)
    total = mask.shape[0]
    mid = pre_five.shape[1]
    is_first, is_last = place.blk == 0, place.blk == 3
    greet(place.others + [place.mate, place.across])
    late = message_end.shape[0]
    share = message_own.shape[2]
    got = [
        Spread(
            mail,
            place,
            message_own.at[place.blk, 9 - late + at],
            lambda index, at=at: message_end.at[at, pl.ds(pl.multiple_of(index * share, share), share), :],
        )
        for at in range(late)
    ]
    for one in got[: (late + 1) // 2]:
        one.start()
    stats[...] = jnp.zeros_like(stats)
    for cells in (left, right, task, grad_msg):
        clear_ends(cells, total)
    widen(shared_act, left, right, total)

    def heads(rows):
        pre_five[rows, :] = conv_rows(
            (left, shared_act, right), rows, lambda offset, window: dot(window, head[offset]), False
        )

    loop(total, BLOCK, heads)

    def behind():
        for one in got[: (late + 1) // 2]:
            one.forward()
        for one in got[(late + 1) // 2 :]:
            one.start()

    batch_norm_stats(mail, place, pre_five, mask, slots_five, sizes, stats, 0, mid, behind)
    for one in got[(late + 1) // 2 :]:
        one.forward()

    def act_task(rows):
        value = (pre_five[rows, :] - stats[0:1, :]) * stats[1:2, :] * norms[0:1, :] + norms[1:2, :]
        task[pl.ds(pl.multiple_of(PITCH + rows.start, 16), CHUNK), :] = (
            silu(value) * mask[rows, :]
        ).astype(BF16)

    loop(total, CHUNK, act_task)
    widen(task, left, right, total)

    def message_weight(offset):
        if offset < early:
            return message_start[offset]
        return head[9 + offset - early] if offset < 9 - late else message_end[offset - 9 + late]

    def here(rows):
        return pl.ds(pl.multiple_of(PITCH + rows.start, 16), rows.size)

    def start_messages(rows):
        messages[rows, :] = conv_rows(
            (left, task, right),
            rows,
            lambda offset, window: dot(window, message_weight(offset)),
            False,
            range(9 - late),
        )
        opened[rows, :] = jax.nn.sigmoid(dot(task[here(rows), :], gate[...]))

    loop(total, BLOCK, start_messages)
    for one in got:
        one.finish()

    def send_messages(rows):
        messages[rows, :] += conv_rows(
            (left, task, right),
            rows,
            lambda offset, window: dot(window, message_weight(offset)),
            False,
            range(9 - late, 9),
        )
        own = task[here(rows), :]
        part = (opened[rows, :] * messages[rows, :]).astype(BF16)
        gated[rows, :] = part
        depth_part = jnp.where(is_first, own, part)
        sem_part = jnp.where(is_last, own, part)
        slots[place.blk, :, rows] = dot_t(to_depth[...], depth_part) + dot_t(to_classes[...], sem_part)

    loop(total, BLOCK, send_messages)
    share_tiles(mail, place, lambda index: slots.at[index])
    classes = to_depth.shape[0]
    kind = lax.broadcasted_iota(jnp.int32, (classes, 2 * BLOCK), 0)

    def compare(rows):
        value = slots[0, :, rows] + slots[1, :, rows] + slots[2, :, rows] + slots[3, :, rows]
        streams[:, rows] = value
        is_class = (kind >= 1) & (kind <= CLASSES)
        top = jnp.max(jnp.where(is_class, value, -jnp.inf), 0, keepdims=True)
        power = jnp.where(is_class, jnp.exp(value - top), 0.0)
        chance = power / jnp.sum(power, 0, keepdims=True)
        label = targets[1:2, rows]
        chance = chance - jnp.where((kind - 1).astype(F32) == label, 1.0, 0.0)
        slope = jnp.where(kind == 0, value - targets[0:1, rows], jnp.where(is_class, chance, 0.0))
        slopes[:, rows] = (slope * mask_line[0:1, rows]).astype(BF16)

    loop(total, 2 * BLOCK, compare)
    by_part = dot(slopes[...], gated[...])
    by_task = dot(slopes[...], task[PITCH : PITCH + total, :])
    row = lax.broadcasted_iota(jnp.int32, by_part.shape, 0)
    use_task = ((row == 0) & is_first) | ((row > 0) & is_last)
    found = jnp.where(use_task, by_task, by_part)
    found = jnp.concatenate([found, jnp.zeros((LANES - classes, mid), F32)], 0)
    stream_grads[...] = found.T.astype(BF16)

    def grads(rows):
        grad = t_dot(slopes[:, rows], from_gated[...])
        open_part = opened[rows, :]
        grad_msg[here(rows), :] = (grad * open_part).astype(BF16)
        grad_gate[rows, :] = (grad * messages[rows, :] * open_part * (1.0 - open_part)).astype(BF16)

    loop(total, BLOCK, grads)
    gate_grads[...] = t_dot(task[PITCH : PITCH + total, :], grad_gate[...]).astype(BF16)
    widen(grad_msg, left, right, total)
    shifted = (left, grad_msg, right)
    for offset in range(9):
        row, col = 2 - offset // 3, 2 - offset % 3
        window = shifted[col][PITCH * row : PITCH * row + total, :]
        found = t_dot(task[PITCH : PITCH + total, :], window).astype(BF16)
        if offset < early:
            message_grads[offset] = found
        else:
            message_rest[:, (offset - early) * mid : (offset - early + 1) * mid] = found
    mail.close()


CLASSES = 40


def one_task(nb, early, late, shared_act, mask, mask_line, targets, sizes, norms, weights, streams_weights, own):
    total = mask.shape[0]
    padded, mid = shared_act.shape
    lines = streams_weights[0].shape[0]

    def array(*shape, kind=BF16):
        return jax.ShapeDtypeStruct(shape, kind)

    def vmem(*shape, kind=BF16):
        return pltpu.VMEM(shape, kind)

    return pl.pallas_call(
        functools.partial(task_kernel, nb, early),
        out_shape=(
            array(lines, total, kind=F32),
            array(lines, total),
            array(total, mid, kind=F32),
            array(8, mid, kind=F32),
            array(padded, mid),
            array(total, mid),
            array(mid, mid),
            array(mid, LANES),
            array(early, mid, mid),
            array(mid, (9 - early) * mid),
            array(late, mid, mid),
        ),
        in_specs=[VMEM] * 12 + [ANY],
        out_specs=(VMEM,) * 11,
        scratch_shapes=[
            vmem(padded, mid),
            vmem(padded, mid),
            vmem(padded, mid),
            vmem(total, mid, kind=F32),
            vmem(total, mid, kind=F32),
            vmem(total, mid),
            vmem(4, lines, total, kind=F32),
            vmem(nb, 2, mid, kind=F32),
            DMA((2, 64)),
        ],
        cost_estimate=LONG,
        compiler_params=pltpu.CompilerParams(
            collective_id=23, has_side_effects=True, vmem_limit_bytes=60 * 2**20
        ),
    )(shared_act, mask, mask_line, targets, sizes, norms, *weights, *streams_weights, own)


def task_back_kernel(
    images,
    early,
    shared_act,
    mask,
    sizes,
    norms,
    head,
    message_start,
    gate,
    message_end,
    from_direct,
    slopes,
    pre_five,
    stats,
    grad_msg,
    grad_gate,
    message_grads,
    back,
    head_grads,
    head_rest,
    message_done,
    sums_out,
    left,
    right,
    grad_five,
    grad,
    slots_five,
    *rest,
):
    place = Place(images)
    mail = Mail(rest[-1])
    sums_of = [
        Reduce(
            mail,
            place,
            message_grads.at[offset],
            *rest[3 * offset : 3 * offset + 3],
            message_done.at[offset],
        )
        for offset in range(early)
    ]
    total = mask.shape[0]
    late = message_end.shape[0]
    mid = pre_five.shape[1]
    greet(place.others)
    sums_out[...] = jnp.zeros_like(sums_out)
    sums_of[0].start()
    sums_of[1].start()
    for cells in (left, right, grad_five):
        clear_ends(cells, total)
    widen(grad_msg, left, right, total)

    def message_weight(offset):
        if offset < early:
            return message_start[offset]
        return head[9 + offset - early] if offset < 9 - late else message_end[offset - 9 + late]

    def task_grads(rows):
        found = conv_rows(
            (left, grad_msg, right), rows, lambda offset, window: dot_t(window, message_weight(offset)), True
        )
        found = found + dot_t(grad_gate[rows, :], gate[...])
        grad[rows, :] = found + t_dot(slopes[:, rows], from_direct[...])

    loop(total, BLOCK, task_grads)
    sums = norm_back(stats, norms, mask, grad, pre_five, 0, mid, lambda rows: grad[rows, :])
    copies = send_sums(mail, place, slots_five, sums)
    sums_of[0].middle()
    sums_of[1].middle()
    for one in sums_of[2:]:
        one.start()
    for copy in copies:
        copy.wait_recv()
    bias_sum, gain_sum = add_up(slots_five)
    sums_out[0:1, :] = gain_sum
    sums_out[1:2, :] = bias_sum

    def put(rows, value):
        grad_five[pl.ds(pl.multiple_of(PITCH + rows.start, 16), CHUNK), :] = value

    through(stats, norms, mask, sizes, grad, pre_five, 0, mid, bias_sum, gain_sum, put)
    widen(grad_five, left, right, total)
    shifted = (left, grad_five, right)

    def head_back(rows):
        back[rows, :] = conv_rows(
            shifted, rows, lambda offset, window: dot_t(window, head[offset]), True
        ).astype(BF16)

    loop(total, BLOCK, head_back)
    for one in sums_of[2:]:
        one.middle()
    sums_of[0].finish()
    sums_of[1].finish()
    for offset in range(9):
        row, col = 2 - offset // 3, 2 - offset % 3
        window = shifted[col][PITCH * row : PITCH * row + total, :]
        found = t_dot(shared_act[PITCH : PITCH + total, :], window).astype(BF16)
        kept = head_grads.shape[0]
        if offset < kept:
            head_grads[offset] = found
        else:
            head_rest[:, (offset - kept) * mid : (offset - kept + 1) * mid] = found
    for one in sums_of[2:]:
        one.finish()
    mail.close()


def one_task_back(nb, early, kept, shared_act, mask, sizes, norms, weights, from_direct, slopes, rest):
    total = mask.shape[0]
    padded, mid = shared_act.shape
    lines, share = nb // 2, mid // nb

    def array(*shape, kind=BF16):
        return jax.ShapeDtypeStruct(shape, kind)

    def vmem(*shape, kind=BF16):
        return pltpu.VMEM(shape, kind)

    return pl.pallas_call(
        functools.partial(task_back_kernel, nb, early),
        out_shape=(
            array(total, mid),
            array(kept, mid, mid),
            array(mid, (9 - kept) * mid),
            array(early, share, mid),
            array(8, mid, kind=F32),
        ),
        in_specs=[VMEM] * 15,
        out_specs=(VMEM,) * 5,
        scratch_shapes=[
            vmem(padded, mid),
            vmem(padded, mid),
            vmem(padded, mid),
            vmem(total, mid, kind=F32),
            vmem(nb, 2, mid, kind=F32),
        ]
        + early * reduce_scratch(lines, share, mid, False)
        + [DMA((2, 48))],
        cost_estimate=LONG,
        compiler_params=pltpu.CompilerParams(
            collective_id=24, has_side_effects=True, vmem_limit_bytes=60 * 2**20
        ),
    )(shared_act, mask, sizes, norms, *weights, from_direct, slopes, *rest)


def last_kernel(shares, sums, all_shares, all_sums, sems):
    place = Place(2)
    mail = Mail(sems)
    blk = place.blk
    greet([place.mate, place.across])
    here = [mail.local(shares, all_shares.at[blk]), mail.local(sums, all_sums.at[blk])]
    both = []
    for source, slots in ((sums, all_sums), (shares, all_shares)):
        far = mail.send(source, slots.at[blk], place.across)
        near = mail.send(source, slots.at[blk], place.mate)
        both.append((far, near, slots))
    for far, near, slots in both:
        far.wait_recv()
        passed = slots.at[blk ^ 2]
        last = mail.send(passed, passed, place.mate)
        near.wait_recv()
        last.wait_recv()
    for copy in here:
        copy.wait()
    mail.close()


def gather_last(shares, sums):
    return pl.pallas_call(
        last_kernel,
        out_shape=(
            jax.ShapeDtypeStruct((4,) + shares.shape, shares.dtype),
            jax.ShapeDtypeStruct((4,) + sums.shape, sums.dtype),
        ),
        in_specs=[ANY] * 2,
        out_specs=(ANY, ANY),
        scratch_shapes=[DMA((2, 16))],
        compiler_params=pltpu.CompilerParams(collective_id=25, has_side_effects=True),
    )(shares, sums)


def on_device(
    nt,
    nb,
    features,
    crop_rows,
    crop_cols,
    depth_target,
    labels,
    first_weight,
    spatial_weight,
    last_weight,
    shared_weight,
    head_weights,
    message_weights,
    gate_weights,
    depth_weight,
    class_weight,
    mid_gain,
    mid_bias,
    out_gain,
    out_bias,
):
    tile_rows, cols, width = features.shape[1:]
    tile = tile_rows * cols
    rows = tile_rows * nt
    pixels = rows * cols
    tasks = head_weights.shape[0]
    mid = first_weight.shape[1]
    share = mid // nb
    slim = mid // nt
    classes = class_weight.shape[1]
    blk, batch = lax.axis_index("blk"), lax.axis_index("batch")

    image_rows = lax.dynamic_index_in_dim(crop_rows, batch, 0, False)
    image_cols = lax.dynamic_index_in_dim(crop_cols, batch, 0, False)
    row_ids = jnp.arange(rows, dtype=jnp.int32)
    col_ids = jnp.arange(PITCH, dtype=jnp.int32)
    inside_grid = (row_ids[:, None] < image_rows) & (col_ids[None, :] < image_cols)
    inside_grid = inside_grid.astype(F32)
    inside_wide = inside_grid.reshape(rows * PITCH, 1)
    inside = inside_grid[:, :cols].reshape(pixels, 1)
    inside_tile = lax.dynamic_slice_in_dim(inside, blk * tile, tile, 0)
    sizes_flat = (crop_rows * crop_cols).astype(F32)
    valid_count = jnp.sum(sizes_flat)
    sizes = jnp.broadcast_to(sizes_flat[:, None, None], (nb, 1, mid))
    tile_counts = jnp.sum(inside.reshape(nt, tile), 1)
    tile_sizes = jnp.broadcast_to(tile_counts[:, None, None], (nt, 1, mid))
    image_size = jnp.maximum(jnp.sum(inside), 1.0)

    params = jnp.concatenate(
        [
            mid_gain.reshape(-1),
            mid_bias.reshape(-1),
            out_gain,
            out_bias,
            depth_weight,
            class_weight.reshape(-1),
        ]
    )
    room = -(-params.shape[0] // (16 * LANES)) * 16 * LANES
    small = jnp.pad(params, (0, room - params.shape[0])).reshape(-1, LANES)
    feat = jnp.pad(features[0], ((0, 0), (0, PITCH - cols), (0, 0))).reshape(tile_rows * PITCH, width)
    piece = shared_weight.shape[0] // nt
    order = [
        (t * nb + b, (b * nt // nb) * nb + (b % (nb // nt)) * nt + t)
        for t in range(nt)
        for b in range(nb)
    ]
    shared_own = lax.ppermute(
        lax.dynamic_slice_in_dim(shared_weight, blk * piece, piece, 0), ("blk", "batch"), order
    )
    pair = jnp.stack([depth_target[0], labels[0].astype(F32)])
    pair = jnp.pad(pair, ((0, 6), (0, 0), (0, PITCH - cols))).reshape(8, tile_rows * PITCH)
    full_first, smalls, targets, wide_features, spatial, pre_one, stats, large = begin(
        nb, first_weight, small, spatial_weight, pair, head_weights, feat, inside_wide, sizes, tile_sizes
    )
    full_first = full_first.reshape(width, mid)
    smalls = smalls.reshape(nb, room)
    at = 0

    def taken(count):
        nonlocal at
        found = smalls[:, at : at + count]
        at += count
        return found

    norms_count = mid_gain.shape[0]
    out_share = out_gain.shape[0]
    gain_mid = taken(norms_count * share).reshape(nb, norms_count, share).swapaxes(0, 1)
    gain_mid = gain_mid.reshape(norms_count, mid).astype(F32)
    bias_mid = taken(norms_count * share).reshape(nb, norms_count, share).swapaxes(0, 1)
    bias_mid = bias_mid.reshape(norms_count, mid).astype(F32)
    gain_out = lax.dynamic_slice_in_dim(taken(out_share).reshape(width), blk * mid, mid, 0).astype(F32)
    bias_out = lax.dynamic_slice_in_dim(taken(out_share).reshape(width), blk * mid, mid, 0).astype(F32)
    full_depth = taken(share).reshape(mid, 1)
    full_classes = taken(share * classes).reshape(mid, classes)

    def slim_of(vector):
        return lax.dynamic_slice_in_dim(vector, blk * slim, slim, 0)

    def filled(vector):
        return jnp.pad(vector, (0, mid - vector.shape[0]))

    gain_two, bias_two = slim_of(gain_mid[1]), slim_of(bias_mid[1])
    gain_four, bias_four = slim_of(gain_mid[2]), slim_of(bias_mid[2])
    norms = jnp.stack(
        [
            gain_mid[0],
            bias_mid[0],
            filled(gain_two),
            filled(bias_two),
            gain_out,
            bias_out,
            filled(gain_four),
            filled(bias_four),
        ]
    )
    early, late = 4, 5
    large = lax.all_gather(large, "batch", axis=1, tiled=True)
    (
        last,
        shared,
        gate,
        message_start,
        act_one,
        act_two,
        act_three,
        shared_act,
        pre_two,
        pre_three,
        pre_four,
        stats,
    ) = bottleneck(
        nb,
        early,
        pre_one,
        stats,
        spatial,
        wide_features,
        inside_wide,
        norms,
        sizes,
        last_weight,
        shared_own,
        gate_weights,
        message_weights,
    )

    task_norms = jnp.stack(
        [
            lax.dynamic_index_in_dim(gain_mid, 3 + blk, 0, False),
            lax.dynamic_index_in_dim(bias_mid, 3 + blk, 0, False),
        ]
    )
    task_norms = jnp.pad(task_norms, ((0, 6), (0, 0)))
    lines = -(-(1 + classes) // 16) * 16
    stream_weight = jnp.concatenate([full_depth, full_classes], 1).T
    stream_weight = jnp.pad(stream_weight, ((0, lines - 1 - classes), (0, 0)))
    is_depth = jnp.arange(lines)[:, None] == 0
    none = jnp.zeros((), BF16)
    is_first, is_last = blk == 0, blk == tasks - 1
    own_stream = jnp.where(is_depth, is_first, is_last)
    to_depth = jnp.where(is_depth, stream_weight, none)
    to_classes = jnp.where(is_depth, none, stream_weight)
    from_gated = jnp.where(own_stream, none, stream_weight)
    from_direct = jnp.where(own_stream, stream_weight, none)
    mask_line = jnp.broadcast_to(inside_wide.reshape(1, -1), (8, rows * PITCH))
    weights = (large, message_start, gate)
    (
        streams,
        slopes,
        pre_five,
        task_stats,
        grad_msg,
        grad_gate,
        gate_grads,
        stream_grads,
        message_grads,
        message_rest,
        message_end,
    ) = one_task(
        nb,
        early,
        late,
        shared_act,
        inside_wide,
        mask_line,
        targets,
        sizes,
        task_norms,
        weights,
        (to_depth, to_classes, from_gated),
        message_weights,
    )
    own_streams = lax.dynamic_slice_in_dim(streams, blk * tile_rows * PITCH, tile_rows * PITCH, 1)
    own_streams = own_streams.reshape(lines, tile_rows, PITCH)[:, :, :cols]
    depth_out = own_streams[0]
    logits = own_streams[1 : 1 + classes].transpose(1, 2, 0)
    rest_share = lax.psum_scatter(message_rest, "batch", scatter_dimension=0, tiled=True)
    message_grads = message_grads.reshape(early, nb // 2, 2, share, mid)
    kept = 7
    back, head_grads, head_rest, message_done, task_sums = one_task_back(
        nb,
        early,
        kept,
        shared_act,
        inside_wide,
        sizes,
        task_norms,
        weights + (message_end,),
        from_direct,
        slopes,
        (pre_five, task_stats, grad_msg, grad_gate, message_grads),
    )
    message_share = message_done.reshape(early * share, mid)
    head_share = lax.psum_scatter(head_rest, "batch", scatter_dimension=0, tiled=True)

    (
        grad_input,
        share_shared,
        share_first,
        all_last,
        all_spatial,
        all_gates,
        all_stream,
        all_heads,
        all_messages,
        sums,
    ) = bottleneck_back(
        nb,
        back,
        (pre_one, pre_two, pre_three, pre_four),
        stats,
        norms,
        inside_wide,
        sizes,
        wide_features,
        (act_one, act_two, act_three),
        (spatial, last, shared, full_first),
        gate_grads,
        stream_grads,
        (message_share, head_grads, task_sums),
    )
    grad_input = grad_input.reshape(tile_rows, PITCH, width)[:, :cols]

    rest_share, head_share, share_first = lax.optimization_barrier((rest_share, head_share, share_first))
    rest_share = jnp.concatenate([rest_share, head_share], 1)
    left = 18 - early - kept
    rest_share = rest_share.reshape(share, left, mid).swapaxes(0, 1).reshape(left * share, mid)
    red_first, red_shared, all_rest = finish(nb, share_first, share_shared, rest_share)
    red_first = red_first.astype(F32).reshape(nt * share, mid)
    red_shared = red_shared.astype(F32).reshape(nt * share, mid)
    all_rest = all_rest.reshape(nt, left, share, mid)
    red_messages = jnp.concatenate(
        [all_messages.reshape(nt, early, share, mid), all_rest[:, : 9 - early]], 1
    ).astype(F32)
    red_last = all_last.astype(F32).transpose(1, 0, 2).reshape(share, width)
    red_gates = all_gates.astype(F32)
    red_spatial = all_spatial.astype(F32).reshape(nt, share, 9, slim)
    red_spatial = red_spatial.transpose(2, 1, 0, 3).reshape(9, share, mid)
    streams_red = jnp.sum(all_stream.astype(F32), 0)
    red_depth = streams_red[:, 0]
    red_classes = streams_red[:, 1 : 1 + classes]
    red_heads = jnp.concatenate(
        [all_heads.reshape(nt, kept, share, mid), all_rest[:, 9 - early :]], 1
    ).astype(F32)
    two_gain, two_bias = sums[:, 2, :slim].reshape(1, mid), sums[:, 3, :slim].reshape(1, mid)
    four_gain, four_bias = sums[:, 6, :slim].reshape(1, mid), sums[:, 7, :slim].reshape(1, mid)
    mid_gains = jnp.concatenate([sums[0, 0:1], two_gain, four_gain, sums[:, 8]], 0)
    mid_biases = jnp.concatenate([sums[0, 1:2], two_bias, four_bias, sums[:, 9]], 0)
    grad_mid_gain = lax.dynamic_slice_in_dim(mid_gains, batch * share, share, 1)
    grad_mid_bias = lax.dynamic_slice_in_dim(mid_biases, batch * share, share, 1)
    grad_out_gain = lax.dynamic_slice_in_dim(sums[:, 4].reshape(width), batch * out_share, out_share, 0)
    grad_out_bias = lax.dynamic_slice_in_dim(sums[:, 5].reshape(width), batch * out_share, out_share, 0)
    return (
        depth_out.reshape(1, tile_rows, cols),
        logits.reshape(1, tile_rows, cols, classes),
        grad_input.reshape(1, tile_rows, cols, width),
        red_first,
        red_spatial,
        red_last,
        red_shared,
        red_heads,
        red_messages,
        red_gates,
        red_depth,
        red_classes,
        grad_mid_gain,
        grad_mid_bias,
        grad_out_gain,
        grad_out_bias,
    )


def solution(mesh):
    nt, nb = mesh.shape["blk"], mesh.shape["batch"]
    placed = (
        P("batch", "blk", None, None),
        P(),
        P(),
        P("batch", "blk", None),
        P("batch", "blk", None),
        P("batch", None),
        P(None, "batch", None),
        P("batch", None),
        P("batch", None),
        P(None, None, "batch", None),
        P(None, None, "batch", None),
        P(None, "batch", None),
        P("batch"),
        P("batch", None),
        P(None, "batch"),
        P(None, "batch"),
        P("batch"),
        P("batch"),
    )
    return jax.shard_map(
        functools.partial(on_device if nb == 8 else on_device_any, nt, nb),
        mesh=mesh,
        in_specs=placed,
        out_specs=(
            P("batch", "blk", None),
            P("batch", "blk", None, None),
            P("batch", "blk", None, None),
            P("batch", None),
            P(None, "batch", None),
            P("batch", None),
            P("batch", None),
            P(None, None, "batch", None),
            P(None, None, "batch", None),
            P(None, "batch", None),
            P("batch"),
            P("batch", None),
            P(None, "batch"),
            P(None, "batch"),
            P("batch"),
            P("batch"),
        ),
        check_vma=False,
    )
```

```python
import functools

import jax
import jax.numpy as jnp
from jax import lax
from jax.experimental import pallas as pl
from jax.experimental.pallas import tpu as pltpu
from jax.sharding import PartitionSpec as P

EPSILON = 1e-05
MESH = pl.DeviceIdType.MESH
BF16 = jnp.bfloat16
F32 = jnp.float32
LANES = 128


def greet(peers):
    barrier = pltpu.get_barrier_semaphore()
    for peer in peers:
        pl.semaphore_signal(barrier, inc=1, device_id=peer, device_id_type=MESH)
    pl.semaphore_wait(barrier, len(peers))


def send(src, dst, send_sem, recv_sem, peer):
    copy = pltpu.make_async_remote_copy(
        src_ref=src,
        dst_ref=dst,
        send_sem=send_sem,
        recv_sem=recv_sem,
        device_id=peer,
        device_id_type=MESH,
    )
    copy.start()
    return copy


def first_kernel(images, weight, small, full, smalls, own, zs, xs, cs, ps):
    blk, batch = lax.axis_index("blk"), lax.axis_index("batch")
    half = weight.shape[0] // 2
    rows = pl.ds(pl.multiple_of(lax.rem(blk, 2) * half, half), half)
    side = (blk, batch ^ 1)
    mate = (blk ^ 1, batch)
    lines = range(1, images // 2)
    others = [(blk, batch ^ mask) for mask in range(1, images)]
    greet(others + [mate])
    copies = []
    here = pltpu.make_async_copy(weight, full.at[batch], own.at[0])
    here.start()
    here_small = pltpu.make_async_copy(small, smalls.at[batch], own.at[1])
    here_small.start()
    z_copies = {}
    for mask in lines:
        z_copies[mask] = send(
            weight.at[rows],
            full.at[batch, rows],
            zs.at[0, mask],
            zs.at[1, mask],
            (blk, batch ^ (2 * mask)),
        )
    x_copies = {
        0: send(weight.at[rows], full.at[batch, rows], xs.at[0, 0], xs.at[1, 0], side)
    }
    for place, peer in enumerate(others):
        copies.append(
            send(small, smalls.at[batch], ps.at[0, place], ps.at[1, place], peer)
        )
    core_copies = []

    def hand_over(source, mask):
        block = full.at[source, rows]
        core_copies.append(send(block, block, cs.at[0, mask], cs.at[1, mask], mate))

    for mask in lines:
        z_copies[mask].wait_recv()
        source = batch ^ (2 * mask)
        block = full.at[source, rows]
        x_copies[mask] = send(block, block, xs.at[0, mask], xs.at[1, mask], side)
        hand_over(source, 2 * mask)
    for mask in range(images // 2):
        x_copies[mask].wait_recv()
        hand_over(batch ^ (2 * mask + 1), 2 * mask + 1)
    for copy in core_copies + copies:
        copy.wait()
    for mask in lines:
        z_copies[mask].wait_send()
    for mask in range(images // 2):
        x_copies[mask].wait_send()
    here.wait()
    here_small.wait()


def gather_first(weight, small, images):
    any_place = pl.BlockSpec(memory_space=pl.ANY)
    dma = pltpu.SemaphoreType.DMA
    return pl.pallas_call(
        functools.partial(first_kernel, images),
        out_shape=(
            jax.ShapeDtypeStruct((images,) + weight.shape, weight.dtype),
            jax.ShapeDtypeStruct((images,) + small.shape, small.dtype),
        ),
        in_specs=[any_place] * 2,
        out_specs=(any_place, any_place),
        scratch_shapes=[
            dma((2,)),
            dma((2, images)),
            dma((2, images)),
            dma((2, images)),
            dma((2, images)),
        ],
        compiler_params=pltpu.CompilerParams(collective_id=0, has_side_effects=True),
    )(weight, small)


def tiles_kernel(block, every, own, sems):
    blk, batch = lax.axis_index("blk"), lax.axis_index("batch")
    mate, across = (blk ^ 1, batch), (blk ^ 2, batch)
    greet([mate, across])
    far = send(block, every.at[blk], sems.at[0, 0], sems.at[1, 0], across)
    near = send(block, every.at[blk], sems.at[0, 1], sems.at[1, 1], mate)
    here = pltpu.make_async_copy(block, every.at[blk], own.at[0])
    here.start()
    far.wait_recv()
    passed = every.at[blk ^ 2]
    last = send(passed, passed, sems.at[0, 2], sems.at[1, 2], mate)
    near.wait()
    last.wait()
    far.wait_send()
    here.wait()


def gather_tiles(block, ident):
    any_place = pl.BlockSpec(memory_space=pl.ANY)
    dma = pltpu.SemaphoreType.DMA
    return pl.pallas_call(
        tiles_kernel,
        out_shape=jax.ShapeDtypeStruct((4,) + block.shape, block.dtype),
        in_specs=[any_place],
        out_specs=any_place,
        scratch_shapes=[dma((1,)), dma((2, 3))],
        compiler_params=pltpu.CompilerParams(collective_id=ident, has_side_effects=True),
    )(block)


def sum_kernel(parts, total, near_in, pair, far_in, sems):
    blk, batch = lax.axis_index("blk"), lax.axis_index("batch")
    mate, across = (blk ^ 1, batch), (blk ^ 2, batch)
    greet([mate, across])
    far_first = send(parts.at[blk ^ 3], near_in.at[0], sems.at[0, 0], sems.at[1, 0], mate)
    near_next = send(parts.at[blk ^ 1], near_in.at[1], sems.at[0, 1], sems.at[1, 1], mate)
    far_first.wait_recv()
    pair[...] = (parts[blk ^ 2].astype(F32) + near_in[0].astype(F32)).astype(pair.dtype)
    far = send(pair, far_in, sems.at[0, 2], sems.at[1, 2], across)
    near_next.wait_recv()
    total[...] = parts[blk].astype(F32) + near_in[1].astype(F32)
    far.wait_recv()
    total[...] += far_in[...].astype(F32)
    far_first.wait_send()
    near_next.wait_send()
    far.wait_send()


def sum_tiles(parts, ident):
    dma = pltpu.SemaphoreType.DMA
    block = parts.shape[1:]
    vmem = pl.BlockSpec(memory_space=pltpu.VMEM)
    return pl.pallas_call(
        sum_kernel,
        out_shape=jax.ShapeDtypeStruct(block, F32),
        in_specs=[vmem],
        out_specs=vmem,
        scratch_shapes=[
            pltpu.VMEM((2,) + block, parts.dtype),
            pltpu.VMEM(block, parts.dtype),
            pltpu.VMEM(block, parts.dtype),
            dma((2, 3)),
        ],
        compiler_params=pltpu.CompilerParams(
            collective_id=ident, has_side_effects=True, vmem_limit_bytes=32 * 2**20
        ),
    )(parts)


def combine(slots, weights, half, centred):
    count = slots.shape[0]
    if not centred:
        total = slots[0]
        for at in range(1, count):
            total = total + slots[at]
        return total
    size = weights[0]
    mean = slots[0, :half] * weights[0]
    for at in range(1, count):
        size = size + weights[at]
        mean = mean + slots[at, :half] * weights[at]
    mean = mean / size
    spread = None
    for at in range(count):
        gap = slots[at, :half] - mean
        term = slots[at, half : 2 * half] + weights[at] * gap * gap
        spread = term if spread is None else spread + term
    rest = [jnp.zeros((slots.shape[1] - 2 * half, LANES), F32)] * (slots.shape[1] > 2 * half)
    return jnp.concatenate([mean, spread] + rest, 0)


def sums_kernel(images, half, centred, tiled, own, tile_sizes, sizes, total, *scratch):
    blk, batch = lax.axis_index("blk"), lax.axis_index("batch")
    slots, sems = scratch[0], scratch[1]
    peers = [(blk, batch ^ mask) for mask in range(1, images)]
    mates = [(blk ^ mask, batch) for mask in range(1, 4)] if tiled else []
    greet(peers + mates)
    if tiled:
        tile_slots, tile_sems = scratch[2], scratch[3]
        tile_slots[blk] = own[...]
        copies = [
            send(own, tile_slots.at[blk], tile_sems.at[0, at], tile_sems.at[1, at], peer)
            for at, peer in enumerate(mates)
        ]
        for copy in copies:
            copy.wait()
        slots[batch] = combine(tile_slots, tile_sizes, half, centred)
    else:
        slots[batch] = own[...]
    copies = [
        send(slots.at[batch], slots.at[batch], sems.at[0, at], sems.at[1, at], peer)
        for at, peer in enumerate(peers)
    ]
    for copy in copies:
        copy.wait()
    total[...] = combine(slots, sizes, half, centred)


def all_sums(first, second, tile_sizes, sizes, centred, tiled, ident):
    images = sizes.shape[0]
    channels = first.shape[0]
    half = channels // LANES
    rows = -(-2 * half // 8) * 8
    own = jnp.concatenate(
        [first, second, jnp.zeros(((rows - 2 * half) * LANES,), F32)]
    ).reshape(rows, LANES)
    dma = pltpu.SemaphoreType.DMA
    vmem = pl.BlockSpec(memory_space=pltpu.VMEM)
    scratch = [pltpu.VMEM((images, rows, LANES), F32), dma((2, images))]
    if tiled:
        scratch += [pltpu.VMEM((4, rows, LANES), F32), dma((2, 3))]
    total = pl.pallas_call(
        functools.partial(sums_kernel, images, half, centred, tiled),
        out_shape=jax.ShapeDtypeStruct((rows, LANES), F32),
        in_specs=[vmem] * 3,
        out_specs=vmem,
        scratch_shapes=scratch,
        compiler_params=pltpu.CompilerParams(collective_id=ident, has_side_effects=True),
    )(own, sizes if tile_sizes is None else tile_sizes, sizes)
    flat = total.reshape(-1)
    return flat[:channels], flat[channels : 2 * channels]


def silu_slope(values):
    sigmoid_value = jax.nn.sigmoid(values)
    return sigmoid_value * (1.0 + values * (1.0 - sigmoid_value))


def windows(cells, rows, cols, back):
    channels = cells.shape[1]
    padded = jnp.pad(cells.reshape(rows, cols, channels), ((1, 1), (1, 1), (0, 0)))
    taken = []
    for offset in range(9):
        row, col = offset // 3, offset % 3
        if back:
            row, col = 2 - row, 2 - col
        taken.append(padded[row : row + rows, col : col + cols].reshape(rows * cols, channels))
    return jnp.concatenate(taken, 1)


def dot(left, right):
    return jnp.dot(left, right, preferred_element_type=F32)


def dot_t(left, right):
    return jnp.einsum("pd,cd->pc", left, right, preferred_element_type=F32)


def t_dot(left, right):
    return jnp.einsum("pc,pd->cd", left, right, preferred_element_type=F32)


def on_device_any(
    nt,
    nb,
    features,
    crop_rows,
    crop_cols,
    depth_target,
    labels,
    first_weight,
    spatial_weight,
    last_weight,
    shared_weight,
    head_weights,
    message_weights,
    gate_weights,
    depth_weight,
    class_weight,
    mid_gain,
    mid_bias,
    out_gain,
    out_bias,
):
    tile_rows, cols, width = features.shape[1:]
    tile = tile_rows * cols
    rows = tile_rows * nt
    pixels = rows * cols
    tasks = head_weights.shape[0]
    mid = first_weight.shape[1]
    share = mid // nb
    slim = mid // nt
    piece = width // (nb * nt)
    wide = nb * piece
    classes = class_weight.shape[1]
    blk, batch = lax.axis_index("blk"), lax.axis_index("batch")

    image_rows = lax.dynamic_index_in_dim(crop_rows, batch, 0, False)
    image_cols = lax.dynamic_index_in_dim(crop_cols, batch, 0, False)
    row_ids = jnp.arange(rows, dtype=jnp.int32)
    col_ids = jnp.arange(cols, dtype=jnp.int32)
    inside_grid = (row_ids[:, None] < image_rows) & (col_ids[None, :] < image_cols)
    inside = inside_grid.astype(F32).reshape(pixels, 1)
    inside_tile = lax.dynamic_slice_in_dim(inside, blk * tile, tile, 0)
    sizes_flat = (crop_rows * crop_cols).astype(F32)
    valid_count = jnp.sum(sizes_flat)
    sizes = jnp.broadcast_to(sizes_flat[:, None, None], (nb, 1, LANES))
    tile_counts = jnp.sum(inside.reshape(nt, tile), 1)
    tile_sizes = jnp.broadcast_to(tile_counts[:, None, None], (nt, 1, LANES))
    image_size = jnp.maximum(jnp.sum(inside), 1.0)
    tile_size = jnp.maximum(jnp.sum(inside_tile), 1.0)

    params = jnp.concatenate(
        [
            mid_gain.reshape(-1),
            mid_bias.reshape(-1),
            out_gain,
            out_bias,
            depth_weight,
            class_weight.reshape(-1),
        ]
    )
    room = -(-params.shape[0] // (16 * LANES)) * 16 * LANES
    small = jnp.pad(params, (0, room - params.shape[0])).reshape(-1, LANES)
    full_first, smalls = gather_first(first_weight, small, nb)
    full_first = full_first.reshape(width, mid)
    smalls = smalls.reshape(nb, room)
    at = 0

    def taken(count):
        nonlocal at
        found = smalls[:, at : at + count]
        at += count
        return found

    norms = mid_gain.shape[0]
    gain_mid = taken(norms * share).reshape(nb, norms, share).swapaxes(0, 1)
    gain_mid = gain_mid.reshape(norms, mid).astype(F32)
    bias_mid = taken(norms * share).reshape(nb, norms, share).swapaxes(0, 1)
    bias_mid = bias_mid.reshape(norms, mid).astype(F32)
    gain_out = lax.dynamic_index_in_dim(taken(nt * piece).reshape(nb, nt, piece), blk, 1, False)
    gain_out = gain_out.reshape(wide).astype(F32)
    bias_out = lax.dynamic_index_in_dim(taken(nt * piece).reshape(nb, nt, piece), blk, 1, False)
    bias_out = bias_out.reshape(wide).astype(F32)
    full_depth = taken(share).reshape(mid, 1)
    full_classes = taken(share * classes).reshape(mid, classes)
    stream_weight = jnp.concatenate([full_depth, full_classes], 1)

    spatial = lax.all_gather(
        lax.dynamic_slice_in_dim(spatial_weight, blk * slim, slim, 2), "batch", axis=1, tiled=True
    )
    last = lax.dynamic_index_in_dim(last_weight.reshape(share, nb, nt, piece), blk, 2, False)
    last = lax.all_gather(last.reshape(share, wide), "batch", axis=0, tiled=True)
    shared = lax.dynamic_slice_in_dim(shared_weight, blk * piece, piece, 0)
    shared = lax.all_gather(shared, "batch", axis=0, tiled=True)
    head = lax.all_gather(
        lax.dynamic_index_in_dim(head_weights, blk, 0, False), "batch", axis=1, tiled=True
    )
    message = lax.all_gather(
        lax.dynamic_index_in_dim(message_weights, blk, 0, False), "batch", axis=1, tiled=True
    )
    gate = lax.all_gather(
        lax.dynamic_index_in_dim(gate_weights, blk, 0, False), "batch", axis=0, tiled=True
    )

    flat_features = features.reshape(tile, width)
    cut = flat_features.reshape(tile, nb, nt, piece).transpose(2, 0, 1, 3).reshape(nt, tile, wide)
    wide_features = swap_tiles(cut, blk, nt)

    def slim_of(vector):
        return lax.dynamic_slice_in_dim(vector, blk * slim, slim, 0)

    def normalize(values, mask, local_size, gain, bias, tiled, ident):
        mean = jnp.sum(values * mask, 0) / local_size
        gap = values - mean
        spread = jnp.sum(gap * gap * mask, 0)
        centre, total = all_sums(mean, spread, tile_sizes, sizes, True, tiled, ident)
        inverse = lax.rsqrt(total / valid_count + EPSILON)
        normed = (values - centre) * inverse
        return normed * gain + bias, normed, inverse

    def normalize_back(grad, normed, inverse, gain, mask, tiled, ident):
        bias_sum, gain_sum = all_sums(
            jnp.sum(grad, 0), jnp.sum(grad * normed, 0), tile_sizes, sizes, False, tiled, ident
        )
        back = (
            inverse * gain * (grad - bias_sum / valid_count - normed * gain_sum / valid_count) * mask
        )
        return back.astype(BF16), gain_sum, bias_sum

    def act(values, mask):
        return (jax.nn.silu(values) * mask).astype(BF16)

    def by_rows(blocks):
        return blocks.reshape(pixels, blocks.shape[2])

    def by_channels(blocks):
        return blocks.swapaxes(0, 1).reshape(pixels, nt * blocks.shape[2])

    def cut_channels(values):
        return values.astype(BF16).reshape(pixels, nt, slim).swapaxes(0, 1)

    pre_one = dot(flat_features, full_first)
    norm_one, normed_one, inverse_one = normalize(
        pre_one, inside_tile, tile_size, gain_mid[0], bias_mid[0], True, 1
    )
    act_one = by_rows(gather_tiles(act(norm_one, inside_tile), 2))
    pre_two = dot(windows(act_one, rows, cols, False), spatial.reshape(9 * mid, slim))
    gain_two, bias_two = slim_of(gain_mid[1]), slim_of(bias_mid[1])
    norm_two, normed_two, inverse_two = normalize(
        pre_two, inside, image_size, gain_two, bias_two, False, 3
    )
    act_two = by_channels(gather_tiles(act(norm_two, inside), 4))
    pre_three = dot(act_two, last)
    norm_three, normed_three, inverse_three = normalize(
        pre_three, inside, image_size, gain_out, bias_out, False, 5
    )
    joined = norm_three + wide_features.astype(F32)
    act_three = act(joined, inside)
    pre_four = sum_tiles(cut_channels(dot(act_three, shared)), 6)
    gain_four, bias_four = slim_of(gain_mid[2]), slim_of(bias_mid[2])
    norm_four, normed_four, inverse_four = normalize(
        pre_four, inside, image_size, gain_four, bias_four, False, 3
    )
    shared_act = by_channels(gather_tiles(act(norm_four, inside), 4))

    gain_task = lax.dynamic_index_in_dim(gain_mid, 3 + blk, 0, False)
    bias_task = lax.dynamic_index_in_dim(bias_mid, 3 + blk, 0, False)
    pre_five = dot(windows(shared_act, rows, cols, False), head.reshape(9 * mid, mid))
    norm_five, normed_five, inverse_five = normalize(
        pre_five, inside, image_size, gain_task, bias_task, False, 5
    )
    task_act = act(norm_five, inside)
    messages = dot(windows(task_act, rows, cols, False), message.reshape(9 * mid, mid))
    gate_open = jax.nn.sigmoid(dot(task_act, gate))
    gated = (gate_open * messages).astype(BF16)
    is_first, is_last = blk == 0, blk == tasks - 1
    depth_part = jnp.where(is_first, task_act, gated)
    sem_part = jnp.where(is_last, task_act, gated)
    depth_share = jnp.einsum("pc,co->op", depth_part, full_depth, preferred_element_type=F32)
    class_share = jnp.einsum("pc,co->op", sem_part, full_classes, preferred_element_type=F32)
    lift = -(-(1 + classes) // 8) * 8 - 1 - classes
    shares = jnp.concatenate([depth_share, class_share, jnp.zeros((lift, pixels), F32)], 0)
    streams = jnp.sum(gather_tiles(shares, 7), 0).T
    depth_out = lax.dynamic_slice_in_dim(streams, blk * tile, tile, 0)[:, 0]
    logits = lax.dynamic_slice_in_dim(streams, blk * tile, tile, 0)[:, 1 : 1 + classes]
    targets = by_rows(gather_tiles_pair(depth_target, labels, tile))
    all_depth, all_logits = streams[:, :1], streams[:, 1 : 1 + classes]
    depth_slope = ((all_depth - targets[:, :1]) * inside).astype(BF16)
    onehot = (targets[:, 1:2] == jnp.arange(classes, dtype=jnp.int32)[None, :].astype(F32)).astype(F32)
    logit_slope = ((jax.nn.softmax(all_logits, axis=1) - onehot) * inside).astype(BF16)
    grad_depth = t_dot(depth_part, depth_slope)
    grad_classes = t_dot(sem_part, logit_slope)
    depth_back = depth_slope.astype(F32) * full_depth.astype(F32).reshape(1, mid)
    sem_back = dot_t(logit_slope, full_classes)
    zero = jnp.zeros((), F32)
    grad_gated = jnp.where(is_first, zero, depth_back) + jnp.where(is_last, zero, sem_back)
    grad_direct = jnp.where(is_first, depth_back, zero) + jnp.where(is_last, sem_back, zero)

    grad_msg = (grad_gated * gate_open).astype(BF16)
    grad_gate = (grad_gated * messages * gate_open * (1.0 - gate_open)).astype(BF16)
    msg_windows = windows(grad_msg, rows, cols, True)
    gate_grads = t_dot(task_act, grad_gate).astype(BF16)
    message_grads = t_dot(task_act, msg_windows).astype(BF16)
    share_messages = lax.psum_scatter(message_grads, "batch", scatter_dimension=0, tiled=True)
    task_grad = (
        grad_direct
        + dot_t(grad_gate, gate)
        + dot(msg_windows, message.swapaxes(1, 2).reshape(9 * mid, mid))
    )
    grad_norm_five = task_grad * inside * silu_slope(norm_five)
    grad_pre_five, gain_sum_five, bias_sum_five = normalize_back(
        grad_norm_five, normed_five, inverse_five, gain_task, inside, False, 8
    )
    five_windows = windows(grad_pre_five, rows, cols, True)
    head_grads = t_dot(shared_act, five_windows).astype(BF16)
    share_heads = lax.psum_scatter(head_grads, "batch", scatter_dimension=0, tiled=True)
    shared_back = dot(five_windows, head.swapaxes(1, 2).reshape(9 * mid, mid))
    shared_back = sum_tiles(cut_channels(shared_back), 6)

    grad_norm_four = shared_back * inside * silu_slope(norm_four)
    grad_pre_four, gain_sum_four, bias_sum_four = normalize_back(
        grad_norm_four, normed_four, inverse_four, gain_four, inside, False, 9
    )
    grad_four = by_channels(gather_tiles(grad_pre_four, 4))
    shared_grads = t_dot(act_three, grad_four).astype(BF16)
    grad_joined = dot_t(grad_four, shared) * inside * silu_slope(joined)
    grad_three, gain_sum_three, bias_sum_three = normalize_back(
        grad_joined, normed_three, inverse_three, gain_out, inside, False, 8
    )
    last_grads = t_dot(act_two, grad_three).astype(BF16)
    two_back = sum_tiles(cut_channels(dot_t(grad_three, last)), 6)
    grad_norm_two = two_back * inside * silu_slope(norm_two)
    grad_two, gain_sum_two, bias_sum_two = normalize_back(
        grad_norm_two, normed_two, inverse_two, gain_two, inside, False, 9
    )
    two_windows = windows(grad_two, rows, cols, True)
    spatial_grads = t_dot(act_one, two_windows).astype(BF16)
    one_back = dot(two_windows, spatial.swapaxes(1, 2).reshape(9 * slim, mid))
    one_back = sum_tiles(one_back.astype(BF16).reshape(nt, tile, mid), 10)
    grad_norm_one = one_back * inside_tile * silu_slope(norm_one)
    grad_one, gain_sum_one, bias_sum_one = normalize_back(
        grad_norm_one, normed_one, inverse_one, gain_mid[0], inside_tile, True, 11
    )
    all_one = by_rows(gather_tiles(grad_one, 2))
    first_grads = t_dot(wide_features, all_one).astype(BF16)
    joined_tiles = swap_tiles(grad_joined.astype(BF16).reshape(nt, tile, wide), blk, nt)
    joined_tiles = joined_tiles.reshape(nt, tile, nb, piece).transpose(1, 2, 0, 3).reshape(tile, width)
    grad_input = dot_t(grad_one, full_first) + joined_tiles.astype(F32)

    stream_grads = jnp.concatenate([grad_depth, grad_classes], 1)
    stream_grads = jnp.pad(stream_grads, ((0, 0), (0, LANES - 1 - classes))).astype(BF16)
    late = jnp.concatenate(
        [spatial_grads, shared_grads.reshape(nb, piece, mid).reshape(mid, -1),
         last_grads, first_grads.reshape(mid, -1), gate_grads, stream_grads],
        1,
    )
    late_share = lax.psum_scatter(late, "batch", scatter_dimension=0, tiled=True)
    early_share = jnp.concatenate([share_messages, share_heads], 1)
    early = lax.all_gather(early_share, "blk", axis=0, tiled=False).astype(F32)
    late_all = gather_tiles(late_share, 12).astype(F32)
    early = early.reshape(nt, share, 2, 9, mid).transpose(2, 0, 3, 1, 4)
    red_messages, red_heads = early[0], early[1]
    at = 0

    def part(count):
        nonlocal at
        found = late_all[:, :, at : at + count]
        at += count
        return found

    red_spatial = part(9 * slim).reshape(nt, share, 9, slim).transpose(2, 1, 0, 3).reshape(9, share, mid)
    red_shared = part(wide * mid // mid).reshape(nt * piece, mid)
    red_last = part(wide).reshape(nt, share, nb, piece).transpose(1, 2, 0, 3).reshape(share, width)
    red_first = part(wide * mid // mid).reshape(nt * piece, mid)
    red_gates = part(mid)
    streams_red = jnp.sum(part(LANES), 0)
    red_depth = streams_red[:, 0]
    red_classes = streams_red[:, 1 : 1 + classes]

    sums = jnp.concatenate(
        [
            gain_sum_five,
            bias_sum_five,
            gain_sum_three,
            bias_sum_three,
            gain_sum_two,
            bias_sum_two,
            gain_sum_four,
            bias_sum_four,
        ]
    ).reshape(-1, LANES)
    sums = jnp.pad(sums, ((0, -sums.shape[0] % 8), (0, 0)))
    sums = gather_tiles(sums, 13).reshape(nt, -1)
    five_gain, five_bias = sums[:, :mid], sums[:, mid : 2 * mid]
    at_out = 2 * mid
    three_gain = sums[:, at_out : at_out + wide].reshape(nt, nb, piece)
    three_bias = sums[:, at_out + wide : at_out + 2 * wide].reshape(nt, nb, piece)
    at_slim = at_out + 2 * wide
    slims = [
        sums[:, at_slim + i * slim : at_slim + (i + 1) * slim].reshape(1, mid) for i in range(4)
    ]
    mid_gains = jnp.concatenate([gain_sum_one[None], slims[0], slims[2], five_gain], 0)
    mid_biases = jnp.concatenate([bias_sum_one[None], slims[1], slims[3], five_bias], 0)
    grad_mid_gain = lax.dynamic_slice_in_dim(mid_gains, batch * share, share, 1)
    grad_mid_bias = lax.dynamic_slice_in_dim(mid_biases, batch * share, share, 1)
    grad_out_gain = lax.dynamic_index_in_dim(three_gain, batch, 1, False).reshape(nt * piece)
    grad_out_bias = lax.dynamic_index_in_dim(three_bias, batch, 1, False).reshape(nt * piece)
    return (
        depth_out.reshape(1, tile_rows, cols),
        logits.reshape(1, tile_rows, cols, classes),
        grad_input.reshape(1, tile_rows, cols, width),
        red_first,
        red_spatial,
        red_last,
        red_shared,
        red_heads,
        red_messages,
        red_gates,
        red_depth,
        red_classes,
        grad_mid_gain,
        grad_mid_bias,
        grad_out_gain,
        grad_out_bias,
    )


def swap_tiles(blocks, blk, nt):
    out = jnp.zeros_like(blocks)
    out = lax.dynamic_update_index_in_dim(
        out, lax.dynamic_index_in_dim(blocks, blk, 0, False), blk, 0
    )
    for mask in range(1, nt):
        sent = lax.dynamic_index_in_dim(blocks, blk ^ mask, 0, False)
        came = lax.ppermute(sent, "blk", [(i, i ^ mask) for i in range(nt)])
        out = lax.dynamic_update_index_in_dim(out, came, blk ^ mask, 0)
    return out.reshape(-1, blocks.shape[2])


def gather_tiles_pair(depth_target, labels, tile):
    pair = jnp.stack([depth_target.reshape(tile), labels.reshape(tile).astype(F32)], 0)
    pair = jnp.pad(pair, ((0, 6), (0, 0)))
    return gather_tiles(pair, 14).swapaxes(1, 2)


PITCH = 48
CHUNK = 64
BLOCK = 256
ANY = pl.BlockSpec(memory_space=pl.ANY)
VMEM = pl.BlockSpec(memory_space=pltpu.VMEM)
DMA = pltpu.SemaphoreType.DMA
LONG = pl.CostEstimate(flops=80_000_000_000, bytes_accessed=30_000_000, transcendentals=2_000_000)


class Mail:
    def __init__(self, sems):
        self.sems, self.used, self.open = sems, 0, []

    def send(self, src, dst, peer, keep=True):
        copy = send(src, dst, self.sems.at[0, self.used], self.sems.at[1, self.used], peer)
        self.used += 1
        if keep:
            self.open.append(copy.wait_send)
        return copy

    def local(self, src, dst):
        copy = pltpu.make_async_copy(src, dst, self.sems.at[0, self.used])
        copy.start()
        self.used += 1
        return copy

    def close(self):
        for wait in self.open:
            wait()
        self.open = []


class Place:
    def __init__(self, images):
        self.blk, self.batch = lax.axis_index("blk"), lax.axis_index("batch")
        self.images = images
        self.mate = (self.blk ^ 1, self.batch)
        self.across = (self.blk ^ 2, self.batch)
        self.tiles = [(self.blk ^ mask, self.batch) for mask in range(1, 4)]
        self.others = [(self.blk, self.batch ^ mask) for mask in range(1, images)]
        self.side = (self.blk, self.batch ^ 1)


class Spread:
    def __init__(self, mail, place, own, slot):
        self.mail, self.place, self.own, self.slot = mail, place, own, slot
        self.z_copies, self.x_copies = [], []

    def start(self):
        place, here = self.place, self.slot(self.place.batch)
        self.here = self.mail.local(self.own, here)
        for mask in range(1, place.images // 2):
            peer = (place.blk, place.batch ^ (2 * mask))
            self.z_copies.append(self.mail.send(self.own, here, peer))
        self.x_copies.append(self.mail.send(self.own, here, place.side))
        return self

    def forward(self):
        for mask, copy in enumerate(self.z_copies, 1):
            copy.wait_recv()
            block = self.slot(self.place.batch ^ (2 * mask))
            self.x_copies.append(self.mail.send(block, block, self.place.side))

    def finish(self):
        self.here.wait()
        for copy in self.x_copies:
            copy.wait_recv()


def share_tiles(mail, place, slot):
    own = slot(place.blk)
    far = mail.send(own, own, place.across, False)
    near = mail.send(own, own, place.mate, False)
    far.wait_recv()
    passed = slot(place.blk ^ 2)
    last = mail.send(passed, passed, place.mate, False)
    near.wait()
    last.wait()
    far.wait_send()


def loop(total, step, body, base=0):
    def run(at, carry):
        body(pl.ds(pl.multiple_of(base + at * step, step), step))
        return carry

    lax.fori_loop(0, total // step, run, 0)


PIECES = 3


def pieces_of(total):
    size = total // PIECES
    return [(at * size, size) for at in range(PIECES)]


def share_pieces(mail, place, slot, total, produce=None, consume=None, meanwhile=None):
    pieces = pieces_of(total)
    far, near, last = [], [], []
    for first, size in pieces:
        if produce is not None:
            produce(first, size)
        own = slot(place.blk, first, size)
        far.append(mail.send(own, own, place.across, False))
        near.append(mail.send(own, own, place.mate, False))
    if meanwhile is not None:
        meanwhile()

    def use(at):
        near[at].wait_recv()
        last[at].wait_recv()
        if consume is not None:
            consume(*pieces[at])

    for at, (first, size) in enumerate(pieces):
        far[at].wait_recv()
        passed = slot(place.blk ^ 2, first, size)
        last.append(mail.send(passed, passed, place.mate, False))
        if at > 0:
            use(at - 1)
    use(len(pieces) - 1)
    for copy in far + near + last:
        copy.wait_send()


def folded(values):
    return jnp.sum(values.reshape(values.shape[0] // 8, 8, values.shape[1]), 0)


def loop_sums(total, channels, count, body, base=0):
    def run(at, carry):
        found = body(pl.ds(pl.multiple_of(base + at * CHUNK, CHUNK), CHUNK))
        return tuple(kept + folded(one) for kept, one in zip(carry, found))

    start = tuple(jnp.zeros((8, channels), F32) for _ in range(count))
    return [jnp.sum(one, 0, keepdims=True) for one in lax.fori_loop(0, total // CHUNK, run, start)]


def merge(slots, sizes, channels):
    count = slots.shape[0]
    size, mean = None, None
    for at in range(count):
        weight = sizes[at, :, :channels]
        term = slots[at, 0:1, :] * weight
        size = weight if size is None else size + weight
        mean = term if mean is None else mean + term
    mean = mean / size
    spread = None
    for at in range(count):
        gap = slots[at, 0:1, :] - mean
        term = slots[at, 1:2, :] + sizes[at, :, :channels] * gap * gap
        spread = term if spread is None else spread + term
    return mean, spread, size


def add_up(slots):
    total = slots[0]
    for at in range(1, slots.shape[0]):
        total = total + slots[at]
    return total[0:1, :], total[1:2, :]


def swap_sums(mail, place, slots, meanwhile=None):
    own = slots.at[place.batch]
    copies = [mail.send(own, own, peer) for peer in place.others]
    if meanwhile is not None:
        meanwhile()
    for copy in copies:
        copy.wait_recv()


def swap_tile_sums(mail, place, slots):
    own = slots.at[place.blk]
    copies = [mail.send(own, own, peer) for peer in place.tiles]
    for copy in copies:
        copy.wait_recv()


def local_stats(pre, mask, base, total, channels, size):
    def first(rows):
        return (pre[rows, :] * mask[at_base(base, rows), :],)

    (summed,) = loop_sums(total, channels, 1, first)
    mean = summed / jnp.maximum(size, 1.0)

    def second(rows):
        gap = pre[rows, :] - mean
        return (gap * gap * mask[at_base(base, rows), :],)

    (spread,) = loop_sums(total, channels, 1, second)
    return mean, spread


def at_base(base, rows):
    if base is None:
        return rows
    return pl.ds(pl.multiple_of(base + rows.start, CHUNK), rows.size)


def batch_norm_stats(mail, place, pre, mask, slots, sizes, stats, row, channels, meanwhile=None):
    total = pre.shape[0]
    mean, spread = local_stats(pre, mask, None, total, channels, sizes[place.batch, :, :channels])
    slots[place.batch] = jnp.concatenate([mean, spread], 0)
    swap_sums(mail, place, slots, meanwhile)
    keep_stats(slots, sizes, stats, row, channels)


def keep_stats(slots, sizes, stats, row, channels):
    mean, spread, size = merge(slots, sizes, channels)
    stats[row : row + 1, :channels] = mean
    stats[row + 1 : row + 2, :channels] = lax.rsqrt(spread / size + EPSILON)


def silu(values):
    return values * jax.nn.sigmoid(values)


def widen(cells, left, right, total):
    def body(rows):
        seen = cells[pl.ds(pl.multiple_of(rows.start + PITCH - 16, 16), CHUNK + 32), :].astype(F32)
        here = pl.ds(pl.multiple_of(rows.start + PITCH, 16), CHUNK)
        left[here, :] = seen[15 : 15 + CHUNK].astype(BF16)
        right[here, :] = seen[17 : 17 + CHUNK].astype(BF16)

    loop(total, CHUNK, body)


def clear_ends(cells, total):
    zeros = jnp.zeros((PITCH, cells.shape[1]), cells.dtype)
    cells[0:PITCH, :] = zeros
    cells[PITCH + total : 2 * PITCH + total, :] = zeros


def conv_rows(shifted, rows, weight, back, offsets=range(9)):
    total = None
    for offset in offsets:
        row, col = offset // 3, offset % 3
        if back:
            row, col = 2 - row, 2 - col
        window = shifted[col][pl.ds(pl.multiple_of(rows.start + PITCH * row, 16), rows.size), :]
        product = weight(offset, window)
        total = product if total is None else total + product
    return total


def sum_over_tiles(mail, place, part, near_in, pair, far_in, total, out, meanwhile=None, produce=None):
    mine_far, mine = part(place.blk ^ 2), part(place.blk)
    pieces = pieces_of(total)
    near_far, near_own, far = [], [], []

    def pairs(rows):
        pair[rows, :] = (mine_far[rows, :].astype(F32) + near_in[0, rows, :].astype(F32)).astype(BF16)

    def pass_on(at):
        first, size = pieces[at]
        near_far[at].wait_recv()
        loop(size, CHUNK, pairs, first)
        here = pl.ds(first, size)
        far.append(mail.send(pair.at[here], far_in.at[here], place.across))

    for at, (first, size) in enumerate(pieces):
        if produce is not None:
            produce(first, size)
        here = pl.ds(first, size)
        near_far.append(mail.send(part(place.blk ^ 3).at[here], near_in.at[0, here], place.mate))
        near_own.append(mail.send(part(place.blk ^ 1).at[here], near_in.at[1, here], place.mate))
        if at > 0:
            pass_on(at - 1)
    pass_on(len(pieces) - 1)
    if meanwhile is not None:
        meanwhile()

    def finish(rows):
        out[rows, :] = (
            mine[rows, :].astype(F32) + near_in[1, rows, :].astype(F32) + far_in[rows, :].astype(F32)
        )

    for at, (first, size) in enumerate(pieces):
        near_own[at].wait_recv()
        far[at].wait_recv()
        loop(size, CHUNK, finish, first)


def start_kernel(
    images,
    weight,
    small,
    spatial_own,
    pair,
    head_all,
    feat,
    mask,
    sizes,
    tile_sizes,
    full,
    smalls,
    targets,
    wide,
    spatial,
    pre_one,
    stats,
    head_own,
    slots_tile,
    slots_one,
    sems,
):
    place = Place(images)
    mail = Mail(sems)
    blk, batch = place.blk, place.batch
    depth = weight.shape[0]
    half = depth // 2
    mid = weight.shape[1]
    tile = feat.shape[0]
    slim = mid // 4
    share = spatial_own.shape[1]
    mine = pl.ds(pl.multiple_of(lax.rem(blk, 2) * half, half), half)
    greet(place.others + place.tiles)
    here = mail.local(weight, full.at[batch])
    here_small = mail.local(small, smalls.at[batch])
    here_head = mail.local(head_all.at[blk], head_own)
    z_copies, x_copies, arrived, late = {}, [], [], []
    for peer in place.others:
        late.append(mail.send(small, smalls.at[batch], peer))
    for mask_z in range(1, images // 2):
        z_copies[mask_z] = mail.send(
            weight.at[mine], full.at[batch, mine], (blk, batch ^ (2 * mask_z))
        )
    x_copies.append(mail.send(weight.at[mine], full.at[batch, mine], place.side))
    lanes = pl.ds(pl.multiple_of(blk * slim, slim), slim)
    got_spatial = Spread(
        mail,
        place,
        spatial_own.at[:, :, lanes],
        lambda index: spatial.at[:, pl.ds(pl.multiple_of(index * share, share), share), :],
    ).start()

    def columns(index):
        return feat.at[:, pl.ds(pl.multiple_of(index * mid, mid), mid)]

    landing = wide.at[pl.ds(pl.multiple_of(blk * tile, tile), tile), :]
    here_wide = mail.local(columns(blk), landing)
    line = targets.at[:, pl.ds(pl.multiple_of(blk * tile, tile), tile)]
    here_line = mail.local(pair, line)
    for mask_t in range(1, 4):
        late.append(mail.send(pair, line, (blk ^ mask_t, batch)))
        late.append(mail.send(columns(blk ^ mask_t), landing, (blk ^ mask_t, batch)))

    def hand_over(source):
        block = full.at[source, mine]
        arrived.append(mail.send(block, block, place.mate))

    for mask_z in range(1, images // 2):
        z_copies[mask_z].wait_recv()
        source = batch ^ (2 * mask_z)
        block = full.at[source, mine]
        x_copies.append(mail.send(block, block, place.side))
        hand_over(source)
    for mask_z in range(images // 2):
        x_copies[mask_z].wait_recv()
        hand_over(batch ^ (2 * mask_z + 1))
    stats[...] = jnp.zeros_like(stats)
    here.wait()
    for copy in arrived:
        copy.wait_recv()

    def reduce(rows):
        total = None
        for index in range(images):
            product = dot(feat[rows, index * depth : (index + 1) * depth], full[index])
            total = product if total is None else total + product
        pre_one[rows, :] = total

    loop(tile, tile // 2, reduce)
    base = blk * tile
    mean, spread = local_stats(pre_one, mask, base, tile, mid, tile_sizes[blk, :, :])
    slots_tile[blk] = jnp.concatenate([mean, spread], 0)
    swap_tile_sums(mail, place, slots_tile)
    mean, spread, _ = merge(slots_tile, tile_sizes, mid)
    slots_one[batch] = jnp.concatenate([mean, spread], 0)
    swap_sums(mail, place, slots_one, got_spatial.forward)
    keep_stats(slots_one, sizes, stats, 0, mid)
    got_spatial.finish()
    for copy in late:
        copy.wait_recv()
    here_small.wait()
    here_wide.wait()
    here_line.wait()
    here_head.wait()
    mail.close()


def begin(nb, weight, small, spatial, pair, heads, feat, mask, sizes, tile_sizes):
    depth, mid = weight.shape
    tile = feat.shape[0]

    def array(*shape, kind=BF16):
        return jax.ShapeDtypeStruct(shape, kind)

    return pl.pallas_call(
        functools.partial(start_kernel, nb),
        out_shape=(
            array(nb, depth, mid),
            array(nb, *small.shape),
            array(8, 4 * tile, kind=F32),
            array(4 * tile, mid),
            array(9, mid, mid // 4),
            array(tile, mid, kind=F32),
            array(8, mid, kind=F32),
            array(*heads.shape[1:]),
        ),
        in_specs=[ANY] * 5 + [VMEM] * 4,
        out_specs=(VMEM, ANY, ANY, VMEM, VMEM, VMEM, VMEM, ANY),
        scratch_shapes=[
            pltpu.VMEM((4, 2, mid), F32),
            pltpu.VMEM((nb, 2, mid), F32),
            DMA((2, 64)),
        ],
        cost_estimate=LONG,
        compiler_params=pltpu.CompilerParams(
            collective_id=21, has_side_effects=True, vmem_limit_bytes=40 * 2**20
        ),
    )(weight, small, spatial, pair, heads, feat, mask, sizes, tile_sizes)


def forward_kernel(
    images,
    early,
    pre_one,
    first_stats,
    spatial,
    wide,
    mask,
    norms,
    sizes,
    last_own,
    shared_own,
    gate_own,
    message_own,
    last,
    shared,
    gate,
    message,
    act_one,
    act_two,
    act_three,
    shared_act,
    pre_two,
    pre_three,
    pre_four,
    stats,
    one_left,
    one_right,
    parts,
    near_in,
    pair,
    far_in,
    slots_two,
    slots_three,
    slots_four,
    sems,
):
    place = Place(images)
    mail = Mail(sems)
    blk, batch = place.blk, place.batch
    tile, total = pre_one.shape[0], mask.shape[0]
    mid = pre_one.shape[1]
    slim = pre_two.shape[1]
    share = last_own.shape[0]
    base = blk * tile
    greet(place.others + place.tiles)

    def rows_of(index):
        return pl.ds(pl.multiple_of(index * share, share), share)

    def slim_lanes(index):
        return pl.ds(pl.multiple_of(index * slim, slim), slim)

    lanes = slim_lanes(blk)
    wide_lanes = pl.ds(pl.multiple_of(blk * mid, mid), mid)
    got_last = Spread(mail, place, last_own.at[:, wide_lanes], lambda index: last.at[rows_of(index), :])
    got_shared = Spread(mail, place, shared_own, lambda index: shared.at[rows_of(index), :])
    got_gate = Spread(mail, place, gate_own.at[blk], lambda index: gate.at[rows_of(index), :])
    got_message = [
        Spread(
            mail,
            place,
            message_own.at[blk, offset],
            lambda index, offset=offset: message.at[offset, rows_of(index), :],
        )
        for offset in range(early)
    ]
    got_last.start()
    got_shared.start()
    stats[...] = first_stats[...]
    clear_ends(act_one, total)
    clear_ends(shared_act, total)
    clear_ends(one_left, total)
    clear_ends(one_right, total)

    def act_first(rows):
        value = (pre_one[rows, :] - stats[0:1, :]) * stats[1:2, :] * norms[0:1, :] + norms[1:2, :]
        value = silu(value) * mask[at_base(base, rows), :]
        act_one[pl.ds(pl.multiple_of(PITCH + base + rows.start, 16), CHUNK), :] = value.astype(BF16)

    share_pieces(
        mail,
        place,
        lambda index, first, size: act_one.at[
            pl.ds(pl.multiple_of(PITCH + index * tile + first, 16), size), :
        ],
        tile,
        lambda first, size: loop(size, CHUNK, act_first, first),
    )
    widen(act_one, one_left, one_right, total)
    got_last.forward()
    got_shared.forward()

    shifted = (one_left, act_one, one_right)

    def conv_two(rows):
        pre_two[rows, :] = conv_rows(
            shifted, rows, lambda offset, window: dot(window, spatial[offset]), False
        )

    loop(total, BLOCK, conv_two)

    def after_two():
        got_gate.start()
        got_message[0].start()
        got_message[1].start()

    batch_norm_stats(mail, place, pre_two, mask, slots_two, sizes, stats, 2, slim, after_two)

    def act_second(rows):
        value = (pre_two[rows, :] - stats[2:3, :slim]) * stats[3:4, :slim]
        value = silu(value * norms[2:3, :slim] + norms[3:4, :slim]) * mask[rows, :]
        act_two[rows, lanes] = value.astype(BF16)

    got_last.finish()

    def expand(rows):
        pre_three[rows, :] = dot(act_two[rows, :], last[...])

    share_pieces(
        mail,
        place,
        lambda index, first, size: act_two.at[pl.ds(first, size), slim_lanes(index)],
        total,
        lambda first, size: loop(size, CHUNK, act_second, first),
        lambda first, size: loop(size, BLOCK, expand, first),
    )
    got_gate.forward()

    def after_three():
        got_message[0].forward()
        got_message[1].forward()
        got_message[2].start()
        got_message[3].start()

    batch_norm_stats(mail, place, pre_three, mask, slots_three, sizes, stats, 4, mid, after_three)
    got_shared.finish()

    def act_third(rows):
        normed = (pre_three[rows, :] - stats[4:5, :]) * stats[5:6, :]
        value = normed * norms[4:5, :] + norms[5:6, :] + wide[rows, :].astype(F32)
        act_three[rows, :] = (silu(value) * mask[rows, :]).astype(BF16)

    loop(total, CHUNK, act_third)

    def reduce(rows):
        parts[rows, :] = dot(act_three[rows, :], shared[...]).astype(BF16)

    sum_over_tiles(
        mail,
        place,
        lambda index: parts.at[:, slim_lanes(index)],
        near_in,
        pair,
        far_in,
        total,
        pre_four,
        None,
        lambda first, size: loop(size, BLOCK, reduce, first),
    )

    def after_four():
        got_message[2].forward()
        got_message[3].forward()
        for later in got_message[4:]:
            later.start()

    batch_norm_stats(mail, place, pre_four, mask, slots_four, sizes, stats, 6, slim, after_four)

    def act_fourth(rows):
        value = (pre_four[rows, :] - stats[6:7, :slim]) * stats[7:8, :slim]
        value = silu(value * norms[6:7, :slim] + norms[7:8, :slim]) * mask[rows, :]
        shared_act[pl.ds(pl.multiple_of(PITCH + rows.start, 16), CHUNK), lanes] = value.astype(BF16)

    share_pieces(
        mail,
        place,
        lambda index, first, size: shared_act.at[pl.ds(PITCH + first, size), slim_lanes(index)],
        total,
        lambda first, size: loop(size, CHUNK, act_fourth, first),
    )
    for later in got_message[4:]:
        later.forward()
    got_gate.finish()
    for one in got_message:
        one.finish()
    mail.close()


def bottleneck(nb, early, pre_one, stats, spatial, wide, mask, norms, sizes, last, shared, gate, message):
    tile, total = pre_one.shape[0], mask.shape[0]
    mid = pre_one.shape[1]
    slim = mid // 4
    padded = total + 2 * PITCH

    def array(*shape, kind=BF16):
        return jax.ShapeDtypeStruct(shape, kind)

    outs = (
        array(mid, mid),
        array(mid, mid),
        array(mid, mid),
        array(early, mid, mid),
        array(padded, mid),
        array(total, mid),
        array(total, mid),
        array(padded, mid),
        array(total, slim, kind=F32),
        array(total, mid, kind=F32),
        array(total, slim, kind=F32),
        array(8, mid, kind=F32),
    )
    return pl.pallas_call(
        functools.partial(forward_kernel, nb, early),
        out_shape=outs,
        in_specs=[VMEM] * 7 + [ANY] * 4,
        out_specs=(VMEM, VMEM, ANY, ANY) + (VMEM,) * 8,
        scratch_shapes=[
            pltpu.VMEM((padded, mid), BF16),
            pltpu.VMEM((padded, mid), BF16),
            pltpu.VMEM((total, mid), BF16),
            pltpu.VMEM((2, total, slim), BF16),
            pltpu.VMEM((total, slim), BF16),
            pltpu.VMEM((total, slim), BF16),
            pltpu.VMEM((nb, 2, slim), F32),
            pltpu.VMEM((nb, 2, mid), F32),
            pltpu.VMEM((nb, 2, slim), F32),
            DMA((2, 192)),
        ],
        cost_estimate=LONG,
        compiler_params=pltpu.CompilerParams(
            collective_id=20, has_side_effects=True, vmem_limit_bytes=60 * 2**20
        ),
    )(pre_one, stats, spatial, wide, mask, norms, sizes, last, shared, gate, message)


class Tiles:
    def __init__(self, mail, place, slot, own=None):
        self.mail, self.place, self.slot, self.own = mail, place, slot, own

    def start(self):
        own, here = self.own, self.slot(self.place.blk)
        if own is None:
            own = here
        else:
            self.mail.open.append(self.mail.local(own, here).wait)
        self.far = self.mail.send(own, here, self.place.across)
        self.near = self.mail.send(own, here, self.place.mate)

    def forward(self):
        self.far.wait_recv()
        passed = self.slot(self.place.blk ^ 2)
        self.last = self.mail.send(passed, passed, self.place.mate)

    def end(self):
        self.near.wait_recv()
        self.last.wait_recv()


class Reduce:
    def __init__(self, mail, place, grad, from_side, summed, from_line, out):
        self.mail, self.place = mail, place
        self.grad, self.from_side, self.summed = grad, from_side, summed
        self.from_line, self.out = from_line, out
        self.side = lax.rem(place.batch, 2)
        self.line = lax.div(place.batch, 2)

    def start(self):
        self.from_x = self.mail.send(self.grad.at[:, 1 - self.side], self.from_side, self.place.side)

    def own_half(self, at):
        return self.grad[at, self.side]

    def add_side(self):
        self.from_x.wait_recv()
        lines = self.from_side.shape[0]
        for at in range(lines):
            self.summed[at] = (self.own_half(at).astype(F32) + self.from_side[at].astype(F32)).astype(BF16)

    def middle(self):
        self.add_side()
        self.send_lines()

    def send_lines(self):
        place = self.place
        lines = self.summed.shape[0]
        self.copies = [
            self.mail.send(
                self.summed.at[self.line ^ mask],
                self.from_line.at[mask - 1],
                (place.blk, place.batch ^ (2 * mask)),
            )
            for mask in range(1, lines)
        ]

    def finish(self):
        total = self.summed[self.line].astype(F32)
        for at, copy in enumerate(self.copies):
            copy.wait_recv()
            total = total + self.from_line[at].astype(F32)
        self.out[...] = total.astype(BF16)


class ReduceFar(Reduce):
    def start(self):
        super().start()
        self.fetch = self.mail.local(self.grad.at[:, self.side], self.summed)

    def own_half(self, at):
        if at == 0:
            self.fetch.wait()
        return self.summed[at]


class Job:
    def __init__(self, reduce, tiles):
        self.steps = []
        if reduce is not None:
            self.steps += [reduce.start, reduce.middle, reduce.finish]
        if tiles is not None:
            self.steps += [tiles.start, tiles.forward, tiles.end]


def step(*jobs):
    for job in jobs:
        if job.steps:
            job.steps.pop(0)()


def reduce_scratch(lines, share, columns, own):
    found = [pltpu.VMEM((lines, 2, share, columns), BF16)] if own else []
    return found + [
        pltpu.VMEM((lines, share, columns), BF16),
        pltpu.VMEM((lines, share, columns), BF16),
        pltpu.VMEM((lines - 1, share, columns), BF16),
    ]


def send_sums(mail, place, slots, sums):
    slots[place.batch] = jnp.concatenate(sums, 0)
    own = slots.at[place.batch]
    return [mail.send(own, own, peer) for peer in place.others]


def silu_back(value):
    sigmoid_value = jax.nn.sigmoid(value)
    return sigmoid_value * (1.0 + value * (1.0 - sigmoid_value))


def norm_back(stats, norms, mask, grad, pre, row, channels, lead, offset=None, skip=None, rows_of=None):
    def body(rows):
        normed = (pre[rows, :] - stats[row : row + 1, :channels]) * stats[row + 1 : row + 2, :channels]
        value = normed * norms[row : row + 1, :channels] + norms[row + 1 : row + 2, :channels]
        if skip is not None:
            value = value + skip[rows, :].astype(F32)
        found = lead(rows) * mask[at_base(offset, rows), :] * silu_back(value)
        grad[rows, :] = found
        return found, found * normed

    first, size = (0, pre.shape[0]) if rows_of is None else rows_of
    return loop_sums(size, channels, 2, body, first)


def through(stats, norms, mask, sizes, grad, pre, row, channels, bias_sum, gain_sum, put, offset=None, rows_of=None):
    count = sizes[0, :, :channels]
    for at in range(1, sizes.shape[0]):
        count = count + sizes[at, :, :channels]
    scale = stats[row + 1 : row + 2, :channels] * norms[row : row + 1, :channels]
    bias_part, gain_part = bias_sum / count, gain_sum / count

    def body(rows):
        normed = (pre[rows, :] - stats[row : row + 1, :channels]) * stats[row + 1 : row + 2, :channels]
        found = scale * (grad[rows, :] - bias_part - normed * gain_part)
        put(rows, (found * mask[at_base(offset, rows), :]).astype(BF16))

    first, size = (0, pre.shape[0]) if rows_of is None else rows_of
    loop(size, CHUNK, body, first)


def backward_kernel(
    images,
    back,
    pre_one,
    pre_two,
    pre_three,
    pre_four,
    stats,
    norms,
    mask,
    sizes,
    wide,
    act_one,
    act_two,
    act_three,
    spatial,
    last,
    shared,
    first,
    gate_grads,
    stream_grads,
    message_share,
    head_grads,
    task_sums,
    grad_input,
    share_shared,
    share_first,
    all_last,
    all_spatial,
    all_gates,
    all_stream,
    all_heads,
    all_messages,
    all_sums,
    near_four,
    pair_four,
    far_four,
    grad_four,
    all_four,
    grad_three,
    low_three,
    low_joined,
    joined_rows,
    near_two,
    pair_two,
    far_two,
    grad_two,
    two_left,
    two_here,
    two_right,
    turned,
    strip,
    near_one,
    pair_one,
    far_one,
    grad_one,
    all_one,
    slots_four,
    slots_three,
    slots_two,
    slots_tile,
    slots_one,
    *rest,
):
    place = Place(images)
    sems = rest[-1]
    mail = Mail(sems)
    blk, batch = place.blk, place.batch
    tile, total = pre_one.shape[0], mask.shape[0]
    mid = pre_one.shape[1]
    slim = pre_two.shape[1]
    base = blk * tile
    red_shared = Reduce(mail, place, *rest[0:4], share_shared)
    red_last = Reduce(mail, place, *rest[4:8], all_last.at[blk])
    red_first = Reduce(mail, place, *rest[8:12], share_first)
    red_spatial = Reduce(mail, place, *rest[12:16], all_spatial.at[blk])
    red_gates = Reduce(mail, place, gate_grads, *rest[16:19], all_gates.at[blk])
    red_stream = Reduce(mail, place, stream_grads, *rest[19:22], all_stream.at[blk])
    share = share_shared.shape[0]
    results, sums_out, at = rest[22], rest[23], 24
    heads, messages = [], []

    def tiles_of(slots, first_row, count, own):
        rows_at = pl.ds(first_row, count)
        return Tiles(mail, place, lambda index: slots.at[index, rows_at], own)

    def slots_of(slots):
        return Tiles(mail, place, lambda index: slots.at[index])

    kept = head_grads.shape[0]
    for offset in range(kept):
        result = results.at[offset]
        reduce = ReduceFar(mail, place, head_grads.at[offset], *rest[at : at + 3], result)
        at += 3
        heads.append(Job(reduce, tiles_of(all_heads, offset * share, share, result)))
    heads += [Job(None, None)] * (9 - kept)
    early = message_share.shape[0] // share
    ends = [0, early // 3, 2 * early // 3, early]
    for begin_at, end_at in zip(ends[:-1], ends[1:]):
        count = (end_at - begin_at) * share
        own = message_share.at[pl.ds(begin_at * share, count)]
        messages.append(Job(None, tiles_of(all_messages, begin_at * share, count, own)))
    job_shared, job_first = Job(red_shared, None), Job(red_first, None)
    job_sums = Job(None, Tiles(mail, place, lambda index: all_sums.at[index], sums_out))
    job_last, job_spatial = Job(red_last, slots_of(all_last)), Job(red_spatial, slots_of(all_spatial))
    job_gates, job_stream = Job(red_gates, slots_of(all_gates)), Job(red_stream, slots_of(all_stream))
    greet(place.others + place.tiles)

    def slim_lanes(index):
        return pl.ds(pl.multiple_of(index * slim, slim), slim)

    def tile_rows(index):
        return pl.ds(pl.multiple_of(index * tile, tile), tile)

    def keep(row, bias_sum, gain_sum, channels):
        sums_out[row : row + 1, :channels] = gain_sum
        sums_out[row + 1 : row + 2, :channels] = bias_sum

    sums_out[...] = jnp.zeros_like(sums_out)
    sums_out[8:10, :] = task_sums[0:2, :]
    for cells in (two_left, two_here, two_right):
        clear_ends(cells, total)
    step(heads[0], heads[1], job_gates, job_stream)

    sum_over_tiles(
        mail, place, lambda index: back.at[:, slim_lanes(index)], near_four, pair_four, far_four, total, grad_four
    )
    sums = norm_back(stats, norms, mask, grad_four, pre_four, 6, slim, lambda rows: grad_four[rows, :])
    copies = send_sums(mail, place, slots_four, sums)
    step(heads[0], heads[1], job_gates, job_stream)
    step(heads[2], heads[3], heads[4])
    for offset in range(9):
        turned[offset * slim : (offset + 1) * slim, :] = spatial[offset].T
    for copy in copies:
        copy.wait_recv()
    bias_sum, gain_sum = add_up(slots_four)
    keep(6, bias_sum, gain_sum, slim)
    lanes = slim_lanes(blk)

    def put_four(rows, value):
        all_four[rows, lanes] = value

    def joined_back(rows):
        return dot_t(all_four[rows, :], shared[...])

    sums = []

    def make_four(first, size):
        through(
            stats, norms, mask, sizes, grad_four, pre_four, 6, slim, bias_sum, gain_sum, put_four, None, (first, size)
        )

    def use_four(first, size):
        sums.append(
            norm_back(
                stats, norms, mask, grad_three, pre_three, 4, mid, joined_back, None, wide, (first, size)
            )
        )

    share_pieces(
        mail,
        place,
        lambda index, first, size: all_four.at[pl.ds(first, size), slim_lanes(index)],
        total,
        make_four,
        use_four,
    )
    step(messages[0])
    sums = [sum(one[1:], one[0]) for one in zip(*sums)]
    copies = send_sums(mail, place, slots_three, sums)
    step(heads[2], heads[3], heads[4])
    step(heads[5], heads[6])
    step(heads[0], heads[1], job_gates, job_stream)
    step(messages[0])
    grads, lines = red_shared.grad, red_shared.grad.shape[0]
    grads[...] = t_dot(act_three[...], all_four[...]).astype(BF16).reshape(grads.shape)
    step(job_shared)

    def lower(rows):
        low_joined[rows, :] = grad_three[rows, :].astype(BF16)

    loop(total, CHUNK, lower)
    for copy in copies:
        copy.wait_recv()
    bias_sum, gain_sum = add_up(slots_three)
    keep(4, bias_sum, gain_sum, mid)

    def put_three(rows, value):
        low_three[rows, :] = value

    def two_part(rows):
        all_four[rows, :] = dot_t(low_three[rows, :], last[...]).astype(BF16)

    def make_two(first, size):
        through(
            stats, norms, mask, sizes, grad_three, pre_three, 4, mid, bias_sum, gain_sum, put_three, None, (first, size)
        )
        loop(size, BLOCK, two_part, first)

    sum_over_tiles(
        mail,
        place,
        lambda index: all_four.at[:, slim_lanes(index)],
        near_two,
        pair_two,
        far_two,
        total,
        grad_two,
        None,
        make_two,
    )
    step(messages[1])
    landing = joined_rows.at[:, pl.ds(pl.multiple_of(blk * mid, mid), mid)]
    joined_here = mail.local(low_joined.at[tile_rows(blk)], landing)
    joined_copies = [
        mail.send(low_joined.at[tile_rows(blk ^ mask_t)], landing, (blk ^ mask_t, batch))
        for mask_t in range(1, 4)
    ]
    sums = norm_back(stats, norms, mask, grad_two, pre_two, 2, slim, lambda rows: grad_two[rows, :])
    copies = send_sums(mail, place, slots_two, sums)
    step(heads[5], heads[6], job_shared)
    step(heads[7], heads[8])
    step(heads[2], heads[3], heads[4])
    grads = red_last.grad
    grads[...] = t_dot(act_two[...], low_three[...]).astype(BF16).reshape(grads.shape)
    step(job_last)
    for copy in copies:
        copy.wait_recv()
    bias_sum, gain_sum = add_up(slots_two)
    keep(2, bias_sum, gain_sum, slim)

    def put_two(rows, value):
        two_here[pl.ds(pl.multiple_of(rows.start + PITCH, 16), CHUNK), :] = value

    through(stats, norms, mask, sizes, grad_two, pre_two, 2, slim, bias_sum, gain_sum, put_two)
    widen(two_here, two_left, two_right, total)
    shifted = (two_left, two_here, two_right)

    def one_part(rows):
        for offset in range(9):
            row, col = 2 - offset // 3, 2 - offset % 3
            window = shifted[col][pl.ds(pl.multiple_of(rows.start + PITCH * row, 16), BLOCK), :]
            strip[:, offset * slim : (offset + 1) * slim] = window
        low_three[rows, :] = dot(strip[...], turned[...]).astype(BF16)

    loop(total, BLOCK, one_part)

    def spatial_grads():
        grads = red_spatial.grad
        for offset in range(9):
            row, col = 2 - offset // 3, 2 - offset % 3
            window = shifted[col][PITCH * row : PITCH * row + total, :]
            found = t_dot(act_one[PITCH : PITCH + total, :], window).astype(BF16)
            grads[:, :, :, offset * slim : (offset + 1) * slim] = found.reshape(grads.shape[:3] + (slim,))
        step(job_spatial)

    sum_over_tiles(
        mail,
        place,
        lambda index: low_three.at[tile_rows(index)],
        near_one,
        pair_one,
        far_one,
        tile,
        grad_one,
        spatial_grads,
    )
    sums = norm_back(stats, norms, mask, grad_one, pre_one, 0, mid, lambda rows: grad_one[rows, :], base)
    slots_tile[blk] = jnp.concatenate(sums, 0)
    swap_tile_sums(mail, place, slots_tile)
    copies = send_sums(mail, place, slots_one, list(add_up(slots_tile)))
    step(messages[1])
    step(messages[2])
    step(heads[0], heads[1], job_gates, job_stream)
    step(heads[7], heads[8], job_last, job_spatial)
    step(heads[5], heads[6], job_shared)
    for copy in copies:
        copy.wait_recv()
    bias_sum, gain_sum = add_up(slots_one)
    keep(0, bias_sum, gain_sum, mid)

    def put_one(rows, value):
        all_one[at_base(base, rows), :] = value

    def make_one(first, size):
        through(
            stats, norms, mask, sizes, grad_one, pre_one, 0, mid, bias_sum, gain_sum, put_one, base, (first, size)
        )

    def inputs_back():
        joined_here.wait()
        for copy in joined_copies:
            copy.wait_recv()

        def input_grads(rows):
            own = all_one[pl.ds(pl.multiple_of(base + rows.start, CHUNK), rows.size), :]
            grad_input[rows, :] = dot_t(own, first[...]) + joined_rows[rows, :].astype(F32)

        loop(tile, tile // 3, input_grads)

    share_pieces(
        mail,
        place,
        lambda index, first, size: all_one.at[
            pl.ds(pl.multiple_of(index * tile + first, CHUNK), size), :
        ],
        tile,
        make_one,
        None,
        inputs_back,
    )
    grads = red_first.grad
    grads[...] = t_dot(wide[...], all_one[...]).astype(BF16).reshape(grads.shape)
    step(job_first)
    step(messages[2], job_sums)
    step(heads[0], heads[1], job_gates, job_stream)
    step(heads[2], heads[3], heads[4], heads[5], heads[6])
    step(job_first)
    step(heads[2], heads[3], heads[4], heads[5], heads[6], job_sums)
    step(heads[7], heads[8], job_last, job_spatial)
    step(heads[7], heads[8], job_last, job_spatial)
    step(job_first)
    step(heads[7], heads[8], job_last, job_spatial)
    for job in messages + heads + [job_gates, job_stream, job_last, job_spatial, job_sums]:
        step(job)
    mail.close()


def bottleneck_back(nb, back, pres, stats, norms, mask, sizes, wide, acts, weights, gate_grads, stream_grads, task_grads):
    tile, total = pres[0].shape[0], mask.shape[0]
    mid = pres[0].shape[1]
    slim = mid // 4
    lines, share = nb // 2, mid // nb
    padded = total + 2 * PITCH
    width = weights[3].shape[0]

    def array(*shape, kind=BF16):
        return jax.ShapeDtypeStruct(shape, kind)

    def vmem(*shape, kind=BF16):
        return pltpu.VMEM(shape, kind)

    scratch = [
        vmem(2, total, slim),
        vmem(total, slim),
        vmem(total, slim),
        vmem(total, slim, kind=F32),
        vmem(total, mid),
        vmem(total, mid, kind=F32),
        vmem(total, mid),
        vmem(total, mid),
        vmem(tile, width),
        vmem(2, total, slim),
        vmem(total, slim),
        vmem(total, slim),
        vmem(total, slim, kind=F32),
        vmem(padded, slim),
        vmem(padded, slim),
        vmem(padded, slim),
        vmem(9 * slim, mid),
        vmem(BLOCK, 9 * slim),
        vmem(2, tile, mid),
        vmem(tile, mid),
        vmem(tile, mid),
        vmem(tile, mid, kind=F32),
        vmem(total, mid),
        vmem(nb, 2, slim, kind=F32),
        vmem(nb, 2, mid, kind=F32),
        vmem(nb, 2, slim, kind=F32),
        vmem(4, 2, mid, kind=F32),
        vmem(nb, 2, mid, kind=F32),
    ]
    for columns in (mid, mid, mid, 9 * slim):
        scratch += reduce_scratch(lines, share, columns, True)
    for columns in (mid, LANES):
        scratch += reduce_scratch(lines, share, columns, False)
    message_share, head_grads, task_sums = task_grads
    kept = head_grads.shape[0]
    scratch += [vmem(kept, share, mid), vmem(16, mid, kind=F32)]
    for _ in range(kept):
        scratch += reduce_scratch(lines, share, mid, False)
    scratch.append(DMA((2, 256)))
    return pl.pallas_call(
        functools.partial(backward_kernel, nb),
        out_shape=(
            array(tile, width, kind=F32),
            array(share, mid),
            array(share, mid),
            array(4, share, mid),
            array(4, share, 9 * slim),
            array(4, share, mid),
            array(4, share, LANES),
            array(4, kept * share, mid),
            array(4, message_share.shape[0], mid),
            array(4, 16, mid, kind=F32),
        ),
        in_specs=[VMEM] * 19 + [ANY] * 2 + [VMEM],
        out_specs=(VMEM,) * 7 + (ANY, ANY, VMEM),
        scratch_shapes=scratch,
        cost_estimate=LONG,
        compiler_params=pltpu.CompilerParams(
            collective_id=22, has_side_effects=True, vmem_limit_bytes=62 * 2**20
        ),
    )(
        back,
        *pres,
        stats,
        norms,
        mask,
        sizes,
        wide,
        *acts,
        *weights,
        gate_grads.reshape(lines, 2, share, mid),
        stream_grads.reshape(lines, 2, share, LANES),
        message_share,
        head_grads.reshape(kept, lines, 2, share, mid),
        task_sums,
    )


def finish_kernel(images, first, shared, rest, first_rows, shared_rows, all_rest, sems):
    place = Place(images)
    mail = Mail(sems)
    blk, batch = place.blk, place.batch
    target = (lax.rem(batch, 4), 2 * blk + lax.div(batch, 4))
    source = (lax.div(batch, 2), 4 * lax.rem(batch, 2) + blk)
    stays = (target[0] == blk) & (target[1] == batch)
    moves = jnp.logical_not(stays)
    barrier = pltpu.get_barrier_semaphore()
    for peer in (place.mate, place.across):
        pl.semaphore_signal(barrier, inc=1, device_id=peer, device_id_type=MESH)

    @pl.when(moves)
    def _():
        pl.semaphore_signal(barrier, inc=1, device_id=source, device_id_type=MESH)
        pl.semaphore_wait(barrier, 3)

    @pl.when(stays)
    def _():
        pl.semaphore_wait(barrier, 2)

    def hop(at, own, slots):
        return pltpu.make_async_remote_copy(
            src_ref=own,
            dst_ref=slots.at[target[0]],
            send_sem=sems.at[0, at],
            recv_sem=sems.at[1, at],
            device_id=target,
            device_id_type=MESH,
        )

    def stay(at, own, slots):
        return pltpu.make_async_copy(own, slots.at[blk], sems.at[0, at])

    mail.used = 2
    pairs = [(0, first, first_rows), (1, shared, shared_rows)]

    @pl.when(moves)
    def _():
        for pair in pairs:
            hop(*pair).start()

    @pl.when(stays)
    def _():
        for pair in pairs:
            stay(*pair).start()

    tiles = Tiles(mail, place, lambda index: all_rest.at[index], rest)
    tiles.start()
    jobs = [Tiles(mail, place, lambda index, slots=slots: slots.at[index]) for _, _, slots in pairs]

    @pl.when(moves)
    def _():
        for pair in pairs:
            hop(*pair).wait()

    @pl.when(stays)
    def _():
        for pair in pairs:
            stay(*pair).wait()

    for job in jobs:
        job.start()
    for job in [tiles] + jobs:
        job.forward()
    for job in [tiles] + jobs:
        job.end()
    mail.close()


def finish(nb, first, shared, rest):
    share, mid = first.shape
    return pl.pallas_call(
        functools.partial(finish_kernel, nb),
        out_shape=(
            jax.ShapeDtypeStruct((4, share, mid), BF16),
            jax.ShapeDtypeStruct((4, share, mid), BF16),
            jax.ShapeDtypeStruct((4,) + rest.shape, BF16),
        ),
        in_specs=[ANY] * 3,
        out_specs=(ANY,) * 3,
        scratch_shapes=[DMA((2, 32))],
        compiler_params=pltpu.CompilerParams(collective_id=26, has_side_effects=True),
    )(first, shared, rest)


def task_kernel(
    images,
    early,
    shared_act,
    mask,
    mask_line,
    targets,
    sizes,
    norms,
    head,
    message_start,
    gate,
    to_depth,
    to_classes,
    from_gated,
    message_own,
    streams,
    slopes,
    pre_five,
    stats,
    grad_msg,
    grad_gate,
    gate_grads,
    stream_grads,
    message_grads,
    message_rest,
    message_end,
    left,
    right,
    task,
    messages,
    opened,
    gated,
    slots,
    slots_five,
    sems,
):
    place = Place(images)
    mail = Mail(sems)
    total = mask.shape[0]
    mid = pre_five.shape[1]
    is_first, is_last = place.blk == 0, place.blk == 3
    greet(place.others + [place.mate, place.across])
    late = message_end.shape[0]
    share = message_own.shape[2]
    got = [
        Spread(
            mail,
            place,
            message_own.at[place.blk, 9 - late + at],
            lambda index, at=at: message_end.at[at, pl.ds(pl.multiple_of(index * share, share), share), :],
        )
        for at in range(late)
    ]
    for one in got[: (late + 1) // 2]:
        one.start()
    stats[...] = jnp.zeros_like(stats)
    for cells in (left, right, task, grad_msg):
        clear_ends(cells, total)
    widen(shared_act, left, right, total)

    def heads(rows):
        pre_five[rows, :] = conv_rows(
            (left, shared_act, right), rows, lambda offset, window: dot(window, head[offset]), False
        )

    loop(total, BLOCK, heads)

    def behind():
        for one in got[: (late + 1) // 2]:
            one.forward()
        for one in got[(late + 1) // 2 :]:
            one.start()

    batch_norm_stats(mail, place, pre_five, mask, slots_five, sizes, stats, 0, mid, behind)
    for one in got[(late + 1) // 2 :]:
        one.forward()

    def act_task(rows):
        value = (pre_five[rows, :] - stats[0:1, :]) * stats[1:2, :] * norms[0:1, :] + norms[1:2, :]
        task[pl.ds(pl.multiple_of(PITCH + rows.start, 16), CHUNK), :] = (
            silu(value) * mask[rows, :]
        ).astype(BF16)

    loop(total, CHUNK, act_task)
    widen(task, left, right, total)

    def message_weight(offset):
        if offset < early:
            return message_start[offset]
        return head[9 + offset - early] if offset < 9 - late else message_end[offset - 9 + late]

    def here(rows):
        return pl.ds(pl.multiple_of(PITCH + rows.start, 16), rows.size)

    def start_messages(rows):
        messages[rows, :] = conv_rows(
            (left, task, right),
            rows,
            lambda offset, window: dot(window, message_weight(offset)),
            False,
            range(9 - late),
        )
        opened[rows, :] = jax.nn.sigmoid(dot(task[here(rows), :], gate[...]))

    loop(total, BLOCK, start_messages)
    for one in got:
        one.finish()

    def send_messages(rows):
        messages[rows, :] += conv_rows(
            (left, task, right),
            rows,
            lambda offset, window: dot(window, message_weight(offset)),
            False,
            range(9 - late, 9),
        )
        own = task[here(rows), :]
        part = (opened[rows, :] * messages[rows, :]).astype(BF16)
        gated[rows, :] = part
        depth_part = jnp.where(is_first, own, part)
        sem_part = jnp.where(is_last, own, part)
        slots[place.blk, :, rows] = dot_t(to_depth[...], depth_part) + dot_t(to_classes[...], sem_part)

    loop(total, BLOCK, send_messages)
    share_tiles(mail, place, lambda index: slots.at[index])
    classes = to_depth.shape[0]
    kind = lax.broadcasted_iota(jnp.int32, (classes, 2 * BLOCK), 0)

    def compare(rows):
        value = slots[0, :, rows] + slots[1, :, rows] + slots[2, :, rows] + slots[3, :, rows]
        streams[:, rows] = value
        is_class = (kind >= 1) & (kind <= CLASSES)
        top = jnp.max(jnp.where(is_class, value, -jnp.inf), 0, keepdims=True)
        power = jnp.where(is_class, jnp.exp(value - top), 0.0)
        chance = power / jnp.sum(power, 0, keepdims=True)
        label = targets[1:2, rows]
        chance = chance - jnp.where((kind - 1).astype(F32) == label, 1.0, 0.0)
        slope = jnp.where(kind == 0, value - targets[0:1, rows], jnp.where(is_class, chance, 0.0))
        slopes[:, rows] = (slope * mask_line[0:1, rows]).astype(BF16)

    loop(total, 2 * BLOCK, compare)
    by_part = dot(slopes[...], gated[...])
    by_task = dot(slopes[...], task[PITCH : PITCH + total, :])
    row = lax.broadcasted_iota(jnp.int32, by_part.shape, 0)
    use_task = ((row == 0) & is_first) | ((row > 0) & is_last)
    found = jnp.where(use_task, by_task, by_part)
    found = jnp.concatenate([found, jnp.zeros((LANES - classes, mid), F32)], 0)
    stream_grads[...] = found.T.astype(BF16)

    def grads(rows):
        grad = t_dot(slopes[:, rows], from_gated[...])
        open_part = opened[rows, :]
        grad_msg[here(rows), :] = (grad * open_part).astype(BF16)
        grad_gate[rows, :] = (grad * messages[rows, :] * open_part * (1.0 - open_part)).astype(BF16)

    loop(total, BLOCK, grads)
    gate_grads[...] = t_dot(task[PITCH : PITCH + total, :], grad_gate[...]).astype(BF16)
    widen(grad_msg, left, right, total)
    shifted = (left, grad_msg, right)
    for offset in range(9):
        row, col = 2 - offset // 3, 2 - offset % 3
        window = shifted[col][PITCH * row : PITCH * row + total, :]
        found = t_dot(task[PITCH : PITCH + total, :], window).astype(BF16)
        if offset < early:
            message_grads[offset] = found
        else:
            message_rest[:, (offset - early) * mid : (offset - early + 1) * mid] = found
    mail.close()


CLASSES = 40


def one_task(nb, early, late, shared_act, mask, mask_line, targets, sizes, norms, weights, streams_weights, own):
    total = mask.shape[0]
    padded, mid = shared_act.shape
    lines = streams_weights[0].shape[0]

    def array(*shape, kind=BF16):
        return jax.ShapeDtypeStruct(shape, kind)

    def vmem(*shape, kind=BF16):
        return pltpu.VMEM(shape, kind)

    return pl.pallas_call(
        functools.partial(task_kernel, nb, early),
        out_shape=(
            array(lines, total, kind=F32),
            array(lines, total),
            array(total, mid, kind=F32),
            array(8, mid, kind=F32),
            array(padded, mid),
            array(total, mid),
            array(mid, mid),
            array(mid, LANES),
            array(early, mid, mid),
            array(mid, (9 - early) * mid),
            array(late, mid, mid),
        ),
        in_specs=[VMEM] * 12 + [ANY],
        out_specs=(VMEM,) * 11,
        scratch_shapes=[
            vmem(padded, mid),
            vmem(padded, mid),
            vmem(padded, mid),
            vmem(total, mid, kind=F32),
            vmem(total, mid, kind=F32),
            vmem(total, mid),
            vmem(4, lines, total, kind=F32),
            vmem(nb, 2, mid, kind=F32),
            DMA((2, 64)),
        ],
        cost_estimate=LONG,
        compiler_params=pltpu.CompilerParams(
            collective_id=23, has_side_effects=True, vmem_limit_bytes=60 * 2**20
        ),
    )(shared_act, mask, mask_line, targets, sizes, norms, *weights, *streams_weights, own)


def task_back_kernel(
    images,
    early,
    shared_act,
    mask,
    sizes,
    norms,
    head,
    message_start,
    gate,
    message_end,
    from_direct,
    slopes,
    pre_five,
    stats,
    grad_msg,
    grad_gate,
    message_grads,
    back,
    head_grads,
    head_rest,
    message_done,
    sums_out,
    left,
    right,
    grad_five,
    grad,
    slots_five,
    *rest,
):
    place = Place(images)
    mail = Mail(rest[-1])
    sums_of = [
        Reduce(
            mail,
            place,
            message_grads.at[offset],
            *rest[3 * offset : 3 * offset + 3],
            message_done.at[offset],
        )
        for offset in range(early)
    ]
    total = mask.shape[0]
    late = message_end.shape[0]
    mid = pre_five.shape[1]
    greet(place.others)
    sums_out[...] = jnp.zeros_like(sums_out)
    sums_of[0].start()
    sums_of[1].start()
    for cells in (left, right, grad_five):
        clear_ends(cells, total)
    widen(grad_msg, left, right, total)

    def message_weight(offset):
        if offset < early:
            return message_start[offset]
        return head[9 + offset - early] if offset < 9 - late else message_end[offset - 9 + late]

    def task_grads(rows):
        found = conv_rows(
            (left, grad_msg, right), rows, lambda offset, window: dot_t(window, message_weight(offset)), True
        )
        found = found + dot_t(grad_gate[rows, :], gate[...])
        grad[rows, :] = found + t_dot(slopes[:, rows], from_direct[...])

    loop(total, BLOCK, task_grads)
    sums = norm_back(stats, norms, mask, grad, pre_five, 0, mid, lambda rows: grad[rows, :])
    copies = send_sums(mail, place, slots_five, sums)
    sums_of[0].middle()
    sums_of[1].middle()
    for one in sums_of[2:]:
        one.start()
    for copy in copies:
        copy.wait_recv()
    bias_sum, gain_sum = add_up(slots_five)
    sums_out[0:1, :] = gain_sum
    sums_out[1:2, :] = bias_sum

    def put(rows, value):
        grad_five[pl.ds(pl.multiple_of(PITCH + rows.start, 16), CHUNK), :] = value

    through(stats, norms, mask, sizes, grad, pre_five, 0, mid, bias_sum, gain_sum, put)
    widen(grad_five, left, right, total)
    shifted = (left, grad_five, right)

    def head_back(rows):
        back[rows, :] = conv_rows(
            shifted, rows, lambda offset, window: dot_t(window, head[offset]), True
        ).astype(BF16)

    loop(total, BLOCK, head_back)
    for one in sums_of[2:]:
        one.middle()
    sums_of[0].finish()
    sums_of[1].finish()
    for offset in range(9):
        row, col = 2 - offset // 3, 2 - offset % 3
        window = shifted[col][PITCH * row : PITCH * row + total, :]
        found = t_dot(shared_act[PITCH : PITCH + total, :], window).astype(BF16)
        kept = head_grads.shape[0]
        if offset < kept:
            head_grads[offset] = found
        else:
            head_rest[:, (offset - kept) * mid : (offset - kept + 1) * mid] = found
    for one in sums_of[2:]:
        one.finish()
    mail.close()


def one_task_back(nb, early, kept, shared_act, mask, sizes, norms, weights, from_direct, slopes, rest):
    total = mask.shape[0]
    padded, mid = shared_act.shape
    lines, share = nb // 2, mid // nb

    def array(*shape, kind=BF16):
        return jax.ShapeDtypeStruct(shape, kind)

    def vmem(*shape, kind=BF16):
        return pltpu.VMEM(shape, kind)

    return pl.pallas_call(
        functools.partial(task_back_kernel, nb, early),
        out_shape=(
            array(total, mid),
            array(kept, mid, mid),
            array(mid, (9 - kept) * mid),
            array(early, share, mid),
            array(8, mid, kind=F32),
        ),
        in_specs=[VMEM] * 15,
        out_specs=(VMEM,) * 5,
        scratch_shapes=[
            vmem(padded, mid),
            vmem(padded, mid),
            vmem(padded, mid),
            vmem(total, mid, kind=F32),
            vmem(nb, 2, mid, kind=F32),
        ]
        + early * reduce_scratch(lines, share, mid, False)
        + [DMA((2, 48))],
        cost_estimate=LONG,
        compiler_params=pltpu.CompilerParams(
            collective_id=24, has_side_effects=True, vmem_limit_bytes=60 * 2**20
        ),
    )(shared_act, mask, sizes, norms, *weights, from_direct, slopes, *rest)


def last_kernel(shares, sums, all_shares, all_sums, sems):
    place = Place(2)
    mail = Mail(sems)
    blk = place.blk
    greet([place.mate, place.across])
    here = [mail.local(shares, all_shares.at[blk]), mail.local(sums, all_sums.at[blk])]
    both = []
    for source, slots in ((sums, all_sums), (shares, all_shares)):
        far = mail.send(source, slots.at[blk], place.across)
        near = mail.send(source, slots.at[blk], place.mate)
        both.append((far, near, slots))
    for far, near, slots in both:
        far.wait_recv()
        passed = slots.at[blk ^ 2]
        last = mail.send(passed, passed, place.mate)
        near.wait_recv()
        last.wait_recv()
    for copy in here:
        copy.wait()
    mail.close()


def gather_last(shares, sums):
    return pl.pallas_call(
        last_kernel,
        out_shape=(
            jax.ShapeDtypeStruct((4,) + shares.shape, shares.dtype),
            jax.ShapeDtypeStruct((4,) + sums.shape, sums.dtype),
        ),
        in_specs=[ANY] * 2,
        out_specs=(ANY, ANY),
        scratch_shapes=[DMA((2, 16))],
        compiler_params=pltpu.CompilerParams(collective_id=25, has_side_effects=True),
    )(shares, sums)


def on_device(
    nt,
    nb,
    features,
    crop_rows,
    crop_cols,
    depth_target,
    labels,
    first_weight,
    spatial_weight,
    last_weight,
    shared_weight,
    head_weights,
    message_weights,
    gate_weights,
    depth_weight,
    class_weight,
    mid_gain,
    mid_bias,
    out_gain,
    out_bias,
):
    tile_rows, cols, width = features.shape[1:]
    tile = tile_rows * cols
    rows = tile_rows * nt
    pixels = rows * cols
    tasks = head_weights.shape[0]
    mid = first_weight.shape[1]
    share = mid // nb
    slim = mid // nt
    classes = class_weight.shape[1]
    blk, batch = lax.axis_index("blk"), lax.axis_index("batch")

    image_rows = lax.dynamic_index_in_dim(crop_rows, batch, 0, False)
    image_cols = lax.dynamic_index_in_dim(crop_cols, batch, 0, False)
    row_ids = jnp.arange(rows, dtype=jnp.int32)
    col_ids = jnp.arange(PITCH, dtype=jnp.int32)
    inside_grid = (row_ids[:, None] < image_rows) & (col_ids[None, :] < image_cols)
    inside_grid = inside_grid.astype(F32)
    inside_wide = inside_grid.reshape(rows * PITCH, 1)
    inside = inside_grid[:, :cols].reshape(pixels, 1)
    inside_tile = lax.dynamic_slice_in_dim(inside, blk * tile, tile, 0)
    sizes_flat = (crop_rows * crop_cols).astype(F32)
    valid_count = jnp.sum(sizes_flat)
    sizes = jnp.broadcast_to(sizes_flat[:, None, None], (nb, 1, mid))
    tile_counts = jnp.sum(inside.reshape(nt, tile), 1)
    tile_sizes = jnp.broadcast_to(tile_counts[:, None, None], (nt, 1, mid))
    image_size = jnp.maximum(jnp.sum(inside), 1.0)

    params = jnp.concatenate(
        [
            mid_gain.reshape(-1),
            mid_bias.reshape(-1),
            out_gain,
            out_bias,
            depth_weight,
            class_weight.reshape(-1),
        ]
    )
    room = -(-params.shape[0] // (16 * LANES)) * 16 * LANES
    small = jnp.pad(params, (0, room - params.shape[0])).reshape(-1, LANES)
    feat = jnp.pad(features[0], ((0, 0), (0, PITCH - cols), (0, 0))).reshape(tile_rows * PITCH, width)
    piece = shared_weight.shape[0] // nt
    order = [
        (t * nb + b, (b * nt // nb) * nb + (b % (nb // nt)) * nt + t)
        for t in range(nt)
        for b in range(nb)
    ]
    shared_own = lax.ppermute(
        lax.dynamic_slice_in_dim(shared_weight, blk * piece, piece, 0), ("blk", "batch"), order
    )
    pair = jnp.stack([depth_target[0], labels[0].astype(F32)])
    pair = jnp.pad(pair, ((0, 6), (0, 0), (0, PITCH - cols))).reshape(8, tile_rows * PITCH)
    full_first, smalls, targets, wide_features, spatial, pre_one, stats, large = begin(
        nb, first_weight, small, spatial_weight, pair, head_weights, feat, inside_wide, sizes, tile_sizes
    )
    full_first = full_first.reshape(width, mid)
    smalls = smalls.reshape(nb, room)
    at = 0

    def taken(count):
        nonlocal at
        found = smalls[:, at : at + count]
        at += count
        return found

    norms_count = mid_gain.shape[0]
    out_share = out_gain.shape[0]
    gain_mid = taken(norms_count * share).reshape(nb, norms_count, share).swapaxes(0, 1)
    gain_mid = gain_mid.reshape(norms_count, mid).astype(F32)
    bias_mid = taken(norms_count * share).reshape(nb, norms_count, share).swapaxes(0, 1)
    bias_mid = bias_mid.reshape(norms_count, mid).astype(F32)
    gain_out = lax.dynamic_slice_in_dim(taken(out_share).reshape(width), blk * mid, mid, 0).astype(F32)
    bias_out = lax.dynamic_slice_in_dim(taken(out_share).reshape(width), blk * mid, mid, 0).astype(F32)
    full_depth = taken(share).reshape(mid, 1)
    full_classes = taken(share * classes).reshape(mid, classes)

    def slim_of(vector):
        return lax.dynamic_slice_in_dim(vector, blk * slim, slim, 0)

    def filled(vector):
        return jnp.pad(vector, (0, mid - vector.shape[0]))

    gain_two, bias_two = slim_of(gain_mid[1]), slim_of(bias_mid[1])
    gain_four, bias_four = slim_of(gain_mid[2]), slim_of(bias_mid[2])
    norms = jnp.stack(
        [
            gain_mid[0],
            bias_mid[0],
            filled(gain_two),
            filled(bias_two),
            gain_out,
            bias_out,
            filled(gain_four),
            filled(bias_four),
        ]
    )
    early, late = 4, 5
    large = lax.all_gather(large, "batch", axis=1, tiled=True)
    (
        last,
        shared,
        gate,
        message_start,
        act_one,
        act_two,
        act_three,
        shared_act,
        pre_two,
        pre_three,
        pre_four,
        stats,
    ) = bottleneck(
        nb,
        early,
        pre_one,
        stats,
        spatial,
        wide_features,
        inside_wide,
        norms,
        sizes,
        last_weight,
        shared_own,
        gate_weights,
        message_weights,
    )

    task_norms = jnp.stack(
        [
            lax.dynamic_index_in_dim(gain_mid, 3 + blk, 0, False),
            lax.dynamic_index_in_dim(bias_mid, 3 + blk, 0, False),
        ]
    )
    task_norms = jnp.pad(task_norms, ((0, 6), (0, 0)))
    lines = -(-(1 + classes) // 16) * 16
    stream_weight = jnp.concatenate([full_depth, full_classes], 1).T
    stream_weight = jnp.pad(stream_weight, ((0, lines - 1 - classes), (0, 0)))
    is_depth = jnp.arange(lines)[:, None] == 0
    none = jnp.zeros((), BF16)
    is_first, is_last = blk == 0, blk == tasks - 1
    own_stream = jnp.where(is_depth, is_first, is_last)
    to_depth = jnp.where(is_depth, stream_weight, none)
    to_classes = jnp.where(is_depth, none, stream_weight)
    from_gated = jnp.where(own_stream, none, stream_weight)
    from_direct = jnp.where(own_stream, stream_weight, none)
    mask_line = jnp.broadcast_to(inside_wide.reshape(1, -1), (8, rows * PITCH))
    weights = (large, message_start, gate)
    (
        streams,
        slopes,
        pre_five,
        task_stats,
        grad_msg,
        grad_gate,
        gate_grads,
        stream_grads,
        message_grads,
        message_rest,
        message_end,
    ) = one_task(
        nb,
        early,
        late,
        shared_act,
        inside_wide,
        mask_line,
        targets,
        sizes,
        task_norms,
        weights,
        (to_depth, to_classes, from_gated),
        message_weights,
    )
    own_streams = lax.dynamic_slice_in_dim(streams, blk * tile_rows * PITCH, tile_rows * PITCH, 1)
    own_streams = own_streams.reshape(lines, tile_rows, PITCH)[:, :, :cols]
    depth_out = own_streams[0]
    logits = own_streams[1 : 1 + classes].transpose(1, 2, 0)
    rest_share = lax.psum_scatter(message_rest, "batch", scatter_dimension=0, tiled=True)
    message_grads = message_grads.reshape(early, nb // 2, 2, share, mid)
    kept = 7
    back, head_grads, head_rest, message_done, task_sums = one_task_back(
        nb,
        early,
        kept,
        shared_act,
        inside_wide,
        sizes,
        task_norms,
        weights + (message_end,),
        from_direct,
        slopes,
        (pre_five, task_stats, grad_msg, grad_gate, message_grads),
    )
    message_share = message_done.reshape(early * share, mid)
    head_share = lax.psum_scatter(head_rest, "batch", scatter_dimension=0, tiled=True)

    (
        grad_input,
        share_shared,
        share_first,
        all_last,
        all_spatial,
        all_gates,
        all_stream,
        all_heads,
        all_messages,
        sums,
    ) = bottleneck_back(
        nb,
        back,
        (pre_one, pre_two, pre_three, pre_four),
        stats,
        norms,
        inside_wide,
        sizes,
        wide_features,
        (act_one, act_two, act_three),
        (spatial, last, shared, full_first),
        gate_grads,
        stream_grads,
        (message_share, head_grads, task_sums),
    )
    grad_input = grad_input.reshape(tile_rows, PITCH, width)[:, :cols]

    rest_share, head_share, share_first = lax.optimization_barrier((rest_share, head_share, share_first))
    rest_share = jnp.concatenate([rest_share, head_share], 1)
    left = 18 - early - kept
    rest_share = rest_share.reshape(share, left, mid).swapaxes(0, 1).reshape(left * share, mid)
    red_first, red_shared, all_rest = finish(nb, share_first, share_shared, rest_share)
    red_first = red_first.astype(F32).reshape(nt * share, mid)
    red_shared = red_shared.astype(F32).reshape(nt * share, mid)
    all_rest = all_rest.reshape(nt, left, share, mid)
    red_messages = jnp.concatenate(
        [all_messages.reshape(nt, early, share, mid), all_rest[:, : 9 - early]], 1
    ).astype(F32)
    red_last = all_last.astype(F32).transpose(1, 0, 2).reshape(share, width)
    red_gates = all_gates.astype(F32)
    red_spatial = all_spatial.astype(F32).reshape(nt, share, 9, slim)
    red_spatial = red_spatial.transpose(2, 1, 0, 3).reshape(9, share, mid)
    streams_red = jnp.sum(all_stream.astype(F32), 0)
    red_depth = streams_red[:, 0]
    red_classes = streams_red[:, 1 : 1 + classes]
    red_heads = jnp.concatenate(
        [all_heads.reshape(nt, kept, share, mid), all_rest[:, 9 - early :]], 1
    ).astype(F32)
    two_gain, two_bias = sums[:, 2, :slim].reshape(1, mid), sums[:, 3, :slim].reshape(1, mid)
    four_gain, four_bias = sums[:, 6, :slim].reshape(1, mid), sums[:, 7, :slim].reshape(1, mid)
    mid_gains = jnp.concatenate([sums[0, 0:1], two_gain, four_gain, sums[:, 8]], 0)
    mid_biases = jnp.concatenate([sums[0, 1:2], two_bias, four_bias, sums[:, 9]], 0)
    grad_mid_gain = lax.dynamic_slice_in_dim(mid_gains, batch * share, share, 1)
    grad_mid_bias = lax.dynamic_slice_in_dim(mid_biases, batch * share, share, 1)
    grad_out_gain = lax.dynamic_slice_in_dim(sums[:, 4].reshape(width), batch * out_share, out_share, 0)
    grad_out_bias = lax.dynamic_slice_in_dim(sums[:, 5].reshape(width), batch * out_share, out_share, 0)
    return (
        depth_out.reshape(1, tile_rows, cols),
        logits.reshape(1, tile_rows, cols, classes),
        grad_input.reshape(1, tile_rows, cols, width),
        red_first,
        red_spatial,
        red_last,
        red_shared,
        red_heads,
        red_messages,
        red_gates,
        red_depth,
        red_classes,
        grad_mid_gain,
        grad_mid_bias,
        grad_out_gain,
        grad_out_bias,
    )


def solution(mesh):
    nt, nb = mesh.shape["blk"], mesh.shape["batch"]
    placed = (
        P("batch", "blk", None, None),
        P(),
        P(),
        P("batch", "blk", None),
        P("batch", "blk", None),
        P("batch", None),
        P(None, "batch", None),
        P("batch", None),
        P("batch", None),
        P(None, None, "batch", None),
        P(None, None, "batch", None),
        P(None, "batch", None),
        P("batch"),
        P("batch", None),
        P(None, "batch"),
        P(None, "batch"),
        P("batch"),
        P("batch"),
    )
    return jax.shard_map(
        functools.partial(on_device if nb == 8 else on_device_any, nt, nb),
        mesh=mesh,
        in_specs=placed,
        out_specs=(
            P("batch", "blk", None),
            P("batch", "blk", None, None),
            P("batch", "blk", None, None),
            P("batch", None),
            P(None, "batch", None),
            P("batch", None),
            P("batch", None),
            P(None, None, "batch", None),
            P(None, None, "batch", None),
            P(None, "batch", None),
            P("batch"),
            P("batch", None),
            P(None, "batch"),
            P(None, "batch"),
            P("batch"),
            P("batch"),
        ),
        check_vma=False,
    )
```
